32 devices in a mesh: grp: 2 (over x), tract: 16 (over z, y, core).
Axes of the slice: x: 2, y: 2, z: 4, core: 2. Of those that a mesh axis runs over, the one named last changes fastest.
Arguments:
- table: float32 [384, 23, 7, 7, 128], P(('grp', 'tract')), parts along dimension 0, may hold values from 0.25 to 4
- age_sex: float32 [384, 46], P(('grp', 'tract')), parts along dimension 0, may hold values from 1960 to 15680
- race_hisp: float32 [384, 14], P(('grp', 'tract')), parts along dimension 0, may hold values from 6440 to 51520
- size_tenure: float32 [384, 14], P(('grp', 'tract')), parts along dimension 0, may hold values from 6440 to 51520
- tenure_income: float32 [384, 32], P(('grp', 'tract')), parts along dimension 0, may hold values from 2817.5 to 22540
- puma_age: float32 [48, 1472], P('grp'), parts along dimension 0, may hold values from 3920 to 31360
- puma_race: float32 [48, 3136], P('grp'), parts along dimension 0, may hold values from 1840 to 14720
- tract_puma: int32 [384], P(('grp', 'tract')), parts along dimension 0, may hold values from 0 to 23, as said below
Outputs:
- raked: float32 [384, 23, 7, 7, 128], P(('grp', 'tract')), parts along dimension 0
The draws below stay inside these ranges and needn't reach their ends.
There are 2 independent parts, one for each index of `grp`. The reference program is written for one: setup_inputs(seed, part) draws one part's arguments, and reference() takes and returns one part's arrays. A program takes and returns all parts, laid end to end along the dimension named above; each array names one. Nothing has to cross between parts.
Inputs may be any that keep to these rules, and one draw needn't show every extreme that they name: `tract_puma`: each PUMA holds exactly 8 tracts, which may lie anywhere in the tract order.
All inputs are finite; a program needn't handle non-finite values.
Results may differ from the reference program's by a relative error of at most 0.000092.
Values sent between devices are 32-bit elements; how exact they have to be, the bound alone decides.
No kernel may reach another device: no remote copies, remote signals or barrier semaphores. Data moves between devices by JAX's collectives and lax.ppermute only.
A program may use at most 64 MiB of HBM per device.

```python
import math
import jax
import jax.numpy as jnp

AGE = 23
RACE = 7
HHS = 7
INC = 16
TRACTS = 192
PUMAS = 24


def draw_tract_puma(key, part):
    key = jax.random.fold_in(key, 11)
    order = jax.random.permutation(key, TRACTS)
    return (order // 8).astype(jnp.int32)


def level_of(stream_key, dims, shards, smallest, largest):
    level, own = 1.0, jax.random.fold_in(stream_key, 6)
    for dim, blocks in shards:
        steps = jnp.exp(jax.random.uniform(jax.random.fold_in(own, dim), (blocks,), jnp.float32, smallest / len(shards), largest / len(shards)))
        level = level * jnp.repeat(steps, dims[dim] // blocks).reshape([-1 if axis == dim else 1 for axis in range(len(dims))])
    return level


def setup_inputs(seed: int = 0, part: int = 0) -> dict:
    arg_keys = jax.random.split(jax.random.key(seed), 9)
    own_keys = jax.random.split(jax.random.fold_in(arg_keys[8], part), 9)
    return {
        "table": jnp.clip(jnp.exp(math.log(4.0) - 2.7725887 * jax.random.uniform(own_keys[0], (TRACTS, AGE, RACE, HHS, 8 * INC), jnp.float32) ** level_of(own_keys[0], (TRACTS, AGE, RACE, HHS, 8 * INC), ((0, 16),), -0.2, 0.2)), 0.25, 4.0),
        "age_sex": jnp.clip(jnp.exp(math.log(15680.0) - 2.0794415 * jax.random.uniform(own_keys[1], (TRACTS, AGE * 2), jnp.float32) ** level_of(own_keys[1], (TRACTS, AGE * 2), ((0, 16),), -0.2, 0.2)), 1960.0, 15680.0),
        "race_hisp": jnp.clip(jnp.exp(math.log(51520.0) - 2.0794415 * jax.random.uniform(own_keys[2], (TRACTS, RACE * 2), jnp.float32) ** level_of(own_keys[2], (TRACTS, RACE * 2), ((0, 16),), -0.2, 0.2)), 6440.0, 51520.0),
        "size_tenure": jnp.clip(jnp.exp(math.log(51520.0) - 2.0794415 * jax.random.uniform(own_keys[3], (TRACTS, HHS * 2), jnp.float32) ** level_of(own_keys[3], (TRACTS, HHS * 2), ((0, 16),), -0.2, 0.2)), 6440.0, 51520.0),
        "tenure_income": jnp.clip(jnp.exp(math.log(22540.0) - 2.0794415 * jax.random.uniform(own_keys[4], (TRACTS, 2 * INC), jnp.float32) ** level_of(own_keys[4], (TRACTS, 2 * INC), ((0, 16),), -0.2, 0.2)), 2817.5, 22540.0),
        "puma_age": jnp.clip(jnp.exp(jax.random.uniform(own_keys[5], (PUMAS, AGE * 4 * INC), jnp.float32, math.log(3920.0), math.log(31360.0))), 3920.0, 31360.0),
        "puma_race": jnp.clip(jnp.exp(jax.random.uniform(own_keys[6], (PUMAS, RACE * HHS * 4 * INC), jnp.float32, math.log(1840.0), math.log(14720.0))), 1840.0, 14720.0),
        "tract_puma": draw_tract_puma(jax.random.fold_in(jax.random.fold_in(arg_keys[8], part), 71), part),
    }


def rake_tracts(cells, age_sex, race_hisp, size_tenure, tenure_income):
    margin = cells.sum(axis=(2, 3, 5, 6, 7))
    factor = age_sex.reshape(margin.shape) / margin
    cells = cells * factor[:, :, None, None, :, None, None, None]
    margin = cells.sum(axis=(1, 3, 4, 6, 7))
    factor = race_hisp.reshape(margin.shape) / margin
    cells = cells * factor[:, None, :, None, None, :, None, None]
    margin = cells.sum(axis=(1, 2, 4, 5, 7))
    factor = size_tenure.reshape(margin.shape) / margin
    cells = cells * factor[:, None, None, :, None, None, :, None]
    margin = cells.sum(axis=(1, 2, 3, 4, 5))
    factor = tenure_income.reshape(margin.shape) / margin
    cells = cells * factor[:, None, None, None, None, None, :, :]
    return cells


def puma_factor(margin, targets, tract_puma):
    tract_count = margin.shape[0]
    flat_part = margin.reshape(tract_count, -1)
    puma_total = jax.ops.segment_sum(flat_part, tract_puma, num_segments=targets.shape[0])
    factor = (targets / puma_total)[tract_puma]
    return factor.reshape(margin.shape)


def reference(table, age_sex, race_hisp, size_tenure, tenure_income, puma_age, puma_race, tract_puma):
    tract_count, age_bins, race_bins, size_bins, inner = table.shape
    cells = table.reshape(tract_count, age_bins, race_bins, size_bins, 2, 2, 2, inner // 8)
    cells = rake_tracts(cells, age_sex, race_hisp, size_tenure, tenure_income)
    margin = cells.sum(axis=(2, 3, 5))
    factor = puma_factor(margin, puma_age, tract_puma)
    cells = cells * factor[:, :, None, None, :, None, :, :]
    margin = cells.sum(axis=(1, 4))
    factor = puma_factor(margin, puma_race, tract_puma)
    cells = cells * factor[:, None, :, :, None, :, :, :]
    return cells.reshape(table.shape)
```

```python
import functools
import math

import jax
import jax.numpy as jnp
from jax import lax
from jax.experimental import pallas as pl
from jax.experimental.pallas import tpu as pltpu
from jax.sharding import PartitionSpec as P

LANES = 128
SLOT = 16
F32 = jnp.float32
BF16 = jnp.bfloat16


def lane_ids(rows):
    return lax.broadcasted_iota(jnp.int32, (rows, LANES), 1)


def masked_lane_sum(value, mask):
    return jnp.sum(jnp.where(mask, value, 0.0), axis=-1, keepdims=True)


def column_of(row, rows, step, offset):
    width = row.shape[-1]
    lane = lax.broadcasted_iota(jnp.int32, (rows, width), 1)
    sub = lax.broadcasted_iota(jnp.int32, (rows, width), 0)
    return jnp.sum(jnp.where(lane == step * sub + offset, row, 0.0), axis=-1, keepdims=True)


def load_cells(table_ref, cells_ref, sems):
    tracts = table_ref.shape[0]
    for t in range(tracts):
        pltpu.make_async_copy(table_ref.at[t], cells_ref.at[t], sems.at[t]).start()


def wait_cells(table_ref, cells_ref, sems, t):
    pltpu.make_async_copy(table_ref.at[t], cells_ref.at[t], sems.at[t]).wait()


def rake_kernel(
    ids_ref, table_ref, age_sex_ref, race_hisp_ref, size_tenure_ref, tenure_income_ref,
    send_ref, age_factor_ref, cross_factor_ref,
    cells_ref, sum_ref, cross_ref, sems,
    *, races, sizes, block,
):
    tracts, cross, ages, _ = table_ref.shape
    cross_rows = cross_ref.shape[0] // tracts
    load_cells(table_ref, cells_ref, sems)
    lane = lane_ids(1)
    sex0 = lane < 64
    hisp0 = (lane // 32) % 2 == 0
    ten0 = (lane // 16) % 2 == 0

    def add_cross(t, carry):
        wait_cells(table_ref, cells_ref, sems, t)
        total = cells_ref[t, 0]
        for rs in range(1, cross):
            total = total + cells_ref[t, rs]
        sum_ref[t, 0:ages] = total
        return carry

    lax.fori_loop(0, tracts, add_cross, 0)

    for t in range(tracts):
        total = sum_ref[t, 0:ages]
        row = age_sex_ref[t : t + 1, :]
        first = column_of(row, ages, 2, 0) / masked_lane_sum(total, sex0)
        second = column_of(row, ages, 2, 1) / masked_lane_sum(total, ~sex0)
        age_factor_ref[t, 0:ages] = jnp.where(sex0, first, second)

    def add_ages(t, carry):
        factor = age_factor_ref[t, 0:ages]
        base = t * cross_rows
        for rs in range(cross):
            cross_ref[pl.ds(base + rs, 1), :] = jnp.sum(
                cells_ref[t, rs] * factor, axis=0, keepdims=True
            )
        return carry

    lax.fori_loop(0, tracts, add_ages, 0)

    for t in range(tracts):
        base = t * cross_rows
        by_race = cross_ref[pl.ds(base, races, stride=sizes), :]
        for s in range(1, sizes):
            by_race = by_race + cross_ref[pl.ds(base + s, races, stride=sizes), :]
        row = race_hisp_ref[t : t + 1, :]
        first = column_of(row, races, 2, 0) / masked_lane_sum(by_race, hisp0)
        second = column_of(row, races, 2, 1) / masked_lane_sum(by_race, ~hisp0)
        race_factor = jnp.where(hisp0, first, second)
        by_size = cross_ref[pl.ds(base, sizes), :] * race_factor[0:1]
        for r in range(1, races):
            by_size = by_size + cross_ref[pl.ds(base + r * sizes, sizes), :] * race_factor[r : r + 1]
        row = size_tenure_ref[t : t + 1, :]
        first = column_of(row, sizes, 2, 0) / masked_lane_sum(by_size, ten0)
        second = column_of(row, sizes, 2, 1) / masked_lane_sum(by_size, ~ten0)
        size_factor = jnp.where(ten0, first, second)
        by_income = jnp.sum(by_size * size_factor, axis=0, keepdims=True)
        by_income = by_income + pltpu.roll(by_income, 64, 1)
        by_income = by_income + pltpu.roll(by_income, 32, 1)
        row = tenure_income_ref[t : t + 1, :]
        income_factor = jnp.concatenate([row] * 4, axis=1) / by_income
        age_factor_ref[t, 0:ages] = age_factor_ref[t, 0:ages] * income_factor
        for r in range(races):
            cross_factor_ref[pl.ds(base + r * sizes, sizes), :] = size_factor * race_factor[r : r + 1]

    def add_scaled(t, carry):
        base = t * cross_rows
        total = cells_ref[t, 0] * cross_factor_ref[pl.ds(base, 1), :]
        for rs in range(1, cross):
            total = total + cells_ref[t, rs] * cross_factor_ref[pl.ds(base + rs, 1), :]
        sum_ref[t, 0:ages] = total * age_factor_ref[t, 0:ages]
        sum_ref[t, ages:] = jnp.zeros((sum_ref.shape[1] - ages, LANES), F32)
        return carry

    lax.fori_loop(0, tracts, add_scaled, 0)

    pairs = sum_ref.shape[1] // 2
    send_ref[...] = jnp.zeros(send_ref.shape, F32)
    for t in range(tracts):
        even = sum_ref[t, pl.ds(0, pairs, stride=2)]
        odd = sum_ref[t, pl.ds(1, pairs, stride=2)]
        even = even + pltpu.roll(even, 96, 1)
        odd = odd + pltpu.roll(odd, 96, 1)
        packed = jnp.where(
            lane < 32,
            even,
            jnp.where(
                lane < 64,
                pltpu.roll(even, 96, 1),
                jnp.where(lane < 96, pltpu.roll(odd, 64, 1), pltpu.roll(odd, 32, 1)),
            ),
        )
        send_ref[pl.ds(t, pairs, stride=SLOT), :] = packed
    start = lax.rem(lax.axis_index("tract"), block) * SLOT
    row = jnp.zeros((1, LANES), F32)
    for t in range(tracts):
        row = jnp.where(lane == start + t, (ids_ref[t] + 1).astype(F32), row)
    devices = send_ref.shape[0] // SLOT
    send_ref[pl.ds(tracts, devices, stride=SLOT), :] = jnp.broadcast_to(row, (devices, LANES))


def split_dot(onehot, value, dims):
    total = None
    for _ in range(3):
        part = value.astype(BF16)
        value = value - part.astype(F32)
        term = lax.dot_general(onehot, part, (dims, ((), ())), preferred_element_type=F32)
        total = term if total is None else total + term
    return total


def own_targets(target_ref, wide_ref, owned):
    pumas, columns = target_ref.shape
    full = columns // LANES * LANES
    wide_ref[:, full:] = jnp.ones((pumas, wide_ref.shape[1] - full), F32)
    if full:
        wide_ref[:, 0:full] = target_ref[:, 0:full]
    wide_ref[:, full:columns] = target_ref[:, full:columns]
    width = owned * LANES
    start = pl.multiple_of(lax.axis_index("tract") * width, LANES)
    valid = lax.broadcasted_iota(jnp.int32, (1, width), 1) + start < columns
    return wide_ref[:, pl.ds(start, width)], valid


def age_owner_kernel(recv_ref, target_ref, back_ref, onehot_ref, wide_ref, *, tracts, block):
    pumas = target_ref.shape[0]
    slots = block * SLOT
    blocks = recv_ref.shape[0] // slots
    target, valid = own_targets(target_ref, wide_ref, 1)
    total = jnp.zeros((pumas, LANES), F32)
    for b in range(blocks):
        ids = jnp.sum(recv_ref[pl.ds(b * slots + tracts, block, stride=SLOT), :], axis=0, keepdims=True)
        puma = lax.broadcasted_iota(jnp.int32, (pumas, LANES), 0) + 1
        onehot = jnp.where(ids.astype(jnp.int32) == puma, 1.0, 0.0)[:, 0:slots]
        onehot_ref[b] = onehot
        total = total + split_dot(onehot.astype(BF16), recv_ref[pl.ds(b * slots, slots), :], ((1,), (0,)))
    factor = jnp.where(valid, target / total, 0.0)
    for b in range(blocks):
        back_ref[pl.ds(b * slots, slots), :] = split_dot(onehot_ref[b].astype(BF16), factor, ((0,), (0,)))


def race_owner_kernel(recv_ref, target_ref, onehot_ref, back_ref, wide_ref, slot_ref, *, tracts, owned):
    pumas = target_ref.shape[0]
    blocks, _, slots = onehot_ref.shape
    rows = tracts * owned
    target, valid = own_targets(target_ref, wide_ref, owned)
    total = jnp.zeros((pumas, owned * LANES), F32)
    zeros = jnp.zeros((SLOT - tracts, LANES), F32)
    for b in range(blocks):
        for i in range(slots // SLOT):
            source = (b * (slots // SLOT) + i) * rows
            for k in range(owned):
                lanes = slice(k * LANES, (k + 1) * LANES)
                slot_ref[i * SLOT : i * SLOT + tracts, lanes] = recv_ref[pl.ds(source + k * tracts, tracts), :]
                slot_ref[i * SLOT + tracts : (i + 1) * SLOT, lanes] = zeros
        total = total + split_dot(onehot_ref[b].astype(BF16), slot_ref[...], ((1,), (0,)))
    factor = jnp.where(valid, target / total, 0.0)
    for b in range(blocks):
        slot_ref[...] = split_dot(onehot_ref[b].astype(BF16), factor, ((0,), (0,)))
        for i in range(slots // SLOT):
            source = (b * (slots // SLOT) + i) * rows
            for k in range(owned):
                lanes = slice(k * LANES, (k + 1) * LANES)
                back_ref[pl.ds(source + k * tracts, tracts), :] = slot_ref[i * SLOT : i * SLOT + tracts, lanes]


def race_margin_kernel(
    table_ref, back_ref, age_factor_ref, cross_factor_ref,
    send_ref, scaled_factor_ref,
    cells_ref, cross_ref, sems,
):
    tracts, cross, ages, _ = table_ref.shape
    cross_rows = cross_ref.shape[0] // tracts
    pairs = age_factor_ref.shape[1] // 2
    load_cells(table_ref, cells_ref, sems)
    lane = lane_ids(1)
    for t in range(tracts):
        packed = back_ref[pl.ds(t, pairs, stride=SLOT), :]
        half = pltpu.roll(packed, 64, 1)
        even = jnp.where(lane < 32, packed, jnp.where(lane < 96, pltpu.roll(packed, 32, 1), half))
        odd = jnp.where(lane < 32, half, jnp.where(lane < 96, pltpu.roll(packed, 96, 1), packed))
        scaled_factor_ref[t, pl.ds(0, pairs, stride=2)] = even
        scaled_factor_ref[t, pl.ds(1, pairs, stride=2)] = odd

    def add_ages(t, carry):
        wait_cells(table_ref, cells_ref, sems, t)
        factor = scaled_factor_ref[t, 0:ages] * age_factor_ref[t, 0:ages]
        scaled_factor_ref[t, 0:ages] = factor
        base = t * cross_rows
        for rs in range(cross):
            cross_ref[pl.ds(base + rs, 1), :] = jnp.sum(
                cells_ref[t, rs] * factor, axis=0, keepdims=True
            )
        cross_ref[pl.ds(base + cross, cross_rows - cross), :] = jnp.zeros(
            (cross_rows - cross, LANES), F32
        )
        return carry

    lax.fori_loop(0, tracts, add_ages, 0)

    cross_pairs = (cross + 1) // 2
    send_ref[...] = jnp.zeros(send_ref.shape, F32)
    for t in range(tracts):
        base = t * cross_rows
        margin = cross_ref[pl.ds(base, cross), :] * cross_factor_ref[pl.ds(base, cross), :]
        cross_ref[pl.ds(base, cross), :] = margin + pltpu.roll(margin, 64, 1)
        even = cross_ref[pl.ds(base, cross_pairs, stride=2), :]
        odd = cross_ref[pl.ds(base + 1, cross_pairs, stride=2), :]
        send_ref[pl.ds(t, cross_pairs, stride=tracts), :] = jnp.where(lane < 64, even, odd)


def final_kernel(
    table_ref, back_ref, scaled_factor_ref, cross_factor_ref,
    out_ref,
    cells_ref, cross_ref, in_sems, out_sems,
):
    tracts, cross, ages, _ = table_ref.shape
    cross_rows = cross_ref.shape[0] // tracts
    load_cells(table_ref, cells_ref, in_sems)
    cross_pairs = (cross + 1) // 2
    lane = lane_ids(1)
    for t in range(tracts):
        base = t * cross_rows
        packed = back_ref[pl.ds(t, cross_pairs, stride=tracts), :]
        half = pltpu.roll(packed, 64, 1)
        cross_ref[pl.ds(base, cross_pairs, stride=2), :] = jnp.where(lane < 64, packed, half)
        cross_ref[pl.ds(base + 1, cross_pairs, stride=2), :] = jnp.where(lane < 64, half, packed)
        cross_ref[pl.ds(base, cross), :] = (
            cross_ref[pl.ds(base, cross), :] * cross_factor_ref[pl.ds(base, cross), :]
        )

    def scale(t, carry):
        wait_cells(table_ref, cells_ref, in_sems, t)
        factor = scaled_factor_ref[t, 0:ages]
        base = t * cross_rows
        for rs in range(cross):
            cells_ref[t, rs] = cells_ref[t, rs] * factor * cross_ref[pl.ds(base + rs, 1), :]
        pltpu.make_async_copy(cells_ref.at[t], out_ref.at[t], out_sems.at[t]).start()
        return carry

    lax.fori_loop(0, tracts, scale, 0)
    for t in range(tracts):
        pltpu.make_async_copy(cells_ref.at[t], out_ref.at[t], out_sems.at[t]).wait()


def call(kernel, out_shapes, in_spaces, out_spaces, scratch, cost=None):
    def spec(space):
        return pl.BlockSpec(memory_space=space)

    return pl.pallas_call(
        kernel,
        out_shape=[jax.ShapeDtypeStruct(shape, F32) for shape in out_shapes],
        in_specs=[spec(space) for space in in_spaces],
        out_specs=[spec(space) for space in out_spaces],
        scratch_shapes=scratch,
        compiler_params=pltpu.CompilerParams(vmem_limit_bytes=40 << 20),
    )


def per_device(
    devices,
    table, age_sex, race_hisp, size_tenure, tenure_income, puma_age, puma_race, tract_puma,
):
    tracts, ages, races, sizes, inner = table.shape
    pumas = puma_age.shape[0]
    cross = races * sizes
    age_rows = -(-ages // 8) * 8
    cross_rows = -(-(cross + 1) // 8) * 8
    owned = -(-(cross + 1) // 2 // devices)
    block = math.gcd(devices, LANES // SLOT)
    vmem, smem, hbm = pltpu.VMEM, pltpu.SMEM, pl.ANY

    cells = table.transpose(0, 2, 3, 1, 4).reshape(tracts, cross, ages, inner)
    cells_scratch = pltpu.VMEM((tracts, cross, ages, inner), F32)
    cross_scratch = pltpu.VMEM((tracts * cross_rows, LANES), F32)
    copy_sems = pltpu.SemaphoreType.DMA((tracts,))
    slots = devices * SLOT
    blocks = devices // block

    def exchange(x):
        rows = x.shape[0] // devices
        x = x.reshape(devices, rows, LANES)
        return lax.all_to_all(x, "tract", 0, 0).reshape(devices * rows, LANES)

    send, age_factor, cross_factor = call(
        functools.partial(rake_kernel, races=races, sizes=sizes, block=block),
        [(slots, LANES), (tracts, age_rows, LANES), (tracts * cross_rows, LANES)],
        [smem, hbm, vmem, vmem, vmem, vmem],
        [vmem] * 3,
        [cells_scratch, pltpu.VMEM((tracts, age_rows, LANES), F32), cross_scratch, copy_sems],
    )(tract_puma, cells, age_sex, race_hisp, size_tenure, tenure_income)

    back, onehot = call(
        functools.partial(age_owner_kernel, tracts=tracts, block=block),
        [(slots, LANES), (blocks, pumas, block * SLOT)],
        [vmem] * 2,
        [vmem] * 2,
        [pltpu.VMEM((pumas, devices * LANES), F32)],
    )(exchange(send), puma_age)

    rows = devices * owned * tracts
    send, scaled_factor = call(
        race_margin_kernel,
        [(rows, LANES), (tracts, age_rows, LANES)],
        [hbm] + [vmem] * 3,
        [vmem] * 2,
        [cells_scratch, cross_scratch, copy_sems],
    )(cells, exchange(back), age_factor, cross_factor)

    back, = call(
        functools.partial(race_owner_kernel, tracts=tracts, owned=owned),
        [(rows, LANES)],
        [vmem] * 3,
        [vmem],
        [
            pltpu.VMEM((pumas, devices * owned * LANES), F32),
            pltpu.VMEM((block * SLOT, owned * LANES), F32),
        ],
    )(exchange(send), puma_race, onehot)

    out, = call(
        final_kernel,
        [(tracts, cross, ages, inner)],
        [hbm] + [vmem] * 3,
        [hbm],
        [cells_scratch, cross_scratch, copy_sems, copy_sems],
    )(cells, exchange(back), scaled_factor, cross_factor)
    return out.reshape(tracts, races, sizes, ages, inner).transpose(0, 3, 1, 2, 4)


def solution(mesh):
    in_specs = (
        P(("grp", "tract"), None, None, None, None),
        P(("grp", "tract"), None),
        P(("grp", "tract"), None),
        P(("grp", "tract"), None),
        P(("grp", "tract"), None),
        P("grp", None),
        P("grp", None),
        P(("grp", "tract")),
    )
    out_specs = P(("grp", "tract"), None, None, None, None)
    return jax.shard_map(
        functools.partial(per_device, mesh.shape["tract"]),
        mesh=mesh, in_specs=in_specs, out_specs=out_specs, check_vma=False,
    )
```

```python
import functools
import math

import jax
import jax.numpy as jnp
from jax import lax
from jax.experimental import pallas as pl
from jax.experimental.pallas import tpu as pltpu
from jax.sharding import PartitionSpec as P

LANES = 128
SLOT = 16
F32 = jnp.float32
BF16 = jnp.bfloat16


def lane_ids(rows):
    return lax.broadcasted_iota(jnp.int32, (rows, LANES), 1)


def masked_lane_sum(value, mask):
    return jnp.sum(jnp.where(mask, value, 0.0), axis=-1, keepdims=True)


def column_of(row, rows, step, offset):
    width = row.shape[-1]
    lane = lax.broadcasted_iota(jnp.int32, (rows, width), 1)
    sub = lax.broadcasted_iota(jnp.int32, (rows, width), 0)
    return jnp.sum(jnp.where(lane == step * sub + offset, row, 0.0), axis=-1, keepdims=True)


def own_targets(target_ref, wide_ref, own_ref):
    pumas, columns = target_ref.shape
    full = columns // LANES * LANES
    wide_ref[:, full:] = jnp.zeros((pumas, wide_ref.shape[1] - full), F32)
    if full:
        wide_ref[:, 0:full] = target_ref[:, 0:full]
    wide_ref[:, full:columns] = target_ref[:, full:columns]
    width = own_ref.shape[1]
    start = pl.multiple_of(lax.axis_index("tract") * width, LANES)
    own_ref[...] = wide_ref[:, pl.ds(start, width)]


def rake_kernel(
    ids_hbm, table_hbm, age_sex_hbm, race_hisp_hbm, size_tenure_hbm, tenure_income_hbm, target_hbm,
    send_ref, age_factor_ref, cross_factor_ref, own_target_ref, cells_ref,
    sum_ref, cross_ref, wide_ref,
    ids_ref, age_sex_ref, race_hisp_ref, size_tenure_ref, tenure_income_ref, target_ref,
    sems, small_sems,
    *, races, sizes, block,
):
    tracts, cross, ages, _ = table_hbm.shape
    cross_rows = cross_ref.shape[0] // tracts
    small = [
        pltpu.make_async_copy(source, target, small_sems.at[i])
        for i, (source, target) in enumerate((
            (ids_hbm, ids_ref),
            (age_sex_hbm, age_sex_ref),
            (race_hisp_hbm, race_hisp_ref),
            (size_tenure_hbm, size_tenure_ref),
            (tenure_income_hbm, tenure_income_ref),
            (target_hbm, target_ref),
        ))
    ]
    for copy in small[:-1]:
        copy.start()
    for t in range(tracts):
        pltpu.make_async_copy(table_hbm.at[t], cells_ref.at[t], sems.at[t]).start()
    small[-1].start()
    lane = lane_ids(1)
    sex0 = lane < 64
    hisp0 = (lane // 32) % 2 == 0
    ten0 = (lane // 16) % 2 == 0

    def add_cross(t, carry):
        pltpu.make_async_copy(table_hbm.at[t], cells_ref.at[t], sems.at[t]).wait()
        total = cells_ref[t, 0]
        for rs in range(1, cross):
            total = total + cells_ref[t, rs]
        sum_ref[t, 0:ages] = total
        return carry

    lax.fori_loop(0, tracts, add_cross, 0)
    for copy in small:
        copy.wait()
    own_targets(target_ref, wide_ref, own_target_ref)

    for t in range(tracts):
        total = sum_ref[t, 0:ages]
        row = age_sex_ref[t : t + 1, :]
        first = column_of(row, ages, 2, 0) / masked_lane_sum(total, sex0)
        second = column_of(row, ages, 2, 1) / masked_lane_sum(total, ~sex0)
        age_factor_ref[t, 0:ages] = jnp.where(sex0, first, second)

    def add_ages(t, carry):
        factor = age_factor_ref[t, 0:ages]
        base = t * cross_rows
        for rs in range(cross):
            cross_ref[pl.ds(base + rs, 1), :] = jnp.sum(
                cells_ref[t, rs] * factor, axis=0, keepdims=True
            )
        return carry

    lax.fori_loop(0, tracts, add_ages, 0)

    for t in range(tracts):
        base = t * cross_rows
        by_race = cross_ref[pl.ds(base, races, stride=sizes), :]
        for s in range(1, sizes):
            by_race = by_race + cross_ref[pl.ds(base + s, races, stride=sizes), :]
        row = race_hisp_ref[t : t + 1, :]
        first = column_of(row, races, 2, 0) / masked_lane_sum(by_race, hisp0)
        second = column_of(row, races, 2, 1) / masked_lane_sum(by_race, ~hisp0)
        race_factor = jnp.where(hisp0, first, second)
        by_size = cross_ref[pl.ds(base, sizes), :] * race_factor[0:1]
        for r in range(1, races):
            by_size = by_size + cross_ref[pl.ds(base + r * sizes, sizes), :] * race_factor[r : r + 1]
        row = size_tenure_ref[t : t + 1, :]
        first = column_of(row, sizes, 2, 0) / masked_lane_sum(by_size, ten0)
        second = column_of(row, sizes, 2, 1) / masked_lane_sum(by_size, ~ten0)
        size_factor = jnp.where(ten0, first, second)
        by_income = jnp.sum(by_size * size_factor, axis=0, keepdims=True)
        by_income = by_income + pltpu.roll(by_income, 64, 1)
        by_income = by_income + pltpu.roll(by_income, 32, 1)
        row = tenure_income_ref[t : t + 1, :]
        income_factor = jnp.concatenate([row] * 4, axis=1) / by_income
        age_factor_ref[t, 0:ages] = age_factor_ref[t, 0:ages] * income_factor
        for r in range(races):
            cross_factor_ref[pl.ds(base + r * sizes, sizes), :] = size_factor * race_factor[r : r + 1]

    def add_scaled(t, carry):
        base = t * cross_rows
        total = cells_ref[t, 0] * cross_factor_ref[pl.ds(base, 1), :]
        for rs in range(1, cross):
            total = total + cells_ref[t, rs] * cross_factor_ref[pl.ds(base + rs, 1), :]
        sum_ref[t, 0:ages] = total * age_factor_ref[t, 0:ages]
        sum_ref[t, ages:] = jnp.zeros((sum_ref.shape[1] - ages, LANES), F32)
        return carry

    lax.fori_loop(0, tracts, add_scaled, 0)

    pairs = sum_ref.shape[1] // 2
    send_ref[...] = jnp.zeros(send_ref.shape, F32)
    for t in range(tracts):
        even = sum_ref[t, pl.ds(0, pairs, stride=2)]
        odd = sum_ref[t, pl.ds(1, pairs, stride=2)]
        even = even + pltpu.roll(even, 96, 1)
        odd = odd + pltpu.roll(odd, 96, 1)
        packed = jnp.where(
            lane < 32,
            even,
            jnp.where(
                lane < 64,
                pltpu.roll(even, 96, 1),
                jnp.where(lane < 96, pltpu.roll(odd, 64, 1), pltpu.roll(odd, 32, 1)),
            ),
        )
        send_ref[pl.ds(t, pairs, stride=SLOT), :] = packed
    start = lax.rem(lax.axis_index("tract"), block) * SLOT
    row = jnp.zeros((1, LANES), F32)
    for t in range(tracts):
        row = jnp.where(lane == start + t, (ids_ref[t] + 1).astype(F32), row)
    devices = send_ref.shape[0] // SLOT
    send_ref[pl.ds(tracts, devices, stride=SLOT), :] = jnp.broadcast_to(row, (devices, LANES))


def split_dot(onehot, value, dims):
    total = None
    for _ in range(3):
        part = value.astype(BF16)
        value = value - part.astype(F32)
        term = lax.dot_general(onehot, part, (dims, ((), ())), preferred_element_type=F32)
        total = term if total is None else total + term
    return total


def age_owner_kernel(recv_ref, target_ref, back_ref, onehot_ref, *, tracts, block):
    pumas = target_ref.shape[0]
    slots = block * SLOT
    blocks = recv_ref.shape[0] // slots
    total = jnp.zeros((pumas, LANES), F32)
    for b in range(blocks):
        ids = jnp.sum(recv_ref[pl.ds(b * slots + tracts, block, stride=SLOT), :], axis=0, keepdims=True)
        puma = lax.broadcasted_iota(jnp.int32, (pumas, LANES), 0) + 1
        onehot = jnp.where(ids.astype(jnp.int32) == puma, 1.0, 0.0)[:, 0:slots]
        onehot_ref[b] = onehot
        total = total + split_dot(onehot.astype(BF16), recv_ref[pl.ds(b * slots, slots), :], ((1,), (0,)))
    target = target_ref[...]
    factor = jnp.where(target > 0.0, target / total, 0.0)
    for b in range(blocks):
        back_ref[pl.ds(b * slots, slots), :] = split_dot(onehot_ref[b].astype(BF16), factor, ((0,), (0,)))


def race_owner_kernel(recv_ref, target_ref, onehot_ref, back_ref, slot_ref, *, tracts, owned):
    pumas = target_ref.shape[0]
    blocks, _, slots = onehot_ref.shape
    rows = tracts * owned
    total = jnp.zeros((pumas, owned * LANES), F32)
    zeros = jnp.zeros((SLOT - tracts, LANES), F32)
    for b in range(blocks):
        for i in range(slots // SLOT):
            source = (b * (slots // SLOT) + i) * rows
            for k in range(owned):
                lanes = slice(k * LANES, (k + 1) * LANES)
                slot_ref[i * SLOT : i * SLOT + tracts, lanes] = recv_ref[pl.ds(source + k * tracts, tracts), :]
                slot_ref[i * SLOT + tracts : (i + 1) * SLOT, lanes] = zeros
        total = total + split_dot(onehot_ref[b].astype(BF16), slot_ref[...], ((1,), (0,)))
    target = target_ref[...]
    factor = jnp.where(target > 0.0, target / total, 0.0)
    for b in range(blocks):
        slot_ref[...] = split_dot(onehot_ref[b].astype(BF16), factor, ((0,), (0,)))
        for i in range(slots // SLOT):
            source = (b * (slots // SLOT) + i) * rows
            for k in range(owned):
                lanes = slice(k * LANES, (k + 1) * LANES)
                back_ref[pl.ds(source + k * tracts, tracts), :] = slot_ref[i * SLOT : i * SLOT + tracts, lanes]


def race_margin_kernel(
    cells_ref, back_ref, age_factor_ref, cross_factor_ref, target_ref,
    send_ref, scaled_factor_ref, own_target_ref,
    cross_ref, wide_ref,
):
    tracts, cross, ages, _ = cells_ref.shape
    cross_rows = cross_ref.shape[0] // tracts
    pairs = age_factor_ref.shape[1] // 2
    own_targets(target_ref, wide_ref, own_target_ref)
    lane = lane_ids(1)
    for t in range(tracts):
        packed = back_ref[pl.ds(t, pairs, stride=SLOT), :]
        half = pltpu.roll(packed, 64, 1)
        even = jnp.where(lane < 32, packed, jnp.where(lane < 96, pltpu.roll(packed, 32, 1), half))
        odd = jnp.where(lane < 32, half, jnp.where(lane < 96, pltpu.roll(packed, 96, 1), packed))
        scaled_factor_ref[t, pl.ds(0, pairs, stride=2)] = even
        scaled_factor_ref[t, pl.ds(1, pairs, stride=2)] = odd

    def add_ages(t, carry):
        factor = scaled_factor_ref[t, 0:ages] * age_factor_ref[t, 0:ages]
        scaled_factor_ref[t, 0:ages] = factor
        base = t * cross_rows
        for rs in range(cross):
            cross_ref[pl.ds(base + rs, 1), :] = jnp.sum(
                cells_ref[t, rs] * factor, axis=0, keepdims=True
            )
        cross_ref[pl.ds(base + cross, cross_rows - cross), :] = jnp.zeros(
            (cross_rows - cross, LANES), F32
        )
        return carry

    lax.fori_loop(0, tracts, add_ages, 0)

    cross_pairs = (cross + 1) // 2
    send_ref[...] = jnp.zeros(send_ref.shape, F32)
    for t in range(tracts):
        base = t * cross_rows
        margin = cross_ref[pl.ds(base, cross), :] * cross_factor_ref[pl.ds(base, cross), :]
        cross_ref[pl.ds(base, cross), :] = margin + pltpu.roll(margin, 64, 1)
        even = cross_ref[pl.ds(base, cross_pairs, stride=2), :]
        odd = cross_ref[pl.ds(base + 1, cross_pairs, stride=2), :]
        send_ref[pl.ds(t, cross_pairs, stride=tracts), :] = jnp.where(lane < 64, even, odd)


def final_kernel(
    cells_ref, back_ref, scaled_factor_ref, cross_factor_ref,
    out_ref,
    result_ref, cross_ref, sems,
):
    tracts, cross, ages, _ = cells_ref.shape
    cross_rows = cross_ref.shape[0] // tracts
    cross_pairs = (cross + 1) // 2
    lane = lane_ids(1)
    for t in range(tracts):
        base = t * cross_rows
        packed = back_ref[pl.ds(t, cross_pairs, stride=tracts), :]
        half = pltpu.roll(packed, 64, 1)
        cross_ref[pl.ds(base, cross_pairs, stride=2), :] = jnp.where(lane < 64, packed, half)
        cross_ref[pl.ds(base + 1, cross_pairs, stride=2), :] = jnp.where(lane < 64, half, packed)
        cross_ref[pl.ds(base, cross), :] = (
            cross_ref[pl.ds(base, cross), :] * cross_factor_ref[pl.ds(base, cross), :]
        )

    def scale(t, carry):
        factor = scaled_factor_ref[t, 0:ages]
        base = t * cross_rows
        for rs in range(cross):
            result_ref[t, rs] = cells_ref[t, rs] * factor * cross_ref[pl.ds(base + rs, 1), :]
        pltpu.make_async_copy(result_ref.at[t], out_ref.at[t], sems.at[t]).start()
        return carry

    lax.fori_loop(0, tracts, scale, 0)
    for t in range(tracts):
        pltpu.make_async_copy(result_ref.at[t], out_ref.at[t], sems.at[t]).wait()


def call(kernel, out_shapes, in_spaces, out_spaces, scratch):
    def spec(space):
        return pl.BlockSpec(memory_space=space)

    run = pl.pallas_call(
        kernel,
        out_shape=[
            space(shape, F32) for shape, space in zip(out_shapes, out_spaces, strict=True)
        ],
        in_specs=[spec(space) for space in in_spaces],
        out_specs=[spec(space) for space in out_spaces],
        scratch_shapes=scratch,
        compiler_params=pltpu.CompilerParams(vmem_limit_bytes=40 << 20),
    )

    def placed(*args):
        return run(*map(pltpu.with_memory_space_constraint, args, in_spaces))

    return placed


def per_device(
    devices,
    table, age_sex, race_hisp, size_tenure, tenure_income, puma_age, puma_race, tract_puma,
):
    tracts, ages, races, sizes, inner = table.shape
    pumas = puma_age.shape[0]
    cross = races * sizes
    age_rows = -(-ages // 8) * 8
    cross_rows = -(-(cross + 1) // 8) * 8
    owned = -(-(cross + 1) // 2 // devices)
    block = math.gcd(devices, LANES // SLOT)
    vmem, hbm = pltpu.VMEM, pltpu.HBM

    cells = table.transpose(0, 2, 3, 1, 4).reshape(tracts, cross, ages, inner)
    cells_scratch = pltpu.VMEM((tracts, cross, ages, inner), F32)
    cross_scratch = pltpu.VMEM((tracts * cross_rows, LANES), F32)
    copy_sems = pltpu.SemaphoreType.DMA((tracts,))
    slots = devices * SLOT
    blocks = devices // block

    def exchange(x):
        rows = x.shape[0] // devices
        x = x.reshape(devices, rows, LANES)
        return lax.all_to_all(x, "tract", 0, 0).reshape(devices * rows, LANES)

    small = [age_sex, race_hisp, size_tenure, tenure_income, puma_age]
    send, age_factor, cross_factor, own_age, cells = call(
        functools.partial(rake_kernel, races=races, sizes=sizes, block=block),
        [
            (slots, LANES),
            (tracts, age_rows, LANES),
            (tracts * cross_rows, LANES),
            (pumas, LANES),
            cells.shape,
        ],
        [hbm] * 7,
        [vmem] * 5,
        [
            pltpu.VMEM((tracts, age_rows, LANES), F32),
            cross_scratch,
            pltpu.VMEM((pumas, devices * LANES), F32),
            pltpu.SMEM((tracts,), jnp.int32),
        ]
        + [pltpu.VMEM(x.shape, F32) for x in small]
        + [copy_sems, pltpu.SemaphoreType.DMA((1 + len(small),))],
    )(tract_puma, cells, *small)

    back, onehot = call(
        functools.partial(age_owner_kernel, tracts=tracts, block=block),
        [(slots, LANES), (blocks, pumas, block * SLOT)],
        [vmem] * 2,
        [vmem] * 2,
        [],
    )(exchange(send), own_age)

    rows = devices * owned * tracts
    send, scaled_factor, own_race = call(
        race_margin_kernel,
        [(rows, LANES), (tracts, age_rows, LANES), (pumas, owned * LANES)],
        [vmem] * 5,
        [vmem] * 3,
        [cross_scratch, pltpu.VMEM((pumas, devices * owned * LANES), F32)],
    )(cells, exchange(back), age_factor, cross_factor, puma_race)

    back, = call(
        functools.partial(race_owner_kernel, tracts=tracts, owned=owned),
        [(rows, LANES)],
        [vmem] * 3,
        [vmem],
        [pltpu.VMEM((block * SLOT, owned * LANES), F32)],
    )(exchange(send), own_race, onehot)

    out, = call(
        final_kernel,
        [(tracts, cross, ages, inner)],
        [vmem] * 4,
        [hbm],
        [cells_scratch, cross_scratch, copy_sems],
    )(cells, exchange(back), scaled_factor, cross_factor)
    return out.reshape(tracts, races, sizes, ages, inner).transpose(0, 3, 1, 2, 4)


def solution(mesh):
    in_specs = (
        P(("grp", "tract"), None, None, None, None),
        P(("grp", "tract"), None),
        P(("grp", "tract"), None),
        P(("grp", "tract"), None),
        P(("grp", "tract"), None),
        P("grp", None),
        P("grp", None),
        P(("grp", "tract")),
    )
    out_specs = P(("grp", "tract"), None, None, None, None)
    return jax.shard_map(
        functools.partial(per_device, mesh.shape["tract"]),
        mesh=mesh, in_specs=in_specs, out_specs=out_specs, check_vma=False,
    )
```

```python
import functools
import math

import jax
import jax.numpy as jnp
from jax import lax
from jax.experimental import pallas as pl
from jax.experimental.pallas import tpu as pltpu
from jax.sharding import PartitionSpec as P

LANES = 128
SLOT = 16
NEAR = 4
F32 = jnp.float32
BF16 = jnp.bfloat16


def lane_ids(rows):
    return lax.broadcasted_iota(jnp.int32, (rows, LANES), 1)


def masked_lane_sum(value, mask):
    return jnp.sum(jnp.where(mask, value, 0.0), axis=-1, keepdims=True)


def column_of(row, rows, step, offset):
    width = row.shape[-1]
    lane = lax.broadcasted_iota(jnp.int32, (rows, width), 1)
    sub = lax.broadcasted_iota(jnp.int32, (rows, width), 0)
    return jnp.sum(jnp.where(lane == step * sub + offset, row, 0.0), axis=-1, keepdims=True)


def own_targets(target_ref, wide_ref, own_ref):
    pumas, columns = target_ref.shape
    full = columns // LANES * LANES
    wide_ref[:, full:] = jnp.zeros((pumas, wide_ref.shape[1] - full), F32)
    if full:
        wide_ref[:, 0:full] = target_ref[:, 0:full]
    wide_ref[:, full:columns] = target_ref[:, full:columns]
    width = own_ref.shape[1]
    start = pl.multiple_of(lax.axis_index("tract") // NEAR * width, LANES)
    own_ref[...] = wide_ref[:, pl.ds(start, width)]


def take_pieces(blocks_ref, piece_refs):
    rows = piece_refs[0].shape[0]
    own = lax.axis_index("tract") // NEAR
    for d, piece_ref in enumerate(piece_refs):
        start = pl.multiple_of(lax.bitwise_xor(own, d) * rows, 8)
        piece_ref[...] = blocks_ref[pl.ds(start, rows), :]


def place_pieces(piece_refs, rows_ref, owned, tracts):
    own = lax.axis_index("tract") // NEAR
    for d, piece_ref in enumerate(piece_refs):
        start = lax.bitwise_xor(own, d) * (owned * SLOT)
        for k in range(owned):
            rows_ref[pl.ds(pl.multiple_of(start + k * SLOT, SLOT), tracts), :] = piece_ref[
                k * tracts : (k + 1) * tracts, :
            ]


def rake_kernel(
    ids_hbm, table_hbm, age_sex_hbm, race_hisp_hbm, size_tenure_hbm, tenure_income_hbm, target_hbm,
    age_factor_ref, cross_factor_ref, own_target_ref, cells_ref, *refs,
    races, sizes, block,
):
    *piece_refs, sum_ref, cross_ref, wide_ref, send_ref, packed_ref = refs[:-8]
    (
        ids_ref, age_sex_ref, race_hisp_ref, size_tenure_ref, tenure_income_ref, target_ref,
        sems, small_sems,
    ) = refs[-8:]
    tracts, cross, ages, _ = table_hbm.shape
    cross_rows = cross_ref.shape[0] // tracts
    small = [
        pltpu.make_async_copy(source, target, small_sems.at[i])
        for i, (source, target) in enumerate((
            (ids_hbm, ids_ref),
            (age_sex_hbm, age_sex_ref),
            (race_hisp_hbm, race_hisp_ref),
            (size_tenure_hbm, size_tenure_ref),
            (tenure_income_hbm, tenure_income_ref),
            (target_hbm, target_ref),
        ))
    ]
    for copy in small[:-1]:
        copy.start()
    for t in range(tracts):
        pltpu.make_async_copy(table_hbm.at[t], cells_ref.at[t], sems.at[t]).start()
    small[-1].start()
    lane = lane_ids(1)
    sex0 = lane < 64
    hisp0 = (lane // 32) % 2 == 0
    ten0 = (lane // 16) % 2 == 0

    def add_cross(t, carry):
        pltpu.make_async_copy(table_hbm.at[t], cells_ref.at[t], sems.at[t]).wait()
        total = cells_ref[t, 0]
        for rs in range(1, cross):
            total = total + cells_ref[t, rs]
        sum_ref[t, 0:ages] = total
        return carry

    lax.fori_loop(0, tracts, add_cross, 0)
    for copy in small:
        copy.wait()
    own_targets(target_ref, wide_ref, own_target_ref)

    for t in range(tracts):
        total = sum_ref[t, 0:ages]
        row = age_sex_ref[t : t + 1, :]
        first = column_of(row, ages, 2, 0) / masked_lane_sum(total, sex0)
        second = column_of(row, ages, 2, 1) / masked_lane_sum(total, ~sex0)
        age_factor_ref[t, 0:ages] = jnp.where(sex0, first, second)

    def add_ages(t, carry):
        factor = age_factor_ref[t, 0:ages]
        base = t * cross_rows
        for rs in range(cross):
            cross_ref[pl.ds(base + rs, 1), :] = jnp.sum(
                cells_ref[t, rs] * factor, axis=0, keepdims=True
            )
        return carry

    lax.fori_loop(0, tracts, add_ages, 0)

    for t in range(tracts):
        base = t * cross_rows
        by_race = cross_ref[pl.ds(base, races, stride=sizes), :]
        for s in range(1, sizes):
            by_race = by_race + cross_ref[pl.ds(base + s, races, stride=sizes), :]
        row = race_hisp_ref[t : t + 1, :]
        first = column_of(row, races, 2, 0) / masked_lane_sum(by_race, hisp0)
        second = column_of(row, races, 2, 1) / masked_lane_sum(by_race, ~hisp0)
        race_factor = jnp.where(hisp0, first, second)
        by_size = cross_ref[pl.ds(base, sizes), :] * race_factor[0:1]
        for r in range(1, races):
            by_size = by_size + cross_ref[pl.ds(base + r * sizes, sizes), :] * race_factor[r : r + 1]
        row = size_tenure_ref[t : t + 1, :]
        first = column_of(row, sizes, 2, 0) / masked_lane_sum(by_size, ten0)
        second = column_of(row, sizes, 2, 1) / masked_lane_sum(by_size, ~ten0)
        size_factor = jnp.where(ten0, first, second)
        by_income = jnp.sum(by_size * size_factor, axis=0, keepdims=True)
        by_income = by_income + pltpu.roll(by_income, 64, 1)
        by_income = by_income + pltpu.roll(by_income, 32, 1)
        row = tenure_income_ref[t : t + 1, :]
        income_factor = jnp.concatenate([row] * 4, axis=1) / by_income
        age_factor_ref[t, 0:ages] = age_factor_ref[t, 0:ages] * income_factor
        for r in range(races):
            cross_factor_ref[pl.ds(base + r * sizes, sizes), :] = size_factor * race_factor[r : r + 1]

    def add_scaled(t, carry):
        base = t * cross_rows
        total = cells_ref[t, 0] * cross_factor_ref[pl.ds(base, 1), :]
        for rs in range(1, cross):
            total = total + cells_ref[t, rs] * cross_factor_ref[pl.ds(base + rs, 1), :]
        sum_ref[t, 0:ages] = total * age_factor_ref[t, 0:ages]
        sum_ref[t, ages:] = jnp.zeros((sum_ref.shape[1] - ages, LANES), F32)
        return carry

    lax.fori_loop(0, tracts, add_scaled, 0)

    pairs = sum_ref.shape[1] // 2
    piece_rows = piece_refs[0].shape[0]
    owned = own_target_ref.shape[1] // LANES
    send_ref[...] = jnp.zeros(send_ref.shape, F32)
    for t in range(tracts):
        even = sum_ref[t, pl.ds(0, pairs, stride=2)]
        odd = sum_ref[t, pl.ds(1, pairs, stride=2)]
        even = even + pltpu.roll(even, 96, 1)
        odd = odd + pltpu.roll(odd, 96, 1)
        packed_ref[t * SLOT : t * SLOT + pairs] = jnp.where(
            lane < 32,
            even,
            jnp.where(
                lane < 64,
                pltpu.roll(even, 96, 1),
                jnp.where(lane < 96, pltpu.roll(odd, 64, 1), pltpu.roll(odd, 32, 1)),
            ),
        )
    for q in range(pairs):
        send_ref[pl.ds(q // owned * piece_rows + q % owned * tracts, tracts), :] = packed_ref[
            pl.ds(q, tracts, stride=SLOT), :
        ]
    take_pieces(send_ref, piece_refs)
    for d, piece_ref in enumerate(piece_refs):
        row = jnp.zeros((1, LANES), F32)
        for t in range(tracts):
            row = jnp.where(lane == d % block * SLOT + t, (ids_ref[t] + 1).astype(F32), row)
        piece_ref[pl.ds(owned * tracts, 1), :] = row


def split_dot(onehot, value, dims):
    total = None
    for _ in range(3):
        part = value.astype(BF16)
        value = value - part.astype(F32)
        term = lax.dot_general(onehot, part, (dims, ((), ())), preferred_element_type=F32)
        total = term if total is None else total + term
    return total


def block_sum(onehot, piece_refs, slot_ref, tracts):
    owned = slot_ref.shape[1] // LANES
    zeros = jnp.zeros((SLOT - tracts, LANES), F32)
    for i, piece_ref in enumerate(piece_refs):
        for k in range(owned):
            lanes = slice(k * LANES, (k + 1) * LANES)
            slot_ref[i * SLOT : i * SLOT + tracts, lanes] = piece_ref[k * tracts : (k + 1) * tracts, :]
            slot_ref[i * SLOT + tracts : (i + 1) * SLOT, lanes] = zeros
    return split_dot(onehot.astype(BF16), slot_ref[...], ((1,), (0,)))


def age_sum_kernel(*refs, tracts, block):
    *piece_refs, total_ref, onehot_ref, slot_ref = refs
    pumas = total_ref.shape[0]
    owned = slot_ref.shape[1] // LANES
    puma = lax.broadcasted_iota(jnp.int32, (pumas, LANES), 0) + 1
    total = jnp.zeros(total_ref.shape, F32)
    for b in range(len(piece_refs) // block):
        part = piece_refs[b * block : (b + 1) * block]
        ids = part[0][pl.ds(owned * tracts, 1), :]
        for piece_ref in part[1:]:
            ids = ids + piece_ref[pl.ds(owned * tracts, 1), :]
        onehot = jnp.where(ids.astype(jnp.int32) == puma, 1.0, 0.0)[:, 0 : block * SLOT]
        onehot_ref[b] = onehot
        total = total + block_sum(onehot, part, slot_ref, tracts)
    total_ref[...] = total


def race_sum_kernel(onehot_ref, *refs, tracts, block):
    *piece_refs, total_ref, slot_ref = refs
    total = jnp.zeros(total_ref.shape, F32)
    for b in range(len(piece_refs) // block):
        part = piece_refs[b * block : (b + 1) * block]
        total = total + block_sum(onehot_ref[b], part, slot_ref, tracts)
    total_ref[...] = total


def factor_kernel(onehot_ref, target_ref, *refs, tracts, block):
    part_refs, piece_refs, slot_ref = refs[:NEAR], refs[NEAR:-1], refs[-1]
    owned = target_ref.shape[1] // LANES
    total = part_refs[0][...]
    for part_ref in part_refs[1:]:
        total = total + part_ref[...]
    target = target_ref[...]
    factor = jnp.where(target > 0.0, target / total, 0.0)
    for b in range(len(piece_refs) // block):
        slot_ref[...] = split_dot(onehot_ref[b].astype(BF16), factor, ((0,), (0,)))
        for i, piece_ref in enumerate(piece_refs[b * block : (b + 1) * block]):
            for k in range(owned):
                lanes = slice(k * LANES, (k + 1) * LANES)
                piece_ref[k * tracts : (k + 1) * tracts, :] = slot_ref[i * SLOT : i * SLOT + tracts, lanes]
            used = owned * tracts
            piece_ref[used:, :] = jnp.zeros((piece_ref.shape[0] - used, LANES), F32)


def race_margin_kernel(
    cells_ref, age_factor_ref, cross_factor_ref, target_ref, *refs, owned_ages
):
    devices = (len(refs) - 6) // 2
    back_refs, (scaled_factor_ref, own_target_ref) = refs[:devices], refs[devices : devices + 2]
    piece_refs, (back_ref, cross_ref, wide_ref, send_ref) = refs[devices + 2 : -4], refs[-4:]
    tracts, cross, ages, _ = cells_ref.shape
    cross_rows = cross_ref.shape[0] // tracts
    pairs = age_factor_ref.shape[1] // 2
    own_targets(target_ref, wide_ref, own_target_ref)
    lane = lane_ids(1)
    place_pieces(back_refs, back_ref, owned_ages, tracts)
    for t in range(tracts):
        packed = back_ref[pl.ds(t, pairs, stride=SLOT), :]
        half = pltpu.roll(packed, 64, 1)
        even = jnp.where(lane < 32, packed, jnp.where(lane < 96, pltpu.roll(packed, 32, 1), half))
        odd = jnp.where(lane < 32, half, jnp.where(lane < 96, pltpu.roll(packed, 96, 1), packed))
        scaled_factor_ref[t, pl.ds(0, pairs, stride=2)] = even
        scaled_factor_ref[t, pl.ds(1, pairs, stride=2)] = odd

    def add_ages(t, carry):
        factor = scaled_factor_ref[t, 0:ages] * age_factor_ref[t, 0:ages]
        scaled_factor_ref[t, 0:ages] = factor
        base = t * cross_rows
        for rs in range(cross):
            cross_ref[pl.ds(base + rs, 1), :] = jnp.sum(
                cells_ref[t, rs] * factor, axis=0, keepdims=True
            )
        cross_ref[pl.ds(base + cross, cross_rows - cross), :] = jnp.zeros(
            (cross_rows - cross, LANES), F32
        )
        return carry

    lax.fori_loop(0, tracts, add_ages, 0)

    cross_pairs = (cross + 1) // 2
    piece_rows = piece_refs[0].shape[0]
    owned = own_target_ref.shape[1] // LANES
    send_ref[...] = jnp.zeros(send_ref.shape, F32)
    packed_rows = -(-cross_pairs // 8) * 8
    for t in range(tracts):
        base = t * cross_rows
        margin = cross_ref[pl.ds(base, cross), :] * cross_factor_ref[pl.ds(base, cross), :]
        cross_ref[pl.ds(base, cross), :] = margin + pltpu.roll(margin, 64, 1)
        even = cross_ref[pl.ds(base, cross_pairs, stride=2), :]
        odd = cross_ref[pl.ds(base + 1, cross_pairs, stride=2), :]
        back_ref[t * packed_rows : t * packed_rows + cross_pairs, :] = jnp.where(lane < 64, even, odd)
    for q in range(cross_pairs):
        send_ref[pl.ds(q // owned * piece_rows + q % owned * tracts, tracts), :] = back_ref[
            pl.ds(q, tracts, stride=packed_rows), :
        ]
    take_pieces(send_ref, piece_refs)


def final_kernel(
    cells_ref, scaled_factor_ref, cross_factor_ref, *refs, owned
):
    *back_refs, out_ref, result_ref, back_ref, cross_ref, sems = refs
    tracts, cross, ages, _ = cells_ref.shape
    cross_rows = cross_ref.shape[0] // tracts
    cross_pairs = (cross + 1) // 2
    lane = lane_ids(1)
    place_pieces(back_refs, back_ref, owned, tracts)
    for t in range(tracts):
        base = t * cross_rows
        packed = back_ref[pl.ds(t, cross_pairs, stride=SLOT), :]
        half = pltpu.roll(packed, 64, 1)
        cross_ref[pl.ds(base, cross_pairs, stride=2), :] = jnp.where(lane < 64, packed, half)
        cross_ref[pl.ds(base + 1, cross_pairs, stride=2), :] = jnp.where(lane < 64, half, packed)
        cross_ref[pl.ds(base, cross), :] = (
            cross_ref[pl.ds(base, cross), :] * cross_factor_ref[pl.ds(base, cross), :]
        )

    def scale(t, carry):
        factor = scaled_factor_ref[t, 0:ages]
        base = t * cross_rows
        for rs in range(cross):
            result_ref[t, rs] = cells_ref[t, rs] * factor * cross_ref[pl.ds(base + rs, 1), :]
        pltpu.make_async_copy(result_ref.at[t], out_ref.at[t], sems.at[t]).start()
        return carry

    lax.fori_loop(0, tracts, scale, 0)
    for t in range(tracts):
        pltpu.make_async_copy(result_ref.at[t], out_ref.at[t], sems.at[t]).wait()


def call(kernel, out_shapes, in_spaces, out_spaces, scratch):
    def spec(space):
        return pl.BlockSpec(memory_space=space)

    run = pl.pallas_call(
        kernel,
        out_shape=[
            space(shape, F32) for shape, space in zip(out_shapes, out_spaces, strict=True)
        ],
        in_specs=[spec(space) for space in in_spaces],
        out_specs=[spec(space) for space in out_spaces],
        scratch_shapes=scratch,
        compiler_params=pltpu.CompilerParams(vmem_limit_bytes=40 << 20),
    )

    def placed(*args):
        return run(*map(pltpu.with_memory_space_constraint, args, in_spaces))

    return placed


def per_device(
    devices,
    table, age_sex, race_hisp, size_tenure, tenure_income, puma_age, puma_race, tract_puma,
):
    tracts, ages, races, sizes, inner = table.shape
    pumas = puma_age.shape[0]
    cross = races * sizes
    age_rows = -(-ages // 8) * 8
    cross_rows = -(-(cross + 1) // 8) * 8
    blocks = devices // NEAR
    block = math.gcd(blocks, LANES // SLOT)
    age_owned = -(-(age_rows // 2) // blocks)
    race_owned = -(-((cross + 1) // 2) // blocks)
    age_piece = -(-(age_owned * tracts + 1) // 8) * 8
    race_piece = -(-(race_owned * tracts) // 8) * 8
    vmem, hbm = pltpu.VMEM, pltpu.HBM

    cells = table.transpose(0, 2, 3, 1, 4).reshape(tracts, cross, ages, inner)
    cells_scratch = pltpu.VMEM((tracts, cross, ages, inner), F32)
    cross_scratch = pltpu.VMEM((tracts * cross_rows, LANES), F32)
    copy_sems = pltpu.SemaphoreType.DMA((tracts,))

    def swap(x, bits):
        return lax.ppermute(x, "tract", [(i, i ^ bits) for i in range(devices)])

    def swap_far(pieces):
        return [swap(x, d * NEAR) if d else x for d, x in enumerate(pieces)]

    def factors(total, onehot, target, piece):
        owned = target.shape[1] // LANES
        return call(
            functools.partial(factor_kernel, tracts=tracts, block=block),
            [(piece, LANES)] * blocks,
            [vmem] * (2 + NEAR),
            [vmem] * blocks,
            [pltpu.VMEM((block * SLOT, owned * LANES), F32)],
        )(onehot, target, total, *[swap(total, d) for d in range(1, NEAR)])

    small = [age_sex, race_hisp, size_tenure, tenure_income, puma_age]
    age_factor, cross_factor, own_age, cells, *pieces = call(
        functools.partial(rake_kernel, races=races, sizes=sizes, block=block),
        [
            (tracts, age_rows, LANES),
            (tracts * cross_rows, LANES),
            (pumas, age_owned * LANES),
            cells.shape,
        ]
        + [(age_piece, LANES)] * blocks,
        [hbm] * 7,
        [vmem] * (4 + blocks),
        [
            pltpu.VMEM((tracts, age_rows, LANES), F32),
            cross_scratch,
            pltpu.VMEM((pumas, blocks * age_owned * LANES), F32),
            pltpu.VMEM((blocks * age_piece, LANES), F32),
            pltpu.VMEM((tracts * SLOT, LANES), F32),
            pltpu.SMEM((tracts,), jnp.int32),
        ]
        + [pltpu.VMEM(x.shape, F32) for x in small]
        + [copy_sems, pltpu.SemaphoreType.DMA((1 + len(small),))],
    )(tract_puma, cells, *small)

    total, onehot = call(
        functools.partial(age_sum_kernel, tracts=tracts, block=block),
        [(pumas, age_owned * LANES), (blocks // block, pumas, block * SLOT)],
        [vmem] * blocks,
        [vmem] * 2,
        [pltpu.VMEM((block * SLOT, age_owned * LANES), F32)],
    )(*swap_far(pieces))
    pieces = factors(total, onehot, own_age, age_piece)

    back_rows = max(blocks * age_owned * SLOT, tracts * (-(-((cross + 1) // 2) // 8) * 8))
    scaled_factor, own_race, *pieces = call(
        functools.partial(race_margin_kernel, owned_ages=age_owned),
        [(tracts, age_rows, LANES), (pumas, race_owned * LANES)] + [(race_piece, LANES)] * blocks,
        [vmem] * (4 + blocks),
        [vmem] * (2 + blocks),
        [
            pltpu.VMEM((back_rows, LANES), F32),
            cross_scratch,
            pltpu.VMEM((pumas, blocks * race_owned * LANES), F32),
            pltpu.VMEM((blocks * race_piece, LANES), F32),
        ],
    )(cells, age_factor, cross_factor, puma_race, *swap_far(pieces))

    total, = call(
        functools.partial(race_sum_kernel, tracts=tracts, block=block),
        [(pumas, race_owned * LANES)],
        [vmem] * (1 + blocks),
        [vmem],
        [pltpu.VMEM((block * SLOT, race_owned * LANES), F32)],
    )(onehot, *swap_far(pieces))
    pieces = factors(total, onehot, own_race, race_piece)

    out, = call(
        functools.partial(final_kernel, owned=race_owned),
        [(tracts, cross, ages, inner)],
        [vmem] * (3 + blocks),
        [hbm],
        [
            cells_scratch,
            pltpu.VMEM((blocks * race_owned * SLOT, LANES), F32),
            cross_scratch,
            copy_sems,
        ],
    )(cells, scaled_factor, cross_factor, *swap_far(pieces))
    return out.reshape(tracts, races, sizes, ages, inner).transpose(0, 3, 1, 2, 4)


def solution(mesh):
    in_specs = (
        P(("grp", "tract"), None, None, None, None),
        P(("grp", "tract"), None),
        P(("grp", "tract"), None),
        P(("grp", "tract"), None),
        P(("grp", "tract"), None),
        P("grp", None),
        P("grp", None),
        P(("grp", "tract")),
    )
    out_specs = P(("grp", "tract"), None, None, None, None)
    return jax.shard_map(
        functools.partial(per_device, mesh.shape["tract"]),
        mesh=mesh, in_specs=in_specs, out_specs=out_specs, check_vma=False,
    )
```

```python
import functools
import math

import jax
import jax.numpy as jnp
from jax import lax
from jax.experimental import pallas as pl
from jax.experimental.pallas import tpu as pltpu
from jax.sharding import PartitionSpec as P

LANES = 128
SLOT = 16
NEAR = 4
F32 = jnp.float32
BF16 = jnp.bfloat16


def piece_rows(owned, tracts, more=0):
    return -(-(owned * tracts + more) // 8) * 8


def lane_ids(rows):
    return lax.broadcasted_iota(jnp.int32, (rows, LANES), 1)


def masked_lane_sum(value, mask):
    return jnp.sum(jnp.where(mask, value, 0.0), axis=-1, keepdims=True)


def column_of(row, rows, step, offset):
    width = row.shape[-1]
    lane = lax.broadcasted_iota(jnp.int32, (rows, width), 1)
    sub = lax.broadcasted_iota(jnp.int32, (rows, width), 0)
    return jnp.sum(jnp.where(lane == step * sub + offset, row, 0.0), axis=-1, keepdims=True)


def own_targets(target_ref, wide_ref, own_ref):
    pumas, columns = target_ref.shape
    full = columns // LANES * LANES
    wide_ref[:, full:] = jnp.zeros((pumas, wide_ref.shape[1] - full), F32)
    if full:
        wide_ref[:, 0:full] = target_ref[:, 0:full]
    wide_ref[:, full:columns] = target_ref[:, full:columns]
    width = own_ref.shape[1]
    start = pl.multiple_of(lax.axis_index("tract") // NEAR * width, LANES)
    own_ref[...] = wide_ref[:, pl.ds(start, width)]


def place_rows(back_ref, rows_ref, owned, tracts, pairs):
    piece = piece_rows(owned, tracts)
    for q in range(pairs):
        start = q // owned * piece + q % owned * tracts
        rows_ref[q * SLOT : q * SLOT + tracts, :] = back_ref[start : start + tracts, :]


def rake_kernel(
    ids_hbm, table_hbm, age_sex_hbm, race_hisp_hbm, size_tenure_hbm, tenure_income_hbm, target_hbm,
    age_factor_ref, cross_factor_ref, own_target_ref, cells_ref, *refs,
    races, sizes, block,
):
    send_ref, sum_ref, cross_ref, wide_ref, packed_ref = refs[:-8]
    (
        ids_ref, age_sex_ref, race_hisp_ref, size_tenure_ref, tenure_income_ref, target_ref,
        sems, small_sems,
    ) = refs[-8:]
    tracts, cross, ages, _ = table_hbm.shape
    cross_rows = cross_ref.shape[0] // tracts
    small = [
        pltpu.make_async_copy(source, target, small_sems.at[i])
        for i, (source, target) in enumerate((
            (ids_hbm, ids_ref),
            (age_sex_hbm, age_sex_ref),
            (race_hisp_hbm, race_hisp_ref),
            (size_tenure_hbm, size_tenure_ref),
            (tenure_income_hbm, tenure_income_ref),
            (target_hbm, target_ref),
        ))
    ]
    for copy in small[:-1]:
        copy.start()
    for t in range(tracts):
        pltpu.make_async_copy(table_hbm.at[t], cells_ref.at[t], sems.at[t]).start()
    small[-1].start()
    lane = lane_ids(1)
    sex0 = lane < 64
    hisp0 = (lane // 32) % 2 == 0
    ten0 = (lane // 16) % 2 == 0

    def add_cross(t, carry):
        pltpu.make_async_copy(table_hbm.at[t], cells_ref.at[t], sems.at[t]).wait()
        total = cells_ref[t, 0]
        for rs in range(1, cross):
            total = total + cells_ref[t, rs]
        sum_ref[t, 0:ages] = total
        return carry

    lax.fori_loop(0, tracts, add_cross, 0)
    for copy in small:
        copy.wait()
    own_targets(target_ref, wide_ref, own_target_ref)

    for t in range(tracts):
        total = sum_ref[t, 0:ages]
        row = age_sex_ref[t : t + 1, :]
        first = column_of(row, ages, 2, 0) / masked_lane_sum(total, sex0)
        second = column_of(row, ages, 2, 1) / masked_lane_sum(total, ~sex0)
        age_factor_ref[t, 0:ages] = jnp.where(sex0, first, second)

    def add_ages(t, carry):
        factor = age_factor_ref[t, 0:ages]
        base = t * cross_rows
        for rs in range(cross):
            cross_ref[pl.ds(base + rs, 1), :] = jnp.sum(
                cells_ref[t, rs] * factor, axis=0, keepdims=True
            )
        return carry

    lax.fori_loop(0, tracts, add_ages, 0)

    for t in range(tracts):
        base = t * cross_rows
        by_race = cross_ref[pl.ds(base, races, stride=sizes), :]
        for s in range(1, sizes):
            by_race = by_race + cross_ref[pl.ds(base + s, races, stride=sizes), :]
        row = race_hisp_ref[t : t + 1, :]
        first = column_of(row, races, 2, 0) / masked_lane_sum(by_race, hisp0)
        second = column_of(row, races, 2, 1) / masked_lane_sum(by_race, ~hisp0)
        race_factor = jnp.where(hisp0, first, second)
        by_size = cross_ref[pl.ds(base, sizes), :] * race_factor[0:1]
        for r in range(1, races):
            by_size = by_size + cross_ref[pl.ds(base + r * sizes, sizes), :] * race_factor[r : r + 1]
        row = size_tenure_ref[t : t + 1, :]
        first = column_of(row, sizes, 2, 0) / masked_lane_sum(by_size, ten0)
        second = column_of(row, sizes, 2, 1) / masked_lane_sum(by_size, ~ten0)
        size_factor = jnp.where(ten0, first, second)
        by_income = jnp.sum(by_size * size_factor, axis=0, keepdims=True)
        by_income = by_income + pltpu.roll(by_income, 64, 1)
        by_income = by_income + pltpu.roll(by_income, 32, 1)
        row = tenure_income_ref[t : t + 1, :]
        income_factor = jnp.concatenate([row] * 4, axis=1) / by_income
        age_factor_ref[t, 0:ages] = age_factor_ref[t, 0:ages] * income_factor
        for r in range(races):
            cross_factor_ref[pl.ds(base + r * sizes, sizes), :] = size_factor * race_factor[r : r + 1]

    def add_scaled(t, carry):
        base = t * cross_rows
        total = cells_ref[t, 0] * cross_factor_ref[pl.ds(base, 1), :]
        for rs in range(1, cross):
            total = total + cells_ref[t, rs] * cross_factor_ref[pl.ds(base + rs, 1), :]
        sum_ref[t, 0:ages] = total * age_factor_ref[t, 0:ages]
        sum_ref[t, ages:] = jnp.zeros((sum_ref.shape[1] - ages, LANES), F32)
        return carry

    lax.fori_loop(0, tracts, add_scaled, 0)

    pairs = sum_ref.shape[1] // 2
    owned = own_target_ref.shape[1] // LANES
    piece = piece_rows(owned, tracts, 1)
    send_ref[...] = jnp.zeros(send_ref.shape, F32)
    for t in range(tracts):
        even = sum_ref[t, pl.ds(0, pairs, stride=2)]
        odd = sum_ref[t, pl.ds(1, pairs, stride=2)]
        even = even + pltpu.roll(even, 96, 1)
        odd = odd + pltpu.roll(odd, 96, 1)
        packed_ref[t * SLOT : t * SLOT + pairs] = jnp.where(
            lane < 32,
            even,
            jnp.where(
                lane < 64,
                pltpu.roll(even, 96, 1),
                jnp.where(lane < 96, pltpu.roll(odd, 64, 1), pltpu.roll(odd, 32, 1)),
            ),
        )
    for q in range(pairs):
        send_ref[pl.ds(q // owned * piece + q % owned * tracts, tracts), :] = packed_ref[
            pl.ds(q, tracts, stride=SLOT), :
        ]
    start = lax.rem(lax.axis_index("tract") // NEAR, block) * SLOT
    row = jnp.zeros((1, LANES), F32)
    for t in range(tracts):
        row = jnp.where(lane == start + t, (ids_ref[t] + 1).astype(F32), row)
    for i in range(send_ref.shape[0] // piece):
        send_ref[pl.ds(i * piece + owned * tracts, 1), :] = row


def split_dot(onehot, value, dims):
    total = None
    for _ in range(3):
        part = value.astype(BF16)
        value = value - part.astype(F32)
        term = lax.dot_general(onehot, part, (dims, ((), ())), preferred_element_type=F32)
        total = term if total is None else total + term
    return total


def block_sum(onehot, recv_ref, first, piece, slot_ref, tracts):
    owned = slot_ref.shape[1] // LANES
    zeros = jnp.zeros((SLOT - tracts, LANES), F32)
    for i in range(slot_ref.shape[0] // SLOT):
        for k in range(owned):
            lanes = slice(k * LANES, (k + 1) * LANES)
            start = (first + i) * piece + k * tracts
            slot_ref[i * SLOT : i * SLOT + tracts, lanes] = recv_ref[start : start + tracts, :]
            slot_ref[i * SLOT + tracts : (i + 1) * SLOT, lanes] = zeros
    return split_dot(onehot.astype(BF16), slot_ref[...], ((1,), (0,)))


def put_copies(total_ref, total):
    rows = total.shape[0]
    for i in range(NEAR):
        total_ref[i * rows : (i + 1) * rows, :] = total


def age_sum_kernel(recv_ref, total_ref, onehot_ref, slot_ref, *, tracts):
    blocks, pumas, slots = onehot_ref.shape
    block = slots // SLOT
    owned = slot_ref.shape[1] // LANES
    piece = piece_rows(owned, tracts, 1)
    puma = lax.broadcasted_iota(jnp.int32, (pumas, LANES), 0) + 1
    total = None
    for b in range(blocks):
        ids = jnp.zeros((1, LANES), F32)
        for i in range(b * block, (b + 1) * block):
            ids = ids + recv_ref[pl.ds(i * piece + owned * tracts, 1), :]
        onehot = jnp.where(ids.astype(jnp.int32) == puma, 1.0, 0.0)[:, 0:slots]
        onehot_ref[b] = onehot
        term = block_sum(onehot, recv_ref, b * block, piece, slot_ref, tracts)
        total = term if total is None else total + term
    put_copies(total_ref, total)


def race_sum_kernel(onehot_ref, recv_ref, total_ref, slot_ref, *, tracts):
    blocks, _, slots = onehot_ref.shape
    block = slots // SLOT
    piece = piece_rows(slot_ref.shape[1] // LANES, tracts)
    total = None
    for b in range(blocks):
        term = block_sum(onehot_ref[b], recv_ref, b * block, piece, slot_ref, tracts)
        total = term if total is None else total + term
    put_copies(total_ref, total)


def factor_kernel(onehot_ref, target_ref, total_ref, back_ref, slot_ref, *, tracts):
    blocks, pumas, slots = onehot_ref.shape
    block = slots // SLOT
    owned = target_ref.shape[1] // LANES
    piece = piece_rows(owned, tracts)
    total = total_ref[0:pumas, :]
    for i in range(1, NEAR):
        total = total + total_ref[i * pumas : (i + 1) * pumas, :]
    target = target_ref[...]
    factor = jnp.where(target > 0.0, target / total, 0.0)
    for b in range(blocks):
        slot_ref[...] = split_dot(onehot_ref[b].astype(BF16), factor, ((0,), (0,)))
        for i in range(block):
            start = (b * block + i) * piece
            for k in range(owned):
                lanes = slice(k * LANES, (k + 1) * LANES)
                rows = slice(start + k * tracts, start + (k + 1) * tracts)
                back_ref[rows, :] = slot_ref[i * SLOT : i * SLOT + tracts, lanes]
            if piece > owned * tracts:
                rows = slice(start + owned * tracts, start + piece)
                back_ref[rows, :] = jnp.zeros((piece - owned * tracts, LANES), F32)


def race_margin_kernel(
    cells_ref, age_factor_ref, cross_factor_ref, target_ref, back_ref,
    scaled_factor_ref, own_target_ref, send_ref,
    rows_ref, cross_ref, wide_ref,
    *, owned_ages,
):
    tracts, cross, ages, _ = cells_ref.shape
    cross_rows = cross_ref.shape[0] // tracts
    pairs = age_factor_ref.shape[1] // 2
    own_targets(target_ref, wide_ref, own_target_ref)
    lane = lane_ids(1)
    place_rows(back_ref, rows_ref, owned_ages, tracts, pairs)
    for t in range(tracts):
        packed = rows_ref[pl.ds(t, pairs, stride=SLOT), :]
        half = pltpu.roll(packed, 64, 1)
        even = jnp.where(lane < 32, packed, jnp.where(lane < 96, pltpu.roll(packed, 32, 1), half))
        odd = jnp.where(lane < 32, half, jnp.where(lane < 96, pltpu.roll(packed, 96, 1), packed))
        scaled_factor_ref[t, pl.ds(0, pairs, stride=2)] = even
        scaled_factor_ref[t, pl.ds(1, pairs, stride=2)] = odd

    def add_ages(t, carry):
        factor = scaled_factor_ref[t, 0:ages] * age_factor_ref[t, 0:ages]
        scaled_factor_ref[t, 0:ages] = factor
        base = t * cross_rows
        for rs in range(cross):
            cross_ref[pl.ds(base + rs, 1), :] = jnp.sum(
                cells_ref[t, rs] * factor, axis=0, keepdims=True
            )
        cross_ref[pl.ds(base + cross, cross_rows - cross), :] = jnp.zeros(
            (cross_rows - cross, LANES), F32
        )
        return carry

    lax.fori_loop(0, tracts, add_ages, 0)

    cross_pairs = (cross + 1) // 2
    owned = own_target_ref.shape[1] // LANES
    piece = piece_rows(owned, tracts)
    send_ref[...] = jnp.zeros(send_ref.shape, F32)
    packed_rows = -(-cross_pairs // 8) * 8
    for t in range(tracts):
        base = t * cross_rows
        margin = cross_ref[pl.ds(base, cross), :] * cross_factor_ref[pl.ds(base, cross), :]
        cross_ref[pl.ds(base, cross), :] = margin + pltpu.roll(margin, 64, 1)
        even = cross_ref[pl.ds(base, cross_pairs, stride=2), :]
        odd = cross_ref[pl.ds(base + 1, cross_pairs, stride=2), :]
        rows_ref[t * packed_rows : t * packed_rows + cross_pairs, :] = jnp.where(lane < 64, even, odd)
    for q in range(cross_pairs):
        send_ref[pl.ds(q // owned * piece + q % owned * tracts, tracts), :] = rows_ref[
            pl.ds(q, tracts, stride=packed_rows), :
        ]


def final_kernel(
    cells_ref, scaled_factor_ref, cross_factor_ref, back_ref,
    out_ref,
    result_ref, rows_ref, cross_ref, sems,
    *, owned,
):
    tracts, cross, ages, _ = cells_ref.shape
    cross_rows = cross_ref.shape[0] // tracts
    cross_pairs = (cross + 1) // 2
    lane = lane_ids(1)
    place_rows(back_ref, rows_ref, owned, tracts, cross_pairs)
    for t in range(tracts):
        base = t * cross_rows
        packed = rows_ref[pl.ds(t, cross_pairs, stride=SLOT), :]
        half = pltpu.roll(packed, 64, 1)
        cross_ref[pl.ds(base, cross_pairs, stride=2), :] = jnp.where(lane < 64, packed, half)
        cross_ref[pl.ds(base + 1, cross_pairs, stride=2), :] = jnp.where(lane < 64, half, packed)
        cross_ref[pl.ds(base, cross), :] = (
            cross_ref[pl.ds(base, cross), :] * cross_factor_ref[pl.ds(base, cross), :]
        )

    def scale(t, carry):
        factor = scaled_factor_ref[t, 0:ages]
        base = t * cross_rows
        for rs in range(cross):
            result_ref[t, rs] = cells_ref[t, rs] * factor * cross_ref[pl.ds(base + rs, 1), :]
        pltpu.make_async_copy(result_ref.at[t], out_ref.at[t], sems.at[t]).start()
        return carry

    lax.fori_loop(0, tracts, scale, 0)
    for t in range(tracts):
        pltpu.make_async_copy(result_ref.at[t], out_ref.at[t], sems.at[t]).wait()


def call(kernel, out_shapes, in_spaces, out_spaces, scratch):
    def spec(space):
        return pl.BlockSpec(memory_space=space)

    run = pl.pallas_call(
        kernel,
        out_shape=[
            space(shape, F32) for shape, space in zip(out_shapes, out_spaces, strict=True)
        ],
        in_specs=[spec(space) for space in in_spaces],
        out_specs=[spec(space) for space in out_spaces],
        scratch_shapes=scratch,
        compiler_params=pltpu.CompilerParams(vmem_limit_bytes=40 << 20),
    )

    def placed(*args):
        return run(*map(pltpu.with_memory_space_constraint, args, in_spaces))

    return placed


def per_device(
    devices,
    table, age_sex, race_hisp, size_tenure, tenure_income, puma_age, puma_race, tract_puma,
):
    tracts, ages, races, sizes, inner = table.shape
    pumas = puma_age.shape[0]
    cross = races * sizes
    age_rows = -(-ages // 8) * 8
    cross_rows = -(-(cross + 1) // 8) * 8
    blocks = devices // NEAR
    block = math.gcd(blocks, LANES // SLOT)
    age_owned = -(-(age_rows // 2) // blocks)
    race_owned = -(-((cross + 1) // 2) // blocks)
    slots = block * SLOT
    vmem, hbm = pltpu.VMEM, pltpu.HBM

    cells = table.transpose(0, 2, 3, 1, 4).reshape(tracts, cross, ages, inner)
    cells_scratch = pltpu.VMEM((tracts, cross, ages, inner), F32)
    cross_scratch = pltpu.VMEM((tracts * cross_rows, LANES), F32)
    copy_sems = pltpu.SemaphoreType.DMA((tracts,))

    def swap(x, groups):
        width = len(groups[0])
        pieces = x.reshape(width, x.shape[0] // width, x.shape[1])
        return lax.all_to_all(pieces, "tract", 0, 0, axis_index_groups=groups).reshape(x.shape)

    def swap_far(x):
        return swap(x, [list(range(near, devices, NEAR)) for near in range(NEAR)])

    def factors(total, onehot, target):
        owned = target.shape[1] // LANES
        total = swap(total, [list(range(i, i + NEAR)) for i in range(0, devices, NEAR)])
        back, = call(
            functools.partial(factor_kernel, tracts=tracts),
            [(blocks * piece_rows(owned, tracts), LANES)],
            [vmem] * 3,
            [vmem],
            [pltpu.VMEM((slots, owned * LANES), F32)],
        )(onehot, target, total)
        return swap_far(back)

    small = [age_sex, race_hisp, size_tenure, tenure_income, puma_age]
    age_factor, cross_factor, own_age, cells, send = call(
        functools.partial(rake_kernel, races=races, sizes=sizes, block=block),
        [
            (tracts, age_rows, LANES),
            (tracts * cross_rows, LANES),
            (pumas, age_owned * LANES),
            cells.shape,
            (blocks * piece_rows(age_owned, tracts, 1), LANES),
        ],
        [hbm] * 7,
        [vmem] * 5,
        [
            pltpu.VMEM((tracts, age_rows, LANES), F32),
            cross_scratch,
            pltpu.VMEM((pumas, blocks * age_owned * LANES), F32),
            pltpu.VMEM((tracts * SLOT, LANES), F32),
            pltpu.SMEM((tracts,), jnp.int32),
        ]
        + [pltpu.VMEM(x.shape, F32) for x in small]
        + [copy_sems, pltpu.SemaphoreType.DMA((1 + len(small),))],
    )(tract_puma, cells, *small)

    total, onehot = call(
        functools.partial(age_sum_kernel, tracts=tracts),
        [(NEAR * pumas, age_owned * LANES), (blocks // block, pumas, slots)],
        [vmem],
        [vmem] * 2,
        [pltpu.VMEM((slots, age_owned * LANES), F32)],
    )(swap_far(send))
    back = factors(total, onehot, own_age)

    age_pairs, cross_pairs = age_rows // 2, (cross + 1) // 2
    scaled_factor, own_race, send = call(
        functools.partial(race_margin_kernel, owned_ages=age_owned),
        [
            (tracts, age_rows, LANES),
            (pumas, race_owned * LANES),
            (blocks * piece_rows(race_owned, tracts), LANES),
        ],
        [vmem] * 5,
        [vmem] * 3,
        [
            pltpu.VMEM((max(age_pairs * SLOT, tracts * (-(-cross_pairs // 8) * 8)), LANES), F32),
            cross_scratch,
            pltpu.VMEM((pumas, blocks * race_owned * LANES), F32),
        ],
    )(cells, age_factor, cross_factor, puma_race, back)

    total, = call(
        functools.partial(race_sum_kernel, tracts=tracts),
        [(NEAR * pumas, race_owned * LANES)],
        [vmem] * 2,
        [vmem],
        [pltpu.VMEM((slots, race_owned * LANES), F32)],
    )(onehot, swap_far(send))
    back = factors(total, onehot, own_race)

    out, = call(
        functools.partial(final_kernel, owned=race_owned),
        [(tracts, cross, ages, inner)],
        [vmem] * 4,
        [hbm],
        [cells_scratch, pltpu.VMEM((cross_pairs * SLOT, LANES), F32), cross_scratch, copy_sems],
    )(cells, scaled_factor, cross_factor, back)
    return out.reshape(tracts, races, sizes, ages, inner).transpose(0, 3, 1, 2, 4)


def solution(mesh):
    in_specs = (
        P(("grp", "tract"), None, None, None, None),
        P(("grp", "tract"), None),
        P(("grp", "tract"), None),
        P(("grp", "tract"), None),
        P(("grp", "tract"), None),
        P("grp", None),
        P("grp", None),
        P(("grp", "tract")),
    )
    out_specs = P(("grp", "tract"), None, None, None, None)
    return jax.shard_map(
        functools.partial(per_device, mesh.shape["tract"]),
        mesh=mesh, in_specs=in_specs, out_specs=out_specs, check_vma=False,
    )
```

```python
import functools

import jax
import jax.numpy as jnp
from jax import lax
from jax.experimental import pallas as pl
from jax.experimental.pallas import tpu as pltpu
from jax.sharding import PartitionSpec as P

LANES = 128
F32 = jnp.float32


def lane_ids(rows):
    return lax.broadcasted_iota(jnp.int32, (rows, LANES), 1)


def masked_lane_sum(value, mask):
    return jnp.sum(jnp.where(mask, value, 0.0), axis=-1, keepdims=True)


def column_of(row, rows, step, offset):
    width = row.shape[-1]
    lane = lax.broadcasted_iota(jnp.int32, (rows, width), 1)
    sub = lax.broadcasted_iota(jnp.int32, (rows, width), 0)
    return jnp.sum(jnp.where(lane == step * sub + offset, row, 0.0), axis=-1, keepdims=True)


def core_of(index):
    return index % 2


def part_of(index):
    return jnp.where(core_of(index) == 0, index // 2 % 2, index // 4 % 2)


def own_targets(target_ref, wide_ref, own_ref):
    pumas, columns = target_ref.shape
    full = columns // LANES * LANES
    wide_ref[:, full:] = jnp.zeros((pumas, wide_ref.shape[1] - full), F32)
    if full:
        wide_ref[:, 0:full] = target_ref[:, 0:full]
    wide_ref[:, full:columns] = target_ref[:, full:columns]
    owned = own_ref.shape[0] // pumas
    index = lax.axis_index("tract")
    quarter = 2 * core_of(index) + part_of(index)
    for k in range(owned):
        start = pl.multiple_of((quarter * owned + k) * LANES, LANES)
        own_ref[k * pumas : (k + 1) * pumas, :] = wide_ref[:, pl.ds(start, LANES)]


def take_half(rows_ref, which, out_ref):
    rows = out_ref.shape[0]
    out_ref[...] = rows_ref[pl.ds(pl.multiple_of(which * rows, 8), rows), :]


def place_quarters(quarter_refs, rows_ref):
    index = lax.axis_index("tract")
    own, near = core_of(index), part_of(index)
    other = part_of(lax.bitwise_xor(index, 1))
    places = (2 * own + near, 2 * own + 1 - near, 2 - 2 * own + other, 3 - 2 * own - other)
    for ref, place in zip(quarter_refs, places, strict=True):
        rows = ref.shape[0]
        rows_ref[pl.ds(pl.multiple_of(place * rows, 8), rows), :] = ref[...]


def rake_kernel(
    ids_hbm, table_hbm, age_sex_hbm, race_hisp_hbm, size_tenure_hbm, tenure_income_hbm, target_hbm,
    keep_ref, send_ref, age_factor_ref, cross_factor_ref, own_target_ref, cells_ref,
    sum_ref, cross_ref, wide_ref, rows_ref,
    ids_ref, age_sex_ref, race_hisp_ref, size_tenure_ref, tenure_income_ref, target_ref,
    sems, small_sems,
    *, races, sizes,
):
    tracts, cross, ages, _ = table_hbm.shape
    cross_rows = cross_ref.shape[0] // tracts
    small = [
        pltpu.make_async_copy(source, target, small_sems.at[i])
        for i, (source, target) in enumerate((
            (ids_hbm, ids_ref),
            (age_sex_hbm, age_sex_ref),
            (race_hisp_hbm, race_hisp_ref),
            (size_tenure_hbm, size_tenure_ref),
            (tenure_income_hbm, tenure_income_ref),
            (target_hbm, target_ref),
        ))
    ]
    for copy in small[:-1]:
        copy.start()
    for t in range(tracts):
        pltpu.make_async_copy(table_hbm.at[t], cells_ref.at[t], sems.at[t]).start()
    small[-1].start()
    lane = lane_ids(1)
    sex0 = lane < 64
    hisp0 = (lane // 32) % 2 == 0
    ten0 = (lane // 16) % 2 == 0

    def add_cross(t, carry):
        pltpu.make_async_copy(table_hbm.at[t], cells_ref.at[t], sems.at[t]).wait()
        total = cells_ref[t, 0]
        for rs in range(1, cross):
            total = total + cells_ref[t, rs]
        sum_ref[t, 0:ages] = total
        return carry

    lax.fori_loop(0, tracts, add_cross, 0)
    for copy in small:
        copy.wait()
    own_targets(target_ref, wide_ref, own_target_ref)

    for t in range(tracts):
        total = sum_ref[t, 0:ages]
        row = age_sex_ref[t : t + 1, :]
        first = column_of(row, ages, 2, 0) / masked_lane_sum(total, sex0)
        second = column_of(row, ages, 2, 1) / masked_lane_sum(total, ~sex0)
        age_factor_ref[t, 0:ages] = jnp.where(sex0, first, second)

    def add_ages(t, carry):
        factor = age_factor_ref[t, 0:ages]
        base = t * cross_rows
        for rs in range(cross):
            cross_ref[pl.ds(base + rs, 1), :] = jnp.sum(
                cells_ref[t, rs] * factor, axis=0, keepdims=True
            )
        return carry

    lax.fori_loop(0, tracts, add_ages, 0)

    for t in range(tracts):
        base = t * cross_rows
        by_race = cross_ref[pl.ds(base, races, stride=sizes), :]
        for s in range(1, sizes):
            by_race = by_race + cross_ref[pl.ds(base + s, races, stride=sizes), :]
        row = race_hisp_ref[t : t + 1, :]
        first = column_of(row, races, 2, 0) / masked_lane_sum(by_race, hisp0)
        second = column_of(row, races, 2, 1) / masked_lane_sum(by_race, ~hisp0)
        race_factor = jnp.where(hisp0, first, second)
        by_size = cross_ref[pl.ds(base, sizes), :] * race_factor[0:1]
        for r in range(1, races):
            by_size = by_size + cross_ref[pl.ds(base + r * sizes, sizes), :] * race_factor[r : r + 1]
        row = size_tenure_ref[t : t + 1, :]
        first = column_of(row, sizes, 2, 0) / masked_lane_sum(by_size, ten0)
        second = column_of(row, sizes, 2, 1) / masked_lane_sum(by_size, ~ten0)
        size_factor = jnp.where(ten0, first, second)
        by_income = jnp.sum(by_size * size_factor, axis=0, keepdims=True)
        by_income = by_income + pltpu.roll(by_income, 64, 1)
        by_income = by_income + pltpu.roll(by_income, 32, 1)
        row = tenure_income_ref[t : t + 1, :]
        income_factor = jnp.concatenate([row] * 4, axis=1) / by_income
        age_factor_ref[t, 0:ages] = age_factor_ref[t, 0:ages] * income_factor
        for r in range(races):
            cross_factor_ref[pl.ds(base + r * sizes, sizes), :] = size_factor * race_factor[r : r + 1]

    def add_scaled(t, carry):
        base = t * cross_rows
        total = cells_ref[t, 0] * cross_factor_ref[pl.ds(base, 1), :]
        for rs in range(1, cross):
            total = total + cells_ref[t, rs] * cross_factor_ref[pl.ds(base + rs, 1), :]
        sum_ref[t, 0:ages] = total * age_factor_ref[t, 0:ages]
        sum_ref[t, ages:] = jnp.zeros((sum_ref.shape[1] - ages, LANES), F32)
        return carry

    lax.fori_loop(0, tracts, add_scaled, 0)

    pairs = sum_ref.shape[1] // 2
    pumas = target_ref.shape[0]
    rows_ref[...] = jnp.zeros(rows_ref.shape, F32)
    for t in range(tracts):
        even = sum_ref[t, pl.ds(0, pairs, stride=2)]
        odd = sum_ref[t, pl.ds(1, pairs, stride=2)]
        even = even + pltpu.roll(even, 96, 1)
        odd = odd + pltpu.roll(odd, 96, 1)
        packed = jnp.where(
            lane < 32,
            even,
            jnp.where(
                lane < 64,
                pltpu.roll(even, 96, 1),
                jnp.where(lane < 96, pltpu.roll(odd, 64, 1), pltpu.roll(odd, 32, 1)),
            ),
        )
        at = pl.ds(ids_ref[t], pairs, stride=pumas)
        rows_ref[at, :] = rows_ref[at, :] + packed
    core = core_of(lax.axis_index("tract"))
    take_half(rows_ref, core, keep_ref)
    take_half(rows_ref, 1 - core, send_ref)


def split_kernel(mine_ref, theirs_ref, keep_ref, send_ref):
    part = part_of(lax.axis_index("tract"))
    rows = keep_ref.shape[0]
    for which, out_ref in ((part, keep_ref), (1 - part, send_ref)):
        at = pl.ds(pl.multiple_of(which * rows, 8), rows)
        out_ref[...] = mine_ref[at, :] + theirs_ref[at, :]


def factor_kernel(target_ref, mine_ref, theirs_ref, factor_ref):
    target = target_ref[...]
    factor_ref[...] = jnp.where(target > 0.0, target / (mine_ref[...] + theirs_ref[...]), 0.0)


def race_margin_kernel(
    ids_ref, cells_ref, age_factor_ref, cross_factor_ref, target_ref,
    own_ref, near_ref, other_ref, far_ref,
    keep_ref, send_ref, scaled_factor_ref, own_target_ref,
    cross_ref, wide_ref, age_rows_ref, rows_ref,
):
    tracts, cross, ages, _ = cells_ref.shape
    cross_rows = cross_ref.shape[0] // tracts
    pairs = age_factor_ref.shape[1] // 2
    pumas = target_ref.shape[0]
    own_targets(target_ref, wide_ref, own_target_ref)
    place_quarters((own_ref, near_ref, other_ref, far_ref), age_rows_ref)
    lane = lane_ids(1)
    for t in range(tracts):
        packed = age_rows_ref[pl.ds(ids_ref[t], pairs, stride=pumas), :]
        half = pltpu.roll(packed, 64, 1)
        even = jnp.where(lane < 32, packed, jnp.where(lane < 96, pltpu.roll(packed, 32, 1), half))
        odd = jnp.where(lane < 32, half, jnp.where(lane < 96, pltpu.roll(packed, 96, 1), packed))
        scaled_factor_ref[t, pl.ds(0, pairs, stride=2)] = even
        scaled_factor_ref[t, pl.ds(1, pairs, stride=2)] = odd

    def add_ages(t, carry):
        factor = scaled_factor_ref[t, 0:ages] * age_factor_ref[t, 0:ages]
        scaled_factor_ref[t, 0:ages] = factor
        base = t * cross_rows
        for rs in range(cross):
            cross_ref[pl.ds(base + rs, 1), :] = jnp.sum(
                cells_ref[t, rs] * factor, axis=0, keepdims=True
            )
        cross_ref[pl.ds(base + cross, cross_rows - cross), :] = jnp.zeros(
            (cross_rows - cross, LANES), F32
        )
        return carry

    lax.fori_loop(0, tracts, add_ages, 0)

    cross_pairs = (cross + 1) // 2
    rows_ref[...] = jnp.zeros(rows_ref.shape, F32)
    for t in range(tracts):
        base = t * cross_rows
        margin = cross_ref[pl.ds(base, cross), :] * cross_factor_ref[pl.ds(base, cross), :]
        cross_ref[pl.ds(base, cross), :] = margin + pltpu.roll(margin, 64, 1)
        even = cross_ref[pl.ds(base, cross_pairs, stride=2), :]
        odd = cross_ref[pl.ds(base + 1, cross_pairs, stride=2), :]
        at = pl.ds(ids_ref[t], cross_pairs, stride=pumas)
        rows_ref[at, :] = rows_ref[at, :] + jnp.where(lane < 64, even, odd)
    core = core_of(lax.axis_index("tract"))
    take_half(rows_ref, core, keep_ref)
    take_half(rows_ref, 1 - core, send_ref)


def final_kernel(
    ids_ref, cells_ref, scaled_factor_ref, cross_factor_ref,
    own_ref, near_ref, other_ref, far_ref,
    out_ref,
    result_ref, cross_ref, rows_ref, sems,
    *, pumas,
):
    tracts, cross, ages, _ = cells_ref.shape
    cross_rows = cross_ref.shape[0] // tracts
    cross_pairs = (cross + 1) // 2
    place_quarters((own_ref, near_ref, other_ref, far_ref), rows_ref)
    lane = lane_ids(1)
    for t in range(tracts):
        base = t * cross_rows
        packed = rows_ref[pl.ds(ids_ref[t], cross_pairs, stride=pumas), :]
        half = pltpu.roll(packed, 64, 1)
        cross_ref[pl.ds(base, cross_pairs, stride=2), :] = jnp.where(lane < 64, packed, half)
        cross_ref[pl.ds(base + 1, cross_pairs, stride=2), :] = jnp.where(lane < 64, half, packed)
        cross_ref[pl.ds(base, cross), :] = (
            cross_ref[pl.ds(base, cross), :] * cross_factor_ref[pl.ds(base, cross), :]
        )

    def scale(t, carry):
        factor = scaled_factor_ref[t, 0:ages]
        base = t * cross_rows
        for rs in range(cross):
            result_ref[t, rs] = cells_ref[t, rs] * factor * cross_ref[pl.ds(base + rs, 1), :]
        pltpu.make_async_copy(result_ref.at[t], out_ref.at[t], sems.at[t]).start()
        return carry

    lax.fori_loop(0, tracts, scale, 0)
    for t in range(tracts):
        pltpu.make_async_copy(result_ref.at[t], out_ref.at[t], sems.at[t]).wait()


def call(kernel, out_shapes, in_spaces, out_spaces, scratch):
    def spec(space):
        return pl.BlockSpec(memory_space=space)

    run = pl.pallas_call(
        kernel,
        out_shape=[
            space(shape, F32) for shape, space in zip(out_shapes, out_spaces, strict=True)
        ],
        in_specs=[spec(space) for space in in_spaces],
        out_specs=[spec(space) for space in out_spaces],
        scratch_shapes=scratch,
        compiler_params=pltpu.CompilerParams(vmem_limit_bytes=40 << 20),
    )

    def placed(*args):
        return run(*map(pltpu.with_memory_space_constraint, args, in_spaces))

    return placed


def per_device(
    devices,
    table, age_sex, race_hisp, size_tenure, tenure_income, puma_age, puma_race, tract_puma,
):
    tracts, ages, races, sizes, inner = table.shape
    pumas = puma_age.shape[0]
    cross = races * sizes
    age_rows = -(-ages // 8) * 8
    cross_rows = -(-(cross + 1) // 8) * 8
    age_owned = -(-(age_rows // 2) // 4)
    race_owned = -(-((cross + 1) // 2) // 4)
    vmem, smem, hbm = pltpu.VMEM, pltpu.SMEM, pltpu.HBM

    cells = table.transpose(0, 2, 3, 1, 4).reshape(tracts, cross, ages, inner)
    cells_scratch = pltpu.VMEM((tracts, cross, ages, inner), F32)
    cross_scratch = pltpu.VMEM((tracts * cross_rows, LANES), F32)
    copy_sems = pltpu.SemaphoreType.DMA((tracts,))

    bits = [1 << k for k in range(1, devices.bit_length() - 1)]
    orders = (bits, bits[1:] + bits[:1])

    def swap(x, step):
        if step is None:
            pairs = [(i, i ^ 1) for i in range(devices)]
        else:
            pairs = [(i, i ^ orders[i % 2][step]) for i in range(devices)]
        return lax.ppermute(x, "tract", pairs)

    def factors(keep, send, target):
        quarter = target.shape
        keep, send = call(split_kernel, [quarter] * 2, [vmem] * 2, [vmem] * 2, [])(
            keep, swap(send, None)
        )
        total, theirs = keep, swap(send, 0)
        for step in range(1, len(bits)):
            total = total + theirs
            theirs = swap(total, step)
        own, = call(factor_kernel, [quarter], [vmem] * 3, [vmem], [])(target, total, theirs)
        near = swap(own, 0)
        return own, near, swap(own, None), swap(near, None)

    small = [age_sex, race_hisp, size_tenure, tenure_income, puma_age]
    keep, send, age_factor, cross_factor, own_age, cells = call(
        functools.partial(rake_kernel, races=races, sizes=sizes),
        [
            (2 * age_owned * pumas, LANES),
            (2 * age_owned * pumas, LANES),
            (tracts, age_rows, LANES),
            (tracts * cross_rows, LANES),
            (age_owned * pumas, LANES),
            cells.shape,
        ],
        [hbm] * 7,
        [vmem] * 6,
        [
            pltpu.VMEM((tracts, age_rows, LANES), F32),
            cross_scratch,
            pltpu.VMEM((pumas, 4 * age_owned * LANES), F32),
            pltpu.VMEM((4 * age_owned * pumas, LANES), F32),
            pltpu.SMEM((tracts,), jnp.int32),
        ]
        + [pltpu.VMEM(x.shape, F32) for x in small]
        + [copy_sems, pltpu.SemaphoreType.DMA((1 + len(small),))],
    )(tract_puma, cells, *small)

    keep, send, scaled_factor, own_race = call(
        race_margin_kernel,
        [
            (2 * race_owned * pumas, LANES),
            (2 * race_owned * pumas, LANES),
            (tracts, age_rows, LANES),
            (race_owned * pumas, LANES),
        ],
        [smem] + [vmem] * 8,
        [vmem] * 4,
        [
            cross_scratch,
            pltpu.VMEM((pumas, 4 * race_owned * LANES), F32),
            pltpu.VMEM((4 * age_owned * pumas, LANES), F32),
            pltpu.VMEM((4 * race_owned * pumas, LANES), F32),
        ],
    )(tract_puma, cells, age_factor, cross_factor, puma_race, *factors(keep, send, own_age))

    out, = call(
        functools.partial(final_kernel, pumas=pumas),
        [(tracts, cross, ages, inner)],
        [smem] + [vmem] * 7,
        [hbm],
        [
            cells_scratch,
            cross_scratch,
            pltpu.VMEM((4 * race_owned * pumas, LANES), F32),
            copy_sems,
        ],
    )(tract_puma, cells, scaled_factor, cross_factor, *factors(keep, send, own_race))
    return out.reshape(tracts, races, sizes, ages, inner).transpose(0, 3, 1, 2, 4)


def solution(mesh):
    in_specs = (
        P(("grp", "tract"), None, None, None, None),
        P(("grp", "tract"), None),
        P(("grp", "tract"), None),
        P(("grp", "tract"), None),
        P(("grp", "tract"), None),
        P("grp", None),
        P("grp", None),
        P(("grp", "tract")),
    )
    out_specs = P(("grp", "tract"), None, None, None, None)
    return jax.shard_map(
        functools.partial(per_device, mesh.shape["tract"]),
        mesh=mesh, in_specs=in_specs, out_specs=out_specs, check_vma=False,
    )
```

```python
import functools

import jax
import jax.numpy as jnp
from jax import lax
from jax.experimental import pallas as pl
from jax.experimental.pallas import tpu as pltpu
from jax.sharding import PartitionSpec as P

LANES = 128
F32 = jnp.float32


def lane_ids(rows):
    return lax.broadcasted_iota(jnp.int32, (rows, LANES), 1)


def masked_lane_sum(value, mask):
    return jnp.sum(jnp.where(mask, value, 0.0), axis=-1, keepdims=True)


def column_of(row, rows, step, offset):
    width = row.shape[-1]
    lane = lax.broadcasted_iota(jnp.int32, (rows, width), 1)
    sub = lax.broadcasted_iota(jnp.int32, (rows, width), 0)
    return jnp.sum(jnp.where(lane == step * sub + offset, row, 0.0), axis=-1, keepdims=True)


def factor_rows(target_ref, own_refs, core_refs, rows_ref):
    pumas, columns = target_ref.shape
    odd = lax.axis_index("tract") % 2 == 1
    start = 0
    for own_ref, core_ref in zip(own_refs, core_refs, strict=True):
        rows = own_ref.shape[0]
        for row in range(start, start + rows, pumas):
            first = row // pumas * LANES
            width = min(columns - first, LANES)
            if width <= 0:
                continue
            at = slice(row - start, row - start + pumas)
            total = jnp.where(odd, own_ref[at, 0:width], core_ref[at, 0:width])
            rows_ref[row : row + pumas, 0:width] = target_ref[:, first : first + width] / total
        start += rows


def puma_numbers(ids_ref, tracts):
    ids = ids_ref[...]
    return [ids[t] for t in range(tracts)]


def put_chains(rows_ref, chain_refs):
    start = 0
    for chain_ref in chain_refs:
        rows = chain_ref.shape[0]
        chain_ref[...] = rows_ref[start : start + rows, :]
        start += rows


def rake_kernel(
    ids_hbm, table_hbm, age_sex_hbm, race_hisp_hbm, size_tenure_hbm, tenure_income_hbm,
    first_ref, second_ref, age_factor_ref, cross_factor_ref, cells_ref,
    sum_ref, cross_ref, rows_ref,
    ids_ref, age_sex_ref, race_hisp_ref, size_tenure_ref, tenure_income_ref,
    sems, small_sems,
    *, races, sizes, pumas,
):
    tracts, cross, ages, _ = table_hbm.shape
    cross_rows = cross_ref.shape[0] // tracts
    small = [
        pltpu.make_async_copy(source, target, small_sems.at[i])
        for i, (source, target) in enumerate((
            (ids_hbm, ids_ref),
            (age_sex_hbm, age_sex_ref),
            (race_hisp_hbm, race_hisp_ref),
            (size_tenure_hbm, size_tenure_ref),
            (tenure_income_hbm, tenure_income_ref),
        ))
    ]
    for copy in small:
        copy.start()
    for t in range(tracts):
        pltpu.make_async_copy(table_hbm.at[t], cells_ref.at[t], sems.at[t]).start()
    lane = lane_ids(1)
    sex0 = lane < 64
    hisp0 = (lane // 32) % 2 == 0
    ten0 = (lane // 16) % 2 == 0

    def add_cross(t, carry):
        pltpu.make_async_copy(table_hbm.at[t], cells_ref.at[t], sems.at[t]).wait()
        total = cells_ref[t, 0]
        for rs in range(1, cross):
            total = total + cells_ref[t, rs]
        sum_ref[t, 0:ages] = total
        return carry

    lax.fori_loop(0, tracts, add_cross, 0)
    for copy in small:
        copy.wait()
    for t in range(tracts):
        total = sum_ref[t, 0:ages]
        row = age_sex_ref[t : t + 1, :]
        first = column_of(row, ages, 2, 0) / masked_lane_sum(total, sex0)
        second = column_of(row, ages, 2, 1) / masked_lane_sum(total, ~sex0)
        age_factor_ref[t, 0:ages] = jnp.where(sex0, first, second)

    def add_ages(t, carry):
        factor = age_factor_ref[t, 0:ages]
        base = t * cross_rows
        for rs in range(cross):
            cross_ref[pl.ds(base + rs, 1), :] = jnp.sum(
                cells_ref[t, rs] * factor, axis=0, keepdims=True
            )
        return carry

    lax.fori_loop(0, tracts, add_ages, 0)

    for t in range(tracts):
        base = t * cross_rows
        by_race = cross_ref[pl.ds(base, races, stride=sizes), :]
        for s in range(1, sizes):
            by_race = by_race + cross_ref[pl.ds(base + s, races, stride=sizes), :]
        row = race_hisp_ref[t : t + 1, :]
        first = column_of(row, races, 2, 0) / masked_lane_sum(by_race, hisp0)
        second = column_of(row, races, 2, 1) / masked_lane_sum(by_race, ~hisp0)
        race_factor = jnp.where(hisp0, first, second)
        by_size = cross_ref[pl.ds(base, sizes), :] * race_factor[0:1]
        for r in range(1, races):
            by_size = by_size + cross_ref[pl.ds(base + r * sizes, sizes), :] * race_factor[r : r + 1]
        row = size_tenure_ref[t : t + 1, :]
        first = column_of(row, sizes, 2, 0) / masked_lane_sum(by_size, ten0)
        second = column_of(row, sizes, 2, 1) / masked_lane_sum(by_size, ~ten0)
        size_factor = jnp.where(ten0, first, second)
        by_income = jnp.sum(by_size * size_factor, axis=0, keepdims=True)
        by_income = by_income + pltpu.roll(by_income, 64, 1)
        by_income = by_income + pltpu.roll(by_income, 32, 1)
        row = tenure_income_ref[t : t + 1, :]
        income_factor = jnp.concatenate([row] * 4, axis=1) / by_income
        age_factor_ref[t, 0:ages] = age_factor_ref[t, 0:ages] * income_factor
        for r in range(races):
            cross_factor_ref[pl.ds(base + r * sizes, sizes), :] = size_factor * race_factor[r : r + 1]

    def add_scaled(t, carry):
        base = t * cross_rows
        total = cells_ref[t, 0] * cross_factor_ref[pl.ds(base, 1), :]
        for rs in range(1, cross):
            total = total + cells_ref[t, rs] * cross_factor_ref[pl.ds(base + rs, 1), :]
        sum_ref[t, 0:ages] = total * age_factor_ref[t, 0:ages]
        sum_ref[t, ages:] = jnp.zeros((sum_ref.shape[1] - ages, LANES), F32)
        return carry

    lax.fori_loop(0, tracts, add_scaled, 0)

    pairs = sum_ref.shape[1] // 2
    rows_ref[...] = jnp.zeros(rows_ref.shape, F32)
    for t in range(tracts):
        even = sum_ref[t, pl.ds(0, pairs, stride=2)]
        odd = sum_ref[t, pl.ds(1, pairs, stride=2)]
        even = even + pltpu.roll(even, 96, 1)
        odd = odd + pltpu.roll(odd, 96, 1)
        packed = jnp.where(
            lane < 32,
            even,
            jnp.where(
                lane < 64,
                pltpu.roll(even, 96, 1),
                jnp.where(lane < 96, pltpu.roll(odd, 64, 1), pltpu.roll(odd, 32, 1)),
            ),
        )
        at = pl.ds(ids_ref[t], pairs, stride=pumas)
        rows_ref[at, :] = rows_ref[at, :] + packed
    put_chains(rows_ref, (first_ref, second_ref))


def race_margin_kernel(
    ids_ref, cells_ref, age_factor_ref, cross_factor_ref, target_ref,
    own_first_ref, own_second_ref, core_first_ref, core_second_ref,
    first_ref, second_ref, scaled_factor_ref,
    cross_ref, age_rows_ref, rows_ref,
):
    tracts, cross, ages, _ = cells_ref.shape
    cross_rows = cross_ref.shape[0] // tracts
    pairs = age_factor_ref.shape[1] // 2
    pumas = target_ref.shape[0]
    ids = puma_numbers(ids_ref, tracts)
    factor_rows(
        target_ref, (own_first_ref, own_second_ref), (core_first_ref, core_second_ref), age_rows_ref
    )
    lane = lane_ids(1)
    for t in range(tracts):
        packed = age_rows_ref[pl.ds(ids[t], pairs, stride=pumas), :]
        half = pltpu.roll(packed, 64, 1)
        even = jnp.where(lane < 32, packed, jnp.where(lane < 96, pltpu.roll(packed, 32, 1), half))
        odd = jnp.where(lane < 32, half, jnp.where(lane < 96, pltpu.roll(packed, 96, 1), packed))
        scaled_factor_ref[t, pl.ds(0, pairs, stride=2)] = even
        scaled_factor_ref[t, pl.ds(1, pairs, stride=2)] = odd

    def add_ages(t, carry):
        factor = scaled_factor_ref[t, 0:ages] * age_factor_ref[t, 0:ages]
        scaled_factor_ref[t, 0:ages] = factor
        base = t * cross_rows
        for rs in range(cross):
            cross_ref[pl.ds(base + rs, 1), :] = jnp.sum(
                cells_ref[t, rs] * factor, axis=0, keepdims=True
            )
        cross_ref[pl.ds(base + cross, cross_rows - cross), :] = jnp.zeros(
            (cross_rows - cross, LANES), F32
        )
        return carry

    lax.fori_loop(0, tracts, add_ages, 0)

    cross_pairs = (cross + 1) // 2
    rows_ref[...] = jnp.zeros(rows_ref.shape, F32)
    for t in range(tracts):
        base = t * cross_rows
        margin = cross_ref[pl.ds(base, cross), :] * cross_factor_ref[pl.ds(base, cross), :]
        cross_ref[pl.ds(base, cross), :] = margin + pltpu.roll(margin, 64, 1)
        even = cross_ref[pl.ds(base, cross_pairs, stride=2), :]
        odd = cross_ref[pl.ds(base + 1, cross_pairs, stride=2), :]
        at = pl.ds(ids[t], cross_pairs, stride=pumas)
        rows_ref[at, :] = rows_ref[at, :] + jnp.where(lane < 64, even, odd)
    put_chains(rows_ref, (first_ref, second_ref))


def final_kernel(
    ids_ref, cells_ref, scaled_factor_ref, cross_factor_ref, target_ref,
    own_first_ref, own_second_ref, core_first_ref, core_second_ref,
    out_ref,
    result_ref, cross_ref, rows_ref, sems,
):
    tracts, cross, ages, _ = cells_ref.shape
    cross_rows = cross_ref.shape[0] // tracts
    cross_pairs = (cross + 1) // 2
    pumas = target_ref.shape[0]
    ids = puma_numbers(ids_ref, tracts)
    factor_rows(
        target_ref, (own_first_ref, own_second_ref), (core_first_ref, core_second_ref), rows_ref
    )
    lane = lane_ids(1)
    for t in range(tracts):
        base = t * cross_rows
        packed = rows_ref[pl.ds(ids[t], cross_pairs, stride=pumas), :]
        half = pltpu.roll(packed, 64, 1)
        cross_ref[pl.ds(base, cross_pairs, stride=2), :] = jnp.where(lane < 64, packed, half)
        cross_ref[pl.ds(base + 1, cross_pairs, stride=2), :] = jnp.where(lane < 64, half, packed)
        cross_ref[pl.ds(base, cross), :] = (
            cross_ref[pl.ds(base, cross), :] * cross_factor_ref[pl.ds(base, cross), :]
        )

    def scale(t, carry):
        factor = scaled_factor_ref[t, 0:ages]
        base = t * cross_rows
        for rs in range(cross):
            result_ref[t, rs] = cells_ref[t, rs] * factor * cross_ref[pl.ds(base + rs, 1), :]
        pltpu.make_async_copy(result_ref.at[t], out_ref.at[t], sems.at[t]).start()
        return carry

    lax.fori_loop(0, tracts, scale, 0)
    for t in range(tracts):
        pltpu.make_async_copy(result_ref.at[t], out_ref.at[t], sems.at[t]).wait()


def call(kernel, out_shapes, in_spaces, out_spaces, scratch):
    def spec(space):
        return pl.BlockSpec(memory_space=space)

    run = pl.pallas_call(
        kernel,
        out_shape=[
            space(shape, F32) for shape, space in zip(out_shapes, out_spaces, strict=True)
        ],
        in_specs=[spec(space) for space in in_spaces],
        out_specs=[spec(space) for space in out_spaces],
        scratch_shapes=scratch,
        compiler_params=pltpu.CompilerParams(vmem_limit_bytes=40 << 20),
    )

    def placed(*args):
        return run(*map(pltpu.with_memory_space_constraint, args, in_spaces))

    return placed


def per_device(
    devices,
    table, age_sex, race_hisp, size_tenure, tenure_income, puma_age, puma_race, tract_puma,
):
    tracts, ages, races, sizes, inner = table.shape
    pumas = puma_age.shape[0]
    cross = races * sizes
    age_rows = -(-ages // 8) * 8
    cross_rows = -(-(cross + 1) // 8) * 8
    age_pairs, cross_pairs = age_rows // 2, (cross + 1) // 2
    vmem, hbm = pltpu.VMEM, pltpu.HBM

    cells = table.transpose(0, 2, 3, 1, 4).reshape(tracts, cross, ages, inner)
    cells_scratch = pltpu.VMEM((tracts, cross, ages, inner), F32)
    cross_scratch = pltpu.VMEM((tracts * cross_rows, LANES), F32)
    copy_sems = pltpu.SemaphoreType.DMA((tracts,))

    bits = [1 << k for k in range(1, devices.bit_length() - 1)]
    orders = (bits, bits[1:] + bits[:1])
    to_odd = [(i, i + 1) for i in range(0, devices, 2)]
    to_even = [(i + 1, i) for i in range(0, devices, 2)]

    def totals(chains):
        chains = [x + lax.ppermute(x, "tract", to_odd) for x in chains]
        for step in range(len(bits)):
            chains = [
                x + lax.ppermute(x, "tract", [(i, i ^ order[step]) for i in range(1, devices, 2)])
                for x, order in zip(chains, orders)
            ]
        return *chains, *[lax.ppermute(x, "tract", to_even) for x in chains]

    def chain_shapes(pairs):
        return [(pairs // 2 * pumas, LANES), ((pairs - pairs // 2) * pumas, LANES)]

    small = [age_sex, race_hisp, size_tenure, tenure_income]
    *chains, age_factor, cross_factor, cells = call(
        functools.partial(rake_kernel, races=races, sizes=sizes, pumas=pumas),
        chain_shapes(age_pairs)
        + [(tracts, age_rows, LANES), (tracts * cross_rows, LANES), cells.shape],
        [hbm] * 6,
        [vmem] * 5,
        [
            pltpu.VMEM((tracts, age_rows, LANES), F32),
            cross_scratch,
            pltpu.VMEM((age_pairs * pumas, LANES), F32),
            pltpu.SMEM((tracts,), jnp.int32),
        ]
        + [pltpu.VMEM(x.shape, F32) for x in small]
        + [copy_sems, pltpu.SemaphoreType.DMA((1 + len(small),))],
    )(tract_puma, cells, *small)

    *chains, scaled_factor = call(
        race_margin_kernel,
        chain_shapes(cross_pairs) + [(tracts, age_rows, LANES)],
        [vmem] * 9,
        [vmem] * 3,
        [
            cross_scratch,
            pltpu.VMEM((age_pairs * pumas, LANES), F32),
            pltpu.VMEM((cross_pairs * pumas, LANES), F32),
        ],
    )(tract_puma, cells, age_factor, cross_factor, puma_age, *totals(chains))

    out, = call(
        final_kernel,
        [(tracts, cross, ages, inner)],
        [vmem] * 9,
        [hbm],
        [
            cells_scratch,
            cross_scratch,
            pltpu.VMEM((cross_pairs * pumas, LANES), F32),
            copy_sems,
        ],
    )(tract_puma, cells, scaled_factor, cross_factor, puma_race, *totals(chains))
    return out.reshape(tracts, races, sizes, ages, inner).transpose(0, 3, 1, 2, 4)


def solution(mesh):
    in_specs = (
        P(("grp", "tract"), None, None, None, None),
        P(("grp", "tract"), None),
        P(("grp", "tract"), None),
        P(("grp", "tract"), None),
        P(("grp", "tract"), None),
        P("grp", None),
        P("grp", None),
        P(("grp", "tract")),
    )
    out_specs = P(("grp", "tract"), None, None, None, None)
    return jax.shard_map(
        functools.partial(per_device, mesh.shape["tract"]),
        mesh=mesh, in_specs=in_specs, out_specs=out_specs, check_vma=False,
    )
```

```python
import functools

import jax
import jax.numpy as jnp
from jax import lax
from jax.experimental import pallas as pl
from jax.experimental.pallas import tpu as pltpu
from jax.sharding import PartitionSpec as P

LANES = 128
F32 = jnp.float32


def lane_ids(rows):
    return lax.broadcasted_iota(jnp.int32, (rows, LANES), 1)


def masked_lane_sum(value, mask):
    return jnp.sum(jnp.where(mask, value, 0.0), axis=-1, keepdims=True)


def column_of(row, rows, step, offset):
    width = row.shape[-1]
    lane = lax.broadcasted_iota(jnp.int32, (rows, width), 1)
    sub = lax.broadcasted_iota(jnp.int32, (rows, width), 0)
    return jnp.sum(jnp.where(lane == step * sub + offset, row, 0.0), axis=-1, keepdims=True)


def half_of(index):
    total = index
    for k in range(1, 16):
        total = total + lax.shift_right_logical(index, k)
    return lax.rem(total, 2)


def factor_rows(target_ref, own_ref, other_ref, rows_ref):
    pumas, columns = target_ref.shape
    half = half_of(lax.axis_index("tract"))
    rows = own_ref.shape[0]
    for ref, which in ((own_ref, half), (other_ref, 1 - half)):
        rows_ref[pl.ds(pl.multiple_of(which * rows, 8), rows), :] = ref[...]
    for first in range(0, columns, LANES):
        width = min(columns - first, LANES)
        at = slice(first // LANES * pumas, (first // LANES + 1) * pumas)
        rows_ref[at, 0:width] = target_ref[:, first : first + width] / rows_ref[at, 0:width]


def puma_numbers(ids_ref, tracts):
    ids = ids_ref[...]
    return [ids[t] for t in range(tracts)]


def put_halves(rows_ref, keep_ref, send_ref):
    half = half_of(lax.axis_index("tract"))
    rows = keep_ref.shape[0]
    for ref, which in ((keep_ref, half), (send_ref, 1 - half)):
        ref[...] = rows_ref[pl.ds(pl.multiple_of(which * rows, 8), rows), :]


def rake_kernel(
    ids_hbm, table_hbm, age_sex_hbm, race_hisp_hbm, size_tenure_hbm, tenure_income_hbm,
    keep_ref, send_ref, age_factor_ref, cross_factor_ref, cells_ref,
    sum_ref, cross_ref, rows_ref,
    ids_ref, age_sex_ref, race_hisp_ref, size_tenure_ref, tenure_income_ref,
    sems, small_sems,
    *, races, sizes, pumas,
):
    tracts, cross, ages, _ = table_hbm.shape
    cross_rows = cross_ref.shape[0] // tracts
    small = [
        pltpu.make_async_copy(source, target, small_sems.at[i])
        for i, (source, target) in enumerate((
            (ids_hbm, ids_ref),
            (age_sex_hbm, age_sex_ref),
            (race_hisp_hbm, race_hisp_ref),
            (size_tenure_hbm, size_tenure_ref),
            (tenure_income_hbm, tenure_income_ref),
        ))
    ]
    for copy in small:
        copy.start()
    for t in range(tracts):
        pltpu.make_async_copy(table_hbm.at[t], cells_ref.at[t], sems.at[t]).start()
    lane = lane_ids(1)
    sex0 = lane < 64
    hisp0 = (lane // 32) % 2 == 0
    ten0 = (lane // 16) % 2 == 0

    def add_cross(t, carry):
        pltpu.make_async_copy(table_hbm.at[t], cells_ref.at[t], sems.at[t]).wait()
        total = cells_ref[t, 0]
        for rs in range(1, cross):
            total = total + cells_ref[t, rs]
        sum_ref[t, 0:ages] = total
        return carry

    lax.fori_loop(0, tracts, add_cross, 0)
    for copy in small:
        copy.wait()
    for t in range(tracts):
        total = sum_ref[t, 0:ages]
        row = age_sex_ref[t : t + 1, :]
        first = column_of(row, ages, 2, 0) / masked_lane_sum(total, sex0)
        second = column_of(row, ages, 2, 1) / masked_lane_sum(total, ~sex0)
        age_factor_ref[t, 0:ages] = jnp.where(sex0, first, second)

    def add_ages(t, carry):
        factor = age_factor_ref[t, 0:ages]
        base = t * cross_rows
        for rs in range(cross):
            cross_ref[pl.ds(base + rs, 1), :] = jnp.sum(
                cells_ref[t, rs] * factor, axis=0, keepdims=True
            )
        return carry

    lax.fori_loop(0, tracts, add_ages, 0)

    for t in range(tracts):
        base = t * cross_rows
        by_race = cross_ref[pl.ds(base, races, stride=sizes), :]
        for s in range(1, sizes):
            by_race = by_race + cross_ref[pl.ds(base + s, races, stride=sizes), :]
        row = race_hisp_ref[t : t + 1, :]
        first = column_of(row, races, 2, 0) / masked_lane_sum(by_race, hisp0)
        second = column_of(row, races, 2, 1) / masked_lane_sum(by_race, ~hisp0)
        race_factor = jnp.where(hisp0, first, second)
        by_size = cross_ref[pl.ds(base, sizes), :] * race_factor[0:1]
        for r in range(1, races):
            by_size = by_size + cross_ref[pl.ds(base + r * sizes, sizes), :] * race_factor[r : r + 1]
        row = size_tenure_ref[t : t + 1, :]
        first = column_of(row, sizes, 2, 0) / masked_lane_sum(by_size, ten0)
        second = column_of(row, sizes, 2, 1) / masked_lane_sum(by_size, ~ten0)
        size_factor = jnp.where(ten0, first, second)
        by_income = jnp.sum(by_size * size_factor, axis=0, keepdims=True)
        by_income = by_income + pltpu.roll(by_income, 64, 1)
        by_income = by_income + pltpu.roll(by_income, 32, 1)
        row = tenure_income_ref[t : t + 1, :]
        income_factor = jnp.concatenate([row] * 4, axis=1) / by_income
        age_factor_ref[t, 0:ages] = age_factor_ref[t, 0:ages] * income_factor
        for r in range(races):
            cross_factor_ref[pl.ds(base + r * sizes, sizes), :] = size_factor * race_factor[r : r + 1]

    def add_scaled(t, carry):
        base = t * cross_rows
        total = cells_ref[t, 0] * cross_factor_ref[pl.ds(base, 1), :]
        for rs in range(1, cross):
            total = total + cells_ref[t, rs] * cross_factor_ref[pl.ds(base + rs, 1), :]
        sum_ref[t, 0:ages] = total * age_factor_ref[t, 0:ages]
        sum_ref[t, ages:] = jnp.zeros((sum_ref.shape[1] - ages, LANES), F32)
        return carry

    lax.fori_loop(0, tracts, add_scaled, 0)

    pairs = sum_ref.shape[1] // 2
    rows_ref[...] = jnp.zeros(rows_ref.shape, F32)
    for t in range(tracts):
        even = sum_ref[t, pl.ds(0, pairs, stride=2)]
        odd = sum_ref[t, pl.ds(1, pairs, stride=2)]
        even = even + pltpu.roll(even, 96, 1)
        odd = odd + pltpu.roll(odd, 96, 1)
        packed = jnp.where(
            lane < 32,
            even,
            jnp.where(
                lane < 64,
                pltpu.roll(even, 96, 1),
                jnp.where(lane < 96, pltpu.roll(odd, 64, 1), pltpu.roll(odd, 32, 1)),
            ),
        )
        at = pl.ds(ids_ref[t], pairs, stride=pumas)
        rows_ref[at, :] = rows_ref[at, :] + packed
    put_halves(rows_ref, keep_ref, send_ref)


def race_margin_kernel(
    ids_ref, cells_ref, age_factor_ref, cross_factor_ref, target_ref,
    own_ref, other_ref,
    keep_ref, send_ref, scaled_factor_ref,
    cross_ref, age_rows_ref, rows_ref,
):
    tracts, cross, ages, _ = cells_ref.shape
    cross_rows = cross_ref.shape[0] // tracts
    pairs = age_factor_ref.shape[1] // 2
    pumas = target_ref.shape[0]
    ids = puma_numbers(ids_ref, tracts)
    factor_rows(target_ref, own_ref, other_ref, age_rows_ref)
    lane = lane_ids(1)
    for t in range(tracts):
        packed = age_rows_ref[pl.ds(ids[t], pairs, stride=pumas), :]
        half = pltpu.roll(packed, 64, 1)
        even = jnp.where(lane < 32, packed, jnp.where(lane < 96, pltpu.roll(packed, 32, 1), half))
        odd = jnp.where(lane < 32, half, jnp.where(lane < 96, pltpu.roll(packed, 96, 1), packed))
        scaled_factor_ref[t, pl.ds(0, pairs, stride=2)] = even
        scaled_factor_ref[t, pl.ds(1, pairs, stride=2)] = odd

    def add_ages(t, carry):
        factor = scaled_factor_ref[t, 0:ages] * age_factor_ref[t, 0:ages]
        scaled_factor_ref[t, 0:ages] = factor
        base = t * cross_rows
        for rs in range(cross):
            cross_ref[pl.ds(base + rs, 1), :] = jnp.sum(
                cells_ref[t, rs] * factor, axis=0, keepdims=True
            )
        cross_ref[pl.ds(base + cross, cross_rows - cross), :] = jnp.zeros(
            (cross_rows - cross, LANES), F32
        )
        return carry

    lax.fori_loop(0, tracts, add_ages, 0)

    cross_pairs = (cross + 1) // 2
    rows_ref[...] = jnp.zeros(rows_ref.shape, F32)
    for t in range(tracts):
        base = t * cross_rows
        margin = cross_ref[pl.ds(base, cross), :] * cross_factor_ref[pl.ds(base, cross), :]
        cross_ref[pl.ds(base, cross), :] = margin + pltpu.roll(margin, 64, 1)
        even = cross_ref[pl.ds(base, cross_pairs, stride=2), :]
        odd = cross_ref[pl.ds(base + 1, cross_pairs, stride=2), :]
        at = pl.ds(ids[t], cross_pairs, stride=pumas)
        rows_ref[at, :] = rows_ref[at, :] + jnp.where(lane < 64, even, odd)
    put_halves(rows_ref, keep_ref, send_ref)


def final_kernel(
    ids_ref, cells_ref, scaled_factor_ref, cross_factor_ref, target_ref,
    own_ref, other_ref,
    out_ref,
    result_ref, cross_ref, rows_ref, sems,
):
    tracts, cross, ages, _ = cells_ref.shape
    cross_rows = cross_ref.shape[0] // tracts
    cross_pairs = (cross + 1) // 2
    pumas = target_ref.shape[0]
    ids = puma_numbers(ids_ref, tracts)
    factor_rows(target_ref, own_ref, other_ref, rows_ref)
    lane = lane_ids(1)
    for t in range(tracts):
        base = t * cross_rows
        packed = rows_ref[pl.ds(ids[t], cross_pairs, stride=pumas), :]
        half = pltpu.roll(packed, 64, 1)
        cross_ref[pl.ds(base, cross_pairs, stride=2), :] = jnp.where(lane < 64, packed, half)
        cross_ref[pl.ds(base + 1, cross_pairs, stride=2), :] = jnp.where(lane < 64, half, packed)
        cross_ref[pl.ds(base, cross), :] = (
            cross_ref[pl.ds(base, cross), :] * cross_factor_ref[pl.ds(base, cross), :]
        )

    def scale(t, carry):
        factor = scaled_factor_ref[t, 0:ages]
        base = t * cross_rows
        for rs in range(cross):
            result_ref[t, rs] = cells_ref[t, rs] * factor * cross_ref[pl.ds(base + rs, 1), :]
        pltpu.make_async_copy(result_ref.at[t], out_ref.at[t], sems.at[t]).start()
        return carry

    lax.fori_loop(0, tracts, scale, 0)
    for t in range(tracts):
        pltpu.make_async_copy(result_ref.at[t], out_ref.at[t], sems.at[t]).wait()


def call(kernel, out_shapes, in_spaces, out_spaces, scratch):
    def spec(space):
        return pl.BlockSpec(memory_space=space)

    run = pl.pallas_call(
        kernel,
        out_shape=[
            space(shape, F32) for shape, space in zip(out_shapes, out_spaces, strict=True)
        ],
        in_specs=[spec(space) for space in in_spaces],
        out_specs=[spec(space) for space in out_spaces],
        scratch_shapes=scratch,
        compiler_params=pltpu.CompilerParams(vmem_limit_bytes=40 << 20),
    )

    def placed(*args):
        return run(*map(pltpu.with_memory_space_constraint, args, in_spaces))

    return placed


def per_device(
    devices,
    table, age_sex, race_hisp, size_tenure, tenure_income, puma_age, puma_race, tract_puma,
):
    tracts, ages, races, sizes, inner = table.shape
    pumas = puma_age.shape[0]
    cross = races * sizes
    age_rows = -(-ages // 8) * 8
    cross_rows = -(-(cross + 1) // 8) * 8
    age_pairs, cross_pairs = age_rows // 2, (cross + 1) // 2
    vmem, hbm = pltpu.VMEM, pltpu.HBM

    cells = table.transpose(0, 2, 3, 1, 4).reshape(tracts, cross, ages, inner)
    cells_scratch = pltpu.VMEM((tracts, cross, ages, inner), F32)
    cross_scratch = pltpu.VMEM((tracts * cross_rows, LANES), F32)
    copy_sems = pltpu.SemaphoreType.DMA((tracts,))

    bits = [1 << k for k in range(1, devices.bit_length() - 1)]
    orders = (bits, bits[1:] + bits[:1])

    def swap(x, partner):
        return lax.ppermute(x, "tract", [(i, partner(i)) for i in range(devices)])

    def totals(keep, send):
        keep = keep + swap(send, lambda i: i ^ 1)
        for step in range(len(bits)):
            keep = keep + swap(keep, lambda i: i ^ orders[i.bit_count() % 2][step] ^ 1)
        return keep, swap(keep, lambda i: i ^ 1)

    age_half, cross_half = -(-age_pairs // 2) * pumas, -(-cross_pairs // 2) * pumas
    small = [age_sex, race_hisp, size_tenure, tenure_income]
    keep, send, age_factor, cross_factor, cells = call(
        functools.partial(rake_kernel, races=races, sizes=sizes, pumas=pumas),
        [(age_half, LANES)] * 2
        + [(tracts, age_rows, LANES), (tracts * cross_rows, LANES), cells.shape],
        [hbm] * 6,
        [vmem] * 5,
        [
            pltpu.VMEM((tracts, age_rows, LANES), F32),
            cross_scratch,
            pltpu.VMEM((2 * age_half, LANES), F32),
            pltpu.SMEM((tracts,), jnp.int32),
        ]
        + [pltpu.VMEM(x.shape, F32) for x in small]
        + [copy_sems, pltpu.SemaphoreType.DMA((1 + len(small),))],
    )(tract_puma, cells, *small)

    keep, send, scaled_factor = call(
        race_margin_kernel,
        [(cross_half, LANES)] * 2 + [(tracts, age_rows, LANES)],
        [vmem] * 7,
        [vmem] * 3,
        [
            cross_scratch,
            pltpu.VMEM((2 * age_half, LANES), F32),
            pltpu.VMEM((2 * cross_half, LANES), F32),
        ],
    )(tract_puma, cells, age_factor, cross_factor, puma_age, *totals(keep, send))

    out, = call(
        final_kernel,
        [(tracts, cross, ages, inner)],
        [vmem] * 7,
        [hbm],
        [
            cells_scratch,
            cross_scratch,
            pltpu.VMEM((2 * cross_half, LANES), F32),
            copy_sems,
        ],
    )(tract_puma, cells, scaled_factor, cross_factor, puma_race, *totals(keep, send))
    return out.reshape(tracts, races, sizes, ages, inner).transpose(0, 3, 1, 2, 4)


def solution(mesh):
    in_specs = (
        P(("grp", "tract"), None, None, None, None),
        P(("grp", "tract"), None),
        P(("grp", "tract"), None),
        P(("grp", "tract"), None),
        P(("grp", "tract"), None),
        P("grp", None),
        P("grp", None),
        P(("grp", "tract")),
    )
    out_specs = P(("grp", "tract"), None, None, None, None)
    return jax.shard_map(
        functools.partial(per_device, mesh.shape["tract"]),
        mesh=mesh, in_specs=in_specs, out_specs=out_specs, check_vma=False,
    )
```

```python
import functools

import jax
import jax.numpy as jnp
from jax import lax
from jax.experimental import pallas as pl
from jax.experimental.pallas import tpu as pltpu
from jax.sharding import PartitionSpec as P

LANES = 128
F32 = jnp.float32


def lane_ids(rows):
    return lax.broadcasted_iota(jnp.int32, (rows, LANES), 1)


def masked_lane_sum(value, mask):
    return jnp.sum(jnp.where(mask, value, 0.0), axis=-1, keepdims=True)


def column_of(row, rows, step, offset):
    width = row.shape[-1]
    lane = lax.broadcasted_iota(jnp.int32, (rows, width), 1)
    sub = lax.broadcasted_iota(jnp.int32, (rows, width), 0)
    return jnp.sum(jnp.where(lane == step * sub + offset, row, 0.0), axis=-1, keepdims=True)


def half_of(index):
    total = index
    for k in range(1, 16):
        total = total + lax.shift_right_logical(index, k)
    return lax.rem(total, 2)


def part_of(index):
    return jnp.where(half_of(index) == 0, lax.rem(index // 2, 2), lax.rem(index // 4, 2))


def split_kernel(mine_ref, theirs_ref, keep_ref, send_ref):
    part = part_of(lax.axis_index("tract"))
    rows = keep_ref.shape[0]
    for which, out_ref in ((part, keep_ref), (1 - part, send_ref)):
        at = pl.ds(pl.multiple_of(which * rows, 8), rows)
        out_ref[...] = mine_ref[at, :] + theirs_ref[at, :]


def join_kernel(own_ref, near_ref, half_ref):
    part = part_of(lax.axis_index("tract"))
    rows = own_ref.shape[0]
    for which, ref in ((part, own_ref), (1 - part, near_ref)):
        half_ref[pl.ds(pl.multiple_of(which * rows, 8), rows), :] = ref[...]


def factor_rows(target_ref, own_ref, other_ref, rows_ref):
    pumas, columns = target_ref.shape
    half = half_of(lax.axis_index("tract"))
    rows = own_ref.shape[0]
    for ref, which in ((own_ref, half), (other_ref, 1 - half)):
        rows_ref[pl.ds(pl.multiple_of(which * rows, 8), rows), :] = ref[...]
    for first in range(0, columns, LANES):
        width = min(columns - first, LANES)
        at = slice(first // LANES * pumas, (first // LANES + 1) * pumas)
        rows_ref[at, 0:width] = target_ref[:, first : first + width] / rows_ref[at, 0:width]


def puma_numbers(ids_ref, tracts):
    ids = ids_ref[...]
    return [ids[t] for t in range(tracts)]


def put_halves(rows_ref, keep_ref, send_ref):
    half = half_of(lax.axis_index("tract"))
    rows = keep_ref.shape[0]
    for ref, which in ((keep_ref, half), (send_ref, 1 - half)):
        ref[...] = rows_ref[pl.ds(pl.multiple_of(which * rows, 8), rows), :]


def rake_kernel(
    ids_hbm, table_hbm, age_sex_hbm, race_hisp_hbm, size_tenure_hbm, tenure_income_hbm,
    keep_ref, send_ref, age_factor_ref, cross_factor_ref, cells_ref,
    sum_ref, cross_ref, rows_ref,
    ids_ref, age_sex_ref, race_hisp_ref, size_tenure_ref, tenure_income_ref,
    sems, small_sems,
    *, races, sizes, pumas,
):
    tracts, cross, ages, _ = table_hbm.shape
    cross_rows = cross_ref.shape[0] // tracts
    small = [
        pltpu.make_async_copy(source, target, small_sems.at[i])
        for i, (source, target) in enumerate((
            (ids_hbm, ids_ref),
            (age_sex_hbm, age_sex_ref),
            (race_hisp_hbm, race_hisp_ref),
            (size_tenure_hbm, size_tenure_ref),
            (tenure_income_hbm, tenure_income_ref),
        ))
    ]
    for copy in small:
        copy.start()
    for t in range(tracts):
        pltpu.make_async_copy(table_hbm.at[t], cells_ref.at[t], sems.at[t]).start()
    lane = lane_ids(1)
    sex0 = lane < 64
    hisp0 = (lane // 32) % 2 == 0
    ten0 = (lane // 16) % 2 == 0

    def add_cross(t, carry):
        pltpu.make_async_copy(table_hbm.at[t], cells_ref.at[t], sems.at[t]).wait()
        total = cells_ref[t, 0]
        for rs in range(1, cross):
            total = total + cells_ref[t, rs]
        sum_ref[t, 0:ages] = total
        return carry

    lax.fori_loop(0, tracts, add_cross, 0)
    for copy in small:
        copy.wait()
    for t in range(tracts):
        total = sum_ref[t, 0:ages]
        row = age_sex_ref[t : t + 1, :]
        first = column_of(row, ages, 2, 0) / masked_lane_sum(total, sex0)
        second = column_of(row, ages, 2, 1) / masked_lane_sum(total, ~sex0)
        age_factor_ref[t, 0:ages] = jnp.where(sex0, first, second)

    def add_ages(t, carry):
        factor = age_factor_ref[t, 0:ages]
        base = t * cross_rows
        for rs in range(cross):
            cross_ref[pl.ds(base + rs, 1), :] = jnp.sum(
                cells_ref[t, rs] * factor, axis=0, keepdims=True
            )
        return carry

    lax.fori_loop(0, tracts, add_ages, 0)

    for t in range(tracts):
        base = t * cross_rows
        by_race = cross_ref[pl.ds(base, races, stride=sizes), :]
        for s in range(1, sizes):
            by_race = by_race + cross_ref[pl.ds(base + s, races, stride=sizes), :]
        row = race_hisp_ref[t : t + 1, :]
        first = column_of(row, races, 2, 0) / masked_lane_sum(by_race, hisp0)
        second = column_of(row, races, 2, 1) / masked_lane_sum(by_race, ~hisp0)
        race_factor = jnp.where(hisp0, first, second)
        by_size = cross_ref[pl.ds(base, sizes), :] * race_factor[0:1]
        for r in range(1, races):
            by_size = by_size + cross_ref[pl.ds(base + r * sizes, sizes), :] * race_factor[r : r + 1]
        row = size_tenure_ref[t : t + 1, :]
        first = column_of(row, sizes, 2, 0) / masked_lane_sum(by_size, ten0)
        second = column_of(row, sizes, 2, 1) / masked_lane_sum(by_size, ~ten0)
        size_factor = jnp.where(ten0, first, second)
        by_income = jnp.sum(by_size * size_factor, axis=0, keepdims=True)
        by_income = by_income + pltpu.roll(by_income, 64, 1)
        by_income = by_income + pltpu.roll(by_income, 32, 1)
        row = tenure_income_ref[t : t + 1, :]
        income_factor = jnp.concatenate([row] * 4, axis=1) / by_income
        age_factor_ref[t, 0:ages] = age_factor_ref[t, 0:ages] * income_factor
        for r in range(races):
            cross_factor_ref[pl.ds(base + r * sizes, sizes), :] = size_factor * race_factor[r : r + 1]

    def add_scaled(t, carry):
        base = t * cross_rows
        total = cells_ref[t, 0] * cross_factor_ref[pl.ds(base, 1), :]
        for rs in range(1, cross):
            total = total + cells_ref[t, rs] * cross_factor_ref[pl.ds(base + rs, 1), :]
        sum_ref[t, 0:ages] = total * age_factor_ref[t, 0:ages]
        sum_ref[t, ages:] = jnp.zeros((sum_ref.shape[1] - ages, LANES), F32)
        return carry

    lax.fori_loop(0, tracts, add_scaled, 0)

    pairs = sum_ref.shape[1] // 2
    rows_ref[...] = jnp.zeros(rows_ref.shape, F32)
    for t in range(tracts):
        even = sum_ref[t, pl.ds(0, pairs, stride=2)]
        odd = sum_ref[t, pl.ds(1, pairs, stride=2)]
        even = even + pltpu.roll(even, 96, 1)
        odd = odd + pltpu.roll(odd, 96, 1)
        packed = jnp.where(
            lane < 32,
            even,
            jnp.where(
                lane < 64,
                pltpu.roll(even, 96, 1),
                jnp.where(lane < 96, pltpu.roll(odd, 64, 1), pltpu.roll(odd, 32, 1)),
            ),
        )
        at = pl.ds(ids_ref[t], pairs, stride=pumas)
        rows_ref[at, :] = rows_ref[at, :] + packed
    put_halves(rows_ref, keep_ref, send_ref)


def race_margin_kernel(
    ids_ref, cells_ref, age_factor_ref, cross_factor_ref, target_ref,
    own_ref, other_ref,
    keep_ref, send_ref, scaled_factor_ref,
    cross_ref, age_rows_ref, rows_ref,
):
    tracts, cross, ages, _ = cells_ref.shape
    cross_rows = cross_ref.shape[0] // tracts
    pairs = age_factor_ref.shape[1] // 2
    pumas = target_ref.shape[0]
    ids = puma_numbers(ids_ref, tracts)
    factor_rows(target_ref, own_ref, other_ref, age_rows_ref)
    lane = lane_ids(1)
    for t in range(tracts):
        packed = age_rows_ref[pl.ds(ids[t], pairs, stride=pumas), :]
        half = pltpu.roll(packed, 64, 1)
        even = jnp.where(lane < 32, packed, jnp.where(lane < 96, pltpu.roll(packed, 32, 1), half))
        odd = jnp.where(lane < 32, half, jnp.where(lane < 96, pltpu.roll(packed, 96, 1), packed))
        scaled_factor_ref[t, pl.ds(0, pairs, stride=2)] = even
        scaled_factor_ref[t, pl.ds(1, pairs, stride=2)] = odd

    def add_ages(t, carry):
        factor = scaled_factor_ref[t, 0:ages] * age_factor_ref[t, 0:ages]
        scaled_factor_ref[t, 0:ages] = factor
        base = t * cross_rows
        for rs in range(cross):
            cross_ref[pl.ds(base + rs, 1), :] = jnp.sum(
                cells_ref[t, rs] * factor, axis=0, keepdims=True
            )
        cross_ref[pl.ds(base + cross, cross_rows - cross), :] = jnp.zeros(
            (cross_rows - cross, LANES), F32
        )
        return carry

    lax.fori_loop(0, tracts, add_ages, 0)

    cross_pairs = (cross + 1) // 2
    rows_ref[...] = jnp.zeros(rows_ref.shape, F32)
    for t in range(tracts):
        base = t * cross_rows
        margin = cross_ref[pl.ds(base, cross), :] * cross_factor_ref[pl.ds(base, cross), :]
        cross_ref[pl.ds(base, cross), :] = margin + pltpu.roll(margin, 64, 1)
        even = cross_ref[pl.ds(base, cross_pairs, stride=2), :]
        odd = cross_ref[pl.ds(base + 1, cross_pairs, stride=2), :]
        at = pl.ds(ids[t], cross_pairs, stride=pumas)
        rows_ref[at, :] = rows_ref[at, :] + jnp.where(lane < 64, even, odd)
    put_halves(rows_ref, keep_ref, send_ref)


def final_kernel(
    ids_ref, cells_ref, scaled_factor_ref, cross_factor_ref, target_ref,
    own_ref, other_ref,
    out_ref,
    result_ref, cross_ref, rows_ref, sems,
):
    tracts, cross, ages, _ = cells_ref.shape
    cross_rows = cross_ref.shape[0] // tracts
    cross_pairs = (cross + 1) // 2
    pumas = target_ref.shape[0]
    ids = puma_numbers(ids_ref, tracts)
    factor_rows(target_ref, own_ref, other_ref, rows_ref)
    lane = lane_ids(1)
    for t in range(tracts):
        base = t * cross_rows
        packed = rows_ref[pl.ds(ids[t], cross_pairs, stride=pumas), :]
        half = pltpu.roll(packed, 64, 1)
        cross_ref[pl.ds(base, cross_pairs, stride=2), :] = jnp.where(lane < 64, packed, half)
        cross_ref[pl.ds(base + 1, cross_pairs, stride=2), :] = jnp.where(lane < 64, half, packed)
        cross_ref[pl.ds(base, cross), :] = (
            cross_ref[pl.ds(base, cross), :] * cross_factor_ref[pl.ds(base, cross), :]
        )

    def scale(t, carry):
        factor = scaled_factor_ref[t, 0:ages]
        base = t * cross_rows
        for rs in range(cross):
            result_ref[t, rs] = cells_ref[t, rs] * factor * cross_ref[pl.ds(base + rs, 1), :]
        pltpu.make_async_copy(result_ref.at[t], out_ref.at[t], sems.at[t]).start()
        return carry

    lax.fori_loop(0, tracts, scale, 0)
    for t in range(tracts):
        pltpu.make_async_copy(result_ref.at[t], out_ref.at[t], sems.at[t]).wait()


def call(kernel, out_shapes, in_spaces, out_spaces, scratch):
    def spec(space):
        return pl.BlockSpec(memory_space=space)

    run = pl.pallas_call(
        kernel,
        out_shape=[
            space(shape, F32) for shape, space in zip(out_shapes, out_spaces, strict=True)
        ],
        in_specs=[spec(space) for space in in_spaces],
        out_specs=[spec(space) for space in out_spaces],
        scratch_shapes=scratch,
        compiler_params=pltpu.CompilerParams(vmem_limit_bytes=40 << 20),
    )

    def placed(*args):
        return run(*map(pltpu.with_memory_space_constraint, args, in_spaces))

    return placed


def per_device(
    devices,
    table, age_sex, race_hisp, size_tenure, tenure_income, puma_age, puma_race, tract_puma,
):
    tracts, ages, races, sizes, inner = table.shape
    pumas = puma_age.shape[0]
    cross = races * sizes
    age_rows = -(-ages // 8) * 8
    cross_rows = -(-(cross + 1) // 8) * 8
    age_pairs, cross_pairs = age_rows // 2, (cross + 1) // 2
    vmem, hbm = pltpu.VMEM, pltpu.HBM

    cells = table.transpose(0, 2, 3, 1, 4).reshape(tracts, cross, ages, inner)
    cells_scratch = pltpu.VMEM((tracts, cross, ages, inner), F32)
    cross_scratch = pltpu.VMEM((tracts * cross_rows, LANES), F32)
    copy_sems = pltpu.SemaphoreType.DMA((tracts,))

    bits = [1 << k for k in range(1, devices.bit_length() - 1)]
    orders = (bits, bits[1:] + bits[:1])

    def swap(x, partner):
        return lax.ppermute(x, "tract", [(i, partner(i)) for i in range(devices)])

    def add_up(x, steps):
        for step in steps:
            x = x + swap(x, lambda i: i ^ orders[i.bit_count() % 2][step] ^ 1)
        return x

    def totals(keep, send, split):
        theirs = swap(send, lambda i: i ^ 1)
        if split:
            shape = (keep.shape[0] // 2, LANES)
            first = lambda i: i ^ orders[i.bit_count() % 2][0] ^ 1
            keep, send = call(split_kernel, [shape] * 2, [vmem] * 2, [vmem] * 2, [])(keep, theirs)
            keep = add_up(keep + swap(send, first), range(1, len(bits)))
            half, = call(join_kernel, [theirs.shape], [vmem] * 2, [vmem], [])(keep, swap(keep, first))
        else:
            half = add_up(keep + theirs, range(len(bits)))
        return half, swap(half, lambda i: i ^ 1)

    age_half, cross_half = -(-age_pairs // 2) * pumas, -(-cross_pairs // 4) * 2 * pumas
    small = [age_sex, race_hisp, size_tenure, tenure_income]
    keep, send, age_factor, cross_factor, cells = call(
        functools.partial(rake_kernel, races=races, sizes=sizes, pumas=pumas),
        [(age_half, LANES)] * 2
        + [(tracts, age_rows, LANES), (tracts * cross_rows, LANES), cells.shape],
        [hbm] * 6,
        [vmem] * 5,
        [
            pltpu.VMEM((tracts, age_rows, LANES), F32),
            cross_scratch,
            pltpu.VMEM((2 * age_half, LANES), F32),
            pltpu.SMEM((tracts,), jnp.int32),
        ]
        + [pltpu.VMEM(x.shape, F32) for x in small]
        + [copy_sems, pltpu.SemaphoreType.DMA((1 + len(small),))],
    )(tract_puma, cells, *small)

    keep, send, scaled_factor = call(
        race_margin_kernel,
        [(cross_half, LANES)] * 2 + [(tracts, age_rows, LANES)],
        [vmem] * 7,
        [vmem] * 3,
        [
            cross_scratch,
            pltpu.VMEM((2 * age_half, LANES), F32),
            pltpu.VMEM((2 * cross_half, LANES), F32),
        ],
    )(tract_puma, cells, age_factor, cross_factor, puma_age, *totals(keep, send, False))

    out, = call(
        final_kernel,
        [(tracts, cross, ages, inner)],
        [vmem] * 7,
        [hbm],
        [
            cells_scratch,
            cross_scratch,
            pltpu.VMEM((2 * cross_half, LANES), F32),
            copy_sems,
        ],
    )(tract_puma, cells, scaled_factor, cross_factor, puma_race, *totals(keep, send, True))
    return out.reshape(tracts, races, sizes, ages, inner).transpose(0, 3, 1, 2, 4)


def solution(mesh):
    in_specs = (
        P(("grp", "tract"), None, None, None, None),
        P(("grp", "tract"), None),
        P(("grp", "tract"), None),
        P(("grp", "tract"), None),
        P(("grp", "tract"), None),
        P("grp", None),
        P("grp", None),
        P(("grp", "tract")),
    )
    out_specs = P(("grp", "tract"), None, None, None, None)
    return jax.shard_map(
        functools.partial(per_device, mesh.shape["tract"]),
        mesh=mesh, in_specs=in_specs, out_specs=out_specs, check_vma=False,
    )
```

```python
import functools

import jax
import jax.numpy as jnp
from jax import lax
from jax.experimental import pallas as pl
from jax.experimental.pallas import tpu as pltpu
from jax.sharding import PartitionSpec as P

LANES = 128
F32 = jnp.float32


def lane_ids(rows):
    return lax.broadcasted_iota(jnp.int32, (rows, LANES), 1)


def masked_lane_sum(value, mask):
    return jnp.sum(jnp.where(mask, value, 0.0), axis=-1, keepdims=True)


def column_of(row, rows, step, offset):
    width = row.shape[-1]
    lane = lax.broadcasted_iota(jnp.int32, (rows, width), 1)
    sub = lax.broadcasted_iota(jnp.int32, (rows, width), 0)
    return jnp.sum(jnp.where(lane == step * sub + offset, row, 0.0), axis=-1, keepdims=True)


def half_of(index):
    total = index
    for k in range(1, 16):
        total = total + lax.shift_right_logical(index, k)
    return lax.rem(total, 2)


def factor_rows(target_ref, own_refs, other_refs, rows_ref):
    pumas, columns = target_ref.shape
    half = half_of(lax.axis_index("tract"))
    for refs, which in ((own_refs, half), (other_refs, 1 - half)):
        start = which * (rows_ref.shape[0] // 2)
        for ref in refs:
            rows_ref[pl.ds(pl.multiple_of(start, 8), ref.shape[0]), :] = ref[...]
            start = start + ref.shape[0]
    for first in range(0, columns, LANES):
        width = min(columns - first, LANES)
        at = slice(first // LANES * pumas, (first // LANES + 1) * pumas)
        rows_ref[at, 0:width] = target_ref[:, first : first + width] / rows_ref[at, 0:width]


def puma_numbers(ids_ref, tracts):
    ids = ids_ref[...]
    return [ids[t] for t in range(tracts)]


def put_halves(rows_ref, keep_refs, send_refs):
    half = half_of(lax.axis_index("tract"))
    for refs, which in ((keep_refs, half), (send_refs, 1 - half)):
        start = which * (rows_ref.shape[0] // 2)
        for ref in refs:
            ref[...] = rows_ref[pl.ds(pl.multiple_of(start, 8), ref.shape[0]), :]
            start = start + ref.shape[0]


def rake_kernel(
    ids_hbm, table_hbm, age_sex_hbm, race_hisp_hbm, size_tenure_hbm, tenure_income_hbm,
    keep_ref, send_ref, age_factor_ref, cross_factor_ref, cells_ref,
    sum_ref, cross_ref, rows_ref,
    ids_ref, age_sex_ref, race_hisp_ref, size_tenure_ref, tenure_income_ref,
    sems, small_sems,
    *, races, sizes, pumas,
):
    tracts, cross, ages, _ = table_hbm.shape
    cross_rows = cross_ref.shape[0] // tracts
    small = [
        pltpu.make_async_copy(source, target, small_sems.at[i])
        for i, (source, target) in enumerate((
            (ids_hbm, ids_ref),
            (age_sex_hbm, age_sex_ref),
            (race_hisp_hbm, race_hisp_ref),
            (size_tenure_hbm, size_tenure_ref),
            (tenure_income_hbm, tenure_income_ref),
        ))
    ]
    for copy in small:
        copy.start()
    for t in range(tracts):
        pltpu.make_async_copy(table_hbm.at[t], cells_ref.at[t], sems.at[t]).start()
    lane = lane_ids(1)
    sex0 = lane < 64
    hisp0 = (lane // 32) % 2 == 0
    ten0 = (lane // 16) % 2 == 0

    def add_cross(t, carry):
        pltpu.make_async_copy(table_hbm.at[t], cells_ref.at[t], sems.at[t]).wait()
        total = cells_ref[t, 0]
        for rs in range(1, cross):
            total = total + cells_ref[t, rs]
        sum_ref[t, 0:ages] = total
        return carry

    lax.fori_loop(0, tracts, add_cross, 0)
    for copy in small:
        copy.wait()
    for t in range(tracts):
        total = sum_ref[t, 0:ages]
        row = age_sex_ref[t : t + 1, :]
        first = column_of(row, ages, 2, 0) / masked_lane_sum(total, sex0)
        second = column_of(row, ages, 2, 1) / masked_lane_sum(total, ~sex0)
        age_factor_ref[t, 0:ages] = jnp.where(sex0, first, second)

    def add_ages(t, carry):
        factor = age_factor_ref[t, 0:ages]
        base = t * cross_rows
        for rs in range(cross):
            cross_ref[pl.ds(base + rs, 1), :] = jnp.sum(
                cells_ref[t, rs] * factor, axis=0, keepdims=True
            )
        return carry

    lax.fori_loop(0, tracts, add_ages, 0)

    for t in range(tracts):
        base = t * cross_rows
        by_race = cross_ref[pl.ds(base, races, stride=sizes), :]
        for s in range(1, sizes):
            by_race = by_race + cross_ref[pl.ds(base + s, races, stride=sizes), :]
        row = race_hisp_ref[t : t + 1, :]
        first = column_of(row, races, 2, 0) / masked_lane_sum(by_race, hisp0)
        second = column_of(row, races, 2, 1) / masked_lane_sum(by_race, ~hisp0)
        race_factor = jnp.where(hisp0, first, second)
        by_size = cross_ref[pl.ds(base, sizes), :] * race_factor[0:1]
        for r in range(1, races):
            by_size = by_size + cross_ref[pl.ds(base + r * sizes, sizes), :] * race_factor[r : r + 1]
        row = size_tenure_ref[t : t + 1, :]
        first = column_of(row, sizes, 2, 0) / masked_lane_sum(by_size, ten0)
        second = column_of(row, sizes, 2, 1) / masked_lane_sum(by_size, ~ten0)
        size_factor = jnp.where(ten0, first, second)
        by_income = jnp.sum(by_size * size_factor, axis=0, keepdims=True)
        by_income = by_income + pltpu.roll(by_income, 64, 1)
        by_income = by_income + pltpu.roll(by_income, 32, 1)
        row = tenure_income_ref[t : t + 1, :]
        income_factor = jnp.concatenate([row] * 4, axis=1) / by_income
        age_factor_ref[t, 0:ages] = age_factor_ref[t, 0:ages] * income_factor
        for r in range(races):
            cross_factor_ref[pl.ds(base + r * sizes, sizes), :] = size_factor * race_factor[r : r + 1]

    def add_scaled(t, carry):
        base = t * cross_rows
        total = cells_ref[t, 0] * cross_factor_ref[pl.ds(base, 1), :]
        for rs in range(1, cross):
            total = total + cells_ref[t, rs] * cross_factor_ref[pl.ds(base + rs, 1), :]
        sum_ref[t, 0:ages] = total * age_factor_ref[t, 0:ages]
        sum_ref[t, ages:] = jnp.zeros((sum_ref.shape[1] - ages, LANES), F32)
        return carry

    lax.fori_loop(0, tracts, add_scaled, 0)

    pairs = sum_ref.shape[1] // 2
    rows_ref[...] = jnp.zeros(rows_ref.shape, F32)
    for t in range(tracts):
        even = sum_ref[t, pl.ds(0, pairs, stride=2)]
        odd = sum_ref[t, pl.ds(1, pairs, stride=2)]
        even = even + pltpu.roll(even, 96, 1)
        odd = odd + pltpu.roll(odd, 96, 1)
        packed = jnp.where(
            lane < 32,
            even,
            jnp.where(
                lane < 64,
                pltpu.roll(even, 96, 1),
                jnp.where(lane < 96, pltpu.roll(odd, 64, 1), pltpu.roll(odd, 32, 1)),
            ),
        )
        at = pl.ds(ids_ref[t], pairs, stride=pumas)
        rows_ref[at, :] = rows_ref[at, :] + packed
    put_halves(rows_ref, [keep_ref], [send_ref])


def race_margin_kernel(
    ids_ref, cells_ref, age_factor_ref, cross_factor_ref, target_ref,
    own_ref, other_ref, *refs
):
    *chunk_refs, scaled_factor_ref, cross_ref, age_rows_ref, rows_ref = refs
    chunks = len(chunk_refs) // 2
    keep_refs, send_refs = chunk_refs[:chunks], chunk_refs[chunks:]
    tracts, cross, ages, _ = cells_ref.shape
    cross_rows = cross_ref.shape[0] // tracts
    pairs = age_factor_ref.shape[1] // 2
    pumas = target_ref.shape[0]
    ids = puma_numbers(ids_ref, tracts)
    factor_rows(target_ref, [own_ref], [other_ref], age_rows_ref)
    lane = lane_ids(1)
    for t in range(tracts):
        packed = age_rows_ref[pl.ds(ids[t], pairs, stride=pumas), :]
        half = pltpu.roll(packed, 64, 1)
        even = jnp.where(lane < 32, packed, jnp.where(lane < 96, pltpu.roll(packed, 32, 1), half))
        odd = jnp.where(lane < 32, half, jnp.where(lane < 96, pltpu.roll(packed, 96, 1), packed))
        scaled_factor_ref[t, pl.ds(0, pairs, stride=2)] = even
        scaled_factor_ref[t, pl.ds(1, pairs, stride=2)] = odd

    def add_ages(t, carry):
        factor = scaled_factor_ref[t, 0:ages] * age_factor_ref[t, 0:ages]
        scaled_factor_ref[t, 0:ages] = factor
        base = t * cross_rows
        for rs in range(cross):
            cross_ref[pl.ds(base + rs, 1), :] = jnp.sum(
                cells_ref[t, rs] * factor, axis=0, keepdims=True
            )
        cross_ref[pl.ds(base + cross, cross_rows - cross), :] = jnp.zeros(
            (cross_rows - cross, LANES), F32
        )
        return carry

    lax.fori_loop(0, tracts, add_ages, 0)

    cross_pairs = (cross + 1) // 2
    rows_ref[...] = jnp.zeros(rows_ref.shape, F32)
    for t in range(tracts):
        base = t * cross_rows
        margin = cross_ref[pl.ds(base, cross), :] * cross_factor_ref[pl.ds(base, cross), :]
        cross_ref[pl.ds(base, cross), :] = margin + pltpu.roll(margin, 64, 1)
        even = cross_ref[pl.ds(base, cross_pairs, stride=2), :]
        odd = cross_ref[pl.ds(base + 1, cross_pairs, stride=2), :]
        at = pl.ds(ids[t], cross_pairs, stride=pumas)
        rows_ref[at, :] = rows_ref[at, :] + jnp.where(lane < 64, even, odd)
    put_halves(rows_ref, keep_refs, send_refs)


def final_kernel(
    ids_ref, cells_ref, scaled_factor_ref, cross_factor_ref, target_ref, *refs
):
    *chunk_refs, out_ref, result_ref, cross_ref, rows_ref, sems = refs
    chunks = len(chunk_refs) // 2
    tracts, cross, ages, _ = cells_ref.shape
    cross_rows = cross_ref.shape[0] // tracts
    cross_pairs = (cross + 1) // 2
    pumas = target_ref.shape[0]
    ids = puma_numbers(ids_ref, tracts)
    factor_rows(target_ref, chunk_refs[:chunks], chunk_refs[chunks:], rows_ref)
    lane = lane_ids(1)
    for t in range(tracts):
        base = t * cross_rows
        packed = rows_ref[pl.ds(ids[t], cross_pairs, stride=pumas), :]
        half = pltpu.roll(packed, 64, 1)
        cross_ref[pl.ds(base, cross_pairs, stride=2), :] = jnp.where(lane < 64, packed, half)
        cross_ref[pl.ds(base + 1, cross_pairs, stride=2), :] = jnp.where(lane < 64, half, packed)
        cross_ref[pl.ds(base, cross), :] = (
            cross_ref[pl.ds(base, cross), :] * cross_factor_ref[pl.ds(base, cross), :]
        )

    def scale(t, carry):
        factor = scaled_factor_ref[t, 0:ages]
        base = t * cross_rows
        for rs in range(cross):
            result_ref[t, rs] = cells_ref[t, rs] * factor * cross_ref[pl.ds(base + rs, 1), :]
        pltpu.make_async_copy(result_ref.at[t], out_ref.at[t], sems.at[t]).start()
        return carry

    lax.fori_loop(0, tracts, scale, 0)
    for t in range(tracts):
        pltpu.make_async_copy(result_ref.at[t], out_ref.at[t], sems.at[t]).wait()


def call(kernel, out_shapes, in_spaces, out_spaces, scratch):
    def spec(space):
        return pl.BlockSpec(memory_space=space)

    run = pl.pallas_call(
        kernel,
        out_shape=[
            space(shape, F32) for shape, space in zip(out_shapes, out_spaces, strict=True)
        ],
        in_specs=[spec(space) for space in in_spaces],
        out_specs=[spec(space) for space in out_spaces],
        scratch_shapes=scratch,
        compiler_params=pltpu.CompilerParams(vmem_limit_bytes=40 << 20),
    )

    def placed(*args):
        return run(*map(pltpu.with_memory_space_constraint, args, in_spaces))

    return placed


def per_device(
    devices,
    table, age_sex, race_hisp, size_tenure, tenure_income, puma_age, puma_race, tract_puma,
):
    tracts, ages, races, sizes, inner = table.shape
    pumas = puma_age.shape[0]
    cross = races * sizes
    age_rows = -(-ages // 8) * 8
    cross_rows = -(-(cross + 1) // 8) * 8
    age_pairs, cross_pairs = age_rows // 2, (cross + 1) // 2
    vmem, hbm = pltpu.VMEM, pltpu.HBM

    cells = table.transpose(0, 2, 3, 1, 4).reshape(tracts, cross, ages, inner)
    cells_scratch = pltpu.VMEM((tracts, cross, ages, inner), F32)
    cross_scratch = pltpu.VMEM((tracts * cross_rows, LANES), F32)
    copy_sems = pltpu.SemaphoreType.DMA((tracts,))

    bits = [1 << k for k in range(1, devices.bit_length() - 1)]
    orders = (bits, bits[1:] + bits[:1])

    def swap(x, partner):
        return lax.ppermute(x, "tract", [(i, partner(i)) for i in range(devices)])

    def totals(keep, send):
        keep = [x + swap(y, lambda i: i ^ 1) for x, y in zip(keep, send)]
        for step in range(len(bits)):
            keep = [x + swap(x, lambda i: i ^ orders[i.bit_count() % 2][step] ^ 1) for x in keep]
        return *keep, *[swap(x, lambda i: i ^ 1) for x in keep]

    age_half, cross_half = -(-age_pairs // 2), -(-cross_pairs // 2)
    cross_chunks = [cross_half - cross_half // 2, cross_half // 2]
    small = [age_sex, race_hisp, size_tenure, tenure_income]
    keep, send, age_factor, cross_factor, cells = call(
        functools.partial(rake_kernel, races=races, sizes=sizes, pumas=pumas),
        [(age_half * pumas, LANES)] * 2
        + [(tracts, age_rows, LANES), (tracts * cross_rows, LANES), cells.shape],
        [hbm] * 6,
        [vmem] * 5,
        [
            pltpu.VMEM((tracts, age_rows, LANES), F32),
            cross_scratch,
            pltpu.VMEM((2 * age_half * pumas, LANES), F32),
            pltpu.SMEM((tracts,), jnp.int32),
        ]
        + [pltpu.VMEM(x.shape, F32) for x in small]
        + [copy_sems, pltpu.SemaphoreType.DMA((1 + len(small),))],
    )(tract_puma, cells, *small)

    *chunks, scaled_factor = call(
        race_margin_kernel,
        [(rows * pumas, LANES) for rows in cross_chunks * 2] + [(tracts, age_rows, LANES)],
        [vmem] * 7,
        [vmem] * (2 * len(cross_chunks) + 1),
        [
            cross_scratch,
            pltpu.VMEM((2 * age_half * pumas, LANES), F32),
            pltpu.VMEM((2 * cross_half * pumas, LANES), F32),
        ],
    )(tract_puma, cells, age_factor, cross_factor, puma_age, *totals([keep], [send]))

    keep, send = chunks[: len(cross_chunks)], chunks[len(cross_chunks) :]
    out, = call(
        final_kernel,
        [(tracts, cross, ages, inner)],
        [vmem] * (5 + 2 * len(cross_chunks)),
        [hbm],
        [
            cells_scratch,
            cross_scratch,
            pltpu.VMEM((2 * cross_half * pumas, LANES), F32),
            copy_sems,
        ],
    )(tract_puma, cells, scaled_factor, cross_factor, puma_race, *totals(keep, send))
    return out.reshape(tracts, races, sizes, ages, inner).transpose(0, 3, 1, 2, 4)


def solution(mesh):
    in_specs = (
        P(("grp", "tract"), None, None, None, None),
        P(("grp", "tract"), None),
        P(("grp", "tract"), None),
        P(("grp", "tract"), None),
        P(("grp", "tract"), None),
        P("grp", None),
        P("grp", None),
        P(("grp", "tract")),
    )
    out_specs = P(("grp", "tract"), None, None, None, None)
    return jax.shard_map(
        functools.partial(per_device, mesh.shape["tract"]),
        mesh=mesh, in_specs=in_specs, out_specs=out_specs, check_vma=False,
    )
```

```python
import functools

import jax
import jax.numpy as jnp
from jax import lax
from jax.experimental import pallas as pl
from jax.experimental.pallas import tpu as pltpu
from jax.sharding import PartitionSpec as P

LANES = 128
F32 = jnp.float32


def round_up(value, step):
    return -(-value // step) * step


def lane_ids(rows):
    return lax.broadcasted_iota(jnp.int32, (rows, LANES), 1)


def masked_lane_sum(value, mask):
    return jnp.sum(jnp.where(mask, value, 0.0), axis=-1, keepdims=True)


def column_of(row, rows, step, offset):
    width = row.shape[-1]
    lane = lax.broadcasted_iota(jnp.int32, (rows, width), 1)
    sub = lax.broadcasted_iota(jnp.int32, (rows, width), 0)
    return jnp.sum(jnp.where(lane == step * sub + offset, row, 0.0), axis=-1, keepdims=True)


def half_of(index):
    total = index
    for k in range(1, 16):
        total = total + lax.shift_right_logical(index, k)
    return lax.rem(total, 2)


def factor_rows(target_ref, own_refs, other_refs, rows_ref):
    pumas, columns = target_ref.shape
    half = half_of(lax.axis_index("tract"))
    half_rows = sum(ref.shape[0] for ref in own_refs)
    for refs, which in ((own_refs, half), (other_refs, 1 - half)):
        start = which * half_rows
        for ref in refs:
            rows_ref[pl.ds(pl.multiple_of(start, 8), ref.shape[0]), :] = ref[...]
            start = start + ref.shape[0]
    for first in range(0, columns, LANES):
        width = min(columns - first, LANES)
        at = slice(first // LANES * pumas, (first // LANES + 1) * pumas)
        rows_ref[at, 0:width] = target_ref[:, first : first + width] / rows_ref[at, 0:width]


def load_puma_numbers(ids_ref, scalar_ref):
    ids = ids_ref[...]
    for t in range(scalar_ref.shape[0]):
        scalar_ref[t] = ids[t]


def put_halves(rows_ref, keep_refs, send_refs):
    half = half_of(lax.axis_index("tract"))
    half_rows = sum(ref.shape[0] for ref in keep_refs)
    for refs, which in ((keep_refs, half), (send_refs, 1 - half)):
        start = which * half_rows
        for ref in refs:
            ref[...] = rows_ref[pl.ds(pl.multiple_of(start, 8), ref.shape[0]), :]
            start = start + ref.shape[0]


def rake_kernel(
    ids_hbm, table_hbm, age_sex_hbm, race_hisp_hbm, size_tenure_hbm, tenure_income_hbm,
    keep_ref, send_ref, age_factor_ref, cross_factor_ref, cells_ref,
    sum_ref, cross_ref, rows_ref, age_target_ref, race_target_ref, size_target_ref,
    ids_ref, age_sex_ref, race_hisp_ref, size_tenure_ref, tenure_income_ref,
    sems, small_sems,
    *, races, sizes, pumas,
):
    tracts, cross, ages, _ = table_hbm.shape
    cross_rows = round_up(cross + 1, 8)
    pairs = (ages + 1) // 2
    every = range(tracts)
    small = [
        pltpu.make_async_copy(source, target, small_sems.at[i])
        for i, (source, target) in enumerate((
            (ids_hbm, ids_ref),
            (age_sex_hbm, age_sex_ref),
            (race_hisp_hbm, race_hisp_ref),
            (size_tenure_hbm, size_tenure_ref),
            (tenure_income_hbm, tenure_income_ref),
        ))
    ]
    for copy in small:
        copy.start()
    for t in every:
        pltpu.make_async_copy(table_hbm.at[t], cells_ref.at[t], sems.at[t]).start()
    lane = lane_ids(1)
    sex0 = lane < 64
    hisp0 = (lane // 32) % 2 == 0
    ten0 = (lane // 16) % 2 == 0

    rows_ref[...] = jnp.zeros(rows_ref.shape, F32)
    for copy in small:
        copy.wait()
    for source_ref, target_ref, rows, mask in (
        (age_sex_ref, age_target_ref, ages, sex0),
        (race_hisp_ref, race_target_ref, races, hisp0),
        (size_tenure_ref, size_target_ref, sizes, ten0),
    ):
        for t in every:
            row = source_ref[t : t + 1, :]
            target_ref[t, 0:rows] = jnp.where(
                mask, column_of(row, rows, 2, 0), column_of(row, rows, 2, 1)
            )

    def add_cross(t):
        pltpu.make_async_copy(table_hbm.at[t], cells_ref.at[t], sems.at[t]).wait()
        total = cells_ref[t, 0]
        for rs in range(1, cross):
            total = total + cells_ref[t, rs]
        margin = jnp.where(sex0, masked_lane_sum(total, sex0), masked_lane_sum(total, ~sex0))
        age_factor_ref[t, 0:ages] = age_target_ref[t, 0:ages] / margin

    def add_ages(t):
        factor = age_factor_ref[t, 0:ages]
        base = t * cross_rows
        for rs in range(cross):
            cross_ref[pl.ds(base + rs, 1), :] = jnp.sum(
                cells_ref[t, rs] * factor, axis=0, keepdims=True
            )

    def arrive(t, carry):
        add_ages(t - 1)
        add_cross(t)
        return carry

    add_cross(0)
    lax.fori_loop(1, tracts, arrive, 0)
    add_ages(tracts - 1)

    bases = [t * cross_rows for t in every]
    by_race = [
        sum(cross_ref[pl.ds(base + s, races, stride=sizes), :] for s in range(sizes))
        for base in bases
    ]
    margin = [jnp.where(hisp0, masked_lane_sum(x, hisp0), masked_lane_sum(x, ~hisp0)) for x in by_race]
    race_factor = [race_target_ref[t, 0:races] / margin[t] for t in every]
    by_size = [
        sum(
            cross_ref[pl.ds(bases[t] + r * sizes, sizes), :] * race_factor[t][r : r + 1]
            for r in range(races)
        )
        for t in every
    ]
    margin = [jnp.where(ten0, masked_lane_sum(x, ten0), masked_lane_sum(x, ~ten0)) for x in by_size]
    size_factor = [size_target_ref[t, 0:sizes] / margin[t] for t in every]
    by_income = [jnp.sum(by_size[t] * size_factor[t], axis=0, keepdims=True) for t in every]
    by_income = [x + pltpu.roll(x, 64, 1) for x in by_income]
    by_income = [x + pltpu.roll(x, 32, 1) for x in by_income]
    for t in every:
        income_factor = jnp.concatenate([tenure_income_ref[t : t + 1, :]] * 4, axis=1) / by_income[t]
        age_factor_ref[t, 0:ages] = age_factor_ref[t, 0:ages] * income_factor
        for r in range(races):
            cross_factor_ref[pl.ds(bases[t] + r * sizes, sizes), :] = (
                size_factor[t] * race_factor[t][r : r + 1]
            )
        cross_factor_ref[pl.ds(bases[t] + cross, cross_rows - cross), :] = jnp.zeros(
            (cross_rows - cross, LANES), F32
        )

    def add_scaled(t):
        base = t * cross_rows
        total = cells_ref[t, 0] * cross_factor_ref[pl.ds(base, 1), :]
        for rs in range(1, cross):
            total = total + cells_ref[t, rs] * cross_factor_ref[pl.ds(base + rs, 1), :]
        sum_ref[t, 0:ages] = total * age_factor_ref[t, 0:ages]
        sum_ref[t, ages : 2 * pairs] = jnp.zeros((2 * pairs - ages, LANES), F32)

    def pack(t):
        even = sum_ref[t, pl.ds(0, pairs, stride=2)]
        odd = sum_ref[t, pl.ds(1, pairs, stride=2)]
        even = even + pltpu.roll(even, 96, 1)
        odd = odd + pltpu.roll(odd, 96, 1)
        packed = jnp.where(
            lane < 32,
            even,
            jnp.where(
                lane < 64,
                pltpu.roll(even, 96, 1),
                jnp.where(lane < 96, pltpu.roll(odd, 64, 1), pltpu.roll(odd, 32, 1)),
            ),
        )
        at = pl.ds(ids_ref[t], pairs, stride=pumas)
        rows_ref[at, :] = rows_ref[at, :] + packed

    def scaled(t, carry):
        pack(t - 1)
        add_scaled(t)
        return carry

    add_scaled(0)
    lax.fori_loop(1, tracts, scaled, 0)
    pack(tracts - 1)
    put_halves(rows_ref, [keep_ref], [send_ref])


def race_margin_kernel(
    ids_ref, cells_ref, age_factor_ref, cross_factor_ref, target_ref,
    own_ref, other_ref, *refs
):
    *chunk_refs, scaled_factor_ref, cross_ref, age_rows_ref, rows_ref, scalar_ref = refs
    chunks = len(chunk_refs) // 2
    keep_refs, send_refs = chunk_refs[:chunks], chunk_refs[chunks:]
    tracts, cross, ages, _ = cells_ref.shape
    cross_rows = round_up(cross + 1, 8)
    pairs, cross_pairs = (ages + 1) // 2, (cross + 1) // 2
    pumas = target_ref.shape[0]
    load_puma_numbers(ids_ref, scalar_ref)
    rows_ref[...] = jnp.zeros(rows_ref.shape, F32)
    factor_rows(target_ref, [own_ref], [other_ref], age_rows_ref)
    lane = lane_ids(1)

    def unpack(t):
        packed = age_rows_ref[pl.ds(scalar_ref[t], pairs, stride=pumas), :]
        half = pltpu.roll(packed, 64, 1)
        even = jnp.where(lane < 32, packed, jnp.where(lane < 96, pltpu.roll(packed, 32, 1), half))
        odd = jnp.where(lane < 32, half, jnp.where(lane < 96, pltpu.roll(packed, 96, 1), packed))
        scaled_factor_ref[t, pl.ds(0, pairs, stride=2)] = even
        scaled_factor_ref[t, pl.ds(1, pairs, stride=2)] = odd

    def add_ages(t):
        factor = scaled_factor_ref[t, 0:ages] * age_factor_ref[t, 0:ages]
        scaled_factor_ref[t, 0:ages] = factor
        base = t * cross_rows
        for rs in range(cross):
            cross_ref[pl.ds(base + rs, 1), :] = jnp.sum(
                cells_ref[t, rs] * factor, axis=0, keepdims=True
            )
        cross_ref[pl.ds(base + cross, cross_rows - cross), :] = jnp.zeros(
            (cross_rows - cross, LANES), F32
        )

    def pack(t):
        halves = []
        for first in range(2):
            at = pl.ds(t * cross_rows + first, cross_pairs, stride=2)
            margin = cross_ref[at, :] * cross_factor_ref[at, :]
            halves.append(margin + pltpu.roll(margin, 64, 1))
        at = pl.ds(scalar_ref[t], cross_pairs, stride=pumas)
        rows_ref[at, :] = rows_ref[at, :] + jnp.where(lane < 64, *halves)

    def step(t, carry):
        pack(t - 1)
        add_ages(t)
        unpack(t + 1)
        return carry

    unpack(0)
    add_ages(0)
    unpack(1)
    lax.fori_loop(1, tracts - 1, step, 0)
    pack(tracts - 2)
    add_ages(tracts - 1)
    pack(tracts - 1)
    put_halves(rows_ref, keep_refs, send_refs)


def final_kernel(
    ids_ref, cells_ref, scaled_factor_ref, cross_factor_ref, target_ref, *refs
):
    *chunk_refs, out_ref, result_ref, cross_ref, rows_ref, scalar_ref, sems = refs
    chunks = len(chunk_refs) // 2
    tracts, cross, ages, _ = cells_ref.shape
    cross_rows = round_up(cross + 1, 8)
    cross_pairs = (cross + 1) // 2
    pumas = target_ref.shape[0]
    load_puma_numbers(ids_ref, scalar_ref)
    factor_rows(target_ref, chunk_refs[:chunks], chunk_refs[chunks:], rows_ref)
    lane = lane_ids(1)

    def unpack(t):
        base = t * cross_rows
        packed = rows_ref[pl.ds(scalar_ref[t], cross_pairs, stride=pumas), :]
        half = pltpu.roll(packed, 64, 1)
        for first, factor in enumerate(
            (jnp.where(lane < 64, packed, half), jnp.where(lane < 64, half, packed))
        ):
            at = pl.ds(base + first, cross_pairs, stride=2)
            cross_ref[at, :] = factor * cross_factor_ref[at, :]

    def scale(t):
        factor = scaled_factor_ref[t, 0:ages]
        base = t * cross_rows
        for rs in range(cross):
            result_ref[t, rs] = cells_ref[t, rs] * factor * cross_ref[pl.ds(base + rs, 1), :]

    def send(t):
        pltpu.make_async_copy(result_ref.at[t], out_ref.at[t], sems.at[t]).start()

    def step(t, carry):
        scale(t)
        unpack(t + 1)
        send(t)
        return carry

    unpack(0)
    lax.fori_loop(0, tracts - 1, step, 0)
    scale(tracts - 1)
    send(tracts - 1)
    for t in range(tracts):
        pltpu.make_async_copy(result_ref.at[t], out_ref.at[t], sems.at[t]).wait()


def call(kernel, out_shapes, in_spaces, out_spaces, scratch):
    def spec(space):
        return pl.BlockSpec(memory_space=space)

    run = pl.pallas_call(
        kernel,
        out_shape=[
            space(shape, F32) for shape, space in zip(out_shapes, out_spaces, strict=True)
        ],
        in_specs=[spec(space) for space in in_spaces],
        out_specs=[spec(space) for space in out_spaces],
        scratch_shapes=scratch,
        compiler_params=pltpu.CompilerParams(vmem_limit_bytes=40 << 20),
    )

    def placed(*args):
        return run(*map(pltpu.with_memory_space_constraint, args, in_spaces))

    return placed


def per_device(
    devices,
    table, age_sex, race_hisp, size_tenure, tenure_income, puma_age, puma_race, tract_puma,
):
    tracts, ages, races, sizes, inner = table.shape
    pumas = puma_age.shape[0]
    cross = races * sizes
    age_pairs, cross_pairs = (ages + 1) // 2, (cross + 1) // 2
    age_rows = 2 * round_up(age_pairs, 8)
    cross_rows = tracts * round_up(cross + 1, 8) + 2 * round_up(cross_pairs, 8) - round_up(cross, 8)
    age_sum_rows, cross_sum_rows = (round_up(x, 8) * pumas for x in (age_pairs, cross_pairs))
    vmem, hbm = pltpu.VMEM, pltpu.HBM

    cells = table.transpose(0, 2, 3, 1, 4).reshape(tracts, cross, ages, inner)
    cells_scratch = pltpu.VMEM((tracts, cross, ages, inner), F32)
    cross_scratch = pltpu.VMEM((cross_rows, LANES), F32)
    copy_sems = pltpu.SemaphoreType.DMA((tracts,))
    numbers_scratch = pltpu.SMEM((tracts,), jnp.int32)

    bits = [1 << k for k in range(1, devices.bit_length() - 1)]
    orders = (bits, bits[1:] + bits[:1])

    def swap(x, partner):
        return lax.ppermute(x, "tract", [(i, partner(i)) for i in range(devices)])

    def totals(keep, send):
        keep = [x + swap(y, lambda i: i ^ 1) for x, y in zip(keep, send)]
        for step in range(len(bits)):
            keep = [x + swap(x, lambda i: i ^ orders[i.bit_count() % 2][step] ^ 1) for x in keep]
        return *keep, *[swap(x, lambda i: i ^ 1) for x in keep]

    age_half, cross_half = -(-age_pairs // 2), -(-cross_pairs // 2)
    cross_chunks = [cross_half - cross_half // 2, cross_half // 2]
    small = [age_sex, race_hisp, size_tenure, tenure_income]
    keep, send, age_factor, cross_factor, cells = call(
        functools.partial(rake_kernel, races=races, sizes=sizes, pumas=pumas),
        [(age_half * pumas, LANES)] * 2
        + [(tracts, age_rows, LANES), (cross_rows, LANES), cells.shape],
        [hbm] * 6,
        [vmem] * 5,
        [
            pltpu.VMEM((tracts, age_rows, LANES), F32),
            cross_scratch,
            pltpu.VMEM((age_sum_rows, LANES), F32),
            pltpu.VMEM((tracts, round_up(ages, 8), LANES), F32),
            pltpu.VMEM((tracts, round_up(races, 8), LANES), F32),
            pltpu.VMEM((tracts, round_up(sizes, 8), LANES), F32),
            numbers_scratch,
        ]
        + [pltpu.VMEM(x.shape, F32) for x in small]
        + [copy_sems, pltpu.SemaphoreType.DMA((1 + len(small),))],
    )(tract_puma, cells, *small)

    *chunks, scaled_factor = call(
        race_margin_kernel,
        [(rows * pumas, LANES) for rows in cross_chunks * 2] + [(tracts, age_rows, LANES)],
        [vmem] * 7,
        [vmem] * (2 * len(cross_chunks) + 1),
        [
            cross_scratch,
            pltpu.VMEM((age_sum_rows, LANES), F32),
            pltpu.VMEM((cross_sum_rows, LANES), F32),
            numbers_scratch,
        ],
    )(tract_puma, cells, age_factor, cross_factor, puma_age, *totals([keep], [send]))

    keep, send = chunks[: len(cross_chunks)], chunks[len(cross_chunks) :]
    out, = call(
        final_kernel,
        [(tracts, cross, ages, inner)],
        [vmem] * (5 + 2 * len(cross_chunks)),
        [hbm],
        [
            cells_scratch,
            cross_scratch,
            pltpu.VMEM((cross_sum_rows, LANES), F32),
            numbers_scratch,
            copy_sems,
        ],
    )(tract_puma, cells, scaled_factor, cross_factor, puma_race, *totals(keep, send))
    return out.reshape(tracts, races, sizes, ages, inner).transpose(0, 3, 1, 2, 4)


def solution(mesh):
    in_specs = (
        P(("grp", "tract"), None, None, None, None),
        P(("grp", "tract"), None),
        P(("grp", "tract"), None),
        P(("grp", "tract"), None),
        P(("grp", "tract"), None),
        P("grp", None),
        P("grp", None),
        P(("grp", "tract")),
    )
    out_specs = P(("grp", "tract"), None, None, None, None)
    return jax.shard_map(
        functools.partial(per_device, mesh.shape["tract"]),
        mesh=mesh, in_specs=in_specs, out_specs=out_specs, check_vma=False,
    )
```

```python
import functools

import jax
import jax.numpy as jnp
from jax import lax
from jax.experimental import pallas as pl
from jax.experimental.pallas import tpu as pltpu
from jax.sharding import PartitionSpec as P

LANES = 128
F32 = jnp.float32


def round_up(value, step):
    return -(-value // step) * step


def lane_ids(rows):
    return lax.broadcasted_iota(jnp.int32, (rows, LANES), 1)


def masked_lane_sum(value, mask):
    return jnp.sum(jnp.where(mask, value, 0.0), axis=-1, keepdims=True)


def column_of(row, rows, step, offset):
    width = row.shape[-1]
    lane = lax.broadcasted_iota(jnp.int32, (rows, width), 1)
    sub = lax.broadcasted_iota(jnp.int32, (rows, width), 0)
    return jnp.sum(jnp.where(lane == step * sub + offset, row, 0.0), axis=-1, keepdims=True)


def half_of(index):
    total = index
    for k in range(1, 16):
        total = total + lax.shift_right_logical(index, k)
    return lax.rem(total, 2)


def factor_rows(target_ref, own_refs, other_refs, rows_ref):
    pumas, columns = target_ref.shape
    half = half_of(lax.axis_index("tract"))
    half_rows = sum(ref.shape[0] for ref in own_refs)
    for refs, which in ((own_refs, half), (other_refs, 1 - half)):
        start = which * half_rows
        for ref in refs:
            rows_ref[pl.ds(pl.multiple_of(start, 8), ref.shape[0]), :] = ref[...]
            start = start + ref.shape[0]
    for first in range(0, columns, LANES):
        width = min(columns - first, LANES)
        at = slice(first // LANES * pumas, (first // LANES + 1) * pumas)
        rows_ref[at, 0:width] = target_ref[:, first : first + width] / rows_ref[at, 0:width]


def load_puma_numbers(ids_ref, scalar_ref):
    ids = ids_ref[...]
    for t in range(scalar_ref.shape[0]):
        scalar_ref[t] = ids[t]


def put_halves(rows_ref, keep_refs, send_refs):
    half = half_of(lax.axis_index("tract"))
    half_rows = sum(ref.shape[0] for ref in keep_refs)
    for refs, which in ((keep_refs, half), (send_refs, 1 - half)):
        start = which * half_rows
        for ref in refs:
            ref[...] = rows_ref[pl.ds(pl.multiple_of(start, 8), ref.shape[0]), :]
            start = start + ref.shape[0]


def arrive_kernel(
    ids_hbm, table_hbm, age_sex_hbm, race_hisp_hbm, size_tenure_hbm, tenure_income_hbm,
    age_factor_ref, cross_ref, cells_ref, race_target_ref, size_target_ref, tenure_income_ref,
    sum_ref, age_target_ref, age_sex_ref, race_hisp_ref, size_tenure_ref,
    sems, small_sems,
    *, races, sizes,
):
    tracts, cross, ages, _ = table_hbm.shape
    cross_rows = round_up(cross + 1, 8)
    small = [
        pltpu.make_async_copy(source, target, small_sems.at[i])
        for i, (source, target) in enumerate((
            (age_sex_hbm, age_sex_ref),
            (race_hisp_hbm, race_hisp_ref),
            (size_tenure_hbm, size_tenure_ref),
            (tenure_income_hbm, tenure_income_ref),
        ))
    ]
    for copy in small:
        copy.start()
    for t in range(tracts):
        pltpu.make_async_copy(table_hbm.at[t], cells_ref.at[t], sems.at[t]).start()
    lane = lane_ids(1)
    sex0 = lane < 64
    hisp0 = (lane // 32) % 2 == 0
    ten0 = (lane // 16) % 2 == 0

    for copy in small:
        copy.wait()
    for source_ref, target_ref, rows, mask in (
        (age_sex_ref, age_target_ref, ages, sex0),
        (race_hisp_ref, race_target_ref, races, hisp0),
        (size_tenure_ref, size_target_ref, sizes, ten0),
    ):
        for t in range(tracts):
            row = source_ref[t : t + 1, :]
            target_ref[t, 0:rows] = jnp.where(
                mask, column_of(row, rows, 2, 0), column_of(row, rows, 2, 1)
            )

    def wait(t):
        pltpu.make_async_copy(table_hbm.at[t], cells_ref.at[t], sems.at[t]).wait()

    def add_cross(t):
        sum_ref[t, 0:ages] = pair_sum(lambda rs: cells_ref[t, rs], cross)

    def divide(t):
        total = sum_ref[t, 0:ages]
        margin = jnp.where(sex0, masked_lane_sum(total, sex0), masked_lane_sum(total, ~sex0))
        age_factor_ref[t, 0:ages] = age_target_ref[t, 0:ages] / margin

    def add_ages(t):
        factor = age_factor_ref[t, 0:ages]
        base = t * cross_rows
        for rs in range(cross):
            cross_ref[pl.ds(base + rs, 1), :] = jnp.sum(
                cells_ref[t, rs] * factor, axis=0, keepdims=True
            )

    def arrive(t, carry):
        wait(t)
        add_ages(t - 2)
        divide(t - 1)
        add_cross(t)
        return carry

    wait(0)
    add_cross(0)
    wait(1)
    divide(0)
    add_cross(1)
    lax.fori_loop(2, tracts, arrive, 0)
    add_ages(tracts - 2)
    divide(tracts - 1)
    add_ages(tracts - 1)


def pair_sum(term, count):
    first, second = term(0), term(1)
    for k in range(2, count, 2):
        first = first + term(k)
        if k + 1 < count:
            second = second + term(k + 1)
    return first + second


def steps_kernel(
    age_factor_ref, cross_ref, race_target_ref, size_target_ref, tenure_income_ref,
    scaled_factor_ref, cross_factor_ref,
    *, races, sizes, ages,
):
    every = range(age_factor_ref.shape[0])
    cross = races * sizes
    cross_rows = round_up(cross + 1, 8)
    lane = lane_ids(1)
    hisp0 = (lane // 32) % 2 == 0
    ten0 = (lane // 16) % 2 == 0
    bases = [t * cross_rows for t in every]
    by_race = [
        sum(cross_ref[pl.ds(base + s, races, stride=sizes), :] for s in range(sizes))
        for base in bases
    ]
    margin = [jnp.where(hisp0, masked_lane_sum(x, hisp0), masked_lane_sum(x, ~hisp0)) for x in by_race]
    race_factor = [race_target_ref[t, 0:races] / margin[t] for t in every]
    by_size = [
        sum(
            cross_ref[pl.ds(bases[t] + r * sizes, sizes), :] * race_factor[t][r : r + 1]
            for r in range(races)
        )
        for t in every
    ]
    margin = [jnp.where(ten0, masked_lane_sum(x, ten0), masked_lane_sum(x, ~ten0)) for x in by_size]
    size_factor = [size_target_ref[t, 0:sizes] / margin[t] for t in every]
    by_income = [jnp.sum(by_size[t] * size_factor[t], axis=0, keepdims=True) for t in every]
    by_income = [x + pltpu.roll(x, 64, 1) for x in by_income]
    by_income = [x + pltpu.roll(x, 32, 1) for x in by_income]
    for t in every:
        income_factor = jnp.concatenate([tenure_income_ref[t : t + 1, :]] * 4, axis=1) / by_income[t]
        scaled_factor_ref[t, 0:ages] = age_factor_ref[t, 0:ages] * income_factor
        for r in range(races):
            cross_factor_ref[pl.ds(bases[t] + r * sizes, sizes), :] = (
                size_factor[t] * race_factor[t][r : r + 1]
            )
        cross_factor_ref[pl.ds(bases[t] + cross, cross_rows - cross), :] = jnp.zeros(
            (cross_rows - cross, LANES), F32
        )


def age_margin_kernel(
    ids_ref, cells_ref, age_factor_ref, cross_factor_ref,
    keep_ref, send_ref,
    sum_ref, rows_ref, scalar_ref,
    *, pumas,
):
    tracts, cross, ages, _ = cells_ref.shape
    cross_rows = round_up(cross + 1, 8)
    pairs = (ages + 1) // 2
    lane = lane_ids(1)
    load_puma_numbers(ids_ref, scalar_ref)
    rows_ref[...] = jnp.zeros(rows_ref.shape, F32)

    def add_scaled(t):
        base = t * cross_rows
        total = pair_sum(
            lambda rs: cells_ref[t, rs] * cross_factor_ref[pl.ds(base + rs, 1), :], cross
        )
        sum_ref[t, 0:ages] = total * age_factor_ref[t, 0:ages]
        sum_ref[t, ages : 2 * pairs] = jnp.zeros((2 * pairs - ages, LANES), F32)

    def pack(t):
        even = sum_ref[t, pl.ds(0, pairs, stride=2)]
        odd = sum_ref[t, pl.ds(1, pairs, stride=2)]
        even = even + pltpu.roll(even, 96, 1)
        odd = odd + pltpu.roll(odd, 96, 1)
        packed = jnp.where(
            lane < 32,
            even,
            jnp.where(
                lane < 64,
                pltpu.roll(even, 96, 1),
                jnp.where(lane < 96, pltpu.roll(odd, 64, 1), pltpu.roll(odd, 32, 1)),
            ),
        )
        at = pl.ds(scalar_ref[t], pairs, stride=pumas)
        rows_ref[at, :] = rows_ref[at, :] + packed

    def scaled(t, carry):
        pack(t - 1)
        add_scaled(t)
        return carry

    add_scaled(0)
    lax.fori_loop(1, tracts, scaled, 0)
    pack(tracts - 1)
    put_halves(rows_ref, [keep_ref], [send_ref])


def race_margin_kernel(
    ids_ref, cells_ref, age_factor_ref, cross_factor_ref, target_ref,
    own_ref, other_ref, *refs
):
    *chunk_refs, scaled_factor_ref, cross_ref, age_rows_ref, rows_ref, scalar_ref = refs
    chunks = len(chunk_refs) // 2
    keep_refs, send_refs = chunk_refs[:chunks], chunk_refs[chunks:]
    tracts, cross, ages, _ = cells_ref.shape
    cross_rows = round_up(cross + 1, 8)
    pairs, cross_pairs = (ages + 1) // 2, (cross + 1) // 2
    pumas = target_ref.shape[0]
    load_puma_numbers(ids_ref, scalar_ref)
    rows_ref[...] = jnp.zeros(rows_ref.shape, F32)
    factor_rows(target_ref, [own_ref], [other_ref], age_rows_ref)
    lane = lane_ids(1)

    def unpack(t):
        packed = age_rows_ref[pl.ds(scalar_ref[t], pairs, stride=pumas), :]
        half = pltpu.roll(packed, 64, 1)
        even = jnp.where(lane < 32, packed, jnp.where(lane < 96, pltpu.roll(packed, 32, 1), half))
        odd = jnp.where(lane < 32, half, jnp.where(lane < 96, pltpu.roll(packed, 96, 1), packed))
        scaled_factor_ref[t, pl.ds(0, pairs, stride=2)] = even
        scaled_factor_ref[t, pl.ds(1, pairs, stride=2)] = odd

    def add_ages(t):
        factor = scaled_factor_ref[t, 0:ages] * age_factor_ref[t, 0:ages]
        scaled_factor_ref[t, 0:ages] = factor
        base = t * cross_rows
        for rs in range(cross):
            cross_ref[pl.ds(base + rs, 1), :] = jnp.sum(
                cells_ref[t, rs] * factor, axis=0, keepdims=True
            )
        cross_ref[pl.ds(base + cross, cross_rows - cross), :] = jnp.zeros(
            (cross_rows - cross, LANES), F32
        )

    def pack(t):
        halves = []
        for first in range(2):
            at = pl.ds(t * cross_rows + first, cross_pairs, stride=2)
            margin = cross_ref[at, :] * cross_factor_ref[at, :]
            halves.append(margin + pltpu.roll(margin, 64, 1))
        at = pl.ds(scalar_ref[t], cross_pairs, stride=pumas)
        rows_ref[at, :] = rows_ref[at, :] + jnp.where(lane < 64, *halves)

    def step(t, carry):
        pack(t - 1)
        add_ages(t)
        unpack(t + 1)
        return carry

    unpack(0)
    add_ages(0)
    unpack(1)
    lax.fori_loop(1, tracts - 1, step, 0)
    pack(tracts - 2)
    add_ages(tracts - 1)
    pack(tracts - 1)
    put_halves(rows_ref, keep_refs, send_refs)


def final_kernel(
    ids_ref, cells_ref, scaled_factor_ref, cross_factor_ref, target_ref, *refs
):
    *chunk_refs, out_ref, result_ref, cross_ref, rows_ref, scalar_ref, sems = refs
    chunks = len(chunk_refs) // 2
    tracts, cross, ages, _ = cells_ref.shape
    cross_rows = round_up(cross + 1, 8)
    cross_pairs = (cross + 1) // 2
    pumas = target_ref.shape[0]
    load_puma_numbers(ids_ref, scalar_ref)
    factor_rows(target_ref, chunk_refs[:chunks], chunk_refs[chunks:], rows_ref)
    lane = lane_ids(1)

    def unpack(t):
        base = t * cross_rows
        packed = rows_ref[pl.ds(scalar_ref[t], cross_pairs, stride=pumas), :]
        half = pltpu.roll(packed, 64, 1)
        for first, factor in enumerate(
            (jnp.where(lane < 64, packed, half), jnp.where(lane < 64, half, packed))
        ):
            at = pl.ds(base + first, cross_pairs, stride=2)
            cross_ref[at, :] = factor * cross_factor_ref[at, :]

    def scale(t):
        factor = scaled_factor_ref[t, 0:ages]
        base = t * cross_rows
        for rs in range(cross):
            result_ref[t, rs] = cells_ref[t, rs] * factor * cross_ref[pl.ds(base + rs, 1), :]

    def send(t):
        pltpu.make_async_copy(result_ref.at[t], out_ref.at[t], sems.at[t]).start()

    def step(t, carry):
        scale(t)
        unpack(t + 1)
        send(t)
        return carry

    unpack(0)
    lax.fori_loop(0, tracts - 1, step, 0)
    scale(tracts - 1)
    send(tracts - 1)
    for t in range(tracts):
        pltpu.make_async_copy(result_ref.at[t], out_ref.at[t], sems.at[t]).wait()


def call(kernel, out_shapes, in_spaces, out_spaces, scratch):
    def spec(space):
        return pl.BlockSpec(memory_space=space)

    run = pl.pallas_call(
        kernel,
        out_shape=[
            space(shape, F32) for shape, space in zip(out_shapes, out_spaces, strict=True)
        ],
        in_specs=[spec(space) for space in in_spaces],
        out_specs=[spec(space) for space in out_spaces],
        scratch_shapes=scratch,
        compiler_params=pltpu.CompilerParams(vmem_limit_bytes=40 << 20),
    )

    def placed(*args):
        return run(*map(pltpu.with_memory_space_constraint, args, in_spaces))

    return placed


def per_device(
    devices,
    table, age_sex, race_hisp, size_tenure, tenure_income, puma_age, puma_race, tract_puma,
):
    tracts, ages, races, sizes, inner = table.shape
    pumas = puma_age.shape[0]
    cross = races * sizes
    age_pairs, cross_pairs = (ages + 1) // 2, (cross + 1) // 2
    age_rows = 2 * round_up(age_pairs, 8)
    cross_rows = tracts * round_up(cross + 1, 8) + 2 * round_up(cross_pairs, 8) - round_up(cross, 8)
    age_sum_rows, cross_sum_rows = (round_up(x, 8) * pumas for x in (age_pairs, cross_pairs))
    vmem, hbm = pltpu.VMEM, pltpu.HBM

    cells = table.transpose(0, 2, 3, 1, 4).reshape(tracts, cross, ages, inner)
    cells_scratch = pltpu.VMEM((tracts, cross, ages, inner), F32)
    cross_scratch = pltpu.VMEM((cross_rows, LANES), F32)
    copy_sems = pltpu.SemaphoreType.DMA((tracts,))
    numbers_scratch = pltpu.SMEM((tracts,), jnp.int32)

    bits = [1 << k for k in range(1, devices.bit_length() - 1)]
    orders = (bits, bits[1:] + bits[:1])

    def swap(x, partner):
        return lax.ppermute(x, "tract", [(i, partner(i)) for i in range(devices)])

    def totals(keep, send):
        keep = [x + swap(y, lambda i: i ^ 1) for x, y in zip(keep, send)]
        for step in range(len(bits)):
            keep = [x + swap(x, lambda i: i ^ orders[i.bit_count() % 2][step] ^ 1) for x in keep]
        return *keep, *[swap(x, lambda i: i ^ 1) for x in keep]

    age_half, cross_half = -(-age_pairs // 2), -(-cross_pairs // 2)
    cross_chunks = [cross_half - cross_half // 2, cross_half // 2]
    race_rows, size_rows = round_up(races, 8), round_up(sizes, 8)
    age_shape, cross_shape = (tracts, age_rows, LANES), (cross_rows, LANES)
    age_factor, cross_sum, cells, race_target, size_target, tenure_income = call(
        functools.partial(arrive_kernel, races=races, sizes=sizes),
        [
            age_shape, cross_shape, cells.shape, (tracts, race_rows, LANES), (tracts, size_rows, LANES),
            tenure_income.shape,
        ],
        [hbm] * 6,
        [vmem] * 6,
        [
            pltpu.VMEM(age_shape, F32),
            pltpu.VMEM(age_shape, F32),
            pltpu.VMEM(age_sex.shape, F32),
            pltpu.VMEM(race_hisp.shape, F32),
            pltpu.VMEM(size_tenure.shape, F32),
            copy_sems,
            pltpu.SemaphoreType.DMA((4,)),
        ],
    )(tract_puma, cells, age_sex, race_hisp, size_tenure, tenure_income)
    age_factor, cross_factor = call(
        functools.partial(steps_kernel, races=races, sizes=sizes, ages=ages),
        [age_shape, cross_shape],
        [vmem] * 5,
        [vmem] * 2,
        [],
    )(age_factor, cross_sum, race_target, size_target, tenure_income)
    keep, send = call(
        functools.partial(age_margin_kernel, pumas=pumas),
        [(age_half * pumas, LANES)] * 2,
        [vmem] * 4,
        [vmem] * 2,
        [pltpu.VMEM(age_shape, F32), pltpu.VMEM((age_sum_rows, LANES), F32), numbers_scratch],
    )(tract_puma, cells, age_factor, cross_factor)

    *chunks, scaled_factor = call(
        race_margin_kernel,
        [(rows * pumas, LANES) for rows in cross_chunks * 2] + [(tracts, age_rows, LANES)],
        [vmem] * 7,
        [vmem] * (2 * len(cross_chunks) + 1),
        [
            cross_scratch,
            pltpu.VMEM((age_sum_rows, LANES), F32),
            pltpu.VMEM((cross_sum_rows, LANES), F32),
            numbers_scratch,
        ],
    )(tract_puma, cells, age_factor, cross_factor, puma_age, *totals([keep], [send]))

    keep, send = chunks[: len(cross_chunks)], chunks[len(cross_chunks) :]
    out, = call(
        final_kernel,
        [(tracts, cross, ages, inner)],
        [vmem] * (5 + 2 * len(cross_chunks)),
        [hbm],
        [
            cells_scratch,
            cross_scratch,
            pltpu.VMEM((cross_sum_rows, LANES), F32),
            numbers_scratch,
            copy_sems,
        ],
    )(tract_puma, cells, scaled_factor, cross_factor, puma_race, *totals(keep, send))
    return out.reshape(tracts, races, sizes, ages, inner).transpose(0, 3, 1, 2, 4)


def solution(mesh):
    in_specs = (
        P(("grp", "tract"), None, None, None, None),
        P(("grp", "tract"), None),
        P(("grp", "tract"), None),
        P(("grp", "tract"), None),
        P(("grp", "tract"), None),
        P("grp", None),
        P("grp", None),
        P(("grp", "tract")),
    )
    out_specs = P(("grp", "tract"), None, None, None, None)
    return jax.shard_map(
        functools.partial(per_device, mesh.shape["tract"]),
        mesh=mesh, in_specs=in_specs, out_specs=out_specs, check_vma=False,
    )
```

```python
import functools

import jax
import jax.numpy as jnp
from jax import lax
from jax.experimental import pallas as pl
from jax.experimental.pallas import tpu as pltpu
from jax.sharding import PartitionSpec as P

LANES = 128
F32 = jnp.float32


def round_up(value, step):
    return -(-value // step) * step


def lane_ids(rows):
    return lax.broadcasted_iota(jnp.int32, (rows, LANES), 1)


def masked_lane_sum(value, mask):
    return jnp.sum(jnp.where(mask, value, 0.0), axis=-1, keepdims=True)


def column_of(row, rows, step, offset):
    width = row.shape[-1]
    lane = lax.broadcasted_iota(jnp.int32, (rows, width), 1)
    sub = lax.broadcasted_iota(jnp.int32, (rows, width), 0)
    return jnp.sum(jnp.where(lane == step * sub + offset, row, 0.0), axis=-1, keepdims=True)


def half_of(index):
    total = index
    for k in range(1, 16):
        total = total + lax.shift_right_logical(index, k)
    return lax.rem(total, 2)


def factor_rows(target_ref, own_refs, other_refs, rows_ref):
    pumas, columns = target_ref.shape
    half = half_of(lax.axis_index("tract"))
    half_rows = sum(ref.shape[0] for ref in own_refs)
    for refs, which in ((own_refs, half), (other_refs, 1 - half)):
        start = which * half_rows
        for ref in refs:
            rows_ref[pl.ds(pl.multiple_of(start, 8), ref.shape[0]), :] = ref[...]
            start = start + ref.shape[0]
    for first in range(0, columns, LANES):
        width = min(columns - first, LANES)
        at = slice(first // LANES * pumas, (first // LANES + 1) * pumas)
        rows_ref[at, 0:width] = target_ref[:, first : first + width] / rows_ref[at, 0:width]


def load_puma_numbers(ids_ref, scalar_ref):
    ids = ids_ref[...]
    for t in range(scalar_ref.shape[0]):
        scalar_ref[t] = ids[t]


def put_halves(rows_ref, keep_refs, send_refs):
    half = half_of(lax.axis_index("tract"))
    half_rows = sum(ref.shape[0] for ref in keep_refs)
    for refs, which in ((keep_refs, half), (send_refs, 1 - half)):
        start = which * half_rows
        for ref in refs:
            ref[...] = rows_ref[pl.ds(pl.multiple_of(start, 8), ref.shape[0]), :]
            start = start + ref.shape[0]


def arrive_kernel(
    ids_hbm, table_hbm, age_sex_hbm, race_hisp_hbm, size_tenure_hbm, tenure_income_hbm,
    age_factor_ref, cross_ref, cells_ref, race_target_ref, size_target_ref, tenure_income_ref,
    sum_ref, age_target_ref, age_sex_ref, race_hisp_ref, size_tenure_ref,
    sems, small_sems,
    *, races, sizes,
):
    tracts, cross, ages, _ = table_hbm.shape
    cross_rows = round_up(cross + 1, 8)
    small = [
        pltpu.make_async_copy(source, target, small_sems.at[i])
        for i, (source, target) in enumerate((
            (age_sex_hbm, age_sex_ref),
            (race_hisp_hbm, race_hisp_ref),
            (size_tenure_hbm, size_tenure_ref),
            (tenure_income_hbm, tenure_income_ref),
        ))
    ]
    for copy in small:
        copy.start()
    for t in range(tracts):
        pltpu.make_async_copy(table_hbm.at[t], cells_ref.at[t], sems.at[t]).start()
    lane = lane_ids(1)
    sex0 = lane < 64
    hisp0 = (lane // 32) % 2 == 0
    ten0 = (lane // 16) % 2 == 0

    for copy in small:
        copy.wait()
    for source_ref, target_ref, rows, mask in (
        (age_sex_ref, age_target_ref, ages, sex0),
        (race_hisp_ref, race_target_ref, races, hisp0),
        (size_tenure_ref, size_target_ref, sizes, ten0),
    ):
        for t in range(tracts):
            row = source_ref[t : t + 1, :]
            target_ref[t, 0:rows] = jnp.where(
                mask, column_of(row, rows, 2, 0), column_of(row, rows, 2, 1)
            )

    def wait(t):
        pltpu.make_async_copy(table_hbm.at[t], cells_ref.at[t], sems.at[t]).wait()

    def add_cross(t):
        sum_ref[t, 0:ages] = pair_sum(lambda rs: cells_ref[t, rs], cross)

    def divide(t):
        total = sum_ref[t, 0:ages]
        margin = jnp.where(sex0, masked_lane_sum(total, sex0), masked_lane_sum(total, ~sex0))
        age_factor_ref[t, 0:ages] = age_target_ref[t, 0:ages] / margin

    def add_ages(t):
        factor = age_factor_ref[t, 0:ages]
        base = t * cross_rows
        for rs in range(cross):
            cross_ref[pl.ds(base + rs, 1), :] = jnp.sum(
                cells_ref[t, rs] * factor, axis=0, keepdims=True
            )

    def arrive(t, carry):
        wait(t)
        add_ages(t - 2)
        divide(t - 1)
        add_cross(t)
        return carry

    wait(0)
    add_cross(0)
    wait(1)
    divide(0)
    add_cross(1)
    lax.fori_loop(2, tracts, arrive, 0)
    add_ages(tracts - 2)
    divide(tracts - 1)
    add_ages(tracts - 1)


def pair_sum(term, count):
    first, second = term(0), term(1)
    for k in range(2, count, 2):
        first = first + term(k)
        if k + 1 < count:
            second = second + term(k + 1)
    return first + second


def steps_kernel(
    age_factor_ref, cross_ref, race_target_ref, size_target_ref, tenure_income_ref,
    scaled_factor_ref, cross_factor_ref, spread_ref,
    *, races, sizes, ages,
):
    every = range(age_factor_ref.shape[0])
    cross = races * sizes
    cross_rows = round_up(cross + 1, 8)
    lane = lane_ids(1)
    hisp0 = (lane // 32) % 2 == 0
    ten0 = (lane // 16) % 2 == 0
    bases = [t * cross_rows for t in every]
    by_race = [
        sum(cross_ref[pl.ds(base + s, races, stride=sizes), :] for s in range(sizes))
        for base in bases
    ]
    margin = [jnp.where(hisp0, masked_lane_sum(x, hisp0), masked_lane_sum(x, ~hisp0)) for x in by_race]
    race_factor = [race_target_ref[t, 0:races] / margin[t] for t in every]
    by_size = [
        sum(
            cross_ref[pl.ds(bases[t] + r * sizes, sizes), :] * race_factor[t][r : r + 1]
            for r in range(races)
        )
        for t in every
    ]
    margin = [jnp.where(ten0, masked_lane_sum(x, ten0), masked_lane_sum(x, ~ten0)) for x in by_size]
    size_factor = [size_target_ref[t, 0:sizes] / margin[t] for t in every]
    by_income = [jnp.sum(by_size[t] * size_factor[t], axis=0, keepdims=True) for t in every]
    by_income = [x + pltpu.roll(x, 64, 1) for x in by_income]
    by_income = [x + pltpu.roll(x, 32, 1) for x in by_income]
    for t in every:
        income_factor = jnp.concatenate([tenure_income_ref[t : t + 1, :]] * 4, axis=1) / by_income[t]
        scaled_factor_ref[t, 0:ages] = age_factor_ref[t, 0:ages] * income_factor
        for r in range(races):
            cross_factor_ref[pl.ds(bases[t] + r * sizes, sizes), :] = (
                size_factor[t] * race_factor[t][r : r + 1]
            )
        cross_factor_ref[pl.ds(bases[t] + cross, cross_rows - cross), :] = jnp.zeros(
            (cross_rows - cross, LANES), F32
        )
        by_race = [jnp.broadcast_to(race_factor[t][r : r + 1], (8, LANES)) for r in range(races)]
        for s in range(sizes):
            by_size = jnp.broadcast_to(size_factor[t][s : s + 1], (8, LANES))
            for r in range(races):
                spread_ref[t, r * sizes + s] = by_size * by_race[r]


def age_margin_kernel(
    ids_ref, cells_ref, age_factor_ref, spread_ref,
    keep_ref, send_ref,
    sum_ref, rows_ref, scalar_ref,
    *, pumas,
):
    tracts, cross, ages, _ = cells_ref.shape
    pairs = (ages + 1) // 2
    lane = lane_ids(1)
    load_puma_numbers(ids_ref, scalar_ref)
    rows_ref[...] = jnp.zeros(rows_ref.shape, F32)

    def add_scaled(t):
        for first in range(0, ages, 8):
            at = slice(first, min(first + 8, ages))
            rows = at.stop - at.start
            total = pair_sum(lambda rs: cells_ref[t, rs, at] * spread_ref[t, rs, 0:rows], cross)
            sum_ref[t, at] = total * age_factor_ref[t, at]
        sum_ref[t, ages : 2 * pairs] = jnp.zeros((2 * pairs - ages, LANES), F32)

    def pack(t):
        even = sum_ref[t, pl.ds(0, pairs, stride=2)]
        odd = sum_ref[t, pl.ds(1, pairs, stride=2)]
        even = even + pltpu.roll(even, 96, 1)
        odd = odd + pltpu.roll(odd, 96, 1)
        packed = jnp.where(
            lane < 32,
            even,
            jnp.where(
                lane < 64,
                pltpu.roll(even, 96, 1),
                jnp.where(lane < 96, pltpu.roll(odd, 64, 1), pltpu.roll(odd, 32, 1)),
            ),
        )
        at = pl.ds(scalar_ref[t], pairs, stride=pumas)
        rows_ref[at, :] = rows_ref[at, :] + packed

    def scaled(t, carry):
        pack(t - 1)
        add_scaled(t)
        return carry

    add_scaled(0)
    lax.fori_loop(1, tracts, scaled, 0)
    pack(tracts - 1)
    put_halves(rows_ref, [keep_ref], [send_ref])


def race_margin_kernel(
    ids_ref, cells_ref, age_factor_ref, cross_factor_ref, target_ref,
    own_ref, other_ref, *refs
):
    *chunk_refs, scaled_factor_ref, cross_ref, age_rows_ref, rows_ref, scalar_ref = refs
    chunks = len(chunk_refs) // 2
    keep_refs, send_refs = chunk_refs[:chunks], chunk_refs[chunks:]
    tracts, cross, ages, _ = cells_ref.shape
    cross_rows = round_up(cross + 1, 8)
    pairs, cross_pairs = (ages + 1) // 2, (cross + 1) // 2
    pumas = target_ref.shape[0]
    load_puma_numbers(ids_ref, scalar_ref)
    rows_ref[...] = jnp.zeros(rows_ref.shape, F32)
    factor_rows(target_ref, [own_ref], [other_ref], age_rows_ref)
    lane = lane_ids(1)

    def unpack(t):
        packed = age_rows_ref[pl.ds(scalar_ref[t], pairs, stride=pumas), :]
        half = pltpu.roll(packed, 64, 1)
        even = jnp.where(lane < 32, packed, jnp.where(lane < 96, pltpu.roll(packed, 32, 1), half))
        odd = jnp.where(lane < 32, half, jnp.where(lane < 96, pltpu.roll(packed, 96, 1), packed))
        scaled_factor_ref[t, pl.ds(0, pairs, stride=2)] = even
        scaled_factor_ref[t, pl.ds(1, pairs, stride=2)] = odd

    def add_ages(t):
        factor = scaled_factor_ref[t, 0:ages] * age_factor_ref[t, 0:ages]
        scaled_factor_ref[t, 0:ages] = factor
        base = t * cross_rows
        for rs in range(cross):
            cross_ref[pl.ds(base + rs, 1), :] = jnp.sum(
                cells_ref[t, rs] * factor, axis=0, keepdims=True
            )
        cross_ref[pl.ds(base + cross, cross_rows - cross), :] = jnp.zeros(
            (cross_rows - cross, LANES), F32
        )

    def pack(t):
        halves = []
        for first in range(2):
            at = pl.ds(t * cross_rows + first, cross_pairs, stride=2)
            margin = cross_ref[at, :] * cross_factor_ref[at, :]
            halves.append(margin + pltpu.roll(margin, 64, 1))
        at = pl.ds(scalar_ref[t], cross_pairs, stride=pumas)
        rows_ref[at, :] = rows_ref[at, :] + jnp.where(lane < 64, *halves)

    def step(t, carry):
        pack(t - 1)
        add_ages(t)
        unpack(t + 1)
        return carry

    unpack(0)
    add_ages(0)
    unpack(1)
    lax.fori_loop(1, tracts - 1, step, 0)
    pack(tracts - 2)
    add_ages(tracts - 1)
    pack(tracts - 1)
    put_halves(rows_ref, keep_refs, send_refs)


def final_kernel(
    ids_ref, cells_ref, scaled_factor_ref, cross_factor_ref, target_ref, *refs
):
    *chunk_refs, out_ref, result_ref, cross_ref, rows_ref, scalar_ref, sems = refs
    chunks = len(chunk_refs) // 2
    tracts, cross, ages, _ = cells_ref.shape
    cross_rows = round_up(cross + 1, 8)
    cross_pairs = (cross + 1) // 2
    pumas = target_ref.shape[0]
    load_puma_numbers(ids_ref, scalar_ref)
    factor_rows(target_ref, chunk_refs[:chunks], chunk_refs[chunks:], rows_ref)
    lane = lane_ids(1)

    def unpack(t):
        base = t * cross_rows
        packed = rows_ref[pl.ds(scalar_ref[t], cross_pairs, stride=pumas), :]
        half = pltpu.roll(packed, 64, 1)
        for first, factor in enumerate(
            (jnp.where(lane < 64, packed, half), jnp.where(lane < 64, half, packed))
        ):
            at = pl.ds(base + first, cross_pairs, stride=2)
            cross_ref[at, :] = factor * cross_factor_ref[at, :]

    def scale(t):
        factor = scaled_factor_ref[t, 0:ages]
        base = t * cross_rows
        for rs in range(cross):
            result_ref[t, rs] = cells_ref[t, rs] * factor * cross_ref[pl.ds(base + rs, 1), :]

    def send(t):
        pltpu.make_async_copy(result_ref.at[t], out_ref.at[t], sems.at[t]).start()

    def step(t, carry):
        scale(t)
        unpack(t + 1)
        send(t)
        return carry

    unpack(0)
    lax.fori_loop(0, tracts - 1, step, 0)
    scale(tracts - 1)
    send(tracts - 1)
    for t in range(tracts):
        pltpu.make_async_copy(result_ref.at[t], out_ref.at[t], sems.at[t]).wait()


def call(kernel, out_shapes, in_spaces, out_spaces, scratch):
    def spec(space):
        return pl.BlockSpec(memory_space=space)

    run = pl.pallas_call(
        kernel,
        out_shape=[
            space(shape, F32) for shape, space in zip(out_shapes, out_spaces, strict=True)
        ],
        in_specs=[spec(space) for space in in_spaces],
        out_specs=[spec(space) for space in out_spaces],
        scratch_shapes=scratch,
        compiler_params=pltpu.CompilerParams(vmem_limit_bytes=40 << 20),
    )

    def placed(*args):
        return run(*map(pltpu.with_memory_space_constraint, args, in_spaces))

    return placed


def per_device(
    devices,
    table, age_sex, race_hisp, size_tenure, tenure_income, puma_age, puma_race, tract_puma,
):
    tracts, ages, races, sizes, inner = table.shape
    pumas = puma_age.shape[0]
    cross = races * sizes
    age_pairs, cross_pairs = (ages + 1) // 2, (cross + 1) // 2
    age_rows = 2 * round_up(age_pairs, 8)
    cross_rows = tracts * round_up(cross + 1, 8) + 2 * round_up(cross_pairs, 8) - round_up(cross, 8)
    age_sum_rows, cross_sum_rows = (round_up(x, 8) * pumas for x in (age_pairs, cross_pairs))
    vmem, hbm = pltpu.VMEM, pltpu.HBM

    cells = table.transpose(0, 2, 3, 1, 4).reshape(tracts, cross, ages, inner)
    cells_scratch = pltpu.VMEM((tracts, cross, ages, inner), F32)
    cross_scratch = pltpu.VMEM((cross_rows, LANES), F32)
    copy_sems = pltpu.SemaphoreType.DMA((tracts,))
    numbers_scratch = pltpu.SMEM((tracts,), jnp.int32)

    bits = [1 << k for k in range(1, devices.bit_length() - 1)]
    orders = (bits, bits[1:] + bits[:1])

    def swap(x, partner):
        return lax.ppermute(x, "tract", [(i, partner(i)) for i in range(devices)])

    def totals(keep, send):
        keep = [x + swap(y, lambda i: i ^ 1) for x, y in zip(keep, send)]
        for step in range(len(bits)):
            keep = [x + swap(x, lambda i: i ^ orders[i.bit_count() % 2][step] ^ 1) for x in keep]
        return *keep, *[swap(x, lambda i: i ^ 1) for x in keep]

    age_half, cross_half = -(-age_pairs // 2), -(-cross_pairs // 2)
    cross_chunks = [cross_half - cross_half // 2, cross_half // 2]
    race_rows, size_rows = round_up(races, 8), round_up(sizes, 8)
    age_shape, cross_shape = (tracts, age_rows, LANES), (cross_rows, LANES)
    age_factor, cross_sum, cells, race_target, size_target, tenure_income = call(
        functools.partial(arrive_kernel, races=races, sizes=sizes),
        [
            age_shape, cross_shape, cells.shape, (tracts, race_rows, LANES), (tracts, size_rows, LANES),
            tenure_income.shape,
        ],
        [hbm] * 6,
        [vmem] * 6,
        [
            pltpu.VMEM(age_shape, F32),
            pltpu.VMEM(age_shape, F32),
            pltpu.VMEM(age_sex.shape, F32),
            pltpu.VMEM(race_hisp.shape, F32),
            pltpu.VMEM(size_tenure.shape, F32),
            copy_sems,
            pltpu.SemaphoreType.DMA((4,)),
        ],
    )(tract_puma, cells, age_sex, race_hisp, size_tenure, tenure_income)
    age_factor, cross_factor, spread = call(
        functools.partial(steps_kernel, races=races, sizes=sizes, ages=ages),
        [age_shape, cross_shape, (tracts, cross, 8, LANES)],
        [vmem] * 5,
        [vmem] * 3,
        [],
    )(age_factor, cross_sum, race_target, size_target, tenure_income)
    keep, send = call(
        functools.partial(age_margin_kernel, pumas=pumas),
        [(age_half * pumas, LANES)] * 2,
        [vmem] * 4,
        [vmem] * 2,
        [pltpu.VMEM(age_shape, F32), pltpu.VMEM((age_sum_rows, LANES), F32), numbers_scratch],
    )(tract_puma, cells, age_factor, spread)

    *chunks, scaled_factor = call(
        race_margin_kernel,
        [(rows * pumas, LANES) for rows in cross_chunks * 2] + [(tracts, age_rows, LANES)],
        [vmem] * 7,
        [vmem] * (2 * len(cross_chunks) + 1),
        [
            cross_scratch,
            pltpu.VMEM((age_sum_rows, LANES), F32),
            pltpu.VMEM((cross_sum_rows, LANES), F32),
            numbers_scratch,
        ],
    )(tract_puma, cells, age_factor, cross_factor, puma_age, *totals([keep], [send]))

    keep, send = chunks[: len(cross_chunks)], chunks[len(cross_chunks) :]
    out, = call(
        final_kernel,
        [(tracts, cross, ages, inner)],
        [vmem] * (5 + 2 * len(cross_chunks)),
        [hbm],
        [
            cells_scratch,
            cross_scratch,
            pltpu.VMEM((cross_sum_rows, LANES), F32),
            numbers_scratch,
            copy_sems,
        ],
    )(tract_puma, cells, scaled_factor, cross_factor, puma_race, *totals(keep, send))
    return out.reshape(tracts, races, sizes, ages, inner).transpose(0, 3, 1, 2, 4)


def solution(mesh):
    in_specs = (
        P(("grp", "tract"), None, None, None, None),
        P(("grp", "tract"), None),
        P(("grp", "tract"), None),
        P(("grp", "tract"), None),
        P(("grp", "tract"), None),
        P("grp", None),
        P("grp", None),
        P(("grp", "tract")),
    )
    out_specs = P(("grp", "tract"), None, None, None, None)
    return jax.shard_map(
        functools.partial(per_device, mesh.shape["tract"]),
        mesh=mesh, in_specs=in_specs, out_specs=out_specs, check_vma=False,
    )
```

```python
import functools

import jax
import jax.numpy as jnp
from jax import lax
from jax.experimental import pallas as pl
from jax.experimental.pallas import tpu as pltpu
from jax.sharding import PartitionSpec as P

LANES = 128
F32 = jnp.float32


def round_up(value, step):
    return -(-value // step) * step


def lane_ids(rows):
    return lax.broadcasted_iota(jnp.int32, (rows, LANES), 1)


def masked_lane_sum(value, mask):
    return jnp.sum(jnp.where(mask, value, 0.0), axis=-1, keepdims=True)


def column_of(row, rows, step, offset):
    width = row.shape[-1]
    lane = lax.broadcasted_iota(jnp.int32, (rows, width), 1)
    sub = lax.broadcasted_iota(jnp.int32, (rows, width), 0)
    return jnp.sum(jnp.where(lane == step * sub + offset, row, 0.0), axis=-1, keepdims=True)


def half_of(index):
    total = index
    for k in range(1, 16):
        total = total + lax.shift_right_logical(index, k)
    return lax.rem(total, 2)


def factor_rows(target_ref, own_refs, other_refs, rows_ref):
    pumas, columns = target_ref.shape
    half = half_of(lax.axis_index("tract"))
    half_rows = sum(ref.shape[0] for ref in own_refs)
    for refs, which in ((own_refs, half), (other_refs, 1 - half)):
        start = which * half_rows
        for ref in refs:
            rows_ref[pl.ds(pl.multiple_of(start, 8), ref.shape[0]), :] = ref[...]
            start = start + ref.shape[0]
    for first in range(0, columns, LANES):
        width = min(columns - first, LANES)
        at = slice(first // LANES * pumas, (first // LANES + 1) * pumas)
        rows_ref[at, 0:width] = target_ref[:, first : first + width] / rows_ref[at, 0:width]


def load_puma_numbers(ids_ref, scalar_ref):
    ids = ids_ref[...]
    for t in range(scalar_ref.shape[0]):
        scalar_ref[t] = ids[t]


def put_halves(rows_ref, keep_refs, send_refs):
    half = half_of(lax.axis_index("tract"))
    half_rows = sum(ref.shape[0] for ref in keep_refs)
    for refs, which in ((keep_refs, half), (send_refs, 1 - half)):
        start = which * half_rows
        for ref in refs:
            ref[...] = rows_ref[pl.ds(pl.multiple_of(start, 8), ref.shape[0]), :]
            start = start + ref.shape[0]


def arrive_kernel(
    ids_hbm, table_hbm, age_sex_hbm, race_hisp_hbm, size_tenure_hbm, tenure_income_hbm,
    age_factor_ref, cross_ref, cells_ref, race_target_ref, size_target_ref, tenure_income_ref,
    sum_ref, age_target_ref, age_sex_ref, race_hisp_ref, size_tenure_ref,
    sems, small_sems,
    *, races, sizes,
):
    tracts, cross, ages, _ = table_hbm.shape
    cross_rows = round_up(cross + 1, 8)
    small = [
        pltpu.make_async_copy(source, target, small_sems.at[i])
        for i, (source, target) in enumerate((
            (age_sex_hbm, age_sex_ref),
            (race_hisp_hbm, race_hisp_ref),
            (size_tenure_hbm, size_tenure_ref),
            (tenure_income_hbm, tenure_income_ref),
        ))
    ]
    for copy in small:
        copy.start()
    for t in range(tracts):
        pltpu.make_async_copy(table_hbm.at[t], cells_ref.at[t], sems.at[t]).start()
    lane = lane_ids(1)
    sex0 = lane < 64
    hisp0 = (lane // 32) % 2 == 0
    ten0 = (lane // 16) % 2 == 0

    for copy in small:
        copy.wait()
    for source_ref, target_ref, rows, mask in (
        (age_sex_ref, age_target_ref, ages, sex0),
        (race_hisp_ref, race_target_ref, races, hisp0),
        (size_tenure_ref, size_target_ref, sizes, ten0),
    ):
        for t in range(tracts):
            row = source_ref[t : t + 1, :]
            target_ref[t, 0:rows] = jnp.where(
                mask, column_of(row, rows, 2, 0), column_of(row, rows, 2, 1)
            )

    def wait(t):
        pltpu.make_async_copy(table_hbm.at[t], cells_ref.at[t], sems.at[t]).wait()

    def add_cross(t):
        sum_ref[t, 0:ages] = pair_sum(lambda rs: cells_ref[t, rs], cross)

    def divide(t):
        total = sum_ref[t, 0:ages]
        margin = jnp.where(sex0, masked_lane_sum(total, sex0), masked_lane_sum(total, ~sex0))
        age_factor_ref[t, 0:ages] = age_target_ref[t, 0:ages] / margin

    def add_ages(t):
        factor = age_factor_ref[t, 0:ages]
        base = t * cross_rows
        for rs in range(cross):
            cross_ref[pl.ds(base + rs, 1), :] = jnp.sum(
                cells_ref[t, rs] * factor, axis=0, keepdims=True
            )

    def arrive(t, carry):
        wait(t)
        add_ages(t - 2)
        divide(t - 1)
        add_cross(t)
        return carry

    wait(0)
    add_cross(0)
    wait(1)
    divide(0)
    add_cross(1)
    lax.fori_loop(2, tracts, arrive, 0)
    add_ages(tracts - 2)
    divide(tracts - 1)
    add_ages(tracts - 1)


def pair_sum(term, count):
    first, second = term(0), term(1)
    for k in range(2, count, 2):
        first = first + term(k)
        if k + 1 < count:
            second = second + term(k + 1)
    return first + second


def steps_kernel(
    age_factor_ref, cross_ref, race_target_ref, size_target_ref, tenure_income_ref,
    scaled_factor_ref, cross_factor_ref,
    *, races, sizes, ages,
):
    every = range(age_factor_ref.shape[0])
    cross = races * sizes
    cross_rows = round_up(cross + 1, 8)
    lane = lane_ids(1)
    hisp0 = (lane // 32) % 2 == 0
    ten0 = (lane // 16) % 2 == 0
    bases = [t * cross_rows for t in every]
    by_race = [
        sum(cross_ref[pl.ds(base + s, races, stride=sizes), :] for s in range(sizes))
        for base in bases
    ]
    margin = [jnp.where(hisp0, masked_lane_sum(x, hisp0), masked_lane_sum(x, ~hisp0)) for x in by_race]
    race_factor = [race_target_ref[t, 0:races] / margin[t] for t in every]
    by_size = [
        sum(
            cross_ref[pl.ds(bases[t] + r * sizes, sizes), :] * race_factor[t][r : r + 1]
            for r in range(races)
        )
        for t in every
    ]
    margin = [jnp.where(ten0, masked_lane_sum(x, ten0), masked_lane_sum(x, ~ten0)) for x in by_size]
    size_factor = [size_target_ref[t, 0:sizes] / margin[t] for t in every]
    by_income = [jnp.sum(by_size[t] * size_factor[t], axis=0, keepdims=True) for t in every]
    by_income = [x + pltpu.roll(x, 64, 1) for x in by_income]
    by_income = [x + pltpu.roll(x, 32, 1) for x in by_income]
    for t in every:
        income_factor = jnp.concatenate([tenure_income_ref[t : t + 1, :]] * 4, axis=1) / by_income[t]
        scaled_factor_ref[t, 0:ages] = age_factor_ref[t, 0:ages] * income_factor
        for r in range(races):
            cross_factor_ref[pl.ds(bases[t] + r * sizes, sizes), :] = (
                size_factor[t] * race_factor[t][r : r + 1]
            )
        cross_factor_ref[pl.ds(bases[t] + cross, cross_rows - cross), :] = jnp.zeros(
            (cross_rows - cross, LANES), F32
        )


def age_margin_kernel(cells_ref, age_factor_ref, cross_factor_ref, sum_ref):
    tracts, cross, ages, _ = cells_ref.shape
    cross_rows = round_up(cross + 1, 8)
    rest = sum_ref.shape[1] - ages

    def add_scaled(t, carry):
        base = t * cross_rows
        total = pair_sum(
            lambda rs: cells_ref[t, rs] * cross_factor_ref[pl.ds(base + rs, 1), :], cross
        )
        sum_ref[t, 0:ages] = total * age_factor_ref[t, 0:ages]
        sum_ref[t, ages:] = jnp.zeros((rest, LANES), F32)
        return carry

    lax.fori_loop(0, tracts, add_scaled, 0)


def age_pack_kernel(ids_ref, sum_ref, keep_ref, send_ref, rows_ref, scalar_ref, *, ages, pumas):
    every = range(sum_ref.shape[0])
    pairs = (ages + 1) // 2
    lane = lane_ids(1)
    load_puma_numbers(ids_ref, scalar_ref)
    rows_ref[...] = jnp.zeros(rows_ref.shape, F32)
    even = [sum_ref[t, pl.ds(0, pairs, stride=2)] for t in every]
    odd = [sum_ref[t, pl.ds(1, pairs, stride=2)] for t in every]
    even = [x + pltpu.roll(x, 96, 1) for x in even]
    odd = [x + pltpu.roll(x, 96, 1) for x in odd]
    packed = [
        jnp.where(
            lane < 32,
            even[t],
            jnp.where(
                lane < 64,
                pltpu.roll(even[t], 96, 1),
                jnp.where(lane < 96, pltpu.roll(odd[t], 64, 1), pltpu.roll(odd[t], 32, 1)),
            ),
        )
        for t in every
    ]
    for t in every:
        at = pl.ds(scalar_ref[t], pairs, stride=pumas)
        rows_ref[at, :] = rows_ref[at, :] + packed[t]
    put_halves(rows_ref, [keep_ref], [send_ref])


def race_margin_kernel(
    ids_ref, cells_ref, age_factor_ref, cross_factor_ref, target_ref,
    own_ref, other_ref, *refs
):
    *chunk_refs, scaled_factor_ref, cross_ref, age_rows_ref, rows_ref, scalar_ref = refs
    chunks = len(chunk_refs) // 2
    keep_refs, send_refs = chunk_refs[:chunks], chunk_refs[chunks:]
    tracts, cross, ages, _ = cells_ref.shape
    cross_rows = round_up(cross + 1, 8)
    pairs, cross_pairs = (ages + 1) // 2, (cross + 1) // 2
    pumas = target_ref.shape[0]
    load_puma_numbers(ids_ref, scalar_ref)
    rows_ref[...] = jnp.zeros(rows_ref.shape, F32)
    factor_rows(target_ref, [own_ref], [other_ref], age_rows_ref)
    lane = lane_ids(1)

    def unpack(t):
        packed = age_rows_ref[pl.ds(scalar_ref[t], pairs, stride=pumas), :]
        half = pltpu.roll(packed, 64, 1)
        even = jnp.where(lane < 32, packed, jnp.where(lane < 96, pltpu.roll(packed, 32, 1), half))
        odd = jnp.where(lane < 32, half, jnp.where(lane < 96, pltpu.roll(packed, 96, 1), packed))
        scaled_factor_ref[t, pl.ds(0, pairs, stride=2)] = even
        scaled_factor_ref[t, pl.ds(1, pairs, stride=2)] = odd

    def add_ages(t):
        factor = scaled_factor_ref[t, 0:ages] * age_factor_ref[t, 0:ages]
        scaled_factor_ref[t, 0:ages] = factor
        base = t * cross_rows
        for rs in range(cross):
            cross_ref[pl.ds(base + rs, 1), :] = jnp.sum(
                cells_ref[t, rs] * factor, axis=0, keepdims=True
            )
        cross_ref[pl.ds(base + cross, cross_rows - cross), :] = jnp.zeros(
            (cross_rows - cross, LANES), F32
        )

    def pack(t):
        halves = []
        for first in range(2):
            at = pl.ds(t * cross_rows + first, cross_pairs, stride=2)
            margin = cross_ref[at, :] * cross_factor_ref[at, :]
            halves.append(margin + pltpu.roll(margin, 64, 1))
        at = pl.ds(scalar_ref[t], cross_pairs, stride=pumas)
        rows_ref[at, :] = rows_ref[at, :] + jnp.where(lane < 64, *halves)

    def step(t, carry):
        pack(t - 1)
        add_ages(t)
        unpack(t + 1)
        return carry

    unpack(0)
    add_ages(0)
    unpack(1)
    lax.fori_loop(1, tracts - 1, step, 0)
    pack(tracts - 2)
    add_ages(tracts - 1)
    pack(tracts - 1)
    put_halves(rows_ref, keep_refs, send_refs)


def final_kernel(
    ids_ref, cells_ref, scaled_factor_ref, cross_factor_ref, target_ref, *refs
):
    *chunk_refs, out_ref, result_ref, cross_ref, rows_ref, scalar_ref, sems = refs
    chunks = len(chunk_refs) // 2
    tracts, cross, ages, _ = cells_ref.shape
    cross_rows = round_up(cross + 1, 8)
    cross_pairs = (cross + 1) // 2
    pumas = target_ref.shape[0]
    load_puma_numbers(ids_ref, scalar_ref)
    factor_rows(target_ref, chunk_refs[:chunks], chunk_refs[chunks:], rows_ref)
    lane = lane_ids(1)

    def unpack(t):
        base = t * cross_rows
        packed = rows_ref[pl.ds(scalar_ref[t], cross_pairs, stride=pumas), :]
        half = pltpu.roll(packed, 64, 1)
        for first, factor in enumerate(
            (jnp.where(lane < 64, packed, half), jnp.where(lane < 64, half, packed))
        ):
            at = pl.ds(base + first, cross_pairs, stride=2)
            cross_ref[at, :] = factor * cross_factor_ref[at, :]

    def scale(t):
        factor = scaled_factor_ref[t, 0:ages]
        base = t * cross_rows
        for rs in range(cross):
            result_ref[t, rs] = cells_ref[t, rs] * factor * cross_ref[pl.ds(base + rs, 1), :]

    def send(t):
        pltpu.make_async_copy(result_ref.at[t], out_ref.at[t], sems.at[t]).start()

    def step(t, carry):
        scale(t)
        unpack(t + 1)
        send(t)
        return carry

    unpack(0)
    lax.fori_loop(0, tracts - 1, step, 0)
    scale(tracts - 1)
    send(tracts - 1)
    for t in range(tracts):
        pltpu.make_async_copy(result_ref.at[t], out_ref.at[t], sems.at[t]).wait()


def call(kernel, out_shapes, in_spaces, out_spaces, scratch):
    def spec(space):
        return pl.BlockSpec(memory_space=space)

    run = pl.pallas_call(
        kernel,
        out_shape=[
            space(shape, F32) for shape, space in zip(out_shapes, out_spaces, strict=True)
        ],
        in_specs=[spec(space) for space in in_spaces],
        out_specs=[spec(space) for space in out_spaces],
        scratch_shapes=scratch,
        compiler_params=pltpu.CompilerParams(vmem_limit_bytes=40 << 20),
    )

    def placed(*args):
        return run(*map(pltpu.with_memory_space_constraint, args, in_spaces))

    return placed


def per_device(
    devices,
    table, age_sex, race_hisp, size_tenure, tenure_income, puma_age, puma_race, tract_puma,
):
    tracts, ages, races, sizes, inner = table.shape
    pumas = puma_age.shape[0]
    cross = races * sizes
    age_pairs, cross_pairs = (ages + 1) // 2, (cross + 1) // 2
    age_rows = 2 * round_up(age_pairs, 8)
    cross_rows = tracts * round_up(cross + 1, 8) + 2 * round_up(cross_pairs, 8) - round_up(cross, 8)
    age_sum_rows, cross_sum_rows = (round_up(x, 8) * pumas for x in (age_pairs, cross_pairs))
    vmem, hbm = pltpu.VMEM, pltpu.HBM

    cells = table.transpose(0, 2, 3, 1, 4).reshape(tracts, cross, ages, inner)
    cells_scratch = pltpu.VMEM((tracts, cross, ages, inner), F32)
    cross_scratch = pltpu.VMEM((cross_rows, LANES), F32)
    copy_sems = pltpu.SemaphoreType.DMA((tracts,))
    numbers_scratch = pltpu.SMEM((tracts,), jnp.int32)

    bits = [1 << k for k in range(1, devices.bit_length() - 1)]
    orders = (bits, bits[1:] + bits[:1])

    def swap(x, partner):
        return lax.ppermute(x, "tract", [(i, partner(i)) for i in range(devices)])

    def totals(keep, send):
        keep = [x + swap(y, lambda i: i ^ 1) for x, y in zip(keep, send)]
        for step in range(len(bits)):
            keep = [x + swap(x, lambda i: i ^ orders[i.bit_count() % 2][step] ^ 1) for x in keep]
        return *keep, *[swap(x, lambda i: i ^ 1) for x in keep]

    age_half, cross_half = -(-age_pairs // 2), -(-cross_pairs // 2)
    cross_chunks = [cross_half - cross_half // 2, cross_half // 2]
    race_rows, size_rows = round_up(races, 8), round_up(sizes, 8)
    age_shape, cross_shape = (tracts, age_rows, LANES), (cross_rows, LANES)
    age_factor, cross_sum, cells, race_target, size_target, tenure_income = call(
        functools.partial(arrive_kernel, races=races, sizes=sizes),
        [
            age_shape, cross_shape, cells.shape, (tracts, race_rows, LANES), (tracts, size_rows, LANES),
            tenure_income.shape,
        ],
        [hbm] * 6,
        [vmem] * 6,
        [
            pltpu.VMEM(age_shape, F32),
            pltpu.VMEM(age_shape, F32),
            pltpu.VMEM(age_sex.shape, F32),
            pltpu.VMEM(race_hisp.shape, F32),
            pltpu.VMEM(size_tenure.shape, F32),
            copy_sems,
            pltpu.SemaphoreType.DMA((4,)),
        ],
    )(tract_puma, cells, age_sex, race_hisp, size_tenure, tenure_income)
    age_factor, cross_factor = call(
        functools.partial(steps_kernel, races=races, sizes=sizes, ages=ages),
        [age_shape, cross_shape],
        [vmem] * 5,
        [vmem] * 2,
        [],
    )(age_factor, cross_sum, race_target, size_target, tenure_income)
    sums, = call(age_margin_kernel, [age_shape], [vmem] * 3, [vmem], [])(
        cells, age_factor, cross_factor
    )
    keep, send = call(
        functools.partial(age_pack_kernel, ages=ages, pumas=pumas),
        [(age_half * pumas, LANES)] * 2,
        [vmem] * 2,
        [vmem] * 2,
        [pltpu.VMEM((age_sum_rows, LANES), F32), numbers_scratch],
    )(tract_puma, sums)

    *chunks, scaled_factor = call(
        race_margin_kernel,
        [(rows * pumas, LANES) for rows in cross_chunks * 2] + [(tracts, age_rows, LANES)],
        [vmem] * 7,
        [vmem] * (2 * len(cross_chunks) + 1),
        [
            cross_scratch,
            pltpu.VMEM((age_sum_rows, LANES), F32),
            pltpu.VMEM((cross_sum_rows, LANES), F32),
            numbers_scratch,
        ],
    )(tract_puma, cells, age_factor, cross_factor, puma_age, *totals([keep], [send]))

    keep, send = chunks[: len(cross_chunks)], chunks[len(cross_chunks) :]
    out, = call(
        final_kernel,
        [(tracts, cross, ages, inner)],
        [vmem] * (5 + 2 * len(cross_chunks)),
        [hbm],
        [
            cells_scratch,
            cross_scratch,
            pltpu.VMEM((cross_sum_rows, LANES), F32),
            numbers_scratch,
            copy_sems,
        ],
    )(tract_puma, cells, scaled_factor, cross_factor, puma_race, *totals(keep, send))
    return out.reshape(tracts, races, sizes, ages, inner).transpose(0, 3, 1, 2, 4)


def solution(mesh):
    in_specs = (
        P(("grp", "tract"), None, None, None, None),
        P(("grp", "tract"), None),
        P(("grp", "tract"), None),
        P(("grp", "tract"), None),
        P(("grp", "tract"), None),
        P("grp", None),
        P("grp", None),
        P(("grp", "tract")),
    )
    out_specs = P(("grp", "tract"), None, None, None, None)
    return jax.shard_map(
        functools.partial(per_device, mesh.shape["tract"]),
        mesh=mesh, in_specs=in_specs, out_specs=out_specs, check_vma=False,
    )
```

```python
import functools

import jax
import jax.numpy as jnp
from jax import lax
from jax.experimental import pallas as pl
from jax.experimental.pallas import tpu as pltpu
from jax.sharding import PartitionSpec as P

LANES = 128
GROUP = 4
F32 = jnp.float32


def round_up(value, step):
    return -(-value // step) * step


def lane_ids(rows):
    return lax.broadcasted_iota(jnp.int32, (rows, LANES), 1)


def masked_lane_sum(value, mask):
    return jnp.sum(jnp.where(mask, value, 0.0), axis=-1, keepdims=True)


def column_of(row, rows, step, offset):
    width = row.shape[-1]
    lane = lax.broadcasted_iota(jnp.int32, (rows, width), 1)
    sub = lax.broadcasted_iota(jnp.int32, (rows, width), 0)
    return jnp.sum(jnp.where(lane == step * sub + offset, row, 0.0), axis=-1, keepdims=True)


def half_of(index):
    total = index
    for k in range(1, 16):
        total = total + lax.shift_right_logical(index, k)
    return lax.rem(total, 2)


def factor_rows(target_ref, own_refs, other_refs, rows_ref):
    pumas, columns = target_ref.shape
    half = half_of(lax.axis_index("tract"))
    half_rows = sum(ref.shape[0] for ref in own_refs)
    for refs, which in ((own_refs, half), (other_refs, 1 - half)):
        start = which * half_rows
        for ref in refs:
            rows_ref[pl.ds(pl.multiple_of(start, 8), ref.shape[0]), :] = ref[...]
            start = start + ref.shape[0]
    for first in range(0, columns, LANES):
        width = min(columns - first, LANES)
        at = slice(first // LANES * pumas, (first // LANES + 1) * pumas)
        rows_ref[at, 0:width] = target_ref[:, first : first + width] / rows_ref[at, 0:width]


def load_puma_numbers(ids_ref, scalar_ref):
    ids = ids_ref[...]
    for t in range(scalar_ref.shape[0]):
        scalar_ref[t] = ids[t]


def put_halves(rows_ref, keep_refs, send_refs):
    half = half_of(lax.axis_index("tract"))
    half_rows = sum(ref.shape[0] for ref in keep_refs)
    for refs, which in ((keep_refs, half), (send_refs, 1 - half)):
        start = which * half_rows
        for ref in refs:
            ref[...] = rows_ref[pl.ds(pl.multiple_of(start, 8), ref.shape[0]), :]
            start = start + ref.shape[0]


def arrive_kernel(
    ids_hbm, table_hbm, age_sex_hbm, race_hisp_hbm, size_tenure_hbm, tenure_income_hbm,
    age_factor_ref, cross_ref, cells_ref, race_target_ref, size_target_ref, tenure_income_ref,
    sum_ref, age_target_ref, age_sex_ref, race_hisp_ref, size_tenure_ref,
    sems, small_sems,
    *, races, sizes,
):
    tracts, cross, ages, _ = table_hbm.shape
    cross_rows = round_up(cross + 1, 8)
    small = [
        pltpu.make_async_copy(source, target, small_sems.at[i])
        for i, (source, target) in enumerate((
            (age_sex_hbm, age_sex_ref),
            (race_hisp_hbm, race_hisp_ref),
            (size_tenure_hbm, size_tenure_ref),
            (tenure_income_hbm, tenure_income_ref),
        ))
    ]
    for copy in small:
        copy.start()
    for t in range(tracts):
        pltpu.make_async_copy(table_hbm.at[t], cells_ref.at[t], sems.at[t]).start()
    lane = lane_ids(1)
    sex0 = lane < 64
    hisp0 = (lane // 32) % 2 == 0
    ten0 = (lane // 16) % 2 == 0

    for copy in small:
        copy.wait()
    for source_ref, target_ref, rows, mask in (
        (age_sex_ref, age_target_ref, ages, sex0),
        (race_hisp_ref, race_target_ref, races, hisp0),
        (size_tenure_ref, size_target_ref, sizes, ten0),
    ):
        for t in range(tracts):
            row = source_ref[t : t + 1, :]
            target_ref[t, 0:rows] = jnp.where(
                mask, column_of(row, rows, 2, 0), column_of(row, rows, 2, 1)
            )

    def divide(group):
        total = [sum_ref[t, 0:ages] for t in group]
        first = [masked_lane_sum(x, sex0) for x in total]
        second = [masked_lane_sum(x, ~sex0) for x in total]
        for t, x, y in zip(group, first, second):
            age_factor_ref[t, 0:ages] = age_target_ref[t, 0:ages] / jnp.where(sex0, x, y)

    def add_ages(t, carry):
        factor = age_factor_ref[t, 0:ages]
        base = t * cross_rows
        for rs in range(cross):
            cross_ref[pl.ds(base + rs, 1), :] = jnp.sum(
                cells_ref[t, rs] * factor, axis=0, keepdims=True
            )
        return carry

    def arrive(t, carry):
        pltpu.make_async_copy(table_hbm.at[t], cells_ref.at[t], sems.at[t]).wait()
        sum_ref[t, 0:ages] = pair_sum(lambda rs: cells_ref[t, rs], cross)
        return carry

    groups = [range(t, min(t + GROUP, tracts)) for t in range(0, tracts, GROUP)]
    for number, group in enumerate(groups):
        lax.fori_loop(group.start, group.stop, arrive, 0)
        if number:
            before = groups[number - 1]
            lax.fori_loop(before.start, before.stop, add_ages, 0)
        divide(group)
    lax.fori_loop(groups[-1].start, groups[-1].stop, add_ages, 0)


def pair_sum(term, count):
    first, second = term(0), term(1)
    for k in range(2, count, 2):
        first = first + term(k)
        if k + 1 < count:
            second = second + term(k + 1)
    return first + second


def steps_kernel(
    age_factor_ref, cross_ref, race_target_ref, size_target_ref, tenure_income_ref,
    scaled_factor_ref, cross_factor_ref,
    *, races, sizes, ages,
):
    every = range(age_factor_ref.shape[0])
    cross = races * sizes
    cross_rows = round_up(cross + 1, 8)
    lane = lane_ids(1)
    hisp0 = (lane // 32) % 2 == 0
    ten0 = (lane // 16) % 2 == 0
    bases = [t * cross_rows for t in every]
    by_race = [
        sum(cross_ref[pl.ds(base + s, races, stride=sizes), :] for s in range(sizes))
        for base in bases
    ]
    margin = [jnp.where(hisp0, masked_lane_sum(x, hisp0), masked_lane_sum(x, ~hisp0)) for x in by_race]
    race_factor = [race_target_ref[t, 0:races] / margin[t] for t in every]
    by_size = [
        sum(
            cross_ref[pl.ds(bases[t] + r * sizes, sizes), :] * race_factor[t][r : r + 1]
            for r in range(races)
        )
        for t in every
    ]
    margin = [jnp.where(ten0, masked_lane_sum(x, ten0), masked_lane_sum(x, ~ten0)) for x in by_size]
    size_factor = [size_target_ref[t, 0:sizes] / margin[t] for t in every]
    by_income = [jnp.sum(by_size[t] * size_factor[t], axis=0, keepdims=True) for t in every]
    by_income = [x + pltpu.roll(x, 64, 1) for x in by_income]
    by_income = [x + pltpu.roll(x, 32, 1) for x in by_income]
    for t in every:
        income_factor = jnp.concatenate([tenure_income_ref[t : t + 1, :]] * 4, axis=1) / by_income[t]
        scaled_factor_ref[t, 0:ages] = age_factor_ref[t, 0:ages] * income_factor
        for r in range(races):
            cross_factor_ref[pl.ds(bases[t] + r * sizes, sizes), :] = (
                size_factor[t] * race_factor[t][r : r + 1]
            )
        cross_factor_ref[pl.ds(bases[t] + cross, cross_rows - cross), :] = jnp.zeros(
            (cross_rows - cross, LANES), F32
        )


def age_margin_kernel(cells_ref, age_factor_ref, cross_factor_ref, sum_ref):
    tracts, cross, ages, _ = cells_ref.shape
    cross_rows = round_up(cross + 1, 8)
    rest = sum_ref.shape[1] - ages

    def add_scaled(t, carry):
        base = t * cross_rows
        total = pair_sum(
            lambda rs: cells_ref[t, rs] * cross_factor_ref[pl.ds(base + rs, 1), :], cross
        )
        sum_ref[t, 0:ages] = total * age_factor_ref[t, 0:ages]
        sum_ref[t, ages:] = jnp.zeros((rest, LANES), F32)
        return carry

    lax.fori_loop(0, tracts, add_scaled, 0)


def age_pack_kernel(ids_ref, sum_ref, keep_ref, send_ref, rows_ref, scalar_ref, *, ages, pumas):
    every = range(sum_ref.shape[0])
    pairs = (ages + 1) // 2
    lane = lane_ids(1)
    load_puma_numbers(ids_ref, scalar_ref)
    rows_ref[...] = jnp.zeros(rows_ref.shape, F32)
    even = [sum_ref[t, pl.ds(0, pairs, stride=2)] for t in every]
    odd = [sum_ref[t, pl.ds(1, pairs, stride=2)] for t in every]
    even = [x + pltpu.roll(x, 96, 1) for x in even]
    odd = [x + pltpu.roll(x, 96, 1) for x in odd]
    packed = [
        jnp.where(
            lane < 32,
            even[t],
            jnp.where(
                lane < 64,
                pltpu.roll(even[t], 96, 1),
                jnp.where(lane < 96, pltpu.roll(odd[t], 64, 1), pltpu.roll(odd[t], 32, 1)),
            ),
        )
        for t in every
    ]
    for t in every:
        at = pl.ds(scalar_ref[t], pairs, stride=pumas)
        rows_ref[at, :] = rows_ref[at, :] + packed[t]
    put_halves(rows_ref, [keep_ref], [send_ref])


def unpack_ages_kernel(
    ids_ref, target_ref, own_ref, other_ref, age_factor_ref,
    scaled_factor_ref,
    rows_ref, scalar_ref,
    *, ages,
):
    every = range(age_factor_ref.shape[0])
    pairs = (ages + 1) // 2
    pumas = target_ref.shape[0]
    load_puma_numbers(ids_ref, scalar_ref)
    factor_rows(target_ref, [own_ref], [other_ref], rows_ref)
    lane = lane_ids(1)
    packed = [rows_ref[pl.ds(scalar_ref[t], pairs, stride=pumas), :] for t in every]
    quarter = [pltpu.roll(x, 32, 1) for x in packed]
    half = [pltpu.roll(x, 64, 1) for x in packed]
    back = [pltpu.roll(x, 96, 1) for x in packed]
    for t in every:
        even = jnp.where(lane < 32, packed[t], jnp.where(lane < 96, quarter[t], half[t]))
        odd = jnp.where(lane < 32, half[t], jnp.where(lane < 96, back[t], packed[t]))
        for first, factor in enumerate((even, odd)):
            at = pl.ds(first, pairs, stride=2)
            scaled_factor_ref[t, at] = factor * age_factor_ref[t, at]


def race_margin_kernel(cells_ref, factor_ref, cross_ref):
    tracts, cross, ages, _ = cells_ref.shape
    cross_rows = round_up(cross + 1, 8)

    def add_ages(t, carry):
        factor = factor_ref[t, 0:ages]
        base = t * cross_rows
        for rs in range(cross):
            cross_ref[pl.ds(base + rs, 1), :] = jnp.sum(
                cells_ref[t, rs] * factor, axis=0, keepdims=True
            )
        cross_ref[pl.ds(base + cross, cross_rows - cross), :] = jnp.zeros(
            (cross_rows - cross, LANES), F32
        )
        return carry

    lax.fori_loop(0, tracts, add_ages, 0)


def race_pack_kernel(ids_ref, cross_ref, cross_factor_ref, *refs, cross, pumas):
    *chunk_refs, rows_ref, scalar_ref = refs
    chunks = len(chunk_refs) // 2
    every = range(scalar_ref.shape[0])
    cross_rows = round_up(cross + 1, 8)
    cross_pairs = (cross + 1) // 2
    load_puma_numbers(ids_ref, scalar_ref)
    rows_ref[...] = jnp.zeros(rows_ref.shape, F32)
    lane = lane_ids(1)
    halves = []
    for first in range(2):
        at = [pl.ds(t * cross_rows + first, cross_pairs, stride=2) for t in every]
        margin = [cross_ref[x, :] * cross_factor_ref[x, :] for x in at]
        halves.append([x + pltpu.roll(x, 64, 1) for x in margin])
    for t in every:
        at = pl.ds(scalar_ref[t], cross_pairs, stride=pumas)
        rows_ref[at, :] = rows_ref[at, :] + jnp.where(lane < 64, halves[0][t], halves[1][t])
    put_halves(rows_ref, chunk_refs[:chunks], chunk_refs[chunks:])


def unpack_race_kernel(ids_ref, target_ref, cross_factor_ref, *refs, cross):
    *chunk_refs, scaled_ref, rows_ref, scalar_ref = refs
    chunks = len(chunk_refs) // 2
    every = range(scalar_ref.shape[0])
    cross_rows = round_up(cross + 1, 8)
    cross_pairs = (cross + 1) // 2
    pumas = target_ref.shape[0]
    load_puma_numbers(ids_ref, scalar_ref)
    factor_rows(target_ref, chunk_refs[:chunks], chunk_refs[chunks:], rows_ref)
    lane = lane_ids(1)
    packed = [rows_ref[pl.ds(scalar_ref[t], cross_pairs, stride=pumas), :] for t in every]
    half = [pltpu.roll(x, 64, 1) for x in packed]
    for t in every:
        even, odd = jnp.where(lane < 64, packed[t], half[t]), jnp.where(lane < 64, half[t], packed[t])
        for first, factor in enumerate((even, odd)):
            at = pl.ds(t * cross_rows + first, cross_pairs, stride=2)
            scaled_ref[at, :] = factor * cross_factor_ref[at, :]


def final_kernel(cells_ref, age_factor_ref, cross_factor_ref, out_ref, result_ref, sems):
    tracts, cross, ages, _ = cells_ref.shape
    cross_rows = round_up(cross + 1, 8)

    def copy(t):
        return pltpu.make_async_copy(result_ref.at[t], out_ref.at[t], sems.at[t])

    def scale(t, carry):
        factor = age_factor_ref[t, 0:ages]
        base = t * cross_rows
        for rs in range(cross):
            result_ref[t, rs] = cells_ref[t, rs] * factor * cross_factor_ref[pl.ds(base + rs, 1), :]
        copy(t).start()
        return carry

    lax.fori_loop(0, tracts, scale, 0)
    for t in range(tracts):
        copy(t).wait()


def call(kernel, out_shapes, in_spaces, out_spaces, scratch):
    def spec(space):
        return pl.BlockSpec(memory_space=space)

    run = pl.pallas_call(
        kernel,
        out_shape=[
            space(shape, F32) for shape, space in zip(out_shapes, out_spaces, strict=True)
        ],
        in_specs=[spec(space) for space in in_spaces],
        out_specs=[spec(space) for space in out_spaces],
        scratch_shapes=scratch,
        compiler_params=pltpu.CompilerParams(vmem_limit_bytes=40 << 20),
    )

    def placed(*args):
        return run(*map(pltpu.with_memory_space_constraint, args, in_spaces))

    return placed


def per_device(
    devices,
    table, age_sex, race_hisp, size_tenure, tenure_income, puma_age, puma_race, tract_puma,
):
    tracts, ages, races, sizes, inner = table.shape
    pumas = puma_age.shape[0]
    cross = races * sizes
    age_pairs, cross_pairs = (ages + 1) // 2, (cross + 1) // 2
    age_rows = 2 * round_up(age_pairs, 8)
    cross_rows = tracts * round_up(cross + 1, 8) + 2 * round_up(cross_pairs, 8) - round_up(cross, 8)
    age_sum_rows, cross_sum_rows = (round_up(x, 8) * pumas for x in (age_pairs, cross_pairs))
    vmem, hbm = pltpu.VMEM, pltpu.HBM

    cells = table.transpose(0, 2, 3, 1, 4).reshape(tracts, cross, ages, inner)
    copy_sems = pltpu.SemaphoreType.DMA((tracts,))
    numbers_scratch = pltpu.SMEM((tracts,), jnp.int32)

    bits = [1 << k for k in range(1, devices.bit_length() - 1)]
    orders = (bits, bits[1:] + bits[:1])

    def swap(x, partner):
        return lax.ppermute(x, "tract", [(i, partner(i)) for i in range(devices)])

    def totals(keep, send):
        keep = [x + swap(y, lambda i: i ^ 1) for x, y in zip(keep, send)]
        for step in range(len(bits)):
            keep = [x + swap(x, lambda i: i ^ orders[i.bit_count() % 2][step] ^ 1) for x in keep]
        return *keep, *[swap(x, lambda i: i ^ 1) for x in keep]

    age_half, cross_half = -(-age_pairs // 2), -(-cross_pairs // 2)
    cross_chunks = [cross_half - cross_half // 2, cross_half // 2]
    race_rows, size_rows = round_up(races, 8), round_up(sizes, 8)
    age_shape, cross_shape = (tracts, age_rows, LANES), (cross_rows, LANES)
    age_factor, cross_sum, cells, race_target, size_target, tenure_income = call(
        functools.partial(arrive_kernel, races=races, sizes=sizes),
        [
            age_shape, cross_shape, cells.shape, (tracts, race_rows, LANES), (tracts, size_rows, LANES),
            tenure_income.shape,
        ],
        [hbm] * 6,
        [vmem] * 6,
        [
            pltpu.VMEM(age_shape, F32),
            pltpu.VMEM(age_shape, F32),
            pltpu.VMEM(age_sex.shape, F32),
            pltpu.VMEM(race_hisp.shape, F32),
            pltpu.VMEM(size_tenure.shape, F32),
            copy_sems,
            pltpu.SemaphoreType.DMA((4,)),
        ],
    )(tract_puma, cells, age_sex, race_hisp, size_tenure, tenure_income)
    age_factor, cross_factor = call(
        functools.partial(steps_kernel, races=races, sizes=sizes, ages=ages),
        [age_shape, cross_shape],
        [vmem] * 5,
        [vmem] * 2,
        [],
    )(age_factor, cross_sum, race_target, size_target, tenure_income)
    sums, = call(age_margin_kernel, [age_shape], [vmem] * 3, [vmem], [])(
        cells, age_factor, cross_factor
    )
    keep, send = call(
        functools.partial(age_pack_kernel, ages=ages, pumas=pumas),
        [(age_half * pumas, LANES)] * 2,
        [vmem] * 2,
        [vmem] * 2,
        [pltpu.VMEM((age_sum_rows, LANES), F32), numbers_scratch],
    )(tract_puma, sums)

    age_factor, = call(
        functools.partial(unpack_ages_kernel, ages=ages),
        [age_shape],
        [vmem] * 5,
        [vmem],
        [pltpu.VMEM((age_sum_rows, LANES), F32), numbers_scratch],
    )(tract_puma, puma_age, *totals([keep], [send]), age_factor)
    cross_sum, = call(race_margin_kernel, [cross_shape], [vmem] * 2, [vmem], [])(cells, age_factor)
    chunks = call(
        functools.partial(race_pack_kernel, cross=cross, pumas=pumas),
        [(rows * pumas, LANES) for rows in cross_chunks * 2],
        [vmem] * 3,
        [vmem] * (2 * len(cross_chunks)),
        [pltpu.VMEM((cross_sum_rows, LANES), F32), numbers_scratch],
    )(tract_puma, cross_sum, cross_factor)

    keep, send = chunks[: len(cross_chunks)], chunks[len(cross_chunks) :]
    cross_factor, = call(
        functools.partial(unpack_race_kernel, cross=cross),
        [cross_shape],
        [vmem] * (3 + 2 * len(cross_chunks)),
        [vmem],
        [pltpu.VMEM((cross_sum_rows, LANES), F32), numbers_scratch],
    )(tract_puma, puma_race, cross_factor, *totals(keep, send))
    out, = call(
        final_kernel,
        [(tracts, cross, ages, inner)],
        [vmem] * 3,
        [hbm],
        [pltpu.VMEM((tracts, cross, ages, inner), F32), copy_sems],
    )(cells, age_factor, cross_factor)
    return out.reshape(tracts, races, sizes, ages, inner).transpose(0, 3, 1, 2, 4)


def solution(mesh):
    in_specs = (
        P(("grp", "tract"), None, None, None, None),
        P(("grp", "tract"), None),
        P(("grp", "tract"), None),
        P(("grp", "tract"), None),
        P(("grp", "tract"), None),
        P("grp", None),
        P("grp", None),
        P(("grp", "tract")),
    )
    out_specs = P(("grp", "tract"), None, None, None, None)
    return jax.shard_map(
        functools.partial(per_device, mesh.shape["tract"]),
        mesh=mesh, in_specs=in_specs, out_specs=out_specs, check_vma=False,
    )
```

```python
import functools

import jax
import jax.numpy as jnp
from jax import lax
from jax.experimental import pallas as pl
from jax.experimental.pallas import tpu as pltpu
from jax.sharding import PartitionSpec as P

LANES = 128
GROUP = 4
IN_FLIGHT = 4
F32 = jnp.float32


def round_up(value, step):
    return -(-value // step) * step


def lane_ids(rows):
    return lax.broadcasted_iota(jnp.int32, (rows, LANES), 1)


def masked_lane_sum(value, mask):
    return jnp.sum(jnp.where(mask, value, 0.0), axis=-1, keepdims=True)


def column_of(row, rows, step, offset):
    width = row.shape[-1]
    lane = lax.broadcasted_iota(jnp.int32, (rows, width), 1)
    sub = lax.broadcasted_iota(jnp.int32, (rows, width), 0)
    return jnp.sum(jnp.where(lane == step * sub + offset, row, 0.0), axis=-1, keepdims=True)


def half_of(index):
    total = index
    for k in range(1, 16):
        total = total + lax.shift_right_logical(index, k)
    return lax.rem(total, 2)


def factor_rows(target_ref, own_refs, other_refs, rows_ref):
    pumas, columns = target_ref.shape
    half = half_of(lax.axis_index("tract"))
    half_rows = sum(ref.shape[0] for ref in own_refs)
    for refs, which in ((own_refs, half), (other_refs, 1 - half)):
        start = which * half_rows
        for ref in refs:
            rows_ref[pl.ds(pl.multiple_of(start, 8), ref.shape[0]), :] = ref[...]
            start = start + ref.shape[0]
    for first in range(0, columns, LANES):
        width = min(columns - first, LANES)
        at = slice(first // LANES * pumas, (first // LANES + 1) * pumas)
        rows_ref[at, 0:width] = target_ref[:, first : first + width] / rows_ref[at, 0:width]


def load_puma_numbers(ids_ref, scalar_ref):
    ids = ids_ref[...]
    for t in range(scalar_ref.shape[0]):
        scalar_ref[t] = ids[t]


def put_halves(rows_ref, keep_refs, send_refs):
    half = half_of(lax.axis_index("tract"))
    half_rows = sum(ref.shape[0] for ref in keep_refs)
    for refs, which in ((keep_refs, half), (send_refs, 1 - half)):
        start = which * half_rows
        for ref in refs:
            ref[...] = rows_ref[pl.ds(pl.multiple_of(start, 8), ref.shape[0]), :]
            start = start + ref.shape[0]


def pair_sum(term, count):
    first, second = term(0), term(1)
    for k in range(2, count, 2):
        first = first + term(k)
        if k + 1 < count:
            second = second + term(k + 1)
    return first + second


def rake_kernel(
    ids_hbm, table_hbm, age_sex_hbm, race_hisp_hbm, size_tenure_hbm, tenure_income_hbm,
    keep_ref, send_ref, age_factor_ref, cross_factor_ref, cells_ref,
    sum_ref, cross_ref, rows_ref, age_target_ref, race_target_ref, size_target_ref,
    ids_ref, age_sex_ref, race_hisp_ref, size_tenure_ref, tenure_income_ref,
    sems, small_sems,
    *, races, sizes, pumas,
):
    tracts, cross, ages, _ = table_hbm.shape
    cross_rows = round_up(cross + 1, 8)
    pairs = (ages + 1) // 2
    small = [
        pltpu.make_async_copy(source, target, small_sems.at[i])
        for i, (source, target) in enumerate((
            (ids_hbm, ids_ref),
            (age_sex_hbm, age_sex_ref),
            (race_hisp_hbm, race_hisp_ref),
            (size_tenure_hbm, size_tenure_ref),
            (tenure_income_hbm, tenure_income_ref),
        ))
    ]

    def table_copy(t):
        return pltpu.make_async_copy(table_hbm.at[t], cells_ref.at[t], sems.at[t])

    for copy in small:
        copy.start()
    for t in range(min(IN_FLIGHT, tracts)):
        table_copy(t).start()
    lane = lane_ids(1)
    sex0 = lane < 64
    hisp0 = (lane // 32) % 2 == 0
    ten0 = (lane // 16) % 2 == 0

    rows_ref[...] = jnp.zeros(rows_ref.shape, F32)
    for copy in small:
        copy.wait()
    for source_ref, target_ref, rows, mask in (
        (age_sex_ref, age_target_ref, ages, sex0),
        (race_hisp_ref, race_target_ref, races, hisp0),
        (size_tenure_ref, size_target_ref, sizes, ten0),
    ):
        for t in range(tracts):
            row = source_ref[t : t + 1, :]
            target_ref[t, 0:rows] = jnp.where(
                mask, column_of(row, rows, 2, 0), column_of(row, rows, 2, 1)
            )

    def group_sums(values, mask):
        first = [masked_lane_sum(x, mask) for x in values]
        second = [masked_lane_sum(x, ~mask) for x in values]
        return [jnp.where(mask, x, y) for x, y in zip(first, second)]

    def arrive(t, carry):
        table_copy(t).wait()

        @pl.when(t + IN_FLIGHT < tracts)
        def _():
            table_copy(t + IN_FLIGHT).start()

        sum_ref[t, 0:ages] = pair_sum(lambda rs: cells_ref[t, rs], cross)
        return carry

    def add_ages(t, carry):
        factor = age_factor_ref[t, 0:ages]
        base = t * cross_rows
        for rs in range(cross):
            cross_ref[pl.ds(base + rs, 1), :] = jnp.sum(
                cells_ref[t, rs] * factor, axis=0, keepdims=True
            )
        return carry

    def add_scaled(t, carry):
        base = t * cross_rows
        total = pair_sum(
            lambda rs: cells_ref[t, rs] * cross_factor_ref[pl.ds(base + rs, 1), :], cross
        )
        sum_ref[t, 0:ages] = total * age_factor_ref[t, 0:ages]
        sum_ref[t, ages : 2 * pairs] = jnp.zeros((2 * pairs - ages, LANES), F32)
        return carry

    def small_steps(group):
        bases = [t * cross_rows for t in group]
        by_race = [
            sum(cross_ref[pl.ds(base + s, races, stride=sizes), :] for s in range(sizes))
            for base in bases
        ]
        race_factor = [
            race_target_ref[t, 0:races] / margin for t, margin in zip(group, group_sums(by_race, hisp0))
        ]
        by_size = [
            sum(
                cross_ref[pl.ds(base + r * sizes, sizes), :] * factor[r : r + 1]
                for r in range(races)
            )
            for base, factor in zip(bases, race_factor)
        ]
        size_factor = [
            size_target_ref[t, 0:sizes] / margin for t, margin in zip(group, group_sums(by_size, ten0))
        ]
        by_income = [jnp.sum(x * y, axis=0, keepdims=True) for x, y in zip(by_size, size_factor)]
        by_income = [x + pltpu.roll(x, 64, 1) for x in by_income]
        by_income = [x + pltpu.roll(x, 32, 1) for x in by_income]
        for i, t in enumerate(group):
            target = jnp.concatenate([tenure_income_ref[t : t + 1, :]] * 4, axis=1)
            age_factor_ref[t, 0:ages] = age_factor_ref[t, 0:ages] * (target / by_income[i])
            for r in range(races):
                cross_factor_ref[pl.ds(bases[i] + r * sizes, sizes), :] = (
                    size_factor[i] * race_factor[i][r : r + 1]
                )
            cross_factor_ref[pl.ds(bases[i] + cross, cross_rows - cross), :] = jnp.zeros(
                (cross_rows - cross, LANES), F32
            )

    def pack(group):
        even = [sum_ref[t, pl.ds(0, pairs, stride=2)] for t in group]
        odd = [sum_ref[t, pl.ds(1, pairs, stride=2)] for t in group]
        even = [x + pltpu.roll(x, 96, 1) for x in even]
        odd = [x + pltpu.roll(x, 96, 1) for x in odd]
        packed = [
            jnp.where(
                lane < 32,
                x,
                jnp.where(
                    lane < 64,
                    pltpu.roll(x, 96, 1),
                    jnp.where(lane < 96, pltpu.roll(y, 64, 1), pltpu.roll(y, 32, 1)),
                ),
            )
            for x, y in zip(even, odd)
        ]
        for t, x in zip(group, packed):
            at = pl.ds(ids_ref[t], pairs, stride=pumas)
            rows_ref[at, :] = rows_ref[at, :] + x

    def work(group):
        margin = group_sums([sum_ref[t, 0:ages] for t in group], sex0)
        for t, x in zip(group, margin):
            age_factor_ref[t, 0:ages] = age_target_ref[t, 0:ages] / x
        lax.fori_loop(group.start, group.stop, add_ages, 0)
        small_steps(group)
        lax.fori_loop(group.start, group.stop, add_scaled, 0)
        pack(group)

    before = None
    for start in range(0, tracts, GROUP):
        if before is not None:
            work(before)
        before = range(start, min(start + GROUP, tracts))
        lax.fori_loop(before.start, before.stop, arrive, 0)
    work(before)
    put_halves(rows_ref, [keep_ref], [send_ref])


def race_margin_kernel(
    ids_ref, cells_ref, age_factor_ref, cross_factor_ref, target_ref,
    own_ref, other_ref, *refs
):
    *chunk_refs, scaled_factor_ref, cross_ref, age_rows_ref, rows_ref, scalar_ref = refs
    chunks = len(chunk_refs) // 2
    keep_refs, send_refs = chunk_refs[:chunks], chunk_refs[chunks:]
    tracts, cross, ages, _ = cells_ref.shape
    cross_rows = round_up(cross + 1, 8)
    pairs, cross_pairs = (ages + 1) // 2, (cross + 1) // 2
    pumas = target_ref.shape[0]
    load_puma_numbers(ids_ref, scalar_ref)
    rows_ref[...] = jnp.zeros(rows_ref.shape, F32)
    factor_rows(target_ref, [own_ref], [other_ref], age_rows_ref)
    lane = lane_ids(1)

    def unpack(t):
        packed = age_rows_ref[pl.ds(scalar_ref[t], pairs, stride=pumas), :]
        half = pltpu.roll(packed, 64, 1)
        even = jnp.where(lane < 32, packed, jnp.where(lane < 96, pltpu.roll(packed, 32, 1), half))
        odd = jnp.where(lane < 32, half, jnp.where(lane < 96, pltpu.roll(packed, 96, 1), packed))
        scaled_factor_ref[t, pl.ds(0, pairs, stride=2)] = even
        scaled_factor_ref[t, pl.ds(1, pairs, stride=2)] = odd

    def add_ages(t):
        factor = scaled_factor_ref[t, 0:ages] * age_factor_ref[t, 0:ages]
        scaled_factor_ref[t, 0:ages] = factor
        base = t * cross_rows
        for rs in range(cross):
            cross_ref[pl.ds(base + rs, 1), :] = jnp.sum(
                cells_ref[t, rs] * factor, axis=0, keepdims=True
            )
        cross_ref[pl.ds(base + cross, cross_rows - cross), :] = jnp.zeros(
            (cross_rows - cross, LANES), F32
        )

    def pack(t):
        halves = []
        for first in range(2):
            at = pl.ds(t * cross_rows + first, cross_pairs, stride=2)
            margin = cross_ref[at, :] * cross_factor_ref[at, :]
            halves.append(margin + pltpu.roll(margin, 64, 1))
        at = pl.ds(scalar_ref[t], cross_pairs, stride=pumas)
        rows_ref[at, :] = rows_ref[at, :] + jnp.where(lane < 64, *halves)

    def step(t, carry):
        pack(t - 1)
        add_ages(t)
        unpack(t + 1)
        return carry

    unpack(0)
    add_ages(0)
    unpack(1)
    lax.fori_loop(1, tracts - 1, step, 0)
    pack(tracts - 2)
    add_ages(tracts - 1)
    pack(tracts - 1)
    put_halves(rows_ref, keep_refs, send_refs)


def final_kernel(
    ids_ref, cells_ref, scaled_factor_ref, cross_factor_ref, target_ref, *refs
):
    *chunk_refs, out_ref, result_ref, cross_ref, rows_ref, scalar_ref, sems = refs
    chunks = len(chunk_refs) // 2
    tracts, cross, ages, _ = cells_ref.shape
    cross_rows = round_up(cross + 1, 8)
    cross_pairs = (cross + 1) // 2
    pumas = target_ref.shape[0]
    load_puma_numbers(ids_ref, scalar_ref)
    factor_rows(target_ref, chunk_refs[:chunks], chunk_refs[chunks:], rows_ref)
    lane = lane_ids(1)

    def unpack(t):
        base = t * cross_rows
        packed = rows_ref[pl.ds(scalar_ref[t], cross_pairs, stride=pumas), :]
        half = pltpu.roll(packed, 64, 1)
        for first, factor in enumerate(
            (jnp.where(lane < 64, packed, half), jnp.where(lane < 64, half, packed))
        ):
            at = pl.ds(base + first, cross_pairs, stride=2)
            cross_ref[at, :] = factor * cross_factor_ref[at, :]

    def scale(t):
        factor = scaled_factor_ref[t, 0:ages]
        base = t * cross_rows
        for rs in range(cross):
            result_ref[t, rs] = cells_ref[t, rs] * factor * cross_ref[pl.ds(base + rs, 1), :]

    def send(t):
        pltpu.make_async_copy(result_ref.at[t], out_ref.at[t], sems.at[t]).start()

    def step(t, carry):
        scale(t)
        unpack(t + 1)
        send(t)
        return carry

    unpack(0)
    lax.fori_loop(0, tracts - 1, step, 0)
    scale(tracts - 1)
    send(tracts - 1)
    for t in range(tracts):
        pltpu.make_async_copy(result_ref.at[t], out_ref.at[t], sems.at[t]).wait()


def call(kernel, out_shapes, in_spaces, out_spaces, scratch):
    def spec(space):
        return pl.BlockSpec(memory_space=space)

    run = pl.pallas_call(
        kernel,
        out_shape=[
            space(shape, F32) for shape, space in zip(out_shapes, out_spaces, strict=True)
        ],
        in_specs=[spec(space) for space in in_spaces],
        out_specs=[spec(space) for space in out_spaces],
        scratch_shapes=scratch,
        compiler_params=pltpu.CompilerParams(vmem_limit_bytes=40 << 20),
    )

    def placed(*args):
        return run(*map(pltpu.with_memory_space_constraint, args, in_spaces))

    return placed


def per_device(
    devices,
    table, age_sex, race_hisp, size_tenure, tenure_income, puma_age, puma_race, tract_puma,
):
    tracts, ages, races, sizes, inner = table.shape
    pumas = puma_age.shape[0]
    cross = races * sizes
    age_pairs, cross_pairs = (ages + 1) // 2, (cross + 1) // 2
    age_rows = 2 * round_up(age_pairs, 8)
    cross_rows = tracts * round_up(cross + 1, 8) + 2 * round_up(cross_pairs, 8) - round_up(cross, 8)
    age_sum_rows, cross_sum_rows = (round_up(x, 8) * pumas for x in (age_pairs, cross_pairs))
    vmem, hbm = pltpu.VMEM, pltpu.HBM

    cells = table.transpose(0, 2, 3, 1, 4).reshape(tracts, cross, ages, inner)
    cells_scratch = pltpu.VMEM((tracts, cross, ages, inner), F32)
    cross_scratch = pltpu.VMEM((cross_rows, LANES), F32)
    copy_sems = pltpu.SemaphoreType.DMA((tracts,))
    numbers_scratch = pltpu.SMEM((tracts,), jnp.int32)

    bits = [1 << k for k in range(1, devices.bit_length() - 1)]
    orders = (bits, bits[1:] + bits[:1])

    def swap(x, partner):
        return lax.ppermute(x, "tract", [(i, partner(i)) for i in range(devices)])

    def totals(keep, send):
        keep = [x + swap(y, lambda i: i ^ 1) for x, y in zip(keep, send)]
        for step in range(len(bits)):
            keep = [x + swap(x, lambda i: i ^ orders[i.bit_count() % 2][step] ^ 1) for x in keep]
        return *keep, *[swap(x, lambda i: i ^ 1) for x in keep]

    age_half, cross_half = -(-age_pairs // 2), -(-cross_pairs // 2)
    cross_chunks = [cross_half - cross_half // 2, cross_half // 2]
    age_shape, cross_shape = (tracts, age_rows, LANES), (cross_rows, LANES)
    small = [age_sex, race_hisp, size_tenure, tenure_income]
    keep, send, age_factor, cross_factor, cells = call(
        functools.partial(rake_kernel, races=races, sizes=sizes, pumas=pumas),
        [(age_half * pumas, LANES)] * 2 + [age_shape, cross_shape, cells.shape],
        [hbm] * 6,
        [vmem] * 5,
        [
            pltpu.VMEM(age_shape, F32),
            cross_scratch,
            pltpu.VMEM((age_sum_rows, LANES), F32),
            pltpu.VMEM(age_shape, F32),
            pltpu.VMEM((tracts, round_up(races, 8), LANES), F32),
            pltpu.VMEM((tracts, round_up(sizes, 8), LANES), F32),
            numbers_scratch,
        ]
        + [pltpu.VMEM(x.shape, F32) for x in small]
        + [copy_sems, pltpu.SemaphoreType.DMA((1 + len(small),))],
    )(tract_puma, cells, *small)

    *chunks, scaled_factor = call(
        race_margin_kernel,
        [(rows * pumas, LANES) for rows in cross_chunks * 2] + [(tracts, age_rows, LANES)],
        [vmem] * 7,
        [vmem] * (2 * len(cross_chunks) + 1),
        [
            cross_scratch,
            pltpu.VMEM((age_sum_rows, LANES), F32),
            pltpu.VMEM((cross_sum_rows, LANES), F32),
            numbers_scratch,
        ],
    )(tract_puma, cells, age_factor, cross_factor, puma_age, *totals([keep], [send]))

    keep, send = chunks[: len(cross_chunks)], chunks[len(cross_chunks) :]
    out, = call(
        final_kernel,
        [(tracts, cross, ages, inner)],
        [vmem] * (5 + 2 * len(cross_chunks)),
        [hbm],
        [
            cells_scratch,
            cross_scratch,
            pltpu.VMEM((cross_sum_rows, LANES), F32),
            numbers_scratch,
            copy_sems,
        ],
    )(tract_puma, cells, scaled_factor, cross_factor, puma_race, *totals(keep, send))
    return out.reshape(tracts, races, sizes, ages, inner).transpose(0, 3, 1, 2, 4)


def solution(mesh):
    in_specs = (
        P(("grp", "tract"), None, None, None, None),
        P(("grp", "tract"), None),
        P(("grp", "tract"), None),
        P(("grp", "tract"), None),
        P(("grp", "tract"), None),
        P("grp", None),
        P("grp", None),
        P(("grp", "tract")),
    )
    out_specs = P(("grp", "tract"), None, None, None, None)
    return jax.shard_map(
        functools.partial(per_device, mesh.shape["tract"]),
        mesh=mesh, in_specs=in_specs, out_specs=out_specs, check_vma=False,
    )
```

```python
import functools

import jax
import jax.numpy as jnp
from jax import lax
from jax.experimental import pallas as pl
from jax.experimental.pallas import tpu as pltpu
from jax.sharding import PartitionSpec as P

LANES = 128
GROUP = 6
IN_FLIGHT = 4
F32 = jnp.float32


def round_up(value, step):
    return -(-value // step) * step


def lane_ids(rows):
    return lax.broadcasted_iota(jnp.int32, (rows, LANES), 1)


def masked_lane_sum(value, mask):
    return jnp.sum(jnp.where(mask, value, 0.0), axis=-1, keepdims=True)


def column_of(row, rows, step, offset):
    width = row.shape[-1]
    lane = lax.broadcasted_iota(jnp.int32, (rows, width), 1)
    sub = lax.broadcasted_iota(jnp.int32, (rows, width), 0)
    return jnp.sum(jnp.where(lane == step * sub + offset, row, 0.0), axis=-1, keepdims=True)


def half_of(index):
    total = index
    for k in range(1, 16):
        total = total + lax.shift_right_logical(index, k)
    return lax.rem(total, 2)


def factor_rows(target_ref, own_refs, other_refs, rows_ref):
    pumas, columns = target_ref.shape
    half = half_of(lax.axis_index("tract"))
    half_rows = sum(ref.shape[0] for ref in own_refs)
    for refs, which in ((own_refs, half), (other_refs, 1 - half)):
        start = which * half_rows
        for ref in refs:
            rows_ref[pl.ds(pl.multiple_of(start, 8), ref.shape[0]), :] = ref[...]
            start = start + ref.shape[0]
    for first in range(0, columns, LANES):
        width = min(columns - first, LANES)
        at = slice(first // LANES * pumas, (first // LANES + 1) * pumas)
        rows_ref[at, 0:width] = target_ref[:, first : first + width] / rows_ref[at, 0:width]


def load_puma_numbers(ids_ref, scalar_ref):
    ids = ids_ref[...]
    for t in range(scalar_ref.shape[0]):
        scalar_ref[t] = ids[t]


def put_halves(rows_ref, keep_refs, send_refs):
    half = half_of(lax.axis_index("tract"))
    half_rows = sum(ref.shape[0] for ref in keep_refs)
    for refs, which in ((keep_refs, half), (send_refs, 1 - half)):
        start = which * half_rows
        for ref in refs:
            ref[...] = rows_ref[pl.ds(pl.multiple_of(start, 8), ref.shape[0]), :]
            start = start + ref.shape[0]


def merge(first, second, step):
    low = lax.rem(lax.broadcasted_iota(jnp.int32, (8, 1), 0) // step, 2) == 0
    if step == 4:
        return jnp.where(low, first, second) + pltpu.roll(jnp.where(low, second, first), 4, 0)
    return jnp.where(low, first + pltpu.roll(first, 8 - step, 0), second + pltpu.roll(second, step, 0))


def age_sums(cells_ref, t, factor, cross_ref, base, cross):
    for start in range(0, cross, 8):
        tiles = []
        for rs in range(start, min(start + 8, cross)):
            parts = [cells_ref[t, rs, k : k + 8] * factor[k : k + 8] for k in range(0, factor.shape[0], 8)]
            tiles.append(sum(parts[1:], parts[0]))
        if len(tiles) < 8:
            for k, tile in enumerate(tiles):
                cross_ref[pl.ds(base + start + k, 1), :] = jnp.sum(tile, axis=0, keepdims=True)
            continue
        tiles = [merge(tiles[k], tiles[k + 4], 4) for k in range(4)]
        tiles = [merge(tiles[k], tiles[k + 2], 2) for k in range(2)]
        cross_ref[pl.ds(pl.multiple_of(base + start, 8), 8), :] = merge(tiles[0], tiles[1], 1)


def pair_sum(term, count):
    first, second = term(0), term(1)
    for k in range(2, count, 2):
        first = first + term(k)
        if k + 1 < count:
            second = second + term(k + 1)
    return first + second


def rake_kernel(
    ids_hbm, table_hbm, age_sex_hbm, race_hisp_hbm, size_tenure_hbm, tenure_income_hbm,
    keep_ref, send_ref, age_factor_ref, cross_factor_ref, cells_ref,
    sum_ref, cross_ref, rows_ref, age_target_ref, race_target_ref, size_target_ref,
    ids_ref, age_sex_ref, race_hisp_ref, size_tenure_ref, tenure_income_ref,
    sems, small_sems,
    *, races, sizes, pumas,
):
    tracts, cross, ages, _ = table_hbm.shape
    full = cells_ref.shape[2]
    cross_rows = round_up(cross + 1, 8)
    pairs = (ages + 1) // 2
    small = [
        pltpu.make_async_copy(source, target, small_sems.at[i])
        for i, (source, target) in enumerate((
            (ids_hbm, ids_ref),
            (age_sex_hbm, age_sex_ref),
            (race_hisp_hbm, race_hisp_ref),
            (size_tenure_hbm, size_tenure_ref),
            (tenure_income_hbm, tenure_income_ref),
        ))
    ]

    def table_copy(t):
        return pltpu.make_async_copy(table_hbm.at[t], cells_ref.at[t, :, 0:ages], sems.at[t])

    for copy in small:
        copy.start()
    for t in range(min(IN_FLIGHT, tracts)):
        table_copy(t).start()
    lane = lane_ids(1)
    sex0 = lane < 64
    hisp0 = (lane // 32) % 2 == 0
    ten0 = (lane // 16) % 2 == 0

    rows_ref[...] = jnp.zeros(rows_ref.shape, F32)
    for t in range(tracts):
        age_factor_ref[t, ages:] = jnp.zeros((age_factor_ref.shape[1] - ages, LANES), F32)
    for copy in small:
        copy.wait()
    for source_ref, target_ref, rows, mask in (
        (age_sex_ref, age_target_ref, ages, sex0),
        (race_hisp_ref, race_target_ref, races, hisp0),
        (size_tenure_ref, size_target_ref, sizes, ten0),
    ):
        for t in range(tracts):
            row = source_ref[t : t + 1, :]
            target_ref[t, 0:rows] = jnp.where(
                mask, column_of(row, rows, 2, 0), column_of(row, rows, 2, 1)
            )

    def group_sums(values, mask):
        first = [masked_lane_sum(x, mask) for x in values]
        second = [masked_lane_sum(x, ~mask) for x in values]
        return [jnp.where(mask, x, y) for x, y in zip(first, second)]

    def arrive(t, carry):
        table_copy(t).wait()

        @pl.when(t + IN_FLIGHT < tracts)
        def _():
            table_copy(t + IN_FLIGHT).start()

        if full > ages:
            for rs in range(cross):
                cells_ref[t, rs, ages:] = jnp.zeros((full - ages, LANES), F32)
        sum_ref[t, 0:full] = pair_sum(lambda rs: cells_ref[t, rs], cross)
        return carry

    def add_ages(t, carry):
        age_sums(cells_ref, t, age_factor_ref[t, 0:full], cross_ref, t * cross_rows, cross)
        return carry

    def add_scaled(t, carry):
        base = t * cross_rows
        total = pair_sum(
            lambda rs: cells_ref[t, rs] * cross_factor_ref[pl.ds(base + rs, 1), :], cross
        )
        sum_ref[t, 0:full] = total * age_factor_ref[t, 0:full]
        return carry

    def small_steps(group):
        bases = [t * cross_rows for t in group]
        by_race = [
            sum(cross_ref[pl.ds(base + s, races, stride=sizes), :] for s in range(sizes))
            for base in bases
        ]
        race_factor = [
            race_target_ref[t, 0:races] / margin for t, margin in zip(group, group_sums(by_race, hisp0))
        ]
        by_size = [
            sum(
                cross_ref[pl.ds(base + r * sizes, sizes), :] * factor[r : r + 1]
                for r in range(races)
            )
            for base, factor in zip(bases, race_factor)
        ]
        size_factor = [
            size_target_ref[t, 0:sizes] / margin for t, margin in zip(group, group_sums(by_size, ten0))
        ]
        by_income = [jnp.sum(x * y, axis=0, keepdims=True) for x, y in zip(by_size, size_factor)]
        by_income = [x + pltpu.roll(x, 64, 1) for x in by_income]
        by_income = [x + pltpu.roll(x, 32, 1) for x in by_income]
        for i, t in enumerate(group):
            target = jnp.concatenate([tenure_income_ref[t : t + 1, :]] * 4, axis=1)
            age_factor_ref[t, 0:ages] = age_factor_ref[t, 0:ages] * (target / by_income[i])
            for r in range(races):
                cross_factor_ref[pl.ds(bases[i] + r * sizes, sizes), :] = (
                    size_factor[i] * race_factor[i][r : r + 1]
                )
            cross_factor_ref[pl.ds(bases[i] + cross, cross_rows - cross), :] = jnp.zeros(
                (cross_rows - cross, LANES), F32
            )

    def pack(group):
        even = [sum_ref[t, pl.ds(0, pairs, stride=2)] for t in group]
        odd = [sum_ref[t, pl.ds(1, pairs, stride=2)] for t in group]
        even = [x + pltpu.roll(x, 96, 1) for x in even]
        odd = [x + pltpu.roll(x, 96, 1) for x in odd]
        packed = [
            jnp.where(
                lane < 32,
                x,
                jnp.where(
                    lane < 64,
                    pltpu.roll(x, 96, 1),
                    jnp.where(lane < 96, pltpu.roll(y, 64, 1), pltpu.roll(y, 32, 1)),
                ),
            )
            for x, y in zip(even, odd)
        ]
        for t, x in zip(group, packed):
            at = pl.ds(ids_ref[t], pairs, stride=pumas)
            rows_ref[at, :] = rows_ref[at, :] + x

    def work(group):
        margin = group_sums([sum_ref[t, 0:ages] for t in group], sex0)
        for t, x in zip(group, margin):
            age_factor_ref[t, 0:ages] = age_target_ref[t, 0:ages] / x
        lax.fori_loop(group.start, group.stop, add_ages, 0)
        small_steps(group)
        lax.fori_loop(group.start, group.stop, add_scaled, 0)
        pack(group)

    before = None
    for start in range(0, tracts, GROUP):
        if before is not None:
            work(before)
        before = range(start, min(start + GROUP, tracts))
        lax.fori_loop(before.start, before.stop, arrive, 0)
    work(before)
    put_halves(rows_ref, [keep_ref], [send_ref])


def race_margin_kernel(
    ids_ref, cells_ref, age_factor_ref, cross_factor_ref, target_ref,
    own_ref, other_ref, *refs, ages
):
    *chunk_refs, scaled_factor_ref, cross_ref, age_rows_ref, rows_ref, scalar_ref = refs
    chunks = len(chunk_refs) // 2
    keep_refs, send_refs = chunk_refs[:chunks], chunk_refs[chunks:]
    tracts, cross, full, _ = cells_ref.shape
    cross_rows = round_up(cross + 1, 8)
    pairs, cross_pairs = (ages + 1) // 2, (cross + 1) // 2
    pumas = target_ref.shape[0]
    load_puma_numbers(ids_ref, scalar_ref)
    rows_ref[...] = jnp.zeros(rows_ref.shape, F32)
    factor_rows(target_ref, [own_ref], [other_ref], age_rows_ref)
    lane = lane_ids(1)

    def unpack(t):
        packed = age_rows_ref[pl.ds(scalar_ref[t], pairs, stride=pumas), :]
        half = pltpu.roll(packed, 64, 1)
        even = jnp.where(lane < 32, packed, jnp.where(lane < 96, pltpu.roll(packed, 32, 1), half))
        odd = jnp.where(lane < 32, half, jnp.where(lane < 96, pltpu.roll(packed, 96, 1), packed))
        scaled_factor_ref[t, pl.ds(0, pairs, stride=2)] = even
        scaled_factor_ref[t, pl.ds(1, pairs, stride=2)] = odd
        if full > ages:
            scaled_factor_ref[t, ages:full] = jnp.zeros((full - ages, LANES), F32)

    def add_ages(t):
        factor = scaled_factor_ref[t, 0:full] * age_factor_ref[t, 0:full]
        scaled_factor_ref[t, 0:full] = factor
        base = t * cross_rows
        age_sums(cells_ref, t, factor, cross_ref, base, cross)
        cross_ref[pl.ds(base + cross, cross_rows - cross), :] = jnp.zeros(
            (cross_rows - cross, LANES), F32
        )

    def pack(t):
        halves = []
        for first in range(2):
            at = pl.ds(t * cross_rows + first, cross_pairs, stride=2)
            margin = cross_ref[at, :] * cross_factor_ref[at, :]
            halves.append(margin + pltpu.roll(margin, 64, 1))
        at = pl.ds(scalar_ref[t], cross_pairs, stride=pumas)
        rows_ref[at, :] = rows_ref[at, :] + jnp.where(lane < 64, *halves)

    def step(t, carry):
        pack(t - 1)
        add_ages(t)
        unpack(t + 1)
        return carry

    unpack(0)
    add_ages(0)
    unpack(1)
    lax.fori_loop(1, tracts - 1, step, 0)
    pack(tracts - 2)
    add_ages(tracts - 1)
    pack(tracts - 1)
    put_halves(rows_ref, keep_refs, send_refs)


def final_kernel(
    ids_ref, cells_ref, scaled_factor_ref, cross_factor_ref, target_ref, *refs
):
    *chunk_refs, out_ref, result_ref, cross_ref, rows_ref, scalar_ref, sems = refs
    chunks = len(chunk_refs) // 2
    tracts, cross, ages, _ = out_ref.shape
    cross_rows = round_up(cross + 1, 8)
    cross_pairs = (cross + 1) // 2
    pumas = target_ref.shape[0]
    load_puma_numbers(ids_ref, scalar_ref)
    factor_rows(target_ref, chunk_refs[:chunks], chunk_refs[chunks:], rows_ref)
    lane = lane_ids(1)

    def unpack(t):
        base = t * cross_rows
        packed = rows_ref[pl.ds(scalar_ref[t], cross_pairs, stride=pumas), :]
        half = pltpu.roll(packed, 64, 1)
        for first, factor in enumerate(
            (jnp.where(lane < 64, packed, half), jnp.where(lane < 64, half, packed))
        ):
            at = pl.ds(base + first, cross_pairs, stride=2)
            cross_ref[at, :] = factor * cross_factor_ref[at, :]

    def scale(t):
        factor = scaled_factor_ref[t, 0:ages]
        base = t * cross_rows
        for rs in range(cross):
            result_ref[t, rs] = cells_ref[t, rs, 0:ages] * factor * cross_ref[pl.ds(base + rs, 1), :]

    def send(t):
        pltpu.make_async_copy(result_ref.at[t], out_ref.at[t], sems.at[t]).start()

    def step(t, carry):
        scale(t)
        unpack(t + 1)
        send(t)
        return carry

    unpack(0)
    lax.fori_loop(0, tracts - 1, step, 0)
    scale(tracts - 1)
    send(tracts - 1)
    for t in range(tracts):
        pltpu.make_async_copy(result_ref.at[t], out_ref.at[t], sems.at[t]).wait()


def call(kernel, out_shapes, in_spaces, out_spaces, scratch):
    def spec(space):
        return pl.BlockSpec(memory_space=space)

    run = pl.pallas_call(
        kernel,
        out_shape=[
            space(shape, F32) for shape, space in zip(out_shapes, out_spaces, strict=True)
        ],
        in_specs=[spec(space) for space in in_spaces],
        out_specs=[spec(space) for space in out_spaces],
        scratch_shapes=scratch,
        compiler_params=pltpu.CompilerParams(vmem_limit_bytes=40 << 20),
    )

    def placed(*args):
        return run(*map(pltpu.with_memory_space_constraint, args, in_spaces))

    return placed


def per_device(
    devices,
    table, age_sex, race_hisp, size_tenure, tenure_income, puma_age, puma_race, tract_puma,
):
    tracts, ages, races, sizes, inner = table.shape
    pumas = puma_age.shape[0]
    cross = races * sizes
    age_pairs, cross_pairs = (ages + 1) // 2, (cross + 1) // 2
    age_rows = 2 * round_up(age_pairs, 8)
    cross_rows = tracts * round_up(cross + 1, 8) + 2 * round_up(cross_pairs, 8) - round_up(cross, 8)
    age_sum_rows, cross_sum_rows = (round_up(x, 8) * pumas for x in (age_pairs, cross_pairs))
    vmem, hbm = pltpu.VMEM, pltpu.HBM

    cells = table.transpose(0, 2, 3, 1, 4).reshape(tracts, cross, ages, inner)
    cells_scratch = pltpu.VMEM((tracts, cross, ages, inner), F32)
    cross_scratch = pltpu.VMEM((cross_rows, LANES), F32)
    copy_sems = pltpu.SemaphoreType.DMA((tracts,))
    numbers_scratch = pltpu.SMEM((tracts,), jnp.int32)

    bits = [1 << k for k in range(1, devices.bit_length() - 1)]
    orders = (bits, bits[1:] + bits[:1])

    def swap(x, partner):
        return lax.ppermute(x, "tract", [(i, partner(i)) for i in range(devices)])

    def totals(keep, send):
        keep = [x + swap(y, lambda i: i ^ 1) for x, y in zip(keep, send)]
        for step in range(len(bits)):
            keep = [x + swap(x, lambda i: i ^ orders[i.bit_count() % 2][step] ^ 1) for x in keep]
        return *keep, *[swap(x, lambda i: i ^ 1) for x in keep]

    age_half, cross_half = -(-age_pairs // 2), -(-cross_pairs // 2)
    cross_chunks = [cross_half - cross_half // 2, cross_half // 2]
    age_shape, cross_shape = (tracts, age_rows, LANES), (cross_rows, LANES)
    small = [age_sex, race_hisp, size_tenure, tenure_income]
    keep, send, age_factor, cross_factor, cells = call(
        functools.partial(rake_kernel, races=races, sizes=sizes, pumas=pumas),
        [(age_half * pumas, LANES)] * 2
        + [age_shape, cross_shape, (tracts, cross, round_up(ages, 8), LANES)],
        [hbm] * 6,
        [vmem] * 5,
        [
            pltpu.VMEM(age_shape, F32),
            cross_scratch,
            pltpu.VMEM((age_sum_rows, LANES), F32),
            pltpu.VMEM(age_shape, F32),
            pltpu.VMEM((tracts, round_up(races, 8), LANES), F32),
            pltpu.VMEM((tracts, round_up(sizes, 8), LANES), F32),
            numbers_scratch,
        ]
        + [pltpu.VMEM(x.shape, F32) for x in small]
        + [copy_sems, pltpu.SemaphoreType.DMA((1 + len(small),))],
    )(tract_puma, cells, *small)

    *chunks, scaled_factor = call(
        functools.partial(race_margin_kernel, ages=ages),
        [(rows * pumas, LANES) for rows in cross_chunks * 2] + [(tracts, age_rows, LANES)],
        [vmem] * 7,
        [vmem] * (2 * len(cross_chunks) + 1),
        [
            cross_scratch,
            pltpu.VMEM((age_sum_rows, LANES), F32),
            pltpu.VMEM((cross_sum_rows, LANES), F32),
            numbers_scratch,
        ],
    )(tract_puma, cells, age_factor, cross_factor, puma_age, *totals([keep], [send]))

    keep, send = chunks[: len(cross_chunks)], chunks[len(cross_chunks) :]
    out, = call(
        final_kernel,
        [(tracts, cross, ages, inner)],
        [vmem] * (5 + 2 * len(cross_chunks)),
        [hbm],
        [
            cells_scratch,
            cross_scratch,
            pltpu.VMEM((cross_sum_rows, LANES), F32),
            numbers_scratch,
            copy_sems,
        ],
    )(tract_puma, cells, scaled_factor, cross_factor, puma_race, *totals(keep, send))
    return out.reshape(tracts, races, sizes, ages, inner).transpose(0, 3, 1, 2, 4)


def solution(mesh):
    in_specs = (
        P(("grp", "tract"), None, None, None, None),
        P(("grp", "tract"), None),
        P(("grp", "tract"), None),
        P(("grp", "tract"), None),
        P(("grp", "tract"), None),
        P("grp", None),
        P("grp", None),
        P(("grp", "tract")),
    )
    out_specs = P(("grp", "tract"), None, None, None, None)
    return jax.shard_map(
        functools.partial(per_device, mesh.shape["tract"]),
        mesh=mesh, in_specs=in_specs, out_specs=out_specs, check_vma=False,
    )
```

```python
import functools

import jax
import jax.numpy as jnp
from jax import lax
from jax.experimental import pallas as pl
from jax.experimental.pallas import tpu as pltpu
from jax.sharding import PartitionSpec as P

LANES = 128
GROUP = 4
IN_FLIGHT = 8
F32 = jnp.float32


def round_up(value, step):
    return -(-value // step) * step


def lane_ids(rows):
    return lax.broadcasted_iota(jnp.int32, (rows, LANES), 1)


def masked_lane_sum(value, mask):
    return jnp.sum(jnp.where(mask, value, 0.0), axis=-1, keepdims=True)


def column_of(row, rows, step, offset):
    width = row.shape[-1]
    lane = lax.broadcasted_iota(jnp.int32, (rows, width), 1)
    sub = lax.broadcasted_iota(jnp.int32, (rows, width), 0)
    return jnp.sum(jnp.where(lane == step * sub + offset, row, 0.0), axis=-1, keepdims=True)


def half_of(index):
    total = index
    for k in range(1, 16):
        total = total + lax.shift_right_logical(index, k)
    return lax.rem(total, 2)


def factor_rows(target_ref, own_refs, other_refs, rows_ref):
    pumas, columns = target_ref.shape
    half = half_of(lax.axis_index("tract"))
    half_rows = sum(ref.shape[0] for ref in own_refs)
    for refs, which in ((own_refs, half), (other_refs, 1 - half)):
        start = which * half_rows
        for ref in refs:
            rows_ref[pl.ds(pl.multiple_of(start, 8), ref.shape[0]), :] = ref[...]
            start = start + ref.shape[0]
    for first in range(0, columns, LANES):
        width = min(columns - first, LANES)
        at = slice(first // LANES * pumas, (first // LANES + 1) * pumas)
        rows_ref[at, 0:width] = target_ref[:, first : first + width] / rows_ref[at, 0:width]


def load_puma_numbers(ids_ref, scalar_ref):
    ids = ids_ref[...]
    for t in range(scalar_ref.shape[0]):
        scalar_ref[t] = ids[t]


def put_halves(rows_ref, keep_refs, send_refs):
    half = half_of(lax.axis_index("tract"))
    half_rows = sum(ref.shape[0] for ref in keep_refs)
    for refs, which in ((keep_refs, half), (send_refs, 1 - half)):
        start = which * half_rows
        for ref in refs:
            ref[...] = rows_ref[pl.ds(pl.multiple_of(start, 8), ref.shape[0]), :]
            start = start + ref.shape[0]


def merge(first, second, step):
    low = lax.rem(lax.broadcasted_iota(jnp.int32, (8, 1), 0) // step, 2) == 0
    if step == 4:
        return jnp.where(low, first, second) + pltpu.roll(jnp.where(low, second, first), 4, 0)
    return jnp.where(low, first + pltpu.roll(first, 8 - step, 0), second + pltpu.roll(second, step, 0))


def age_sums(cells_ref, t, factor, cross_ref, base, cross):
    ages = factor.shape[0]

    def tile(rs):
        total = None
        for k in range(0, ages, 8):
            stop = min(k + 8, ages)
            part = cells_ref[t, rs, k:stop] * factor[k:stop]
            if stop < k + 8:
                part = jnp.concatenate([part, jnp.zeros((k + 8 - stop, LANES), F32)], axis=0)
            total = part if total is None else total + part
        return total

    for start in range(0, cross, 8):
        tiles = [tile(rs) for rs in range(start, min(start + 8, cross))]
        if len(tiles) < 8:
            for k, x in enumerate(tiles):
                cross_ref[pl.ds(base + start + k, 1), :] = jnp.sum(x, axis=0, keepdims=True)
            continue
        tiles = [merge(tiles[k], tiles[k + 4], 4) for k in range(4)]
        tiles = [merge(tiles[k], tiles[k + 2], 2) for k in range(2)]
        cross_ref[pl.ds(pl.multiple_of(base + start, 8), 8), :] = merge(tiles[0], tiles[1], 1)


def pair_sum(term, count):
    first, second = term(0), term(1)
    for k in range(2, count, 2):
        first = first + term(k)
        if k + 1 < count:
            second = second + term(k + 1)
    return first + second


def rake_kernel(
    ids_hbm, table_hbm, age_sex_hbm, race_hisp_hbm, size_tenure_hbm, tenure_income_hbm,
    keep_ref, send_ref, age_factor_ref, cross_factor_ref, cells_ref,
    sum_ref, cross_ref, rows_ref, age_target_ref, race_target_ref, size_target_ref,
    ids_ref, age_sex_ref, race_hisp_ref, size_tenure_ref, tenure_income_ref,
    sems, small_sems,
    *, races, sizes, pumas,
):
    tracts, cross, ages, _ = table_hbm.shape
    cross_rows = round_up(cross + 1, 8)
    pairs = (ages + 1) // 2
    small = [
        pltpu.make_async_copy(source, target, small_sems.at[i])
        for i, (source, target) in enumerate((
            (ids_hbm, ids_ref),
            (age_sex_hbm, age_sex_ref),
            (race_hisp_hbm, race_hisp_ref),
            (size_tenure_hbm, size_tenure_ref),
            (tenure_income_hbm, tenure_income_ref),
        ))
    ]

    def table_copy(t):
        return pltpu.make_async_copy(table_hbm.at[t], cells_ref.at[t], sems.at[t])

    for copy in small:
        copy.start()
    for t in range(min(IN_FLIGHT, tracts)):
        table_copy(t).start()
    lane = lane_ids(1)
    sex0 = lane < 64
    hisp0 = (lane // 32) % 2 == 0
    ten0 = (lane // 16) % 2 == 0

    rows_ref[...] = jnp.zeros(rows_ref.shape, F32)
    for copy in small:
        copy.wait()
    for source_ref, target_ref, rows, mask in (
        (age_sex_ref, age_target_ref, ages, sex0),
        (race_hisp_ref, race_target_ref, races, hisp0),
        (size_tenure_ref, size_target_ref, sizes, ten0),
    ):
        for t in range(tracts):
            row = source_ref[t : t + 1, :]
            target_ref[t, 0:rows] = jnp.where(
                mask, column_of(row, rows, 2, 0), column_of(row, rows, 2, 1)
            )

    def group_sums(values, mask):
        first = [masked_lane_sum(x, mask) for x in values]
        second = [masked_lane_sum(x, ~mask) for x in values]
        return [jnp.where(mask, x, y) for x, y in zip(first, second)]

    def arrive(t, carry):
        table_copy(t).wait()

        @pl.when(t + IN_FLIGHT < tracts)
        def _():
            table_copy(t + IN_FLIGHT).start()

        sum_ref[t, 0:ages] = pair_sum(lambda rs: cells_ref[t, rs], cross)
        return carry

    def add_ages(t, carry):
        age_sums(cells_ref, t, age_factor_ref[t, 0:ages], cross_ref, t * cross_rows, cross)
        return carry

    def add_scaled(t, carry):
        base = t * cross_rows
        total = pair_sum(
            lambda rs: cells_ref[t, rs] * cross_factor_ref[pl.ds(base + rs, 1), :], cross
        )
        sum_ref[t, 0:ages] = total * age_factor_ref[t, 0:ages]
        sum_ref[t, ages : 2 * pairs] = jnp.zeros((2 * pairs - ages, LANES), F32)
        return carry

    def small_steps(group):
        bases = [t * cross_rows for t in group]
        by_race = [
            sum(cross_ref[pl.ds(base + s, races, stride=sizes), :] for s in range(sizes))
            for base in bases
        ]
        race_factor = [
            race_target_ref[t, 0:races] / margin for t, margin in zip(group, group_sums(by_race, hisp0))
        ]
        by_size = [
            sum(
                cross_ref[pl.ds(base + r * sizes, sizes), :] * factor[r : r + 1]
                for r in range(races)
            )
            for base, factor in zip(bases, race_factor)
        ]
        size_factor = [
            size_target_ref[t, 0:sizes] / margin for t, margin in zip(group, group_sums(by_size, ten0))
        ]
        by_income = [jnp.sum(x * y, axis=0, keepdims=True) for x, y in zip(by_size, size_factor)]
        by_income = [x + pltpu.roll(x, 64, 1) for x in by_income]
        by_income = [x + pltpu.roll(x, 32, 1) for x in by_income]
        for i, t in enumerate(group):
            target = jnp.concatenate([tenure_income_ref[t : t + 1, :]] * 4, axis=1)
            age_factor_ref[t, 0:ages] = age_factor_ref[t, 0:ages] * (target / by_income[i])
            for r in range(races):
                cross_factor_ref[pl.ds(bases[i] + r * sizes, sizes), :] = (
                    size_factor[i] * race_factor[i][r : r + 1]
                )
            cross_factor_ref[pl.ds(bases[i] + cross, cross_rows - cross), :] = jnp.zeros(
                (cross_rows - cross, LANES), F32
            )

    def pack(group):
        even = [sum_ref[t, pl.ds(0, pairs, stride=2)] for t in group]
        odd = [sum_ref[t, pl.ds(1, pairs, stride=2)] for t in group]
        even = [x + pltpu.roll(x, 96, 1) for x in even]
        odd = [x + pltpu.roll(x, 96, 1) for x in odd]
        packed = [
            jnp.where(
                lane < 32,
                x,
                jnp.where(
                    lane < 64,
                    pltpu.roll(x, 96, 1),
                    jnp.where(lane < 96, pltpu.roll(y, 64, 1), pltpu.roll(y, 32, 1)),
                ),
            )
            for x, y in zip(even, odd)
        ]
        for t, x in zip(group, packed):
            at = pl.ds(ids_ref[t], pairs, stride=pumas)
            rows_ref[at, :] = rows_ref[at, :] + x

    def work(group):
        margin = group_sums([sum_ref[t, 0:ages] for t in group], sex0)
        for t, x in zip(group, margin):
            age_factor_ref[t, 0:ages] = age_target_ref[t, 0:ages] / x
        lax.fori_loop(group.start, group.stop, add_ages, 0)
        small_steps(group)
        lax.fori_loop(group.start, group.stop, add_scaled, 0)
        pack(group)

    before = None
    for start in range(0, tracts, GROUP):
        if before is not None:
            work(before)
        before = range(start, min(start + GROUP, tracts))
        lax.fori_loop(before.start, before.stop, arrive, 0)
    work(before)
    put_halves(rows_ref, [keep_ref], [send_ref])


def race_margin_kernel(
    ids_ref, cells_ref, age_factor_ref, cross_factor_ref, target_ref,
    own_ref, other_ref, *refs
):
    *chunk_refs, scaled_factor_ref, cross_ref, age_rows_ref, rows_ref, scalar_ref = refs
    chunks = len(chunk_refs) // 2
    keep_refs, send_refs = chunk_refs[:chunks], chunk_refs[chunks:]
    tracts, cross, ages, _ = cells_ref.shape
    cross_rows = round_up(cross + 1, 8)
    pairs, cross_pairs = (ages + 1) // 2, (cross + 1) // 2
    pumas = target_ref.shape[0]
    load_puma_numbers(ids_ref, scalar_ref)
    rows_ref[...] = jnp.zeros(rows_ref.shape, F32)
    factor_rows(target_ref, [own_ref], [other_ref], age_rows_ref)
    lane = lane_ids(1)

    def unpack(t):
        packed = age_rows_ref[pl.ds(scalar_ref[t], pairs, stride=pumas), :]
        half = pltpu.roll(packed, 64, 1)
        even = jnp.where(lane < 32, packed, jnp.where(lane < 96, pltpu.roll(packed, 32, 1), half))
        odd = jnp.where(lane < 32, half, jnp.where(lane < 96, pltpu.roll(packed, 96, 1), packed))
        scaled_factor_ref[t, pl.ds(0, pairs, stride=2)] = even
        scaled_factor_ref[t, pl.ds(1, pairs, stride=2)] = odd

    def add_ages(t):
        factor = scaled_factor_ref[t, 0:ages] * age_factor_ref[t, 0:ages]
        scaled_factor_ref[t, 0:ages] = factor
        base = t * cross_rows
        age_sums(cells_ref, t, factor, cross_ref, base, cross)
        cross_ref[pl.ds(base + cross, cross_rows - cross), :] = jnp.zeros(
            (cross_rows - cross, LANES), F32
        )

    def pack(t):
        halves = []
        for first in range(2):
            at = pl.ds(t * cross_rows + first, cross_pairs, stride=2)
            margin = cross_ref[at, :] * cross_factor_ref[at, :]
            halves.append(margin + pltpu.roll(margin, 64, 1))
        at = pl.ds(scalar_ref[t], cross_pairs, stride=pumas)
        rows_ref[at, :] = rows_ref[at, :] + jnp.where(lane < 64, *halves)

    def step(t, carry):
        pack(t - 1)
        add_ages(t)
        unpack(t + 1)
        return carry

    unpack(0)
    add_ages(0)
    unpack(1)
    lax.fori_loop(1, tracts - 1, step, 0)
    pack(tracts - 2)
    add_ages(tracts - 1)
    pack(tracts - 1)
    put_halves(rows_ref, keep_refs, send_refs)


def final_kernel(
    ids_ref, cells_ref, scaled_factor_ref, cross_factor_ref, target_ref, *refs
):
    *chunk_refs, out_ref, result_ref, cross_ref, rows_ref, scalar_ref, sems = refs
    chunks = len(chunk_refs) // 2
    tracts, cross, ages, _ = cells_ref.shape
    cross_rows = round_up(cross + 1, 8)
    cross_pairs = (cross + 1) // 2
    pumas = target_ref.shape[0]
    load_puma_numbers(ids_ref, scalar_ref)
    factor_rows(target_ref, chunk_refs[:chunks], chunk_refs[chunks:], rows_ref)
    lane = lane_ids(1)

    def unpack(t):
        base = t * cross_rows
        packed = rows_ref[pl.ds(scalar_ref[t], cross_pairs, stride=pumas), :]
        half = pltpu.roll(packed, 64, 1)
        for first, factor in enumerate(
            (jnp.where(lane < 64, packed, half), jnp.where(lane < 64, half, packed))
        ):
            at = pl.ds(base + first, cross_pairs, stride=2)
            cross_ref[at, :] = factor * cross_factor_ref[at, :]

    def scale(t):
        factor = scaled_factor_ref[t, 0:ages]
        base = t * cross_rows
        for rs in range(cross):
            result_ref[t, rs] = cells_ref[t, rs] * factor * cross_ref[pl.ds(base + rs, 1), :]

    def send(t):
        pltpu.make_async_copy(result_ref.at[t], out_ref.at[t], sems.at[t]).start()

    def step(t, carry):
        scale(t)
        unpack(t + 1)
        send(t)
        return carry

    unpack(0)
    lax.fori_loop(0, tracts - 1, step, 0)
    scale(tracts - 1)
    send(tracts - 1)
    for t in range(tracts):
        pltpu.make_async_copy(result_ref.at[t], out_ref.at[t], sems.at[t]).wait()


def call(kernel, out_shapes, in_spaces, out_spaces, scratch):
    def spec(space):
        return pl.BlockSpec(memory_space=space)

    run = pl.pallas_call(
        kernel,
        out_shape=[
            space(shape, F32) for shape, space in zip(out_shapes, out_spaces, strict=True)
        ],
        in_specs=[spec(space) for space in in_spaces],
        out_specs=[spec(space) for space in out_spaces],
        scratch_shapes=scratch,
        compiler_params=pltpu.CompilerParams(vmem_limit_bytes=40 << 20),
    )

    def placed(*args):
        return run(*map(pltpu.with_memory_space_constraint, args, in_spaces))

    return placed


def per_device(
    devices,
    table, age_sex, race_hisp, size_tenure, tenure_income, puma_age, puma_race, tract_puma,
):
    tracts, ages, races, sizes, inner = table.shape
    pumas = puma_age.shape[0]
    cross = races * sizes
    age_pairs, cross_pairs = (ages + 1) // 2, (cross + 1) // 2
    age_rows = 2 * round_up(age_pairs, 8)
    cross_rows = tracts * round_up(cross + 1, 8) + 2 * round_up(cross_pairs, 8) - round_up(cross, 8)
    age_sum_rows, cross_sum_rows = (round_up(x, 8) * pumas for x in (age_pairs, cross_pairs))
    vmem, hbm = pltpu.VMEM, pltpu.HBM

    cells = table.transpose(0, 2, 3, 1, 4).reshape(tracts, cross, ages, inner)
    cells_scratch = pltpu.VMEM((tracts, cross, ages, inner), F32)
    cross_scratch = pltpu.VMEM((cross_rows, LANES), F32)
    copy_sems = pltpu.SemaphoreType.DMA((tracts,))
    numbers_scratch = pltpu.SMEM((tracts,), jnp.int32)

    bits = [1 << k for k in range(1, devices.bit_length() - 1)]
    orders = (bits, bits[1:] + bits[:1])

    def swap(x, partner):
        return lax.ppermute(x, "tract", [(i, partner(i)) for i in range(devices)])

    def totals(keep, send):
        keep = [x + swap(y, lambda i: i ^ 1) for x, y in zip(keep, send)]
        for step in range(len(bits)):
            keep = [x + swap(x, lambda i: i ^ orders[i.bit_count() % 2][step] ^ 1) for x in keep]
        return *keep, *[swap(x, lambda i: i ^ 1) for x in keep]

    age_half, cross_half = -(-age_pairs // 2), -(-cross_pairs // 2)
    cross_chunks = [cross_half - cross_half // 2, cross_half // 2]
    age_shape, cross_shape = (tracts, age_rows, LANES), (cross_rows, LANES)
    small = [age_sex, race_hisp, size_tenure, tenure_income]
    keep, send, age_factor, cross_factor, cells = call(
        functools.partial(rake_kernel, races=races, sizes=sizes, pumas=pumas),
        [(age_half * pumas, LANES)] * 2 + [age_shape, cross_shape, cells.shape],
        [hbm] * 6,
        [vmem] * 5,
        [
            pltpu.VMEM(age_shape, F32),
            cross_scratch,
            pltpu.VMEM((age_sum_rows, LANES), F32),
            pltpu.VMEM(age_shape, F32),
            pltpu.VMEM((tracts, round_up(races, 8), LANES), F32),
            pltpu.VMEM((tracts, round_up(sizes, 8), LANES), F32),
            numbers_scratch,
        ]
        + [pltpu.VMEM(x.shape, F32) for x in small]
        + [copy_sems, pltpu.SemaphoreType.DMA((1 + len(small),))],
    )(tract_puma, cells, *small)

    *chunks, scaled_factor = call(
        race_margin_kernel,
        [(rows * pumas, LANES) for rows in cross_chunks * 2] + [(tracts, age_rows, LANES)],
        [vmem] * 7,
        [vmem] * (2 * len(cross_chunks) + 1),
        [
            cross_scratch,
            pltpu.VMEM((age_sum_rows, LANES), F32),
            pltpu.VMEM((cross_sum_rows, LANES), F32),
            numbers_scratch,
        ],
    )(tract_puma, cells, age_factor, cross_factor, puma_age, *totals([keep], [send]))

    keep, send = chunks[: len(cross_chunks)], chunks[len(cross_chunks) :]
    out, = call(
        final_kernel,
        [(tracts, cross, ages, inner)],
        [vmem] * (5 + 2 * len(cross_chunks)),
        [hbm],
        [
            cells_scratch,
            cross_scratch,
            pltpu.VMEM((cross_sum_rows, LANES), F32),
            numbers_scratch,
            copy_sems,
        ],
    )(tract_puma, cells, scaled_factor, cross_factor, puma_race, *totals(keep, send))
    return out.reshape(tracts, races, sizes, ages, inner).transpose(0, 3, 1, 2, 4)


def solution(mesh):
    in_specs = (
        P(("grp", "tract"), None, None, None, None),
        P(("grp", "tract"), None),
        P(("grp", "tract"), None),
        P(("grp", "tract"), None),
        P(("grp", "tract"), None),
        P("grp", None),
        P("grp", None),
        P(("grp", "tract")),
    )
    out_specs = P(("grp", "tract"), None, None, None, None)
    return jax.shard_map(
        functools.partial(per_device, mesh.shape["tract"]),
        mesh=mesh, in_specs=in_specs, out_specs=out_specs, check_vma=False,
    )
```

```python
import functools

import jax
import jax.numpy as jnp
from jax import lax
from jax.experimental import pallas as pl
from jax.experimental.pallas import tpu as pltpu
from jax.sharding import PartitionSpec as P

LANES = 128
GROUP = 4
IN_FLIGHT = 4
F32 = jnp.float32


def round_up(value, step):
    return -(-value // step) * step


def lane_ids(rows):
    return lax.broadcasted_iota(jnp.int32, (rows, LANES), 1)


def masked_lane_sum(value, mask):
    return jnp.sum(jnp.where(mask, value, 0.0), axis=-1, keepdims=True)


def column_of(row, rows, step, offset):
    width = row.shape[-1]
    lane = lax.broadcasted_iota(jnp.int32, (rows, width), 1)
    sub = lax.broadcasted_iota(jnp.int32, (rows, width), 0)
    return jnp.sum(jnp.where(lane == step * sub + offset, row, 0.0), axis=-1, keepdims=True)


def half_of(index):
    total = index
    for k in range(1, 16):
        total = total + lax.shift_right_logical(index, k)
    return lax.rem(total, 2)


def factor_rows(target_ref, own_refs, other_refs, rows_ref):
    pumas, columns = target_ref.shape
    half = half_of(lax.axis_index("tract"))
    half_rows = sum(ref.shape[0] for ref in own_refs)
    for refs, which in ((own_refs, half), (other_refs, 1 - half)):
        start = which * half_rows
        for ref in refs:
            rows_ref[pl.ds(pl.multiple_of(start, 8), ref.shape[0]), :] = ref[...]
            start = start + ref.shape[0]
    for first in range(0, columns, LANES):
        width = min(columns - first, LANES)
        at = slice(first // LANES * pumas, (first // LANES + 1) * pumas)
        rows_ref[at, 0:width] = target_ref[:, first : first + width] / rows_ref[at, 0:width]


def load_puma_numbers(ids_ref, scalar_ref):
    ids = ids_ref[...]
    for t in range(scalar_ref.shape[0]):
        scalar_ref[t] = ids[t]


def put_halves(rows_ref, keep_refs, send_refs):
    half = half_of(lax.axis_index("tract"))
    half_rows = sum(ref.shape[0] for ref in keep_refs)
    for refs, which in ((keep_refs, half), (send_refs, 1 - half)):
        start = which * half_rows
        for ref in refs:
            ref[...] = rows_ref[pl.ds(pl.multiple_of(start, 8), ref.shape[0]), :]
            start = start + ref.shape[0]


def merge(first, second, step):
    low = lax.rem(lax.broadcasted_iota(jnp.int32, (8, 1), 0) // step, 2) == 0
    if step == 4:
        return jnp.where(low, first, second) + pltpu.roll(jnp.where(low, second, first), 4, 0)
    return jnp.where(low, first + pltpu.roll(first, 8 - step, 0), second + pltpu.roll(second, step, 0))


def age_sums(cells_ref, t, factor, cross_ref, base, cross):
    ages = factor.shape[0]

    def tile(rs):
        total = None
        for k in range(0, ages, 8):
            stop = min(k + 8, ages)
            part = cells_ref[t, rs, k:stop] * factor[k:stop]
            if stop < k + 8:
                part = jnp.concatenate([part, jnp.zeros((k + 8 - stop, LANES), F32)], axis=0)
            total = part if total is None else total + part
        return total

    for start in range(0, cross, 8):
        tiles = [tile(rs) for rs in range(start, min(start + 8, cross))]
        if len(tiles) < 8:
            for k, x in enumerate(tiles):
                cross_ref[pl.ds(base + start + k, 1), :] = jnp.sum(x, axis=0, keepdims=True)
            continue
        tiles = [merge(tiles[k], tiles[k + 4], 4) for k in range(4)]
        tiles = [merge(tiles[k], tiles[k + 2], 2) for k in range(2)]
        cross_ref[pl.ds(pl.multiple_of(base + start, 8), 8), :] = merge(tiles[0], tiles[1], 1)


def pair_sum(term, count):
    first, second = term(0), term(1)
    for k in range(2, count, 2):
        first = first + term(k)
        if k + 1 < count:
            second = second + term(k + 1)
    return first + second


def rake_kernel(
    ids_hbm, table_hbm, age_sex_hbm, race_hisp_hbm, size_tenure_hbm, tenure_income_hbm,
    keep_ref, send_ref, age_factor_ref, cross_factor_ref, cells_ref,
    sum_ref, cross_ref, rows_ref, age_target_ref, race_target_ref, size_target_ref,
    ids_ref, age_sex_ref, race_hisp_ref, size_tenure_ref, tenure_income_ref,
    sems, small_sems,
    *, races, sizes, pumas,
):
    tracts, cross, ages, _ = table_hbm.shape
    cross_rows = round_up(cross + 1, 8)
    pairs = (ages + 1) // 2
    small = [
        pltpu.make_async_copy(source, target, small_sems.at[i])
        for i, (source, target) in enumerate((
            (ids_hbm, ids_ref),
            (age_sex_hbm, age_sex_ref),
            (race_hisp_hbm, race_hisp_ref),
            (size_tenure_hbm, size_tenure_ref),
            (tenure_income_hbm, tenure_income_ref),
        ))
    ]

    def table_copy(t):
        return pltpu.make_async_copy(table_hbm.at[t], cells_ref.at[t], sems.at[t])

    for copy in small:
        copy.start()
    for t in range(min(IN_FLIGHT, tracts)):
        table_copy(t).start()
    lane = lane_ids(1)
    sex0 = lane < 64
    hisp0 = (lane // 32) % 2 == 0
    ten0 = (lane // 16) % 2 == 0

    rows_ref[...] = jnp.zeros(rows_ref.shape, F32)
    for copy in small:
        copy.wait()
    for source_ref, target_ref, rows, mask in (
        (age_sex_ref, age_target_ref, ages, sex0),
        (race_hisp_ref, race_target_ref, races, hisp0),
        (size_tenure_ref, size_target_ref, sizes, ten0),
    ):
        for t in range(tracts):
            row = source_ref[t : t + 1, :]
            target_ref[t, 0:rows] = jnp.where(
                mask, column_of(row, rows, 2, 0), column_of(row, rows, 2, 1)
            )

    def group_sums(values, mask):
        first = [masked_lane_sum(x, mask) for x in values]
        second = [masked_lane_sum(x, ~mask) for x in values]
        return [jnp.where(mask, x, y) for x, y in zip(first, second)]

    def arrive(t, carry):
        table_copy(t).wait()

        @pl.when(t + IN_FLIGHT < tracts)
        def _():
            table_copy(t + IN_FLIGHT).start()

        sum_ref[t, 0:ages] = pair_sum(lambda rs: cells_ref[t, rs], cross)
        return carry

    def add_ages(t, carry):
        age_sums(cells_ref, t, age_factor_ref[t, 0:ages], cross_ref, t * cross_rows, cross)
        return carry

    def add_scaled(t, carry):
        base = t * cross_rows
        total = pair_sum(
            lambda rs: cells_ref[t, rs] * cross_factor_ref[pl.ds(base + rs, 1), :], cross
        )
        sum_ref[t, 0:ages] = total * age_factor_ref[t, 0:ages]
        sum_ref[t, ages : 2 * pairs] = jnp.zeros((2 * pairs - ages, LANES), F32)
        return carry

    def small_steps(group):
        bases = [t * cross_rows for t in group]
        by_race = [
            sum(cross_ref[pl.ds(base + s, races, stride=sizes), :] for s in range(sizes))
            for base in bases
        ]
        race_factor = [
            race_target_ref[t, 0:races] / margin for t, margin in zip(group, group_sums(by_race, hisp0))
        ]
        by_size = [
            sum(
                cross_ref[pl.ds(base + r * sizes, sizes), :] * factor[r : r + 1]
                for r in range(races)
            )
            for base, factor in zip(bases, race_factor)
        ]
        size_factor = [
            size_target_ref[t, 0:sizes] / margin for t, margin in zip(group, group_sums(by_size, ten0))
        ]
        by_income = [jnp.sum(x * y, axis=0, keepdims=True) for x, y in zip(by_size, size_factor)]
        by_income = [x + pltpu.roll(x, 64, 1) for x in by_income]
        by_income = [x + pltpu.roll(x, 32, 1) for x in by_income]
        for i, t in enumerate(group):
            target = jnp.concatenate([tenure_income_ref[t : t + 1, :]] * 4, axis=1)
            age_factor_ref[t, 0:ages] = age_factor_ref[t, 0:ages] * (target / by_income[i])
            for r in range(races):
                cross_factor_ref[pl.ds(bases[i] + r * sizes, sizes), :] = (
                    size_factor[i] * race_factor[i][r : r + 1]
                )
            cross_factor_ref[pl.ds(bases[i] + cross, cross_rows - cross), :] = jnp.zeros(
                (cross_rows - cross, LANES), F32
            )

    def pack(group):
        even = [sum_ref[t, pl.ds(0, pairs, stride=2)] for t in group]
        odd = [sum_ref[t, pl.ds(1, pairs, stride=2)] for t in group]
        even = [x + pltpu.roll(x, 96, 1) for x in even]
        odd = [x + pltpu.roll(x, 96, 1) for x in odd]
        packed = [
            jnp.where(
                lane < 32,
                x,
                jnp.where(
                    lane < 64,
                    pltpu.roll(x, 96, 1),
                    jnp.where(lane < 96, pltpu.roll(y, 64, 1), pltpu.roll(y, 32, 1)),
                ),
            )
            for x, y in zip(even, odd)
        ]
        for t, x in zip(group, packed):
            at = pl.ds(ids_ref[t], pairs, stride=pumas)
            rows_ref[at, :] = rows_ref[at, :] + x

    def work(group):
        margin = group_sums([sum_ref[t, 0:ages] for t in group], sex0)
        for t, x in zip(group, margin):
            age_factor_ref[t, 0:ages] = age_target_ref[t, 0:ages] / x
        lax.fori_loop(group.start, group.stop, add_ages, 0)

    before = None
    for start in range(0, tracts, GROUP):
        if before is not None:
            work(before)
        before = range(start, min(start + GROUP, tracts))
        lax.fori_loop(before.start, before.stop, arrive, 0)
    work(before)
    small_steps(range(tracts))
    lax.fori_loop(0, tracts, add_scaled, 0)
    pack(range(tracts))
    put_halves(rows_ref, [keep_ref], [send_ref])


def race_margin_kernel(
    ids_ref, cells_ref, age_factor_ref, cross_factor_ref, target_ref,
    own_ref, other_ref, *refs
):
    *chunk_refs, scaled_factor_ref, cross_ref, age_rows_ref, rows_ref, scalar_ref = refs
    chunks = len(chunk_refs) // 2
    keep_refs, send_refs = chunk_refs[:chunks], chunk_refs[chunks:]
    tracts, cross, ages, _ = cells_ref.shape
    cross_rows = round_up(cross + 1, 8)
    pairs, cross_pairs = (ages + 1) // 2, (cross + 1) // 2
    pumas = target_ref.shape[0]
    load_puma_numbers(ids_ref, scalar_ref)
    rows_ref[...] = jnp.zeros(rows_ref.shape, F32)
    factor_rows(target_ref, [own_ref], [other_ref], age_rows_ref)
    lane = lane_ids(1)

    def unpack(t):
        packed = age_rows_ref[pl.ds(scalar_ref[t], pairs, stride=pumas), :]
        half = pltpu.roll(packed, 64, 1)
        even = jnp.where(lane < 32, packed, jnp.where(lane < 96, pltpu.roll(packed, 32, 1), half))
        odd = jnp.where(lane < 32, half, jnp.where(lane < 96, pltpu.roll(packed, 96, 1), packed))
        scaled_factor_ref[t, pl.ds(0, pairs, stride=2)] = even
        scaled_factor_ref[t, pl.ds(1, pairs, stride=2)] = odd

    def add_ages(t):
        factor = scaled_factor_ref[t, 0:ages] * age_factor_ref[t, 0:ages]
        scaled_factor_ref[t, 0:ages] = factor
        base = t * cross_rows
        age_sums(cells_ref, t, factor, cross_ref, base, cross)
        cross_ref[pl.ds(base + cross, cross_rows - cross), :] = jnp.zeros(
            (cross_rows - cross, LANES), F32
        )

    def pack(t):
        halves = []
        for first in range(2):
            at = pl.ds(t * cross_rows + first, cross_pairs, stride=2)
            margin = cross_ref[at, :] * cross_factor_ref[at, :]
            halves.append(margin + pltpu.roll(margin, 64, 1))
        at = pl.ds(scalar_ref[t], cross_pairs, stride=pumas)
        rows_ref[at, :] = rows_ref[at, :] + jnp.where(lane < 64, *halves)

    def step(t, carry):
        pack(t - 1)
        add_ages(t)
        unpack(t + 1)
        return carry

    unpack(0)
    add_ages(0)
    unpack(1)
    lax.fori_loop(1, tracts - 1, step, 0)
    pack(tracts - 2)
    add_ages(tracts - 1)
    pack(tracts - 1)
    put_halves(rows_ref, keep_refs, send_refs)


def final_kernel(
    ids_ref, cells_ref, scaled_factor_ref, cross_factor_ref, target_ref, *refs
):
    *chunk_refs, out_ref, result_ref, cross_ref, rows_ref, scalar_ref, sems = refs
    chunks = len(chunk_refs) // 2
    tracts, cross, ages, _ = cells_ref.shape
    cross_rows = round_up(cross + 1, 8)
    cross_pairs = (cross + 1) // 2
    pumas = target_ref.shape[0]
    load_puma_numbers(ids_ref, scalar_ref)
    factor_rows(target_ref, chunk_refs[:chunks], chunk_refs[chunks:], rows_ref)
    lane = lane_ids(1)

    def unpack(t):
        base = t * cross_rows
        packed = rows_ref[pl.ds(scalar_ref[t], cross_pairs, stride=pumas), :]
        half = pltpu.roll(packed, 64, 1)
        for first, factor in enumerate(
            (jnp.where(lane < 64, packed, half), jnp.where(lane < 64, half, packed))
        ):
            at = pl.ds(base + first, cross_pairs, stride=2)
            cross_ref[at, :] = factor * cross_factor_ref[at, :]

    def scale(t):
        factor = scaled_factor_ref[t, 0:ages]
        base = t * cross_rows
        for rs in range(cross):
            result_ref[t, rs] = cells_ref[t, rs] * factor * cross_ref[pl.ds(base + rs, 1), :]

    def send(t):
        pltpu.make_async_copy(result_ref.at[t], out_ref.at[t], sems.at[t]).start()

    def step(t, carry):
        scale(t)
        unpack(t + 1)
        send(t)
        return carry

    unpack(0)
    lax.fori_loop(0, tracts - 1, step, 0)
    scale(tracts - 1)
    send(tracts - 1)
    for t in range(tracts):
        pltpu.make_async_copy(result_ref.at[t], out_ref.at[t], sems.at[t]).wait()


def call(kernel, out_shapes, in_spaces, out_spaces, scratch):
    def spec(space):
        return pl.BlockSpec(memory_space=space)

    run = pl.pallas_call(
        kernel,
        out_shape=[
            space(shape, F32) for shape, space in zip(out_shapes, out_spaces, strict=True)
        ],
        in_specs=[spec(space) for space in in_spaces],
        out_specs=[spec(space) for space in out_spaces],
        scratch_shapes=scratch,
        compiler_params=pltpu.CompilerParams(vmem_limit_bytes=40 << 20),
    )

    def placed(*args):
        return run(*map(pltpu.with_memory_space_constraint, args, in_spaces))

    return placed


def per_device(
    devices,
    table, age_sex, race_hisp, size_tenure, tenure_income, puma_age, puma_race, tract_puma,
):
    tracts, ages, races, sizes, inner = table.shape
    pumas = puma_age.shape[0]
    cross = races * sizes
    age_pairs, cross_pairs = (ages + 1) // 2, (cross + 1) // 2
    age_rows = 2 * round_up(age_pairs, 8)
    cross_rows = tracts * round_up(cross + 1, 8) + 2 * round_up(cross_pairs, 8) - round_up(cross, 8)
    age_sum_rows, cross_sum_rows = (round_up(x, 8) * pumas for x in (age_pairs, cross_pairs))
    vmem, hbm = pltpu.VMEM, pltpu.HBM

    cells = table.transpose(0, 2, 3, 1, 4).reshape(tracts, cross, ages, inner)
    cells_scratch = pltpu.VMEM((tracts, cross, ages, inner), F32)
    cross_scratch = pltpu.VMEM((cross_rows, LANES), F32)
    copy_sems = pltpu.SemaphoreType.DMA((tracts,))
    numbers_scratch = pltpu.SMEM((tracts,), jnp.int32)

    bits = [1 << k for k in range(1, devices.bit_length() - 1)]
    orders = (bits, bits[1:] + bits[:1])

    def swap(x, partner):
        return lax.ppermute(x, "tract", [(i, partner(i)) for i in range(devices)])

    def totals(keep, send):
        keep = [x + swap(y, lambda i: i ^ 1) for x, y in zip(keep, send)]
        for step in range(len(bits)):
            keep = [x + swap(x, lambda i: i ^ orders[i.bit_count() % 2][step] ^ 1) for x in keep]
        return *keep, *[swap(x, lambda i: i ^ 1) for x in keep]

    age_half, cross_half = -(-age_pairs // 2), -(-cross_pairs // 2)
    cross_chunks = [cross_half - cross_half // 2, cross_half // 2]
    age_shape, cross_shape = (tracts, age_rows, LANES), (cross_rows, LANES)
    small = [age_sex, race_hisp, size_tenure, tenure_income]
    keep, send, age_factor, cross_factor, cells = call(
        functools.partial(rake_kernel, races=races, sizes=sizes, pumas=pumas),
        [(age_half * pumas, LANES)] * 2 + [age_shape, cross_shape, cells.shape],
        [hbm] * 6,
        [vmem] * 5,
        [
            pltpu.VMEM(age_shape, F32),
            cross_scratch,
            pltpu.VMEM((age_sum_rows, LANES), F32),
            pltpu.VMEM(age_shape, F32),
            pltpu.VMEM((tracts, round_up(races, 8), LANES), F32),
            pltpu.VMEM((tracts, round_up(sizes, 8), LANES), F32),
            numbers_scratch,
        ]
        + [pltpu.VMEM(x.shape, F32) for x in small]
        + [copy_sems, pltpu.SemaphoreType.DMA((1 + len(small),))],
    )(tract_puma, cells, *small)

    *chunks, scaled_factor = call(
        race_margin_kernel,
        [(rows * pumas, LANES) for rows in cross_chunks * 2] + [(tracts, age_rows, LANES)],
        [vmem] * 7,
        [vmem] * (2 * len(cross_chunks) + 1),
        [
            cross_scratch,
            pltpu.VMEM((age_sum_rows, LANES), F32),
            pltpu.VMEM((cross_sum_rows, LANES), F32),
            numbers_scratch,
        ],
    )(tract_puma, cells, age_factor, cross_factor, puma_age, *totals([keep], [send]))

    keep, send = chunks[: len(cross_chunks)], chunks[len(cross_chunks) :]
    out, = call(
        final_kernel,
        [(tracts, cross, ages, inner)],
        [vmem] * (5 + 2 * len(cross_chunks)),
        [hbm],
        [
            cells_scratch,
            cross_scratch,
            pltpu.VMEM((cross_sum_rows, LANES), F32),
            numbers_scratch,
            copy_sems,
        ],
    )(tract_puma, cells, scaled_factor, cross_factor, puma_race, *totals(keep, send))
    return out.reshape(tracts, races, sizes, ages, inner).transpose(0, 3, 1, 2, 4)


def solution(mesh):
    in_specs = (
        P(("grp", "tract"), None, None, None, None),
        P(("grp", "tract"), None),
        P(("grp", "tract"), None),
        P(("grp", "tract"), None),
        P(("grp", "tract"), None),
        P("grp", None),
        P("grp", None),
        P(("grp", "tract")),
    )
    out_specs = P(("grp", "tract"), None, None, None, None)
    return jax.shard_map(
        functools.partial(per_device, mesh.shape["tract"]),
        mesh=mesh, in_specs=in_specs, out_specs=out_specs, check_vma=False,
    )
```

```python
import functools

import jax
import jax.numpy as jnp
from jax import lax
from jax.experimental import pallas as pl
from jax.experimental.pallas import tpu as pltpu
from jax.sharding import PartitionSpec as P

LANES = 128
GROUP = 6
IN_FLIGHT = 6
F32 = jnp.float32


def round_up(value, step):
    return -(-value // step) * step


def lane_ids(rows):
    return lax.broadcasted_iota(jnp.int32, (rows, LANES), 1)


def masked_lane_sum(value, mask):
    return jnp.sum(jnp.where(mask, value, 0.0), axis=-1, keepdims=True)


def column_of(row, rows, step, offset):
    width = row.shape[-1]
    lane = lax.broadcasted_iota(jnp.int32, (rows, width), 1)
    sub = lax.broadcasted_iota(jnp.int32, (rows, width), 0)
    return jnp.sum(jnp.where(lane == step * sub + offset, row, 0.0), axis=-1, keepdims=True)


def half_of(index):
    total = index
    for k in range(1, 16):
        total = total + lax.shift_right_logical(index, k)
    return lax.rem(total, 2)


def factor_rows(target_ref, own_refs, other_refs, rows_ref):
    pumas, columns = target_ref.shape
    half = half_of(lax.axis_index("tract"))
    half_rows = sum(ref.shape[0] for ref in own_refs)
    for refs, which in ((own_refs, half), (other_refs, 1 - half)):
        start = which * half_rows
        for ref in refs:
            rows_ref[pl.ds(pl.multiple_of(start, 8), ref.shape[0]), :] = ref[...]
            start = start + ref.shape[0]
    for first in range(0, columns, LANES):
        width = min(columns - first, LANES)
        at = slice(first // LANES * pumas, (first // LANES + 1) * pumas)
        rows_ref[at, 0:width] = target_ref[:, first : first + width] / rows_ref[at, 0:width]


def load_puma_numbers(ids_ref, scalar_ref):
    ids = ids_ref[...]
    for t in range(scalar_ref.shape[0]):
        scalar_ref[t] = ids[t]


def put_halves(rows_ref, keep_refs, send_refs):
    half = half_of(lax.axis_index("tract"))
    half_rows = sum(ref.shape[0] for ref in keep_refs)
    for refs, which in ((keep_refs, half), (send_refs, 1 - half)):
        start = which * half_rows
        for ref in refs:
            ref[...] = rows_ref[pl.ds(pl.multiple_of(start, 8), ref.shape[0]), :]
            start = start + ref.shape[0]


def merge(first, second, step):
    low = lax.rem(lax.broadcasted_iota(jnp.int32, (8, 1), 0) // step, 2) == 0
    if step == 4:
        return jnp.where(low, first, second) + pltpu.roll(jnp.where(low, second, first), 4, 0)
    return jnp.where(low, first + pltpu.roll(first, 8 - step, 0), second + pltpu.roll(second, step, 0))


def age_sums(cells_ref, t, factor, cross_ref, base, cross):
    ages = factor.shape[0]

    def tile(rs):
        total = None
        for k in range(0, ages, 8):
            stop = min(k + 8, ages)
            part = cells_ref[t, rs, k:stop] * factor[k:stop]
            if stop < k + 8:
                part = jnp.concatenate([part, jnp.zeros((k + 8 - stop, LANES), F32)], axis=0)
            total = part if total is None else total + part
        return total

    for start in range(0, cross, 8):
        tiles = [tile(rs) for rs in range(start, min(start + 8, cross))]
        if len(tiles) < 8:
            for k, x in enumerate(tiles):
                cross_ref[pl.ds(base + start + k, 1), :] = jnp.sum(x, axis=0, keepdims=True)
            continue
        tiles = [merge(tiles[k], tiles[k + 4], 4) for k in range(4)]
        tiles = [merge(tiles[k], tiles[k + 2], 2) for k in range(2)]
        cross_ref[pl.ds(pl.multiple_of(base + start, 8), 8), :] = merge(tiles[0], tiles[1], 1)


def pair_sum(term, count):
    first, second = term(0), term(1)
    for k in range(2, count, 2):
        first = first + term(k)
        if k + 1 < count:
            second = second + term(k + 1)
    return first + second


def rake_kernel(
    ids_hbm, table_hbm, age_sex_hbm, race_hisp_hbm, size_tenure_hbm, tenure_income_hbm,
    keep_ref, send_ref, age_factor_ref, cross_factor_ref, cells_ref,
    sum_ref, cross_ref, rows_ref, age_target_ref, race_target_ref, size_target_ref,
    ids_ref, age_sex_ref, race_hisp_ref, size_tenure_ref, tenure_income_ref,
    sems, small_sems,
    *, races, sizes, pumas,
):
    tracts, cross, ages, _ = table_hbm.shape
    cross_rows = round_up(cross + 1, 8)
    pairs = (ages + 1) // 2
    small = [
        pltpu.make_async_copy(source, target, small_sems.at[i])
        for i, (source, target) in enumerate((
            (ids_hbm, ids_ref),
            (age_sex_hbm, age_sex_ref),
            (race_hisp_hbm, race_hisp_ref),
            (size_tenure_hbm, size_tenure_ref),
            (tenure_income_hbm, tenure_income_ref),
        ))
    ]

    def table_copy(t):
        return pltpu.make_async_copy(table_hbm.at[t], cells_ref.at[t], sems.at[t])

    for copy in small:
        copy.start()
    for t in range(min(IN_FLIGHT, tracts)):
        table_copy(t).start()
    lane = lane_ids(1)
    sex0 = lane < 64
    hisp0 = (lane // 32) % 2 == 0
    ten0 = (lane // 16) % 2 == 0

    rows_ref[...] = jnp.zeros(rows_ref.shape, F32)
    for copy in small:
        copy.wait()
    for source_ref, target_ref, rows, mask in (
        (age_sex_ref, age_target_ref, ages, sex0),
        (race_hisp_ref, race_target_ref, races, hisp0),
        (size_tenure_ref, size_target_ref, sizes, ten0),
    ):
        for t in range(tracts):
            row = source_ref[t : t + 1, :]
            target_ref[t, 0:rows] = jnp.where(
                mask, column_of(row, rows, 2, 0), column_of(row, rows, 2, 1)
            )

    def group_sums(values, mask):
        first = [masked_lane_sum(x, mask) for x in values]
        second = [masked_lane_sum(x, ~mask) for x in values]
        return [jnp.where(mask, x, y) for x, y in zip(first, second)]

    def arrive(t, carry):
        table_copy(t).wait()

        @pl.when(t + IN_FLIGHT < tracts)
        def _():
            table_copy(t + IN_FLIGHT).start()

        sum_ref[t, 0:ages] = pair_sum(lambda rs: cells_ref[t, rs], cross)
        return carry

    def add_ages(t, carry):
        age_sums(cells_ref, t, age_factor_ref[t, 0:ages], cross_ref, t * cross_rows, cross)
        return carry

    def add_scaled(t, carry):
        base = t * cross_rows
        total = pair_sum(
            lambda rs: cells_ref[t, rs] * cross_factor_ref[pl.ds(base + rs, 1), :], cross
        )
        sum_ref[t, 0:ages] = total * age_factor_ref[t, 0:ages]
        sum_ref[t, ages : 2 * pairs] = jnp.zeros((2 * pairs - ages, LANES), F32)
        return carry

    def small_steps(group):
        bases = [t * cross_rows for t in group]
        by_race = [
            sum(cross_ref[pl.ds(base + s, races, stride=sizes), :] for s in range(sizes))
            for base in bases
        ]
        race_factor = [
            race_target_ref[t, 0:races] / margin for t, margin in zip(group, group_sums(by_race, hisp0))
        ]
        by_size = [
            sum(
                cross_ref[pl.ds(base + r * sizes, sizes), :] * factor[r : r + 1]
                for r in range(races)
            )
            for base, factor in zip(bases, race_factor)
        ]
        size_factor = [
            size_target_ref[t, 0:sizes] / margin for t, margin in zip(group, group_sums(by_size, ten0))
        ]
        by_income = [jnp.sum(x * y, axis=0, keepdims=True) for x, y in zip(by_size, size_factor)]
        by_income = [x + pltpu.roll(x, 64, 1) for x in by_income]
        by_income = [x + pltpu.roll(x, 32, 1) for x in by_income]
        for i, t in enumerate(group):
            target = jnp.concatenate([tenure_income_ref[t : t + 1, :]] * 4, axis=1)
            age_factor_ref[t, 0:ages] = age_factor_ref[t, 0:ages] * (target / by_income[i])
            for r in range(races):
                cross_factor_ref[pl.ds(bases[i] + r * sizes, sizes), :] = (
                    size_factor[i] * race_factor[i][r : r + 1]
                )
            cross_factor_ref[pl.ds(bases[i] + cross, cross_rows - cross), :] = jnp.zeros(
                (cross_rows - cross, LANES), F32
            )

    def pack(group):
        even = [sum_ref[t, pl.ds(0, pairs, stride=2)] for t in group]
        odd = [sum_ref[t, pl.ds(1, pairs, stride=2)] for t in group]
        even = [x + pltpu.roll(x, 96, 1) for x in even]
        odd = [x + pltpu.roll(x, 96, 1) for x in odd]
        packed = [
            jnp.where(
                lane < 32,
                x,
                jnp.where(
                    lane < 64,
                    pltpu.roll(x, 96, 1),
                    jnp.where(lane < 96, pltpu.roll(y, 64, 1), pltpu.roll(y, 32, 1)),
                ),
            )
            for x, y in zip(even, odd)
        ]
        for t, x in zip(group, packed):
            at = pl.ds(ids_ref[t], pairs, stride=pumas)
            rows_ref[at, :] = rows_ref[at, :] + x

    def work(group):
        margin = group_sums([sum_ref[t, 0:ages] for t in group], sex0)
        for t, x in zip(group, margin):
            age_factor_ref[t, 0:ages] = age_target_ref[t, 0:ages] / x
        lax.fori_loop(group.start, group.stop, add_ages, 0)
        small_steps(group)
        lax.fori_loop(group.start, group.stop, add_scaled, 0)
        pack(group)

    before = None
    for start in range(0, tracts, GROUP):
        if before is not None:
            work(before)
        before = range(start, min(start + GROUP, tracts))
        lax.fori_loop(before.start, before.stop, arrive, 0)
    work(before)
    put_halves(rows_ref, [keep_ref], [send_ref])


def race_margin_kernel(
    ids_ref, cells_ref, age_factor_ref, cross_factor_ref, target_ref,
    own_ref, other_ref, *refs
):
    *chunk_refs, scaled_factor_ref, cross_ref, age_rows_ref, rows_ref, scalar_ref = refs
    chunks = len(chunk_refs) // 2
    keep_refs, send_refs = chunk_refs[:chunks], chunk_refs[chunks:]
    tracts, cross, ages, _ = cells_ref.shape
    cross_rows = round_up(cross + 1, 8)
    pairs, cross_pairs = (ages + 1) // 2, (cross + 1) // 2
    pumas = target_ref.shape[0]
    load_puma_numbers(ids_ref, scalar_ref)
    rows_ref[...] = jnp.zeros(rows_ref.shape, F32)
    factor_rows(target_ref, [own_ref], [other_ref], age_rows_ref)
    lane = lane_ids(1)

    def unpack(t):
        packed = age_rows_ref[pl.ds(scalar_ref[t], pairs, stride=pumas), :]
        half = pltpu.roll(packed, 64, 1)
        even = jnp.where(lane < 32, packed, jnp.where(lane < 96, pltpu.roll(packed, 32, 1), half))
        odd = jnp.where(lane < 32, half, jnp.where(lane < 96, pltpu.roll(packed, 96, 1), packed))
        scaled_factor_ref[t, pl.ds(0, pairs, stride=2)] = even
        scaled_factor_ref[t, pl.ds(1, pairs, stride=2)] = odd

    def add_ages(t):
        factor = scaled_factor_ref[t, 0:ages] * age_factor_ref[t, 0:ages]
        scaled_factor_ref[t, 0:ages] = factor
        base = t * cross_rows
        age_sums(cells_ref, t, factor, cross_ref, base, cross)
        cross_ref[pl.ds(base + cross, cross_rows - cross), :] = jnp.zeros(
            (cross_rows - cross, LANES), F32
        )

    def pack(t):
        halves = []
        for first in range(2):
            at = pl.ds(t * cross_rows + first, cross_pairs, stride=2)
            margin = cross_ref[at, :] * cross_factor_ref[at, :]
            halves.append(margin + pltpu.roll(margin, 64, 1))
        at = pl.ds(scalar_ref[t], cross_pairs, stride=pumas)
        rows_ref[at, :] = rows_ref[at, :] + jnp.where(lane < 64, *halves)

    def step(t, carry):
        pack(t - 1)
        add_ages(t)
        unpack(t + 1)
        return carry

    unpack(0)
    add_ages(0)
    unpack(1)
    lax.fori_loop(1, tracts - 1, step, 0)
    pack(tracts - 2)
    add_ages(tracts - 1)
    pack(tracts - 1)
    put_halves(rows_ref, keep_refs, send_refs)


def final_kernel(
    ids_ref, cells_ref, scaled_factor_ref, cross_factor_ref, target_ref, *refs
):
    *chunk_refs, out_ref, result_ref, cross_ref, rows_ref, scalar_ref, sems = refs
    chunks = len(chunk_refs) // 2
    tracts, cross, ages, _ = cells_ref.shape
    cross_rows = round_up(cross + 1, 8)
    cross_pairs = (cross + 1) // 2
    pumas = target_ref.shape[0]
    load_puma_numbers(ids_ref, scalar_ref)
    factor_rows(target_ref, chunk_refs[:chunks], chunk_refs[chunks:], rows_ref)
    lane = lane_ids(1)

    def unpack(t):
        base = t * cross_rows
        packed = rows_ref[pl.ds(scalar_ref[t], cross_pairs, stride=pumas), :]
        half = pltpu.roll(packed, 64, 1)
        for first, factor in enumerate(
            (jnp.where(lane < 64, packed, half), jnp.where(lane < 64, half, packed))
        ):
            at = pl.ds(base + first, cross_pairs, stride=2)
            cross_ref[at, :] = factor * cross_factor_ref[at, :]

    def scale(t):
        factor = scaled_factor_ref[t, 0:ages]
        base = t * cross_rows
        for rs in range(cross):
            result_ref[t, rs] = cells_ref[t, rs] * factor * cross_ref[pl.ds(base + rs, 1), :]

    def send(t):
        pltpu.make_async_copy(result_ref.at[t], out_ref.at[t], sems.at[t]).start()

    def step(t, carry):
        scale(t)
        unpack(t + 1)
        send(t)
        return carry

    unpack(0)
    lax.fori_loop(0, tracts - 1, step, 0)
    scale(tracts - 1)
    send(tracts - 1)
    for t in range(tracts):
        pltpu.make_async_copy(result_ref.at[t], out_ref.at[t], sems.at[t]).wait()


def call(kernel, out_shapes, in_spaces, out_spaces, scratch):
    def spec(space):
        return pl.BlockSpec(memory_space=space)

    run = pl.pallas_call(
        kernel,
        out_shape=[
            space(shape, F32) for shape, space in zip(out_shapes, out_spaces, strict=True)
        ],
        in_specs=[spec(space) for space in in_spaces],
        out_specs=[spec(space) for space in out_spaces],
        scratch_shapes=scratch,
        compiler_params=pltpu.CompilerParams(vmem_limit_bytes=40 << 20),
    )

    def placed(*args):
        return run(*map(pltpu.with_memory_space_constraint, args, in_spaces))

    return placed


def per_device(
    devices,
    table, age_sex, race_hisp, size_tenure, tenure_income, puma_age, puma_race, tract_puma,
):
    tracts, ages, races, sizes, inner = table.shape
    pumas = puma_age.shape[0]
    cross = races * sizes
    age_pairs, cross_pairs = (ages + 1) // 2, (cross + 1) // 2
    age_rows = 2 * round_up(age_pairs, 8)
    cross_rows = tracts * round_up(cross + 1, 8) + 2 * round_up(cross_pairs, 8) - round_up(cross, 8)
    age_sum_rows, cross_sum_rows = (round_up(x, 8) * pumas for x in (age_pairs, cross_pairs))
    vmem, hbm = pltpu.VMEM, pltpu.HBM

    cells = table.transpose(0, 2, 3, 1, 4).reshape(tracts, cross, ages, inner)
    cells_scratch = pltpu.VMEM((tracts, cross, ages, inner), F32)
    cross_scratch = pltpu.VMEM((cross_rows, LANES), F32)
    copy_sems = pltpu.SemaphoreType.DMA((tracts,))
    numbers_scratch = pltpu.SMEM((tracts,), jnp.int32)

    bits = [1 << k for k in range(1, devices.bit_length() - 1)]
    orders = (bits, bits[1:] + bits[:1])

    def swap(x, partner):
        return lax.ppermute(x, "tract", [(i, partner(i)) for i in range(devices)])

    def totals(keep, send):
        keep = [x + swap(y, lambda i: i ^ 1) for x, y in zip(keep, send)]
        for step in range(len(bits)):
            keep = [x + swap(x, lambda i: i ^ orders[i.bit_count() % 2][step] ^ 1) for x in keep]
        return *keep, *[swap(x, lambda i: i ^ 1) for x in keep]

    age_half, cross_half = -(-age_pairs // 2), -(-cross_pairs // 2)
    cross_chunks = [cross_half - cross_half // 2, cross_half // 2]
    age_shape, cross_shape = (tracts, age_rows, LANES), (cross_rows, LANES)
    small = [age_sex, race_hisp, size_tenure, tenure_income]
    keep, send, age_factor, cross_factor, cells = call(
        functools.partial(rake_kernel, races=races, sizes=sizes, pumas=pumas),
        [(age_half * pumas, LANES)] * 2 + [age_shape, cross_shape, cells.shape],
        [hbm] * 6,
        [vmem] * 5,
        [
            pltpu.VMEM(age_shape, F32),
            cross_scratch,
            pltpu.VMEM((age_sum_rows, LANES), F32),
            pltpu.VMEM(age_shape, F32),
            pltpu.VMEM((tracts, round_up(races, 8), LANES), F32),
            pltpu.VMEM((tracts, round_up(sizes, 8), LANES), F32),
            numbers_scratch,
        ]
        + [pltpu.VMEM(x.shape, F32) for x in small]
        + [copy_sems, pltpu.SemaphoreType.DMA((1 + len(small),))],
    )(tract_puma, cells, *small)

    *chunks, scaled_factor = call(
        race_margin_kernel,
        [(rows * pumas, LANES) for rows in cross_chunks * 2] + [(tracts, age_rows, LANES)],
        [vmem] * 7,
        [vmem] * (2 * len(cross_chunks) + 1),
        [
            cross_scratch,
            pltpu.VMEM((age_sum_rows, LANES), F32),
            pltpu.VMEM((cross_sum_rows, LANES), F32),
            numbers_scratch,
        ],
    )(tract_puma, cells, age_factor, cross_factor, puma_age, *totals([keep], [send]))

    keep, send = chunks[: len(cross_chunks)], chunks[len(cross_chunks) :]
    out, = call(
        final_kernel,
        [(tracts, cross, ages, inner)],
        [vmem] * (5 + 2 * len(cross_chunks)),
        [hbm],
        [
            cells_scratch,
            cross_scratch,
            pltpu.VMEM((cross_sum_rows, LANES), F32),
            numbers_scratch,
            copy_sems,
        ],
    )(tract_puma, cells, scaled_factor, cross_factor, puma_race, *totals(keep, send))
    return out.reshape(tracts, races, sizes, ages, inner).transpose(0, 3, 1, 2, 4)


def solution(mesh):
    in_specs = (
        P(("grp", "tract"), None, None, None, None),
        P(("grp", "tract"), None),
        P(("grp", "tract"), None),
        P(("grp", "tract"), None),
        P(("grp", "tract"), None),
        P("grp", None),
        P("grp", None),
        P(("grp", "tract")),
    )
    out_specs = P(("grp", "tract"), None, None, None, None)
    return jax.shard_map(
        functools.partial(per_device, mesh.shape["tract"]),
        mesh=mesh, in_specs=in_specs, out_specs=out_specs, check_vma=False,
    )
```

```python
import functools

import jax
import jax.numpy as jnp
from jax import lax
from jax.experimental import pallas as pl
from jax.experimental.pallas import tpu as pltpu
from jax.sharding import PartitionSpec as P

LANES = 128
GROUP = 6
IN_FLIGHT = 6
F32 = jnp.float32


def round_up(value, step):
    return -(-value // step) * step


def lane_ids(rows):
    return lax.broadcasted_iota(jnp.int32, (rows, LANES), 1)


def masked_lane_sum(value, mask):
    return jnp.sum(jnp.where(mask, value, 0.0), axis=-1, keepdims=True)


def column_of(row, rows, step, offset):
    width = row.shape[-1]
    lane = lax.broadcasted_iota(jnp.int32, (rows, width), 1)
    sub = lax.broadcasted_iota(jnp.int32, (rows, width), 0)
    return jnp.sum(jnp.where(lane == step * sub + offset, row, 0.0), axis=-1, keepdims=True)


def half_of(index):
    total = index
    for k in range(1, 16):
        total = total + lax.shift_right_logical(index, k)
    return lax.rem(total, 2)


def factor_rows(target_ref, own_refs, other_refs, rows_ref):
    pumas, columns = target_ref.shape
    half = half_of(lax.axis_index("tract"))
    half_rows = sum(ref.shape[0] for ref in own_refs)
    for refs, which in ((own_refs, half), (other_refs, 1 - half)):
        start = which * half_rows
        for ref in refs:
            rows_ref[pl.ds(pl.multiple_of(start, 8), ref.shape[0]), :] = ref[...]
            start = start + ref.shape[0]
    for first in range(0, columns, LANES):
        width = min(columns - first, LANES)
        at = slice(first // LANES * pumas, (first // LANES + 1) * pumas)
        rows_ref[at, 0:width] = target_ref[:, first : first + width] / rows_ref[at, 0:width]


def load_puma_numbers(ids_ref, scalar_ref):
    ids = ids_ref[...]
    for t in range(scalar_ref.shape[0]):
        scalar_ref[t] = ids[t]


def put_halves(rows_ref, keep_refs, send_refs):
    half = half_of(lax.axis_index("tract"))
    half_rows = sum(ref.shape[0] for ref in keep_refs)
    for refs, which in ((keep_refs, half), (send_refs, 1 - half)):
        start = which * half_rows
        for ref in refs:
            ref[...] = rows_ref[pl.ds(pl.multiple_of(start, 8), ref.shape[0]), :]
            start = start + ref.shape[0]


def merge(first, second, step):
    low = lax.rem(lax.broadcasted_iota(jnp.int32, (8, 1), 0) // step, 2) == 0
    if step == 4:
        return jnp.where(low, first, second) + pltpu.roll(jnp.where(low, second, first), 4, 0)
    return jnp.where(low, first + pltpu.roll(first, 8 - step, 0), second + pltpu.roll(second, step, 0))


def age_sums(cells_ref, t, factor, cross_ref, base, cross):
    ages = factor.shape[0]

    def tile(rs):
        total = None
        for k in range(0, ages, 8):
            stop = min(k + 8, ages)
            part = cells_ref[t, rs, k:stop] * factor[k:stop]
            if stop < k + 8:
                part = jnp.concatenate([part, jnp.zeros((k + 8 - stop, LANES), F32)], axis=0)
            total = part if total is None else total + part
        return total

    for start in range(0, cross, 8):
        tiles = [tile(rs) for rs in range(start, min(start + 8, cross))]
        if len(tiles) < 8:
            for k, x in enumerate(tiles):
                cross_ref[pl.ds(base + start + k, 1), :] = jnp.sum(x, axis=0, keepdims=True)
            continue
        tiles = [merge(tiles[k], tiles[k + 4], 4) for k in range(4)]
        tiles = [merge(tiles[k], tiles[k + 2], 2) for k in range(2)]
        cross_ref[pl.ds(pl.multiple_of(base + start, 8), 8), :] = merge(tiles[0], tiles[1], 1)


def pair_sum(term, count):
    first, second = term(0), term(1)
    for k in range(2, count, 2):
        first = first + term(k)
        if k + 1 < count:
            second = second + term(k + 1)
    return first + second


def rake_kernel(
    ids_hbm, table_hbm, age_sex_hbm, race_hisp_hbm, size_tenure_hbm, tenure_income_hbm,
    *refs, races, sizes, pumas, chunks
):
    keep_refs, send_refs = refs[:chunks], refs[chunks : 2 * chunks]
    (
        age_factor_ref, cross_factor_ref, cells_ref,
        sum_ref, cross_ref, rows_ref, age_target_ref, race_target_ref, size_target_ref,
        ids_ref, age_sex_ref, race_hisp_ref, size_tenure_ref, tenure_income_ref,
        sems, small_sems,
    ) = refs[2 * chunks :]
    tracts, cross, ages, _ = table_hbm.shape
    cross_rows = round_up(cross + 1, 8)
    pairs = (ages + 1) // 2
    small = [
        pltpu.make_async_copy(source, target, small_sems.at[i])
        for i, (source, target) in enumerate((
            (ids_hbm, ids_ref),
            (age_sex_hbm, age_sex_ref),
            (race_hisp_hbm, race_hisp_ref),
            (size_tenure_hbm, size_tenure_ref),
            (tenure_income_hbm, tenure_income_ref),
        ))
    ]

    def table_copy(t):
        return pltpu.make_async_copy(table_hbm.at[t], cells_ref.at[t], sems.at[t])

    for copy in small:
        copy.start()
    for t in range(min(IN_FLIGHT, tracts)):
        table_copy(t).start()
    lane = lane_ids(1)
    sex0 = lane < 64
    hisp0 = (lane // 32) % 2 == 0
    ten0 = (lane // 16) % 2 == 0

    rows_ref[...] = jnp.zeros(rows_ref.shape, F32)
    for copy in small:
        copy.wait()
    for source_ref, target_ref, rows, mask in (
        (age_sex_ref, age_target_ref, ages, sex0),
        (race_hisp_ref, race_target_ref, races, hisp0),
        (size_tenure_ref, size_target_ref, sizes, ten0),
    ):
        for t in range(tracts):
            row = source_ref[t : t + 1, :]
            target_ref[t, 0:rows] = jnp.where(
                mask, column_of(row, rows, 2, 0), column_of(row, rows, 2, 1)
            )

    def group_sums(values, mask):
        first = [masked_lane_sum(x, mask) for x in values]
        second = [masked_lane_sum(x, ~mask) for x in values]
        return [jnp.where(mask, x, y) for x, y in zip(first, second)]

    def arrive(t, carry):
        table_copy(t).wait()

        @pl.when(t + IN_FLIGHT < tracts)
        def _():
            table_copy(t + IN_FLIGHT).start()

        sum_ref[t, 0:ages] = pair_sum(lambda rs: cells_ref[t, rs], cross)
        return carry

    def add_ages(t, carry):
        age_sums(cells_ref, t, age_factor_ref[t, 0:ages], cross_ref, t * cross_rows, cross)
        return carry

    def add_scaled(t, carry):
        base = t * cross_rows
        total = pair_sum(
            lambda rs: cells_ref[t, rs] * cross_factor_ref[pl.ds(base + rs, 1), :], cross
        )
        sum_ref[t, 0:ages] = total * age_factor_ref[t, 0:ages]
        sum_ref[t, ages : 2 * pairs] = jnp.zeros((2 * pairs - ages, LANES), F32)
        return carry

    def small_steps(group):
        bases = [t * cross_rows for t in group]
        by_race = [
            sum(cross_ref[pl.ds(base + s, races, stride=sizes), :] for s in range(sizes))
            for base in bases
        ]
        race_factor = [
            race_target_ref[t, 0:races] / margin for t, margin in zip(group, group_sums(by_race, hisp0))
        ]
        by_size = [
            sum(
                cross_ref[pl.ds(base + r * sizes, sizes), :] * factor[r : r + 1]
                for r in range(races)
            )
            for base, factor in zip(bases, race_factor)
        ]
        size_factor = [
            size_target_ref[t, 0:sizes] / margin for t, margin in zip(group, group_sums(by_size, ten0))
        ]
        by_income = [jnp.sum(x * y, axis=0, keepdims=True) for x, y in zip(by_size, size_factor)]
        by_income = [x + pltpu.roll(x, 64, 1) for x in by_income]
        by_income = [x + pltpu.roll(x, 32, 1) for x in by_income]
        for i, t in enumerate(group):
            target = jnp.concatenate([tenure_income_ref[t : t + 1, :]] * 4, axis=1)
            age_factor_ref[t, 0:ages] = age_factor_ref[t, 0:ages] * (target / by_income[i])
            for r in range(races):
                cross_factor_ref[pl.ds(bases[i] + r * sizes, sizes), :] = (
                    size_factor[i] * race_factor[i][r : r + 1]
                )
            cross_factor_ref[pl.ds(bases[i] + cross, cross_rows - cross), :] = jnp.zeros(
                (cross_rows - cross, LANES), F32
            )

    def pack(group):
        even = [sum_ref[t, pl.ds(0, pairs, stride=2)] for t in group]
        odd = [sum_ref[t, pl.ds(1, pairs, stride=2)] for t in group]
        even = [x + pltpu.roll(x, 96, 1) for x in even]
        odd = [x + pltpu.roll(x, 96, 1) for x in odd]
        packed = [
            jnp.where(
                lane < 32,
                x,
                jnp.where(
                    lane < 64,
                    pltpu.roll(x, 96, 1),
                    jnp.where(lane < 96, pltpu.roll(y, 64, 1), pltpu.roll(y, 32, 1)),
                ),
            )
            for x, y in zip(even, odd)
        ]
        for t, x in zip(group, packed):
            at = pl.ds(ids_ref[t], pairs, stride=pumas)
            rows_ref[at, :] = rows_ref[at, :] + x

    def work(group):
        margin = group_sums([sum_ref[t, 0:ages] for t in group], sex0)
        for t, x in zip(group, margin):
            age_factor_ref[t, 0:ages] = age_target_ref[t, 0:ages] / x
        lax.fori_loop(group.start, group.stop, add_ages, 0)
        small_steps(group)
        lax.fori_loop(group.start, group.stop, add_scaled, 0)
        pack(group)

    before = None
    for start in range(0, tracts, GROUP):
        if before is not None:
            work(before)
        before = range(start, min(start + GROUP, tracts))
        lax.fori_loop(before.start, before.stop, arrive, 0)
    work(before)
    put_halves(rows_ref, keep_refs, send_refs)


def race_margin_kernel(
    ids_ref, cells_ref, age_factor_ref, cross_factor_ref, target_ref,
    *refs, age_chunks
):
    own_refs, other_refs, refs = refs[:age_chunks], refs[age_chunks : 2 * age_chunks], refs[2 * age_chunks :]
    *chunk_refs, scaled_factor_ref, cross_ref, age_rows_ref, rows_ref, scalar_ref = refs
    chunks = len(chunk_refs) // 2
    keep_refs, send_refs = chunk_refs[:chunks], chunk_refs[chunks:]
    tracts, cross, ages, _ = cells_ref.shape
    cross_rows = round_up(cross + 1, 8)
    pairs, cross_pairs = (ages + 1) // 2, (cross + 1) // 2
    pumas = target_ref.shape[0]
    load_puma_numbers(ids_ref, scalar_ref)
    rows_ref[...] = jnp.zeros(rows_ref.shape, F32)
    factor_rows(target_ref, own_refs, other_refs, age_rows_ref)
    lane = lane_ids(1)

    def unpack(t):
        packed = age_rows_ref[pl.ds(scalar_ref[t], pairs, stride=pumas), :]
        half = pltpu.roll(packed, 64, 1)
        even = jnp.where(lane < 32, packed, jnp.where(lane < 96, pltpu.roll(packed, 32, 1), half))
        odd = jnp.where(lane < 32, half, jnp.where(lane < 96, pltpu.roll(packed, 96, 1), packed))
        scaled_factor_ref[t, pl.ds(0, pairs, stride=2)] = even
        scaled_factor_ref[t, pl.ds(1, pairs, stride=2)] = odd

    def add_ages(t):
        factor = scaled_factor_ref[t, 0:ages] * age_factor_ref[t, 0:ages]
        scaled_factor_ref[t, 0:ages] = factor
        base = t * cross_rows
        age_sums(cells_ref, t, factor, cross_ref, base, cross)
        cross_ref[pl.ds(base + cross, cross_rows - cross), :] = jnp.zeros(
            (cross_rows - cross, LANES), F32
        )

    def pack(t):
        halves = []
        for first in range(2):
            at = pl.ds(t * cross_rows + first, cross_pairs, stride=2)
            margin = cross_ref[at, :] * cross_factor_ref[at, :]
            halves.append(margin + pltpu.roll(margin, 64, 1))
        at = pl.ds(scalar_ref[t], cross_pairs, stride=pumas)
        rows_ref[at, :] = rows_ref[at, :] + jnp.where(lane < 64, *halves)

    def step(t, carry):
        pack(t - 1)
        add_ages(t)
        unpack(t + 1)
        return carry

    unpack(0)
    add_ages(0)
    unpack(1)
    lax.fori_loop(1, tracts - 1, step, 0)
    pack(tracts - 2)
    add_ages(tracts - 1)
    pack(tracts - 1)
    put_halves(rows_ref, keep_refs, send_refs)


def final_kernel(
    ids_ref, cells_ref, scaled_factor_ref, cross_factor_ref, target_ref, *refs
):
    *chunk_refs, out_ref, result_ref, cross_ref, rows_ref, scalar_ref, sems = refs
    chunks = len(chunk_refs) // 2
    tracts, cross, ages, _ = cells_ref.shape
    cross_rows = round_up(cross + 1, 8)
    cross_pairs = (cross + 1) // 2
    pumas = target_ref.shape[0]
    load_puma_numbers(ids_ref, scalar_ref)
    factor_rows(target_ref, chunk_refs[:chunks], chunk_refs[chunks:], rows_ref)
    lane = lane_ids(1)

    def unpack(t):
        base = t * cross_rows
        packed = rows_ref[pl.ds(scalar_ref[t], cross_pairs, stride=pumas), :]
        half = pltpu.roll(packed, 64, 1)
        for first, factor in enumerate(
            (jnp.where(lane < 64, packed, half), jnp.where(lane < 64, half, packed))
        ):
            at = pl.ds(base + first, cross_pairs, stride=2)
            cross_ref[at, :] = factor * cross_factor_ref[at, :]

    def scale(t):
        factor = scaled_factor_ref[t, 0:ages]
        base = t * cross_rows
        for rs in range(cross):
            result_ref[t, rs] = cells_ref[t, rs] * factor * cross_ref[pl.ds(base + rs, 1), :]

    def send(t):
        pltpu.make_async_copy(result_ref.at[t], out_ref.at[t], sems.at[t]).start()

    def step(t, carry):
        scale(t)
        unpack(t + 1)
        send(t)
        return carry

    unpack(0)
    lax.fori_loop(0, tracts - 1, step, 0)
    scale(tracts - 1)
    send(tracts - 1)
    for t in range(tracts):
        pltpu.make_async_copy(result_ref.at[t], out_ref.at[t], sems.at[t]).wait()


def call(kernel, out_shapes, in_spaces, out_spaces, scratch):
    def spec(space):
        return pl.BlockSpec(memory_space=space)

    run = pl.pallas_call(
        kernel,
        out_shape=[
            space(shape, F32) for shape, space in zip(out_shapes, out_spaces, strict=True)
        ],
        in_specs=[spec(space) for space in in_spaces],
        out_specs=[spec(space) for space in out_spaces],
        scratch_shapes=scratch,
        compiler_params=pltpu.CompilerParams(vmem_limit_bytes=40 << 20),
    )

    def placed(*args):
        return run(*map(pltpu.with_memory_space_constraint, args, in_spaces))

    return placed


def per_device(
    devices,
    table, age_sex, race_hisp, size_tenure, tenure_income, puma_age, puma_race, tract_puma,
):
    tracts, ages, races, sizes, inner = table.shape
    pumas = puma_age.shape[0]
    cross = races * sizes
    age_pairs, cross_pairs = (ages + 1) // 2, (cross + 1) // 2
    age_rows = 2 * round_up(age_pairs, 8)
    cross_rows = tracts * round_up(cross + 1, 8) + 2 * round_up(cross_pairs, 8) - round_up(cross, 8)
    age_sum_rows, cross_sum_rows = (round_up(x, 8) * pumas for x in (age_pairs, cross_pairs))
    vmem, hbm = pltpu.VMEM, pltpu.HBM

    cells = table.transpose(0, 2, 3, 1, 4).reshape(tracts, cross, ages, inner)
    cells_scratch = pltpu.VMEM((tracts, cross, ages, inner), F32)
    cross_scratch = pltpu.VMEM((cross_rows, LANES), F32)
    copy_sems = pltpu.SemaphoreType.DMA((tracts,))
    numbers_scratch = pltpu.SMEM((tracts,), jnp.int32)

    bits = [1 << k for k in range(1, devices.bit_length() - 1)]
    orders = (bits, bits[1:] + bits[:1])

    def swap(x, partner):
        return lax.ppermute(x, "tract", [(i, partner(i)) for i in range(devices)])

    def totals(sums):
        keep, send = sums[: len(sums) // 2], sums[len(sums) // 2 :]
        keep = [x + swap(y, lambda i: i ^ 1) for x, y in zip(keep, send)]
        for step in range(len(bits)):
            keep = [x + swap(x, lambda i: i ^ orders[i.bit_count() % 2][step] ^ 1) for x in keep]
        return *keep, *[swap(x, lambda i: i ^ 1) for x in keep]

    age_half, cross_half = -(-age_pairs // 2), -(-cross_pairs // 2)
    age_chunks, cross_chunks = ([x - x // 2, x // 2] for x in (age_half, cross_half))
    age_shape, cross_shape = (tracts, age_rows, LANES), (cross_rows, LANES)
    small = [age_sex, race_hisp, size_tenure, tenure_income]
    *sums, age_factor, cross_factor, cells = call(
        functools.partial(
            rake_kernel, races=races, sizes=sizes, pumas=pumas, chunks=len(age_chunks)
        ),
        [(rows * pumas, LANES) for rows in age_chunks * 2] + [age_shape, cross_shape, cells.shape],
        [hbm] * 6,
        [vmem] * (2 * len(age_chunks) + 3),
        [
            pltpu.VMEM(age_shape, F32),
            cross_scratch,
            pltpu.VMEM((age_sum_rows, LANES), F32),
            pltpu.VMEM(age_shape, F32),
            pltpu.VMEM((tracts, round_up(races, 8), LANES), F32),
            pltpu.VMEM((tracts, round_up(sizes, 8), LANES), F32),
            numbers_scratch,
        ]
        + [pltpu.VMEM(x.shape, F32) for x in small]
        + [copy_sems, pltpu.SemaphoreType.DMA((1 + len(small),))],
    )(tract_puma, cells, *small)

    *sums, scaled_factor = call(
        functools.partial(race_margin_kernel, age_chunks=len(age_chunks)),
        [(rows * pumas, LANES) for rows in cross_chunks * 2] + [(tracts, age_rows, LANES)],
        [vmem] * (5 + 2 * len(age_chunks)),
        [vmem] * (2 * len(cross_chunks) + 1),
        [
            cross_scratch,
            pltpu.VMEM((age_sum_rows, LANES), F32),
            pltpu.VMEM((cross_sum_rows, LANES), F32),
            numbers_scratch,
        ],
    )(tract_puma, cells, age_factor, cross_factor, puma_age, *totals(sums))

    out, = call(
        final_kernel,
        [(tracts, cross, ages, inner)],
        [vmem] * (5 + 2 * len(cross_chunks)),
        [hbm],
        [
            cells_scratch,
            cross_scratch,
            pltpu.VMEM((cross_sum_rows, LANES), F32),
            numbers_scratch,
            copy_sems,
        ],
    )(tract_puma, cells, scaled_factor, cross_factor, puma_race, *totals(sums))
    return out.reshape(tracts, races, sizes, ages, inner).transpose(0, 3, 1, 2, 4)


def solution(mesh):
    in_specs = (
        P(("grp", "tract"), None, None, None, None),
        P(("grp", "tract"), None),
        P(("grp", "tract"), None),
        P(("grp", "tract"), None),
        P(("grp", "tract"), None),
        P("grp", None),
        P("grp", None),
        P(("grp", "tract")),
    )
    out_specs = P(("grp", "tract"), None, None, None, None)
    return jax.shard_map(
        functools.partial(per_device, mesh.shape["tract"]),
        mesh=mesh, in_specs=in_specs, out_specs=out_specs, check_vma=False,
    )
```

```python
import functools

import jax
import jax.numpy as jnp
from jax import lax
from jax.experimental import pallas as pl
from jax.experimental.pallas import tpu as pltpu
from jax.sharding import PartitionSpec as P

LANES = 128
GROUP = 6
IN_FLIGHT = 6
F32 = jnp.float32


def round_up(value, step):
    return -(-value // step) * step


def lane_ids(rows):
    return lax.broadcasted_iota(jnp.int32, (rows, LANES), 1)


def masked_lane_sum(value, mask):
    return jnp.sum(jnp.where(mask, value, 0.0), axis=-1, keepdims=True)


def column_of(row, rows, step, offset):
    width = row.shape[-1]
    lane = lax.broadcasted_iota(jnp.int32, (rows, width), 1)
    sub = lax.broadcasted_iota(jnp.int32, (rows, width), 0)
    return jnp.sum(jnp.where(lane == step * sub + offset, row, 0.0), axis=-1, keepdims=True)


def half_of(index):
    total = index
    for k in range(1, 16):
        total = total + lax.shift_right_logical(index, k)
    return lax.rem(total, 2)


def factor_rows(target_ref, own_refs, other_refs, rows_ref):
    pumas, columns = target_ref.shape
    half = half_of(lax.axis_index("tract"))
    half_rows = sum(ref.shape[0] for ref in own_refs)
    for refs, which in ((own_refs, half), (other_refs, 1 - half)):
        start = which * half_rows
        for ref in refs:
            rows_ref[pl.ds(pl.multiple_of(start, 8), ref.shape[0]), :] = ref[...]
            start = start + ref.shape[0]
    for first in range(0, columns, LANES):
        width = min(columns - first, LANES)
        at = slice(first // LANES * pumas, (first // LANES + 1) * pumas)
        rows_ref[at, 0:width] = target_ref[:, first : first + width] / rows_ref[at, 0:width]


def load_puma_numbers(ids_ref, scalar_ref):
    ids = ids_ref[...]
    for t in range(scalar_ref.shape[0]):
        scalar_ref[t] = ids[t]


def put_halves(rows_ref, keep_refs, send_refs):
    half = half_of(lax.axis_index("tract"))
    half_rows = sum(ref.shape[0] for ref in keep_refs)
    for refs, which in ((keep_refs, half), (send_refs, 1 - half)):
        start = which * half_rows
        for ref in refs:
            ref[...] = rows_ref[pl.ds(pl.multiple_of(start, 8), ref.shape[0]), :]
            start = start + ref.shape[0]


def merge(first, second, step):
    low = lax.rem(lax.broadcasted_iota(jnp.int32, (8, 1), 0) // step, 2) == 0
    if step == 4:
        return jnp.where(low, first, second) + pltpu.roll(jnp.where(low, second, first), 4, 0)
    return jnp.where(low, first + pltpu.roll(first, 8 - step, 0), second + pltpu.roll(second, step, 0))


def age_sums(cells_ref, t, factor, cross_ref, base, cross):
    ages = factor.shape[0]

    def tile(rs):
        total = None
        for k in range(0, ages, 8):
            stop = min(k + 8, ages)
            part = cells_ref[t, rs, k:stop] * factor[k:stop]
            if stop < k + 8:
                part = jnp.concatenate([part, jnp.zeros((k + 8 - stop, LANES), F32)], axis=0)
            total = part if total is None else total + part
        return total

    for start in range(0, cross, 8):
        tiles = [tile(rs) for rs in range(start, min(start + 8, cross))]
        if len(tiles) < 8:
            for k, x in enumerate(tiles):
                cross_ref[pl.ds(base + start + k, 1), :] = jnp.sum(x, axis=0, keepdims=True)
            continue
        tiles = [merge(tiles[k], tiles[k + 4], 4) for k in range(4)]
        tiles = [merge(tiles[k], tiles[k + 2], 2) for k in range(2)]
        cross_ref[pl.ds(pl.multiple_of(base + start, 8), 8), :] = merge(tiles[0], tiles[1], 1)


def pair_sum(term, count):
    first, second = term(0), term(1)
    for k in range(2, count, 2):
        first = first + term(k)
        if k + 1 < count:
            second = second + term(k + 1)
    return first + second


def rake_kernel(
    ids_hbm, table_hbm, age_sex_hbm, race_hisp_hbm, size_tenure_hbm, tenure_income_hbm,
    keep_ref, send_ref, age_factor_ref, cross_factor_ref, cells_ref,
    sum_ref, cross_ref, rows_ref, age_target_ref, race_target_ref, size_target_ref,
    ids_ref, age_sex_ref, race_hisp_ref, size_tenure_ref, tenure_income_ref,
    sems, small_sems,
    *, races, sizes, pumas,
):
    tracts, cross, ages, _ = table_hbm.shape
    cross_rows = round_up(cross + 1, 8)
    pairs = (ages + 1) // 2
    small = [
        pltpu.make_async_copy(source, target, small_sems.at[i])
        for i, (source, target) in enumerate((
            (ids_hbm, ids_ref),
            (age_sex_hbm, age_sex_ref),
            (race_hisp_hbm, race_hisp_ref),
            (size_tenure_hbm, size_tenure_ref),
            (tenure_income_hbm, tenure_income_ref),
        ))
    ]

    def table_copy(t):
        return pltpu.make_async_copy(table_hbm.at[t], cells_ref.at[t], sems.at[t])

    for copy in small:
        copy.start()
    for t in range(min(IN_FLIGHT, tracts)):
        table_copy(t).start()
    lane = lane_ids(1)
    sex0 = lane < 64
    hisp0 = (lane // 32) % 2 == 0
    ten0 = (lane // 16) % 2 == 0

    rows_ref[...] = jnp.zeros(rows_ref.shape, F32)
    for copy in small:
        copy.wait()
    for source_ref, target_ref, rows, mask in (
        (age_sex_ref, age_target_ref, ages, sex0),
        (race_hisp_ref, race_target_ref, races, hisp0),
        (size_tenure_ref, size_target_ref, sizes, ten0),
    ):
        for t in range(tracts):
            row = source_ref[t : t + 1, :]
            target_ref[t, 0:rows] = jnp.where(
                mask, column_of(row, rows, 2, 0), column_of(row, rows, 2, 1)
            )

    def group_sums(values, mask):
        first = [masked_lane_sum(x, mask) for x in values]
        second = [masked_lane_sum(x, ~mask) for x in values]
        return [jnp.where(mask, x, y) for x, y in zip(first, second)]

    def arrive(t, carry):
        table_copy(t).wait()

        @pl.when(t + IN_FLIGHT < tracts)
        def _():
            table_copy(t + IN_FLIGHT).start()

        sum_ref[t, 0:ages] = pair_sum(lambda rs: cells_ref[t, rs], cross)
        return carry

    def add_ages(t, carry):
        age_sums(cells_ref, t, age_factor_ref[t, 0:ages], cross_ref, t * cross_rows, cross)
        return carry

    def add_scaled(t, carry):
        base = t * cross_rows
        total = pair_sum(
            lambda rs: cells_ref[t, rs] * cross_factor_ref[pl.ds(base + rs, 1), :], cross
        )
        sum_ref[t, 0:ages] = total * age_factor_ref[t, 0:ages]
        sum_ref[t, ages : 2 * pairs] = jnp.zeros((2 * pairs - ages, LANES), F32)
        return carry

    def small_steps(group):
        bases = [t * cross_rows for t in group]
        by_race = [
            sum(cross_ref[pl.ds(base + s, races, stride=sizes), :] for s in range(sizes))
            for base in bases
        ]
        race_factor = [
            race_target_ref[t, 0:races] / margin for t, margin in zip(group, group_sums(by_race, hisp0))
        ]
        by_size = [
            sum(
                cross_ref[pl.ds(base + r * sizes, sizes), :] * factor[r : r + 1]
                for r in range(races)
            )
            for base, factor in zip(bases, race_factor)
        ]
        size_factor = [
            size_target_ref[t, 0:sizes] / margin for t, margin in zip(group, group_sums(by_size, ten0))
        ]
        by_income = [jnp.sum(x * y, axis=0, keepdims=True) for x, y in zip(by_size, size_factor)]
        by_income = [x + pltpu.roll(x, 64, 1) for x in by_income]
        by_income = [x + pltpu.roll(x, 32, 1) for x in by_income]
        for i, t in enumerate(group):
            target = jnp.concatenate([tenure_income_ref[t : t + 1, :]] * 4, axis=1)
            age_factor_ref[t, 0:ages] = age_factor_ref[t, 0:ages] * (target / by_income[i])
            for r in range(races):
                cross_factor_ref[pl.ds(bases[i] + r * sizes, sizes), :] = (
                    size_factor[i] * race_factor[i][r : r + 1]
                )
            cross_factor_ref[pl.ds(bases[i] + cross, cross_rows - cross), :] = jnp.zeros(
                (cross_rows - cross, LANES), F32
            )

    def pack(group):
        even = [sum_ref[t, pl.ds(0, pairs, stride=2)] for t in group]
        odd = [sum_ref[t, pl.ds(1, pairs, stride=2)] for t in group]
        even = [x + pltpu.roll(x, 96, 1) for x in even]
        odd = [x + pltpu.roll(x, 96, 1) for x in odd]
        packed = [
            jnp.where(
                lane < 32,
                x,
                jnp.where(
                    lane < 64,
                    pltpu.roll(x, 96, 1),
                    jnp.where(lane < 96, pltpu.roll(y, 64, 1), pltpu.roll(y, 32, 1)),
                ),
            )
            for x, y in zip(even, odd)
        ]
        for t, x in zip(group, packed):
            at = pl.ds(ids_ref[t], pairs, stride=pumas)
            rows_ref[at, :] = rows_ref[at, :] + x

    def work(group):
        margin = group_sums([sum_ref[t, 0:ages] for t in group], sex0)
        for t, x in zip(group, margin):
            age_factor_ref[t, 0:ages] = age_target_ref[t, 0:ages] / x
        lax.fori_loop(group.start, group.stop, add_ages, 0)
        small_steps(group)
        lax.fori_loop(group.start, group.stop, add_scaled, 0)
        pack(group)

    before = None
    for start in range(0, tracts, GROUP):
        if before is not None:
            work(before)
        before = range(start, min(start + GROUP, tracts))
        lax.fori_loop(before.start, before.stop, arrive, 0)
    work(before)
    put_halves(rows_ref, [keep_ref], [send_ref])


def race_margin_kernel(
    ids_ref, cells_ref, age_factor_ref, cross_factor_ref, target_ref,
    own_ref, other_ref, *refs
):
    *chunk_refs, scaled_factor_ref, cross_ref, age_rows_ref, rows_ref, scalar_ref = refs
    chunks = len(chunk_refs) // 2
    keep_refs, send_refs = chunk_refs[:chunks], chunk_refs[chunks:]
    tracts, cross, ages, _ = cells_ref.shape
    cross_rows = round_up(cross + 1, 8)
    pairs, cross_pairs = (ages + 1) // 2, (cross + 1) // 2
    pumas = target_ref.shape[0]
    load_puma_numbers(ids_ref, scalar_ref)
    rows_ref[...] = jnp.zeros(rows_ref.shape, F32)
    factor_rows(target_ref, [own_ref], [other_ref], age_rows_ref)
    lane = lane_ids(1)

    def unpack(t):
        packed = age_rows_ref[pl.ds(scalar_ref[t], pairs, stride=pumas), :]
        half = pltpu.roll(packed, 64, 1)
        even = jnp.where(lane < 32, packed, jnp.where(lane < 96, pltpu.roll(packed, 32, 1), half))
        odd = jnp.where(lane < 32, half, jnp.where(lane < 96, pltpu.roll(packed, 96, 1), packed))
        scaled_factor_ref[t, pl.ds(0, pairs, stride=2)] = even
        scaled_factor_ref[t, pl.ds(1, pairs, stride=2)] = odd

    def add_ages(t):
        factor = scaled_factor_ref[t, 0:ages] * age_factor_ref[t, 0:ages]
        scaled_factor_ref[t, 0:ages] = factor
        base = t * cross_rows
        age_sums(cells_ref, t, factor, cross_ref, base, cross)
        cross_ref[pl.ds(base + cross, cross_rows - cross), :] = jnp.zeros(
            (cross_rows - cross, LANES), F32
        )

    def pack(t):
        halves = []
        for first in range(2):
            at = pl.ds(t * cross_rows + first, cross_pairs, stride=2)
            margin = cross_ref[at, :] * cross_factor_ref[at, :]
            halves.append(margin + pltpu.roll(margin, 64, 1))
        at = pl.ds(scalar_ref[t], cross_pairs, stride=pumas)
        rows_ref[at, :] = rows_ref[at, :] + jnp.where(lane < 64, *halves)

    def step(t, carry):
        pack(t - 1)
        add_ages(t)
        unpack(t + 1)
        return carry

    unpack(0)
    add_ages(0)
    unpack(1)
    lax.fori_loop(1, tracts - 1, step, 0)
    pack(tracts - 2)
    add_ages(tracts - 1)
    pack(tracts - 1)
    put_halves(rows_ref, keep_refs, send_refs)


def final_kernel(
    ids_ref, cells_ref, scaled_factor_ref, cross_factor_ref, target_ref, *refs
):
    *chunk_refs, out_ref, result_ref, cross_ref, rows_ref, scalar_ref, sems = refs
    chunks = len(chunk_refs) // 2
    tracts, cross, ages, _ = cells_ref.shape
    cross_rows = round_up(cross + 1, 8)
    cross_pairs = (cross + 1) // 2
    pumas = target_ref.shape[0]
    load_puma_numbers(ids_ref, scalar_ref)
    factor_rows(target_ref, chunk_refs[:chunks], chunk_refs[chunks:], rows_ref)
    lane = lane_ids(1)

    def unpack(t):
        base = t * cross_rows
        packed = rows_ref[pl.ds(scalar_ref[t], cross_pairs, stride=pumas), :]
        half = pltpu.roll(packed, 64, 1)
        for first, factor in enumerate(
            (jnp.where(lane < 64, packed, half), jnp.where(lane < 64, half, packed))
        ):
            at = pl.ds(base + first, cross_pairs, stride=2)
            cross_ref[at, :] = factor * cross_factor_ref[at, :]

    def scale(t):
        factor = scaled_factor_ref[t, 0:ages]
        base = t * cross_rows
        for rs in range(cross):
            result_ref[t, rs] = cells_ref[t, rs] * factor * cross_ref[pl.ds(base + rs, 1), :]

    def send(t):
        pltpu.make_async_copy(result_ref.at[t], out_ref.at[t], sems.at[t]).start()

    def step(t, carry):
        scale(t)
        unpack(t + 1)
        send(t)
        return carry

    unpack(0)
    lax.fori_loop(0, tracts - 1, step, 0)
    scale(tracts - 1)
    send(tracts - 1)
    for t in range(tracts):
        pltpu.make_async_copy(result_ref.at[t], out_ref.at[t], sems.at[t]).wait()


def call(kernel, out_shapes, in_spaces, out_spaces, scratch):
    def spec(space):
        return pl.BlockSpec(memory_space=space)

    run = pl.pallas_call(
        kernel,
        out_shape=[
            space(shape, F32) for shape, space in zip(out_shapes, out_spaces, strict=True)
        ],
        in_specs=[spec(space) for space in in_spaces],
        out_specs=[spec(space) for space in out_spaces],
        scratch_shapes=scratch,
        compiler_params=pltpu.CompilerParams(vmem_limit_bytes=40 << 20),
    )

    def placed(*args):
        return run(*map(pltpu.with_memory_space_constraint, args, in_spaces))

    return placed


def per_device(
    devices,
    table, age_sex, race_hisp, size_tenure, tenure_income, puma_age, puma_race, tract_puma,
):
    tracts, ages, races, sizes, inner = table.shape
    pumas = puma_age.shape[0]
    cross = races * sizes
    age_pairs, cross_pairs = (ages + 1) // 2, (cross + 1) // 2
    age_rows = 2 * round_up(age_pairs, 8)
    cross_rows = tracts * round_up(cross + 1, 8) + 2 * round_up(cross_pairs, 8) - round_up(cross, 8)
    age_sum_rows, cross_sum_rows = (round_up(x, 8) * pumas for x in (age_pairs, cross_pairs))
    vmem, hbm = pltpu.VMEM, pltpu.HBM

    cells = table.transpose(0, 2, 3, 1, 4).reshape(tracts, cross, ages, inner)
    cells_scratch = pltpu.VMEM((tracts, cross, ages, inner), F32)
    cross_scratch = pltpu.VMEM((cross_rows, LANES), F32)
    copy_sems = pltpu.SemaphoreType.DMA((tracts,))
    numbers_scratch = pltpu.SMEM((tracts,), jnp.int32)

    bits = [1 << k for k in range(1, devices.bit_length() - 1)]
    orders = (bits, bits[-1:] + bits[:-1])

    def swap(x, partner):
        return lax.ppermute(x, "tract", [(i, partner(i)) for i in range(devices)])

    def totals(keep, send):
        keep = [x + swap(y, lambda i: i ^ 1) for x, y in zip(keep, send)]
        for step in range(len(bits)):
            keep = [x + swap(x, lambda i: i ^ orders[i.bit_count() % 2][step] ^ 1) for x in keep]
        return *keep, *[swap(x, lambda i: i ^ 1) for x in keep]

    age_half, cross_half = -(-age_pairs // 2), -(-cross_pairs // 2)
    cross_chunks = [cross_half - cross_half // 2, cross_half // 2]
    age_shape, cross_shape = (tracts, age_rows, LANES), (cross_rows, LANES)
    small = [age_sex, race_hisp, size_tenure, tenure_income]
    keep, send, age_factor, cross_factor, cells = call(
        functools.partial(rake_kernel, races=races, sizes=sizes, pumas=pumas),
        [(age_half * pumas, LANES)] * 2 + [age_shape, cross_shape, cells.shape],
        [hbm] * 6,
        [vmem] * 5,
        [
            pltpu.VMEM(age_shape, F32),
            cross_scratch,
            pltpu.VMEM((age_sum_rows, LANES), F32),
            pltpu.VMEM(age_shape, F32),
            pltpu.VMEM((tracts, round_up(races, 8), LANES), F32),
            pltpu.VMEM((tracts, round_up(sizes, 8), LANES), F32),
            numbers_scratch,
        ]
        + [pltpu.VMEM(x.shape, F32) for x in small]
        + [copy_sems, pltpu.SemaphoreType.DMA((1 + len(small),))],
    )(tract_puma, cells, *small)

    *chunks, scaled_factor = call(
        race_margin_kernel,
        [(rows * pumas, LANES) for rows in cross_chunks * 2] + [(tracts, age_rows, LANES)],
        [vmem] * 7,
        [vmem] * (2 * len(cross_chunks) + 1),
        [
            cross_scratch,
            pltpu.VMEM((age_sum_rows, LANES), F32),
            pltpu.VMEM((cross_sum_rows, LANES), F32),
            numbers_scratch,
        ],
    )(tract_puma, cells, age_factor, cross_factor, puma_age, *totals([keep], [send]))

    keep, send = chunks[: len(cross_chunks)], chunks[len(cross_chunks) :]
    out, = call(
        final_kernel,
        [(tracts, cross, ages, inner)],
        [vmem] * (5 + 2 * len(cross_chunks)),
        [hbm],
        [
            cells_scratch,
            cross_scratch,
            pltpu.VMEM((cross_sum_rows, LANES), F32),
            numbers_scratch,
            copy_sems,
        ],
    )(tract_puma, cells, scaled_factor, cross_factor, puma_race, *totals(keep, send))
    return out.reshape(tracts, races, sizes, ages, inner).transpose(0, 3, 1, 2, 4)


def solution(mesh):
    in_specs = (
        P(("grp", "tract"), None, None, None, None),
        P(("grp", "tract"), None),
        P(("grp", "tract"), None),
        P(("grp", "tract"), None),
        P(("grp", "tract"), None),
        P("grp", None),
        P("grp", None),
        P(("grp", "tract")),
    )
    out_specs = P(("grp", "tract"), None, None, None, None)
    return jax.shard_map(
        functools.partial(per_device, mesh.shape["tract"]),
        mesh=mesh, in_specs=in_specs, out_specs=out_specs, check_vma=False,
    )
```

```python
import functools

import jax
import jax.numpy as jnp
from jax import lax
from jax.experimental import pallas as pl
from jax.experimental.pallas import tpu as pltpu
from jax.sharding import PartitionSpec as P

LANES = 128
GROUP = 6
IN_FLIGHT = 6
F32 = jnp.float32


def round_up(value, step):
    return -(-value // step) * step


def lane_ids(rows):
    return lax.broadcasted_iota(jnp.int32, (rows, LANES), 1)


def masked_lane_sum(value, mask):
    return jnp.sum(jnp.where(mask, value, 0.0), axis=-1, keepdims=True)


def column_of(row, rows, step, offset):
    width = row.shape[-1]
    lane = lax.broadcasted_iota(jnp.int32, (rows, width), 1)
    sub = lax.broadcasted_iota(jnp.int32, (rows, width), 0)
    return jnp.sum(jnp.where(lane == step * sub + offset, row, 0.0), axis=-1, keepdims=True)


def half_of(index):
    total = index
    for k in range(1, 16):
        total = total + lax.shift_right_logical(index, k)
    return lax.rem(total, 2)


def factor_rows(target_ref, own_refs, other_refs, rows_ref):
    pumas, columns = target_ref.shape
    half = half_of(lax.axis_index("tract"))
    half_rows = sum(ref.shape[0] for ref in own_refs)
    for refs, which in ((own_refs, half), (other_refs, 1 - half)):
        start = which * half_rows
        for ref in refs:
            rows_ref[pl.ds(pl.multiple_of(start, 8), ref.shape[0]), :] = ref[...]
            start = start + ref.shape[0]
    for first in range(0, columns, LANES):
        width = min(columns - first, LANES)
        at = slice(first // LANES * pumas, (first // LANES + 1) * pumas)
        rows_ref[at, 0:width] = target_ref[:, first : first + width] / rows_ref[at, 0:width]


def load_puma_numbers(ids_ref, scalar_ref):
    ids = ids_ref[...]
    for t in range(scalar_ref.shape[0]):
        scalar_ref[t] = ids[t]


def put_halves(rows_ref, keep_refs, send_refs):
    half = half_of(lax.axis_index("tract"))
    half_rows = sum(ref.shape[0] for ref in keep_refs)
    for refs, which in ((keep_refs, half), (send_refs, 1 - half)):
        start = which * half_rows
        for ref in refs:
            ref[...] = rows_ref[pl.ds(pl.multiple_of(start, 8), ref.shape[0]), :]
            start = start + ref.shape[0]


def merge(first, second, step):
    low = lax.rem(lax.broadcasted_iota(jnp.int32, (8, 1), 0) // step, 2) == 0
    if step == 4:
        return jnp.where(low, first, second) + pltpu.roll(jnp.where(low, second, first), 4, 0)
    return jnp.where(low, first + pltpu.roll(first, 8 - step, 0), second + pltpu.roll(second, step, 0))


def age_sums(cells_ref, t, factor, cross_ref, base, count, first=0):
    ages = factor.shape[0]
    last = cells_ref.shape[1] - 1

    def tile(k):
        rs = k if isinstance(first, int) else lax.min(first + k, last)
        total = None
        for at in range(0, ages, 8):
            stop = min(at + 8, ages)
            part = cells_ref[t, rs, at:stop] * factor[at:stop]
            if stop < at + 8:
                part = jnp.concatenate([part, jnp.zeros((at + 8 - stop, LANES), F32)], axis=0)
            total = part if total is None else total + part
        return total

    for start in range(0, count, 8):
        tiles = [tile(k) for k in range(start, min(start + 8, count))]
        if len(tiles) < 8:
            for k, x in enumerate(tiles):
                cross_ref[pl.ds(base + start + k, 1), :] = jnp.sum(x, axis=0, keepdims=True)
            continue
        tiles = [merge(tiles[k], tiles[k + 4], 4) for k in range(4)]
        tiles = [merge(tiles[k], tiles[k + 2], 2) for k in range(2)]
        cross_ref[pl.ds(pl.multiple_of(base + start, 8), 8), :] = merge(tiles[0], tiles[1], 1)


def pair_sum(term, count):
    first, second = term(0), term(1)
    for k in range(2, count, 2):
        first = first + term(k)
        if k + 1 < count:
            second = second + term(k + 1)
    return first + second


def rake_kernel(
    ids_hbm, table_hbm, age_sex_hbm, race_hisp_hbm, size_tenure_hbm, tenure_income_hbm,
    keep_ref, send_ref, age_factor_ref, cross_factor_ref, cells_ref,
    sum_ref, cross_ref, rows_ref, age_target_ref, race_target_ref, size_target_ref,
    ids_ref, age_sex_ref, race_hisp_ref, size_tenure_ref, tenure_income_ref,
    sems, small_sems,
    *, races, sizes, pumas,
):
    tracts, cross, ages, _ = table_hbm.shape
    cross_rows = round_up(cross + 1, 8)
    pairs = (ages + 1) // 2
    small = [
        pltpu.make_async_copy(source, target, small_sems.at[i])
        for i, (source, target) in enumerate((
            (ids_hbm, ids_ref),
            (age_sex_hbm, age_sex_ref),
            (race_hisp_hbm, race_hisp_ref),
            (size_tenure_hbm, size_tenure_ref),
            (tenure_income_hbm, tenure_income_ref),
        ))
    ]

    def table_copy(t):
        return pltpu.make_async_copy(table_hbm.at[t], cells_ref.at[t], sems.at[t])

    for copy in small:
        copy.start()
    for t in range(min(IN_FLIGHT, tracts)):
        table_copy(t).start()
    lane = lane_ids(1)
    sex0 = lane < 64
    hisp0 = (lane // 32) % 2 == 0
    ten0 = (lane // 16) % 2 == 0

    rows_ref[...] = jnp.zeros(rows_ref.shape, F32)
    for copy in small:
        copy.wait()
    for source_ref, target_ref, rows, mask in (
        (age_sex_ref, age_target_ref, ages, sex0),
        (race_hisp_ref, race_target_ref, races, hisp0),
        (size_tenure_ref, size_target_ref, sizes, ten0),
    ):
        for t in range(tracts):
            row = source_ref[t : t + 1, :]
            target_ref[t, 0:rows] = jnp.where(
                mask, column_of(row, rows, 2, 0), column_of(row, rows, 2, 1)
            )

    def group_sums(values, mask):
        first = [masked_lane_sum(x, mask) for x in values]
        second = [masked_lane_sum(x, ~mask) for x in values]
        return [jnp.where(mask, x, y) for x, y in zip(first, second)]

    def arrive(t, carry):
        table_copy(t).wait()

        @pl.when(t + IN_FLIGHT < tracts)
        def _():
            table_copy(t + IN_FLIGHT).start()

        sum_ref[t, 0:ages] = pair_sum(lambda rs: cells_ref[t, rs], cross)
        return carry

    def add_ages(t, carry):
        age_sums(cells_ref, t, age_factor_ref[t, 0:ages], cross_ref, t * cross_rows, cross)
        return carry

    def add_scaled(t, carry):
        base = t * cross_rows
        total = pair_sum(
            lambda rs: cells_ref[t, rs] * cross_factor_ref[pl.ds(base + rs, 1), :], cross
        )
        sum_ref[t, 0:ages] = total * age_factor_ref[t, 0:ages]
        sum_ref[t, ages : 2 * pairs] = jnp.zeros((2 * pairs - ages, LANES), F32)
        return carry

    def small_steps(group):
        bases = [t * cross_rows for t in group]
        by_race = [
            sum(cross_ref[pl.ds(base + s, races, stride=sizes), :] for s in range(sizes))
            for base in bases
        ]
        race_factor = [
            race_target_ref[t, 0:races] / margin for t, margin in zip(group, group_sums(by_race, hisp0))
        ]
        by_size = [
            sum(
                cross_ref[pl.ds(base + r * sizes, sizes), :] * factor[r : r + 1]
                for r in range(races)
            )
            for base, factor in zip(bases, race_factor)
        ]
        size_factor = [
            size_target_ref[t, 0:sizes] / margin for t, margin in zip(group, group_sums(by_size, ten0))
        ]
        by_income = [jnp.sum(x * y, axis=0, keepdims=True) for x, y in zip(by_size, size_factor)]
        by_income = [x + pltpu.roll(x, 64, 1) for x in by_income]
        by_income = [x + pltpu.roll(x, 32, 1) for x in by_income]
        for i, t in enumerate(group):
            target = jnp.concatenate([tenure_income_ref[t : t + 1, :]] * 4, axis=1)
            age_factor_ref[t, 0:ages] = age_factor_ref[t, 0:ages] * (target / by_income[i])
            for r in range(races):
                cross_factor_ref[pl.ds(bases[i] + r * sizes, sizes), :] = (
                    size_factor[i] * race_factor[i][r : r + 1]
                )
            cross_factor_ref[pl.ds(bases[i] + cross, cross_rows - cross), :] = jnp.zeros(
                (cross_rows - cross, LANES), F32
            )

    def pack(group):
        even = [sum_ref[t, pl.ds(0, pairs, stride=2)] for t in group]
        odd = [sum_ref[t, pl.ds(1, pairs, stride=2)] for t in group]
        even = [x + pltpu.roll(x, 96, 1) for x in even]
        odd = [x + pltpu.roll(x, 96, 1) for x in odd]
        packed = [
            jnp.where(
                lane < 32,
                x,
                jnp.where(
                    lane < 64,
                    pltpu.roll(x, 96, 1),
                    jnp.where(lane < 96, pltpu.roll(y, 64, 1), pltpu.roll(y, 32, 1)),
                ),
            )
            for x, y in zip(even, odd)
        ]
        for t, x in zip(group, packed):
            at = pl.ds(ids_ref[t], pairs, stride=pumas)
            rows_ref[at, :] = rows_ref[at, :] + x

    def work(group):
        margin = group_sums([sum_ref[t, 0:ages] for t in group], sex0)
        for t, x in zip(group, margin):
            age_factor_ref[t, 0:ages] = age_target_ref[t, 0:ages] / x
        lax.fori_loop(group.start, group.stop, add_ages, 0)
        small_steps(group)
        lax.fori_loop(group.start, group.stop, add_scaled, 0)
        pack(group)

    before = None
    for start in range(0, tracts, GROUP):
        if before is not None:
            work(before)
        before = range(start, min(start + GROUP, tracts))
        lax.fori_loop(before.start, before.stop, arrive, 0)
    work(before)
    put_halves(rows_ref, [keep_ref], [send_ref])


def race_half(cells_ref, factor_ref, cross_factor_ref, chunk_refs, cross_ref, rows_ref, scalar_ref, half, pumas, ages):
    tracts, cross = cells_ref.shape[:2]
    cross_rows = round_up(cross + 1, 8)
    pairs = sum(ref.shape[0] for ref in chunk_refs) // pumas
    count = 2 * pairs
    stride = round_up(count, 8)
    rows_ref[...] = jnp.zeros(rows_ref.shape, F32)
    lane = lane_ids(1)

    def add_ages(t):
        factor = factor_ref[t, 0:ages]
        age_sums(cells_ref, t, factor, cross_ref, t * stride, count, half * count)

    def pack(t):
        halves = []
        for first in range(2):
            margin = cross_ref[pl.ds(t * stride + first, pairs, stride=2), :]
            at = pl.ds(t * cross_rows + half * count + first, pairs, stride=2)
            margin = margin * cross_factor_ref[at, :]
            halves.append(margin + pltpu.roll(margin, 64, 1))
        at = pl.ds(scalar_ref[t], pairs, stride=pumas)
        rows_ref[at, :] = rows_ref[at, :] + jnp.where(lane < 64, *halves)

    def step(t, carry):
        pack(t - 1)
        add_ages(t)
        return carry

    add_ages(0)
    lax.fori_loop(1, tracts, step, 0)
    pack(tracts - 1)
    start = 0
    for ref in chunk_refs:
        ref[...] = rows_ref[start : start + ref.shape[0], :]
        start += ref.shape[0]


def race_send_kernel(
    ids_ref, cells_ref, age_factor_ref, cross_factor_ref, target_ref,
    own_ref, other_ref, *refs
):
    *chunk_refs, scaled_factor_ref, cross_ref, age_rows_ref, rows_ref, scalar_ref = refs
    ages = 2 * (target_ref.shape[1] // LANES) + target_ref.shape[1] % LANES // 64
    pairs = (ages + 1) // 2
    pumas = target_ref.shape[0]
    every = range(cells_ref.shape[0])
    load_puma_numbers(ids_ref, scalar_ref)
    factor_rows(target_ref, [own_ref], [other_ref], age_rows_ref)
    lane = lane_ids(1)
    packed = [age_rows_ref[pl.ds(scalar_ref[t], pairs, stride=pumas), :] for t in every]
    quarter = [pltpu.roll(x, 32, 1) for x in packed]
    half = [pltpu.roll(x, 64, 1) for x in packed]
    back = [pltpu.roll(x, 96, 1) for x in packed]
    for t in every:
        even = jnp.where(lane < 32, packed[t], jnp.where(lane < 96, quarter[t], half[t]))
        odd = jnp.where(lane < 32, half[t], jnp.where(lane < 96, back[t], packed[t]))
        for first, factor in enumerate((even, odd)):
            at = pl.ds(first, pairs, stride=2)
            scaled_factor_ref[t, at] = factor * age_factor_ref[t, at]
    race_half(
        cells_ref, scaled_factor_ref, cross_factor_ref, chunk_refs, cross_ref, rows_ref, scalar_ref,
        1 - half_of(lax.axis_index("tract")), pumas, ages,
    )


def race_keep_kernel(ids_ref, cells_ref, factor_ref, cross_factor_ref, *refs, ages, pumas):
    *chunk_refs, cross_ref, rows_ref, scalar_ref = refs
    load_puma_numbers(ids_ref, scalar_ref)
    race_half(
        cells_ref, factor_ref, cross_factor_ref, chunk_refs, cross_ref, rows_ref, scalar_ref,
        half_of(lax.axis_index("tract")), pumas, ages,
    )


def final_kernel(
    ids_ref, cells_ref, scaled_factor_ref, cross_factor_ref, target_ref, *refs
):
    *chunk_refs, out_ref, result_ref, cross_ref, rows_ref, scalar_ref, sems = refs
    chunks = len(chunk_refs) // 2
    tracts, cross, ages, _ = cells_ref.shape
    cross_rows = round_up(cross + 1, 8)
    cross_pairs = (cross + 1) // 2
    pumas = target_ref.shape[0]
    load_puma_numbers(ids_ref, scalar_ref)
    factor_rows(target_ref, chunk_refs[:chunks], chunk_refs[chunks:], rows_ref)
    lane = lane_ids(1)

    def unpack(t):
        base = t * cross_rows
        packed = rows_ref[pl.ds(scalar_ref[t], cross_pairs, stride=pumas), :]
        half = pltpu.roll(packed, 64, 1)
        for first, factor in enumerate(
            (jnp.where(lane < 64, packed, half), jnp.where(lane < 64, half, packed))
        ):
            at = pl.ds(base + first, cross_pairs, stride=2)
            cross_ref[at, :] = factor * cross_factor_ref[at, :]

    def scale(t):
        factor = scaled_factor_ref[t, 0:ages]
        base = t * cross_rows
        for rs in range(cross):
            result_ref[t, rs] = cells_ref[t, rs] * factor * cross_ref[pl.ds(base + rs, 1), :]

    def send(t):
        pltpu.make_async_copy(result_ref.at[t], out_ref.at[t], sems.at[t]).start()

    def step(t, carry):
        scale(t)
        unpack(t + 1)
        send(t)
        return carry

    unpack(0)
    lax.fori_loop(0, tracts - 1, step, 0)
    scale(tracts - 1)
    send(tracts - 1)
    for t in range(tracts):
        pltpu.make_async_copy(result_ref.at[t], out_ref.at[t], sems.at[t]).wait()


def call(kernel, out_shapes, in_spaces, out_spaces, scratch):
    def spec(space):
        return pl.BlockSpec(memory_space=space)

    run = pl.pallas_call(
        kernel,
        out_shape=[
            space(shape, F32) for shape, space in zip(out_shapes, out_spaces, strict=True)
        ],
        in_specs=[spec(space) for space in in_spaces],
        out_specs=[spec(space) for space in out_spaces],
        scratch_shapes=scratch,
        compiler_params=pltpu.CompilerParams(vmem_limit_bytes=40 << 20),
    )

    def placed(*args):
        return run(*map(pltpu.with_memory_space_constraint, args, in_spaces))

    return placed


def per_device(
    devices,
    table, age_sex, race_hisp, size_tenure, tenure_income, puma_age, puma_race, tract_puma,
):
    tracts, ages, races, sizes, inner = table.shape
    pumas = puma_age.shape[0]
    cross = races * sizes
    age_pairs, cross_pairs = (ages + 1) // 2, (cross + 1) // 2
    age_rows = 2 * round_up(age_pairs, 8)
    cross_rows = tracts * round_up(cross + 1, 8) + 2 * round_up(cross_pairs, 8)
    age_sum_rows, cross_sum_rows = (round_up(x, 8) * pumas for x in (age_pairs, cross_pairs))
    vmem, hbm = pltpu.VMEM, pltpu.HBM

    cells = table.transpose(0, 2, 3, 1, 4).reshape(tracts, cross, ages, inner)
    cells_scratch = pltpu.VMEM((tracts, cross, ages, inner), F32)
    cross_scratch = pltpu.VMEM((cross_rows, LANES), F32)
    copy_sems = pltpu.SemaphoreType.DMA((tracts,))
    numbers_scratch = pltpu.SMEM((tracts,), jnp.int32)

    bits = [1 << k for k in range(1, devices.bit_length() - 1)]
    orders = (bits, bits[1:] + bits[:1])

    def swap(x, partner):
        return lax.ppermute(x, "tract", [(i, partner(i)) for i in range(devices)])

    def totals(keep, send):
        keep = [x + swap(y, lambda i: i ^ 1) for x, y in zip(keep, send)]
        for step in range(len(bits)):
            keep = [x + swap(x, lambda i: i ^ orders[i.bit_count() % 2][step] ^ 1) for x in keep]
        return *keep, *[swap(x, lambda i: i ^ 1) for x in keep]

    age_half, cross_half = -(-age_pairs // 2), -(-cross_pairs // 2)
    cross_chunks = [cross_half - cross_half // 2, cross_half // 2]
    age_shape, cross_shape = (tracts, age_rows, LANES), (cross_rows, LANES)
    small = [age_sex, race_hisp, size_tenure, tenure_income]
    keep, send, age_factor, cross_factor, cells = call(
        functools.partial(rake_kernel, races=races, sizes=sizes, pumas=pumas),
        [(age_half * pumas, LANES)] * 2 + [age_shape, cross_shape, cells.shape],
        [hbm] * 6,
        [vmem] * 5,
        [
            pltpu.VMEM(age_shape, F32),
            cross_scratch,
            pltpu.VMEM((age_sum_rows, LANES), F32),
            pltpu.VMEM(age_shape, F32),
            pltpu.VMEM((tracts, round_up(races, 8), LANES), F32),
            pltpu.VMEM((tracts, round_up(sizes, 8), LANES), F32),
            numbers_scratch,
        ]
        + [pltpu.VMEM(x.shape, F32) for x in small]
        + [copy_sems, pltpu.SemaphoreType.DMA((1 + len(small),))],
    )(tract_puma, cells, *small)

    half_scratch = [
        pltpu.VMEM((tracts * round_up(2 * cross_half, 8) + 16, LANES), F32),
        pltpu.VMEM((round_up(cross_half, 8) * pumas, LANES), F32),
    ]
    chunk_shapes = [(rows * pumas, LANES) for rows in cross_chunks]
    *send, scaled_factor = call(
        race_send_kernel,
        chunk_shapes + [age_shape],
        [vmem] * 7,
        [vmem] * (len(cross_chunks) + 1),
        [half_scratch[0], pltpu.VMEM((age_sum_rows, LANES), F32), half_scratch[1], numbers_scratch],
    )(tract_puma, cells, age_factor, cross_factor, puma_age, *totals([keep], [send]))
    keep = call(
        functools.partial(race_keep_kernel, ages=ages, pumas=pumas),
        chunk_shapes,
        [vmem] * 4,
        [vmem] * len(cross_chunks),
        half_scratch + [numbers_scratch],
    )(tract_puma, cells, scaled_factor, cross_factor)

    out, = call(
        final_kernel,
        [(tracts, cross, ages, inner)],
        [vmem] * (5 + 2 * len(cross_chunks)),
        [hbm],
        [
            cells_scratch,
            cross_scratch,
            pltpu.VMEM((cross_sum_rows, LANES), F32),
            numbers_scratch,
            copy_sems,
        ],
    )(tract_puma, cells, scaled_factor, cross_factor, puma_race, *totals(keep, send))
    return out.reshape(tracts, races, sizes, ages, inner).transpose(0, 3, 1, 2, 4)


def solution(mesh):
    in_specs = (
        P(("grp", "tract"), None, None, None, None),
        P(("grp", "tract"), None),
        P(("grp", "tract"), None),
        P(("grp", "tract"), None),
        P(("grp", "tract"), None),
        P("grp", None),
        P("grp", None),
        P(("grp", "tract")),
    )
    out_specs = P(("grp", "tract"), None, None, None, None)
    return jax.shard_map(
        functools.partial(per_device, mesh.shape["tract"]),
        mesh=mesh, in_specs=in_specs, out_specs=out_specs, check_vma=False,
    )
```

```python
import functools

import jax
import jax.numpy as jnp
from jax import lax
from jax.experimental import pallas as pl
from jax.experimental.pallas import tpu as pltpu
from jax.sharding import PartitionSpec as P

LANES = 128
GROUP = 6
FIRST = 6
F32 = jnp.float32


def round_up(value, step):
    return -(-value // step) * step


def lane_ids(rows):
    return lax.broadcasted_iota(jnp.int32, (rows, LANES), 1)


def masked_lane_sum(value, mask):
    return jnp.sum(jnp.where(mask, value, 0.0), axis=-1, keepdims=True)


def column_of(row, rows, step, offset):
    width = row.shape[-1]
    lane = lax.broadcasted_iota(jnp.int32, (rows, width), 1)
    sub = lax.broadcasted_iota(jnp.int32, (rows, width), 0)
    return jnp.sum(jnp.where(lane == step * sub + offset, row, 0.0), axis=-1, keepdims=True)


def half_of(index):
    total = index
    for k in range(1, 16):
        total = total + lax.shift_right_logical(index, k)
    return lax.rem(total, 2)


def factor_rows(target_ref, own_refs, other_refs, rows_ref):
    pumas, columns = target_ref.shape
    half = half_of(lax.axis_index("tract"))
    half_rows = sum(ref.shape[0] for ref in own_refs)
    for refs, which in ((own_refs, half), (other_refs, 1 - half)):
        start = which * half_rows
        for ref in refs:
            rows_ref[pl.ds(pl.multiple_of(start, 8), ref.shape[0]), :] = ref[...]
            start = start + ref.shape[0]
    for first in range(0, columns, LANES):
        width = min(columns - first, LANES)
        at = slice(first // LANES * pumas, (first // LANES + 1) * pumas)
        rows_ref[at, 0:width] = target_ref[:, first : first + width] / rows_ref[at, 0:width]


def load_puma_numbers(ids_ref, scalar_ref):
    ids = ids_ref[...]
    for t in range(scalar_ref.shape[0]):
        scalar_ref[t] = ids[t]


def put_halves(rows_ref, keep_refs, send_refs):
    half = half_of(lax.axis_index("tract"))
    half_rows = sum(ref.shape[0] for ref in keep_refs)
    for refs, which in ((keep_refs, half), (send_refs, 1 - half)):
        start = which * half_rows
        for ref in refs:
            ref[...] = rows_ref[pl.ds(pl.multiple_of(start, 8), ref.shape[0]), :]
            start = start + ref.shape[0]


def merge(first, second, step):
    low = lax.rem(lax.broadcasted_iota(jnp.int32, (8, 1), 0) // step, 2) == 0
    if step == 4:
        return jnp.where(low, first, second) + pltpu.roll(jnp.where(low, second, first), 4, 0)
    return jnp.where(low, first + pltpu.roll(first, 8 - step, 0), second + pltpu.roll(second, step, 0))


def age_sums(cells_ref, t, factor, cross_ref, base, count, first=0):
    ages = factor.shape[0]
    last = cells_ref.shape[1] - 1

    def tile(k):
        rs = k if isinstance(first, int) else lax.min(first + k, last)
        total = None
        for at in range(0, ages, 8):
            stop = min(at + 8, ages)
            part = cells_ref[t, rs, at:stop] * factor[at:stop]
            if stop < at + 8:
                part = jnp.concatenate([part, jnp.zeros((at + 8 - stop, LANES), F32)], axis=0)
            total = part if total is None else total + part
        return total

    for start in range(0, count, 8):
        tiles = [tile(k) for k in range(start, min(start + 8, count))]
        if len(tiles) < 8:
            for k, x in enumerate(tiles):
                cross_ref[pl.ds(base + start + k, 1), :] = jnp.sum(x, axis=0, keepdims=True)
            continue
        tiles = [merge(tiles[k], tiles[k + 4], 4) for k in range(4)]
        tiles = [merge(tiles[k], tiles[k + 2], 2) for k in range(2)]
        cross_ref[pl.ds(pl.multiple_of(base + start, 8), 8), :] = merge(tiles[0], tiles[1], 1)


def pair_sum(term, count):
    first, second = term(0), term(1)
    for k in range(2, count, 2):
        first = first + term(k)
        if k + 1 < count:
            second = second + term(k + 1)
    return first + second


def rake_kernel(
    ids_hbm, table_hbm, age_sex_hbm, race_hisp_hbm, size_tenure_hbm, tenure_income_hbm,
    keep_ref, send_ref, age_factor_ref, cross_factor_ref, cells_ref,
    sum_ref, cross_ref, rows_ref, age_target_ref, race_target_ref, size_target_ref,
    ids_ref, age_sex_ref, race_hisp_ref, size_tenure_ref, tenure_income_ref,
    sems, small_sems,
    *, races, sizes, pumas,
):
    tracts, cross, ages, _ = table_hbm.shape
    cross_rows = round_up(cross + 1, 8)
    pairs = (ages + 1) // 2
    small = [
        pltpu.make_async_copy(source, target, small_sems.at[i])
        for i, (source, target) in enumerate((
            (ids_hbm, ids_ref),
            (age_sex_hbm, age_sex_ref),
            (race_hisp_hbm, race_hisp_ref),
            (size_tenure_hbm, size_tenure_ref),
            (tenure_income_hbm, tenure_income_ref),
        ))
    ]

    def table_copy(t):
        return pltpu.make_async_copy(table_hbm.at[t], cells_ref.at[t], sems.at[t])

    for copy in small:
        copy.start()
    for t in range(min(FIRST, tracts)):
        table_copy(t).start()
    lane = lane_ids(1)
    sex0 = lane < 64
    hisp0 = (lane // 32) % 2 == 0
    ten0 = (lane // 16) % 2 == 0

    rows_ref[...] = jnp.zeros(rows_ref.shape, F32)
    for copy in small:
        copy.wait()
    for source_ref, target_ref, rows, mask in (
        (age_sex_ref, age_target_ref, ages, sex0),
        (race_hisp_ref, race_target_ref, races, hisp0),
        (size_tenure_ref, size_target_ref, sizes, ten0),
    ):
        for t in range(tracts):
            row = source_ref[t : t + 1, :]
            target_ref[t, 0:rows] = jnp.where(
                mask, column_of(row, rows, 2, 0), column_of(row, rows, 2, 1)
            )

    for t in range(FIRST, tracts):
        table_copy(t).start()

    def group_sums(values, mask):
        first = [masked_lane_sum(x, mask) for x in values]
        second = [masked_lane_sum(x, ~mask) for x in values]
        return [jnp.where(mask, x, y) for x, y in zip(first, second)]

    def arrive(t, carry):
        table_copy(t).wait()
        sum_ref[t, 0:ages] = pair_sum(lambda rs: cells_ref[t, rs], cross)
        return carry

    def add_ages(t, carry):
        age_sums(cells_ref, t, age_factor_ref[t, 0:ages], cross_ref, t * cross_rows, cross)
        return carry

    def add_scaled(t, carry):
        base = t * cross_rows
        total = pair_sum(
            lambda rs: cells_ref[t, rs] * cross_factor_ref[pl.ds(base + rs, 1), :], cross
        )
        sum_ref[t, 0:ages] = total * age_factor_ref[t, 0:ages]
        sum_ref[t, ages : 2 * pairs] = jnp.zeros((2 * pairs - ages, LANES), F32)
        return carry

    def small_steps(group):
        bases = [t * cross_rows for t in group]
        by_race = [
            sum(cross_ref[pl.ds(base + s, races, stride=sizes), :] for s in range(sizes))
            for base in bases
        ]
        race_factor = [
            race_target_ref[t, 0:races] / margin for t, margin in zip(group, group_sums(by_race, hisp0))
        ]
        by_size = [
            sum(
                cross_ref[pl.ds(base + r * sizes, sizes), :] * factor[r : r + 1]
                for r in range(races)
            )
            for base, factor in zip(bases, race_factor)
        ]
        size_factor = [
            size_target_ref[t, 0:sizes] / margin for t, margin in zip(group, group_sums(by_size, ten0))
        ]
        by_income = [jnp.sum(x * y, axis=0, keepdims=True) for x, y in zip(by_size, size_factor)]
        by_income = [x + pltpu.roll(x, 64, 1) for x in by_income]
        by_income = [x + pltpu.roll(x, 32, 1) for x in by_income]
        for i, t in enumerate(group):
            target = jnp.concatenate([tenure_income_ref[t : t + 1, :]] * 4, axis=1)
            age_factor_ref[t, 0:ages] = age_factor_ref[t, 0:ages] * (target / by_income[i])
            for r in range(races):
                cross_factor_ref[pl.ds(bases[i] + r * sizes, sizes), :] = (
                    size_factor[i] * race_factor[i][r : r + 1]
                )
            cross_factor_ref[pl.ds(bases[i] + cross, cross_rows - cross), :] = jnp.zeros(
                (cross_rows - cross, LANES), F32
            )

    def pack(group):
        even = [sum_ref[t, pl.ds(0, pairs, stride=2)] for t in group]
        odd = [sum_ref[t, pl.ds(1, pairs, stride=2)] for t in group]
        even = [x + pltpu.roll(x, 96, 1) for x in even]
        odd = [x + pltpu.roll(x, 96, 1) for x in odd]
        packed = [
            jnp.where(
                lane < 32,
                x,
                jnp.where(
                    lane < 64,
                    pltpu.roll(x, 96, 1),
                    jnp.where(lane < 96, pltpu.roll(y, 64, 1), pltpu.roll(y, 32, 1)),
                ),
            )
            for x, y in zip(even, odd)
        ]
        for t, x in zip(group, packed):
            at = pl.ds(ids_ref[t], pairs, stride=pumas)
            rows_ref[at, :] = rows_ref[at, :] + x

    def work(group):
        margin = group_sums([sum_ref[t, 0:ages] for t in group], sex0)
        for t, x in zip(group, margin):
            age_factor_ref[t, 0:ages] = age_target_ref[t, 0:ages] / x
        lax.fori_loop(group.start, group.stop, add_ages, 0)
        small_steps(group)
        lax.fori_loop(group.start, group.stop, add_scaled, 0)
        pack(group)

    before = None
    for start in range(0, tracts, GROUP):
        if before is not None:
            work(before)
        before = range(start, min(start + GROUP, tracts))
        lax.fori_loop(before.start, before.stop, arrive, 0)
    work(before)
    put_halves(rows_ref, [keep_ref], [send_ref])


def race_half(cells_ref, factor_ref, cross_factor_ref, chunk_refs, cross_ref, rows_ref, scalar_ref, half, pumas, ages):
    tracts, cross = cells_ref.shape[:2]
    cross_rows = round_up(cross + 1, 8)
    pairs = sum(ref.shape[0] for ref in chunk_refs) // pumas
    count = 2 * pairs
    stride = round_up(count, 8)
    rows_ref[...] = jnp.zeros(rows_ref.shape, F32)
    lane = lane_ids(1)

    def add_ages(t, carry):
        factor = factor_ref[t, 0:ages]
        age_sums(cells_ref, t, factor, cross_ref, t * stride, count, half * count)
        return carry

    lax.fori_loop(0, tracts, add_ages, 0)
    every = range(tracts)
    halves = []
    for first in range(2):
        margin = [
            cross_ref[pl.ds(t * stride + first, pairs, stride=2), :]
            * cross_factor_ref[pl.ds(t * cross_rows + half * count + first, pairs, stride=2), :]
            for t in every
        ]
        halves.append([x + pltpu.roll(x, 64, 1) for x in margin])
    for t in every:
        at = pl.ds(scalar_ref[t], pairs, stride=pumas)
        rows_ref[at, :] = rows_ref[at, :] + jnp.where(lane < 64, halves[0][t], halves[1][t])
    start = 0
    for ref in chunk_refs:
        ref[...] = rows_ref[start : start + ref.shape[0], :]
        start += ref.shape[0]


def race_send_kernel(
    ids_ref, cells_ref, age_factor_ref, cross_factor_ref, target_ref,
    own_ref, other_ref, *refs
):
    *chunk_refs, scaled_factor_ref, cross_ref, age_rows_ref, rows_ref, scalar_ref = refs
    ages = 2 * (target_ref.shape[1] // LANES) + target_ref.shape[1] % LANES // 64
    pairs = (ages + 1) // 2
    pumas = target_ref.shape[0]
    every = range(cells_ref.shape[0])
    load_puma_numbers(ids_ref, scalar_ref)
    factor_rows(target_ref, [own_ref], [other_ref], age_rows_ref)
    lane = lane_ids(1)
    packed = [age_rows_ref[pl.ds(scalar_ref[t], pairs, stride=pumas), :] for t in every]
    quarter = [pltpu.roll(x, 32, 1) for x in packed]
    half = [pltpu.roll(x, 64, 1) for x in packed]
    back = [pltpu.roll(x, 96, 1) for x in packed]
    for t in every:
        even = jnp.where(lane < 32, packed[t], jnp.where(lane < 96, quarter[t], half[t]))
        odd = jnp.where(lane < 32, half[t], jnp.where(lane < 96, back[t], packed[t]))
        for first, factor in enumerate((even, odd)):
            at = pl.ds(first, pairs, stride=2)
            scaled_factor_ref[t, at] = factor * age_factor_ref[t, at]
    race_half(
        cells_ref, scaled_factor_ref, cross_factor_ref, chunk_refs, cross_ref, rows_ref, scalar_ref,
        1 - half_of(lax.axis_index("tract")), pumas, ages,
    )


def race_keep_kernel(ids_ref, cells_ref, factor_ref, cross_factor_ref, *refs, ages, pumas):
    *chunk_refs, cross_ref, rows_ref, scalar_ref = refs
    load_puma_numbers(ids_ref, scalar_ref)
    race_half(
        cells_ref, factor_ref, cross_factor_ref, chunk_refs, cross_ref, rows_ref, scalar_ref,
        half_of(lax.axis_index("tract")), pumas, ages,
    )


def final_kernel(
    ids_ref, cells_ref, scaled_factor_ref, cross_factor_ref, target_ref, *refs
):
    *chunk_refs, out_ref, result_ref, cross_ref, rows_ref, scalar_ref, sems = refs
    chunks = len(chunk_refs) // 2
    tracts, cross, ages, _ = cells_ref.shape
    cross_rows = round_up(cross + 1, 8)
    cross_pairs = (cross + 1) // 2
    pumas = target_ref.shape[0]
    load_puma_numbers(ids_ref, scalar_ref)
    factor_rows(target_ref, chunk_refs[:chunks], chunk_refs[chunks:], rows_ref)
    lane = lane_ids(1)

    def unpack(t):
        base = t * cross_rows
        packed = rows_ref[pl.ds(scalar_ref[t], cross_pairs, stride=pumas), :]
        half = pltpu.roll(packed, 64, 1)
        for first, factor in enumerate(
            (jnp.where(lane < 64, packed, half), jnp.where(lane < 64, half, packed))
        ):
            at = pl.ds(base + first, cross_pairs, stride=2)
            cross_ref[at, :] = factor * cross_factor_ref[at, :]

    def scale(t):
        factor = scaled_factor_ref[t, 0:ages]
        base = t * cross_rows
        for rs in range(cross):
            result_ref[t, rs] = cells_ref[t, rs] * factor * cross_ref[pl.ds(base + rs, 1), :]

    def send(t):
        pltpu.make_async_copy(result_ref.at[t], out_ref.at[t], sems.at[t]).start()

    def step(t, carry):
        scale(t)
        unpack(t + 1)
        send(t)
        return carry

    unpack(0)
    lax.fori_loop(0, tracts - 1, step, 0)
    scale(tracts - 1)
    send(tracts - 1)
    for t in range(tracts):
        pltpu.make_async_copy(result_ref.at[t], out_ref.at[t], sems.at[t]).wait()


def call(kernel, out_shapes, in_spaces, out_spaces, scratch):
    def spec(space):
        return pl.BlockSpec(memory_space=space)

    run = pl.pallas_call(
        kernel,
        out_shape=[
            space(shape, F32) for shape, space in zip(out_shapes, out_spaces, strict=True)
        ],
        in_specs=[spec(space) for space in in_spaces],
        out_specs=[spec(space) for space in out_spaces],
        scratch_shapes=scratch,
        compiler_params=pltpu.CompilerParams(vmem_limit_bytes=40 << 20),
    )

    def placed(*args):
        return run(*map(pltpu.with_memory_space_constraint, args, in_spaces))

    return placed


def per_device(
    devices,
    table, age_sex, race_hisp, size_tenure, tenure_income, puma_age, puma_race, tract_puma,
):
    tracts, ages, races, sizes, inner = table.shape
    pumas = puma_age.shape[0]
    cross = races * sizes
    age_pairs, cross_pairs = (ages + 1) // 2, (cross + 1) // 2
    age_rows = 2 * round_up(age_pairs, 8)
    cross_rows = tracts * round_up(cross + 1, 8) + 2 * round_up(cross_pairs, 8)
    age_sum_rows, cross_sum_rows = (round_up(x, 8) * pumas for x in (age_pairs, cross_pairs))
    vmem, hbm = pltpu.VMEM, pltpu.HBM

    cells = table.transpose(0, 2, 3, 1, 4).reshape(tracts, cross, ages, inner)
    cells_scratch = pltpu.VMEM((tracts, cross, ages, inner), F32)
    cross_scratch = pltpu.VMEM((cross_rows, LANES), F32)
    copy_sems = pltpu.SemaphoreType.DMA((tracts,))
    numbers_scratch = pltpu.SMEM((tracts,), jnp.int32)

    bits = [1 << k for k in range(1, devices.bit_length() - 1)]
    orders = (bits, bits[1:] + bits[:1])

    def swap(x, partner):
        return lax.ppermute(x, "tract", [(i, partner(i)) for i in range(devices)])

    def totals(keep, send):
        keep = [x + swap(y, lambda i: i ^ 1) for x, y in zip(keep, send)]
        for step in range(len(bits)):
            keep = [x + swap(x, lambda i: i ^ orders[i.bit_count() % 2][step] ^ 1) for x in keep]
        return *keep, *[swap(x, lambda i: i ^ 1) for x in keep]

    age_half, cross_half = -(-age_pairs // 2), -(-cross_pairs // 2)
    cross_chunks = [cross_half - cross_half // 2, cross_half // 2]
    age_shape, cross_shape = (tracts, age_rows, LANES), (cross_rows, LANES)
    small = [age_sex, race_hisp, size_tenure, tenure_income]
    keep, send, age_factor, cross_factor, cells = call(
        functools.partial(rake_kernel, races=races, sizes=sizes, pumas=pumas),
        [(age_half * pumas, LANES)] * 2 + [age_shape, cross_shape, cells.shape],
        [hbm] * 6,
        [vmem] * 5,
        [
            pltpu.VMEM(age_shape, F32),
            cross_scratch,
            pltpu.VMEM((age_sum_rows, LANES), F32),
            pltpu.VMEM(age_shape, F32),
            pltpu.VMEM((tracts, round_up(races, 8), LANES), F32),
            pltpu.VMEM((tracts, round_up(sizes, 8), LANES), F32),
            numbers_scratch,
        ]
        + [pltpu.VMEM(x.shape, F32) for x in small]
        + [copy_sems, pltpu.SemaphoreType.DMA((1 + len(small),))],
    )(tract_puma, cells, *small)

    half_scratch = [
        pltpu.VMEM((tracts * round_up(2 * cross_half, 8) + 16, LANES), F32),
        pltpu.VMEM((round_up(cross_half, 8) * pumas, LANES), F32),
    ]
    chunk_shapes = [(rows * pumas, LANES) for rows in cross_chunks]
    *send, scaled_factor = call(
        race_send_kernel,
        chunk_shapes + [age_shape],
        [vmem] * 7,
        [vmem] * (len(cross_chunks) + 1),
        [half_scratch[0], pltpu.VMEM((age_sum_rows, LANES), F32), half_scratch[1], numbers_scratch],
    )(tract_puma, cells, age_factor, cross_factor, puma_age, *totals([keep], [send]))
    keep = call(
        functools.partial(race_keep_kernel, ages=ages, pumas=pumas),
        chunk_shapes,
        [vmem] * 4,
        [vmem] * len(cross_chunks),
        half_scratch + [numbers_scratch],
    )(tract_puma, cells, scaled_factor, cross_factor)

    out, = call(
        final_kernel,
        [(tracts, cross, ages, inner)],
        [vmem] * (5 + 2 * len(cross_chunks)),
        [hbm],
        [
            cells_scratch,
            cross_scratch,
            pltpu.VMEM((cross_sum_rows, LANES), F32),
            numbers_scratch,
            copy_sems,
        ],
    )(tract_puma, cells, scaled_factor, cross_factor, puma_race, *totals(keep, send))
    return out.reshape(tracts, races, sizes, ages, inner).transpose(0, 3, 1, 2, 4)


def solution(mesh):
    in_specs = (
        P(("grp", "tract"), None, None, None, None),
        P(("grp", "tract"), None),
        P(("grp", "tract"), None),
        P(("grp", "tract"), None),
        P(("grp", "tract"), None),
        P("grp", None),
        P("grp", None),
        P(("grp", "tract")),
    )
    out_specs = P(("grp", "tract"), None, None, None, None)
    return jax.shard_map(
        functools.partial(per_device, mesh.shape["tract"]),
        mesh=mesh, in_specs=in_specs, out_specs=out_specs, check_vma=False,
    )
```

```python
import functools

import jax
import jax.numpy as jnp
from jax import lax
from jax.experimental import pallas as pl
from jax.experimental.pallas import tpu as pltpu
from jax.sharding import PartitionSpec as P

LANES = 128
GROUP = 6
FIRST = 6
F32 = jnp.float32


def round_up(value, step):
    return -(-value // step) * step


def lane_ids(rows):
    return lax.broadcasted_iota(jnp.int32, (rows, LANES), 1)


def masked_lane_sum(value, mask):
    return jnp.sum(jnp.where(mask, value, 0.0), axis=-1, keepdims=True)


def column_of(row, rows, step, offset):
    width = row.shape[-1]
    lane = lax.broadcasted_iota(jnp.int32, (rows, width), 1)
    sub = lax.broadcasted_iota(jnp.int32, (rows, width), 0)
    return jnp.sum(jnp.where(lane == step * sub + offset, row, 0.0), axis=-1, keepdims=True)


def half_of(index):
    total = index
    for k in range(1, 16):
        total = total + lax.shift_right_logical(index, k)
    return lax.rem(total, 2)


def factor_rows(target_ref, own_refs, other_refs, rows_ref):
    pumas, columns = target_ref.shape
    half = half_of(lax.axis_index("tract"))
    half_rows = sum(ref.shape[0] for ref in own_refs)
    for refs, which in ((own_refs, half), (other_refs, 1 - half)):
        start = which * half_rows
        for ref in refs:
            rows_ref[pl.ds(pl.multiple_of(start, 8), ref.shape[0]), :] = ref[...]
            start = start + ref.shape[0]
    for first in range(0, columns, LANES):
        width = min(columns - first, LANES)
        at = slice(first // LANES * pumas, (first // LANES + 1) * pumas)
        rows_ref[at, 0:width] = target_ref[:, first : first + width] / rows_ref[at, 0:width]


def load_puma_numbers(ids_ref, scalar_ref):
    ids = ids_ref[...]
    for t in range(scalar_ref.shape[0]):
        scalar_ref[t] = ids[t]


def put_halves(rows_ref, keep_refs, send_refs):
    half = half_of(lax.axis_index("tract"))
    half_rows = sum(ref.shape[0] for ref in keep_refs)
    for refs, which in ((keep_refs, half), (send_refs, 1 - half)):
        start = which * half_rows
        for ref in refs:
            ref[...] = rows_ref[pl.ds(pl.multiple_of(start, 8), ref.shape[0]), :]
            start = start + ref.shape[0]


def merge(first, second, step):
    low = lax.rem(lax.broadcasted_iota(jnp.int32, (8, 1), 0) // step, 2) == 0
    if step == 4:
        return jnp.where(low, first, second) + pltpu.roll(jnp.where(low, second, first), 4, 0)
    return jnp.where(low, first + pltpu.roll(first, 8 - step, 0), second + pltpu.roll(second, step, 0))


def each(start, stop, body):
    def turn(i, carry):
        body(start + 2 * i)
        body(start + 2 * i + 1)
        return carry

    lax.fori_loop(0, (stop - start) // 2, turn, 0)
    if (stop - start) % 2:
        body(stop - 1)


def age_sums(cells_ref, factor, cross_ref, base, count):
    ages = factor.shape[0]

    def tile(k):
        total = None
        for at in range(0, ages, 8):
            stop = min(at + 8, ages)
            part = cells_ref[k, at:stop] * factor[at:stop]
            if stop < at + 8:
                part = jnp.concatenate([part, jnp.zeros((at + 8 - stop, LANES), F32)], axis=0)
            total = part if total is None else total + part
        return total

    for start in range(0, count, 8):
        tiles = [tile(k) for k in range(start, min(start + 8, count))]
        if len(tiles) < 8:
            for k, x in enumerate(tiles):
                cross_ref[pl.ds(base + start + k, 1), :] = jnp.sum(x, axis=0, keepdims=True)
            continue
        tiles = [merge(tiles[k], tiles[k + 4], 4) for k in range(4)]
        tiles = [merge(tiles[k], tiles[k + 2], 2) for k in range(2)]
        cross_ref[pl.ds(pl.multiple_of(base + start, 8), 8), :] = merge(tiles[0], tiles[1], 1)


def pair_sum(term, count):
    first, second = term(0), term(1)
    for k in range(2, count, 2):
        first = first + term(k)
        if k + 1 < count:
            second = second + term(k + 1)
    return first + second


def rake_kernel(
    ids_hbm, table_hbm, age_sex_hbm, race_hisp_hbm, size_tenure_hbm, tenure_income_hbm,
    keep_ref, send_ref, age_factor_ref, cross_factor_ref, cells_ref,
    sum_ref, cross_ref, rows_ref, age_target_ref, race_target_ref, size_target_ref,
    ids_ref, age_sex_ref, race_hisp_ref, size_tenure_ref, tenure_income_ref,
    sems, small_sems,
    *, races, sizes, pumas,
):
    tracts, cross, ages, _ = table_hbm.shape
    cross_rows = round_up(cross + 1, 8)
    pairs = (ages + 1) // 2
    small = [
        pltpu.make_async_copy(source, target, small_sems.at[i])
        for i, (source, target) in enumerate((
            (ids_hbm, ids_ref),
            (age_sex_hbm, age_sex_ref),
            (race_hisp_hbm, race_hisp_ref),
            (size_tenure_hbm, size_tenure_ref),
            (tenure_income_hbm, tenure_income_ref),
        ))
    ]

    def table_copy(t):
        return pltpu.make_async_copy(table_hbm.at[t], cells_ref.at[t, 0:cross], sems.at[t])

    for copy in small:
        copy.start()
    for t in range(min(FIRST, tracts)):
        table_copy(t).start()
    lane = lane_ids(1)
    sex0 = lane < 64
    hisp0 = (lane // 32) % 2 == 0
    ten0 = (lane // 16) % 2 == 0

    rows_ref[...] = jnp.zeros(rows_ref.shape, F32)
    for copy in small:
        copy.wait()
    for source_ref, target_ref, rows, mask in (
        (age_sex_ref, age_target_ref, ages, sex0),
        (race_hisp_ref, race_target_ref, races, hisp0),
        (size_tenure_ref, size_target_ref, sizes, ten0),
    ):
        for t in range(tracts):
            row = source_ref[t : t + 1, :]
            target_ref[t, 0:rows] = jnp.where(
                mask, column_of(row, rows, 2, 0), column_of(row, rows, 2, 1)
            )

    for t in range(FIRST, tracts):
        table_copy(t).start()

    def group_sums(values, mask):
        first = [masked_lane_sum(x, mask) for x in values]
        second = [masked_lane_sum(x, ~mask) for x in values]
        return [jnp.where(mask, x, y) for x, y in zip(first, second)]

    def arrive(t, carry):
        table_copy(t).wait()
        sum_ref[t, 0:ages] = pair_sum(lambda rs: cells_ref[t, rs], cross)
        return carry

    def add_ages(t):
        age_sums(cells_ref.at[t], age_factor_ref[t, 0:ages], cross_ref, t * cross_rows, cross)

    def add_scaled(t):
        base = t * cross_rows
        total = pair_sum(
            lambda rs: cells_ref[t, rs] * cross_factor_ref[pl.ds(base + rs, 1), :], cross
        )
        sum_ref[t, 0:ages] = total * age_factor_ref[t, 0:ages]
        sum_ref[t, ages : 2 * pairs] = jnp.zeros((2 * pairs - ages, LANES), F32)

    def small_steps(group):
        bases = [t * cross_rows for t in group]
        by_race = [
            sum(cross_ref[pl.ds(base + s, races, stride=sizes), :] for s in range(sizes))
            for base in bases
        ]
        race_factor = [
            race_target_ref[t, 0:races] / margin for t, margin in zip(group, group_sums(by_race, hisp0))
        ]
        by_size = [
            sum(
                cross_ref[pl.ds(base + r * sizes, sizes), :] * factor[r : r + 1]
                for r in range(races)
            )
            for base, factor in zip(bases, race_factor)
        ]
        size_factor = [
            size_target_ref[t, 0:sizes] / margin for t, margin in zip(group, group_sums(by_size, ten0))
        ]
        by_income = [jnp.sum(x * y, axis=0, keepdims=True) for x, y in zip(by_size, size_factor)]
        by_income = [x + pltpu.roll(x, 64, 1) for x in by_income]
        by_income = [x + pltpu.roll(x, 32, 1) for x in by_income]
        for i, t in enumerate(group):
            target = jnp.concatenate([tenure_income_ref[t : t + 1, :]] * 4, axis=1)
            age_factor_ref[t, 0:ages] = age_factor_ref[t, 0:ages] * (target / by_income[i])
            for r in range(races):
                cross_factor_ref[pl.ds(bases[i] + r * sizes, sizes), :] = (
                    size_factor[i] * race_factor[i][r : r + 1]
                )
            cross_factor_ref[pl.ds(bases[i] + cross, cross_rows - cross), :] = jnp.zeros(
                (cross_rows - cross, LANES), F32
            )

    def pack(group):
        even = [sum_ref[t, pl.ds(0, pairs, stride=2)] for t in group]
        odd = [sum_ref[t, pl.ds(1, pairs, stride=2)] for t in group]
        even = [x + pltpu.roll(x, 96, 1) for x in even]
        odd = [x + pltpu.roll(x, 96, 1) for x in odd]
        packed = [
            jnp.where(
                lane < 32,
                x,
                jnp.where(
                    lane < 64,
                    pltpu.roll(x, 96, 1),
                    jnp.where(lane < 96, pltpu.roll(y, 64, 1), pltpu.roll(y, 32, 1)),
                ),
            )
            for x, y in zip(even, odd)
        ]
        for t, x in zip(group, packed):
            at = pl.ds(ids_ref[t], pairs, stride=pumas)
            rows_ref[at, :] = rows_ref[at, :] + x

    def work(group):
        margin = group_sums([sum_ref[t, 0:ages] for t in group], sex0)
        for t, x in zip(group, margin):
            age_factor_ref[t, 0:ages] = age_target_ref[t, 0:ages] / x
        each(group.start, group.stop, add_ages)
        small_steps(group)
        each(group.start, group.stop, add_scaled)
        pack(group)

    before = None
    for start in range(0, tracts, GROUP):
        if before is not None:
            work(before)
        before = range(start, min(start + GROUP, tracts))
        lax.fori_loop(before.start, before.stop, arrive, 0)
    work(before)
    put_halves(rows_ref, [keep_ref], [send_ref])


def race_half(cells_ref, factor_ref, cross_factor_ref, chunk_refs, cross_ref, rows_ref, scalar_ref, half, pumas, ages, cross):
    tracts = cells_ref.shape[0]
    cross_rows = round_up(cross + 1, 8)
    pairs = sum(ref.shape[0] for ref in chunk_refs) // pumas
    count = 2 * pairs
    stride = round_up(count, 8)
    rows_ref[...] = jnp.zeros(rows_ref.shape, F32)
    lane = lane_ids(1)

    def add_ages(t):
        factor = factor_ref[t, 0:ages]
        cells = cells_ref.at[t, pl.ds(half * count, count)]
        age_sums(cells, factor, cross_ref, t * stride, count)

    each(0, tracts, add_ages)
    every = range(tracts)
    halves = []
    for first in range(2):
        margin = [
            cross_ref[pl.ds(t * stride + first, pairs, stride=2), :]
            * cross_factor_ref[pl.ds(t * cross_rows + half * count + first, pairs, stride=2), :]
            for t in every
        ]
        halves.append([x + pltpu.roll(x, 64, 1) for x in margin])
    for t in every:
        at = pl.ds(scalar_ref[t], pairs, stride=pumas)
        rows_ref[at, :] = rows_ref[at, :] + jnp.where(lane < 64, halves[0][t], halves[1][t])
    start = 0
    for ref in chunk_refs:
        ref[...] = rows_ref[start : start + ref.shape[0], :]
        start += ref.shape[0]


def race_send_kernel(
    ids_ref, cells_ref, age_factor_ref, cross_factor_ref, target_ref,
    own_ref, other_ref, *refs, cross
):
    *chunk_refs, scaled_factor_ref, cross_ref, age_rows_ref, rows_ref, scalar_ref = refs
    ages = 2 * (target_ref.shape[1] // LANES) + target_ref.shape[1] % LANES // 64
    pairs = (ages + 1) // 2
    pumas = target_ref.shape[0]
    every = range(cells_ref.shape[0])
    load_puma_numbers(ids_ref, scalar_ref)
    factor_rows(target_ref, [own_ref], [other_ref], age_rows_ref)
    lane = lane_ids(1)
    packed = [age_rows_ref[pl.ds(scalar_ref[t], pairs, stride=pumas), :] for t in every]
    quarter = [pltpu.roll(x, 32, 1) for x in packed]
    half = [pltpu.roll(x, 64, 1) for x in packed]
    back = [pltpu.roll(x, 96, 1) for x in packed]
    for t in every:
        even = jnp.where(lane < 32, packed[t], jnp.where(lane < 96, quarter[t], half[t]))
        odd = jnp.where(lane < 32, half[t], jnp.where(lane < 96, back[t], packed[t]))
        for first, factor in enumerate((even, odd)):
            at = pl.ds(first, pairs, stride=2)
            scaled_factor_ref[t, at] = factor * age_factor_ref[t, at]
    race_half(
        cells_ref, scaled_factor_ref, cross_factor_ref, chunk_refs, cross_ref, rows_ref, scalar_ref,
        1 - half_of(lax.axis_index("tract")), pumas, ages, cross,
    )


def race_keep_kernel(ids_ref, cells_ref, factor_ref, cross_factor_ref, *refs, ages, pumas, cross):
    *chunk_refs, cross_ref, rows_ref, scalar_ref = refs
    load_puma_numbers(ids_ref, scalar_ref)
    race_half(
        cells_ref, factor_ref, cross_factor_ref, chunk_refs, cross_ref, rows_ref, scalar_ref,
        half_of(lax.axis_index("tract")), pumas, ages, cross,
    )


def final_kernel(
    ids_ref, cells_ref, scaled_factor_ref, cross_factor_ref, target_ref, *refs
):
    *chunk_refs, out_ref, result_ref, cross_ref, rows_ref, scalar_ref, sems = refs
    chunks = len(chunk_refs) // 2
    tracts, cross, ages, _ = out_ref.shape
    cross_rows = round_up(cross + 1, 8)
    cross_pairs = (cross + 1) // 2
    pumas = target_ref.shape[0]
    load_puma_numbers(ids_ref, scalar_ref)
    factor_rows(target_ref, chunk_refs[:chunks], chunk_refs[chunks:], rows_ref)
    lane = lane_ids(1)

    def unpack(t):
        base = t * cross_rows
        packed = rows_ref[pl.ds(scalar_ref[t], cross_pairs, stride=pumas), :]
        half = pltpu.roll(packed, 64, 1)
        for first, factor in enumerate(
            (jnp.where(lane < 64, packed, half), jnp.where(lane < 64, half, packed))
        ):
            at = pl.ds(base + first, cross_pairs, stride=2)
            cross_ref[at, :] = factor * cross_factor_ref[at, :]

    def scale(t):
        factor = scaled_factor_ref[t, 0:ages]
        base = t * cross_rows
        for rs in range(cross):
            result_ref[t, rs] = cells_ref[t, rs] * factor * cross_ref[pl.ds(base + rs, 1), :]

    def send(t):
        pltpu.make_async_copy(result_ref.at[t], out_ref.at[t], sems.at[t]).start()

    def step(t, carry):
        scale(t)
        unpack(t + 1)
        send(t)
        return carry

    unpack(0)
    lax.fori_loop(0, tracts - 1, step, 0)
    scale(tracts - 1)
    send(tracts - 1)
    for t in range(tracts):
        pltpu.make_async_copy(result_ref.at[t], out_ref.at[t], sems.at[t]).wait()


def call(kernel, out_shapes, in_spaces, out_spaces, scratch):
    def spec(space):
        return pl.BlockSpec(memory_space=space)

    run = pl.pallas_call(
        kernel,
        out_shape=[
            space(shape, F32) for shape, space in zip(out_shapes, out_spaces, strict=True)
        ],
        in_specs=[spec(space) for space in in_spaces],
        out_specs=[spec(space) for space in out_spaces],
        scratch_shapes=scratch,
        compiler_params=pltpu.CompilerParams(vmem_limit_bytes=40 << 20),
    )

    def placed(*args):
        return run(*map(pltpu.with_memory_space_constraint, args, in_spaces))

    return placed


def per_device(
    devices,
    table, age_sex, race_hisp, size_tenure, tenure_income, puma_age, puma_race, tract_puma,
):
    tracts, ages, races, sizes, inner = table.shape
    pumas = puma_age.shape[0]
    cross = races * sizes
    age_pairs, cross_pairs = (ages + 1) // 2, (cross + 1) // 2
    age_rows = 2 * round_up(age_pairs, 8)
    cross_rows = tracts * round_up(cross + 1, 8) + 2 * round_up(cross_pairs, 8)
    age_sum_rows, cross_sum_rows = (round_up(x, 8) * pumas for x in (age_pairs, cross_pairs))
    vmem, hbm = pltpu.VMEM, pltpu.HBM

    cells = table.transpose(0, 2, 3, 1, 4).reshape(tracts, cross, ages, inner)
    cells_scratch = pltpu.VMEM((tracts, cross, ages, inner), F32)
    cross_scratch = pltpu.VMEM((cross_rows, LANES), F32)
    copy_sems = pltpu.SemaphoreType.DMA((tracts,))
    numbers_scratch = pltpu.SMEM((tracts,), jnp.int32)

    bits = [1 << k for k in range(1, devices.bit_length() - 1)]
    orders = (bits, bits[1:] + bits[:1])

    def swap(x, partner):
        return lax.ppermute(x, "tract", [(i, partner(i)) for i in range(devices)])

    def totals(keep, send):
        keep = [x + swap(y, lambda i: i ^ 1) for x, y in zip(keep, send)]
        for step in range(len(bits)):
            keep = [x + swap(x, lambda i: i ^ orders[i.bit_count() % 2][step] ^ 1) for x in keep]
        return *keep, *[swap(x, lambda i: i ^ 1) for x in keep]

    age_half, cross_half = -(-age_pairs // 2), -(-cross_pairs // 2)
    cross_chunks = [cross_half - cross_half // 2, cross_half // 2]
    age_shape, cross_shape = (tracts, age_rows, LANES), (cross_rows, LANES)
    small = [age_sex, race_hisp, size_tenure, tenure_income]
    keep, send, age_factor, cross_factor, cells = call(
        functools.partial(rake_kernel, races=races, sizes=sizes, pumas=pumas),
        [(age_half * pumas, LANES)] * 2
        + [age_shape, cross_shape, (tracts, 4 * cross_half, ages, inner)],
        [hbm] * 6,
        [vmem] * 5,
        [
            pltpu.VMEM(age_shape, F32),
            cross_scratch,
            pltpu.VMEM((age_sum_rows, LANES), F32),
            pltpu.VMEM(age_shape, F32),
            pltpu.VMEM((tracts, round_up(races, 8), LANES), F32),
            pltpu.VMEM((tracts, round_up(sizes, 8), LANES), F32),
            numbers_scratch,
        ]
        + [pltpu.VMEM(x.shape, F32) for x in small]
        + [copy_sems, pltpu.SemaphoreType.DMA((1 + len(small),))],
    )(tract_puma, cells, *small)

    half_scratch = [
        pltpu.VMEM((tracts * round_up(2 * cross_half, 8) + 16, LANES), F32),
        pltpu.VMEM((round_up(cross_half, 8) * pumas, LANES), F32),
    ]
    chunk_shapes = [(rows * pumas, LANES) for rows in cross_chunks]
    *send, scaled_factor = call(
        functools.partial(race_send_kernel, cross=cross),
        chunk_shapes + [age_shape],
        [vmem] * 7,
        [vmem] * (len(cross_chunks) + 1),
        [half_scratch[0], pltpu.VMEM((age_sum_rows, LANES), F32), half_scratch[1], numbers_scratch],
    )(tract_puma, cells, age_factor, cross_factor, puma_age, *totals([keep], [send]))
    keep = call(
        functools.partial(race_keep_kernel, ages=ages, pumas=pumas, cross=cross),
        chunk_shapes,
        [vmem] * 4,
        [vmem] * len(cross_chunks),
        half_scratch + [numbers_scratch],
    )(tract_puma, cells, scaled_factor, cross_factor)

    out, = call(
        final_kernel,
        [(tracts, cross, ages, inner)],
        [vmem] * (5 + 2 * len(cross_chunks)),
        [hbm],
        [
            cells_scratch,
            cross_scratch,
            pltpu.VMEM((cross_sum_rows, LANES), F32),
            numbers_scratch,
            copy_sems,
        ],
    )(tract_puma, cells, scaled_factor, cross_factor, puma_race, *totals(keep, send))
    return out.reshape(tracts, races, sizes, ages, inner).transpose(0, 3, 1, 2, 4)


def solution(mesh):
    in_specs = (
        P(("grp", "tract"), None, None, None, None),
        P(("grp", "tract"), None),
        P(("grp", "tract"), None),
        P(("grp", "tract"), None),
        P(("grp", "tract"), None),
        P("grp", None),
        P("grp", None),
        P(("grp", "tract")),
    )
    out_specs = P(("grp", "tract"), None, None, None, None)
    return jax.shard_map(
        functools.partial(per_device, mesh.shape["tract"]),
        mesh=mesh, in_specs=in_specs, out_specs=out_specs, check_vma=False,
    )
```

```python
import functools

import jax
import jax.numpy as jnp
from jax import lax
from jax.experimental import pallas as pl
from jax.experimental.pallas import tpu as pltpu
from jax.sharding import PartitionSpec as P

LANES = 128
GROUP = 6
F32 = jnp.float32


def round_up(value, step):
    return -(-value // step) * step


def lane_ids(rows):
    return lax.broadcasted_iota(jnp.int32, (rows, LANES), 1)


def masked_lane_sum(value, mask):
    return jnp.sum(jnp.where(mask, value, 0.0), axis=-1, keepdims=True)


def column_of(row, rows, step, offset):
    width = row.shape[-1]
    lane = lax.broadcasted_iota(jnp.int32, (rows, width), 1)
    sub = lax.broadcasted_iota(jnp.int32, (rows, width), 0)
    return jnp.sum(jnp.where(lane == step * sub + offset, row, 0.0), axis=-1, keepdims=True)


def half_of(index):
    total = index
    for k in range(1, 16):
        total = total + lax.shift_right_logical(index, k)
    return lax.rem(total, 2)


def factor_rows(target_ref, own_refs, other_refs, rows_ref):
    pumas, columns = target_ref.shape
    half = half_of(lax.axis_index("tract"))
    half_rows = sum(ref.shape[0] for ref in own_refs)
    for refs, which in ((own_refs, half), (other_refs, 1 - half)):
        start = which * half_rows
        for ref in refs:
            rows_ref[pl.ds(pl.multiple_of(start, 8), ref.shape[0]), :] = ref[...]
            start = start + ref.shape[0]
    for first in range(0, columns, LANES):
        width = min(columns - first, LANES)
        at = slice(first // LANES * pumas, (first // LANES + 1) * pumas)
        rows_ref[at, 0:width] = target_ref[:, first : first + width] / rows_ref[at, 0:width]


def load_puma_numbers(ids_ref, scalar_ref):
    ids = ids_ref[...]
    for t in range(scalar_ref.shape[0]):
        scalar_ref[t] = ids[t]


def put_halves(rows_ref, keep_refs, send_refs):
    half = half_of(lax.axis_index("tract"))
    half_rows = sum(ref.shape[0] for ref in keep_refs)
    for refs, which in ((keep_refs, half), (send_refs, 1 - half)):
        start = which * half_rows
        for ref in refs:
            ref[...] = rows_ref[pl.ds(pl.multiple_of(start, 8), ref.shape[0]), :]
            start = start + ref.shape[0]


def merge(first, second, step):
    low = lax.rem(lax.broadcasted_iota(jnp.int32, (8, 1), 0) // step, 2) == 0
    if step == 4:
        return jnp.where(low, first, second) + pltpu.roll(jnp.where(low, second, first), 4, 0)
    return jnp.where(low, first + pltpu.roll(first, 8 - step, 0), second + pltpu.roll(second, step, 0))


def each(start, stop, body):
    def turn(i, carry):
        body(start + 2 * i)
        body(start + 2 * i + 1)
        return carry

    lax.fori_loop(0, (stop - start) // 2, turn, 0)
    if (stop - start) % 2:
        body(stop - 1)


def age_sums(cells_ref, factor, cross_ref, base, count):
    ages = factor.shape[0]

    def tile(k):
        total = None
        for at in range(0, ages, 8):
            stop = min(at + 8, ages)
            part = cells_ref[k, at:stop] * factor[at:stop]
            if stop < at + 8:
                part = jnp.concatenate([part, jnp.zeros((at + 8 - stop, LANES), F32)], axis=0)
            total = part if total is None else total + part
        return total

    for start in range(0, count, 8):
        tiles = [tile(k) for k in range(start, min(start + 8, count))]
        if len(tiles) < 8:
            for k, x in enumerate(tiles):
                cross_ref[pl.ds(base + start + k, 1), :] = jnp.sum(x, axis=0, keepdims=True)
            continue
        tiles = [merge(tiles[k], tiles[k + 4], 4) for k in range(4)]
        tiles = [merge(tiles[k], tiles[k + 2], 2) for k in range(2)]
        cross_ref[pl.ds(pl.multiple_of(base + start, 8), 8), :] = merge(tiles[0], tiles[1], 1)


def pair_sum(term, count):
    first, second = term(0), term(1)
    for k in range(2, count, 2):
        first = first + term(k)
        if k + 1 < count:
            second = second + term(k + 1)
    return first + second


def rake_kernel(
    ids_hbm, table_hbm, age_sex_hbm, race_hisp_hbm, size_tenure_hbm, tenure_income_hbm,
    keep_ref, send_ref, age_factor_ref, cross_factor_ref, cells_ref,
    sum_ref, cross_ref, rows_ref, age_target_ref, race_target_ref, size_target_ref,
    ids_ref, age_sex_ref, race_hisp_ref, size_tenure_ref, tenure_income_ref,
    sems, small_sems,
    *, races, sizes, pumas,
):
    tracts, cross, ages, _ = table_hbm.shape
    cross_rows = round_up(cross + 1, 8)
    pairs = (ages + 1) // 2
    small = [
        pltpu.make_async_copy(source, target, small_sems.at[i])
        for i, (source, target) in enumerate((
            (ids_hbm, ids_ref),
            (age_sex_hbm, age_sex_ref),
            (race_hisp_hbm, race_hisp_ref),
            (size_tenure_hbm, size_tenure_ref),
            (tenure_income_hbm, tenure_income_ref),
        ))
    ]

    def table_copy(t):
        return pltpu.make_async_copy(table_hbm.at[t], cells_ref.at[t, 0:cross], sems.at[t])

    for copy in small:
        copy.start()
    for t in range(tracts):
        table_copy(t).start(priority=1 if t < GROUP else 0)
    lane = lane_ids(1)
    sex0 = lane < 64
    hisp0 = (lane // 32) % 2 == 0
    ten0 = (lane // 16) % 2 == 0

    rows_ref[...] = jnp.zeros(rows_ref.shape, F32)
    for copy in small:
        copy.wait()
    for source_ref, target_ref, rows, mask in (
        (age_sex_ref, age_target_ref, ages, sex0),
        (race_hisp_ref, race_target_ref, races, hisp0),
        (size_tenure_ref, size_target_ref, sizes, ten0),
    ):
        for t in range(tracts):
            row = source_ref[t : t + 1, :]
            target_ref[t, 0:rows] = jnp.where(
                mask, column_of(row, rows, 2, 0), column_of(row, rows, 2, 1)
            )

    def group_sums(values, mask):
        first = [masked_lane_sum(x, mask) for x in values]
        second = [masked_lane_sum(x, ~mask) for x in values]
        return [jnp.where(mask, x, y) for x, y in zip(first, second)]

    def arrive(t, carry):
        table_copy(t).wait()
        sum_ref[t, 0:ages] = pair_sum(lambda rs: cells_ref[t, rs], cross)
        return carry

    def add_ages(t):
        age_sums(cells_ref.at[t], age_factor_ref[t, 0:ages], cross_ref, t * cross_rows, cross)

    def add_scaled(t):
        base = t * cross_rows
        total = pair_sum(
            lambda rs: cells_ref[t, rs] * cross_factor_ref[pl.ds(base + rs, 1), :], cross
        )
        sum_ref[t, 0:ages] = total * age_factor_ref[t, 0:ages]
        sum_ref[t, ages : 2 * pairs] = jnp.zeros((2 * pairs - ages, LANES), F32)

    def small_steps(group):
        bases = [t * cross_rows for t in group]
        by_race = [
            sum(cross_ref[pl.ds(base + s, races, stride=sizes), :] for s in range(sizes))
            for base in bases
        ]
        race_factor = [
            race_target_ref[t, 0:races] / margin for t, margin in zip(group, group_sums(by_race, hisp0))
        ]
        by_size = [
            sum(
                cross_ref[pl.ds(base + r * sizes, sizes), :] * factor[r : r + 1]
                for r in range(races)
            )
            for base, factor in zip(bases, race_factor)
        ]
        size_factor = [
            size_target_ref[t, 0:sizes] / margin for t, margin in zip(group, group_sums(by_size, ten0))
        ]
        by_income = [jnp.sum(x * y, axis=0, keepdims=True) for x, y in zip(by_size, size_factor)]
        by_income = [x + pltpu.roll(x, 64, 1) for x in by_income]
        by_income = [x + pltpu.roll(x, 32, 1) for x in by_income]
        for i, t in enumerate(group):
            target = jnp.concatenate([tenure_income_ref[t : t + 1, :]] * 4, axis=1)
            age_factor_ref[t, 0:ages] = age_factor_ref[t, 0:ages] * (target / by_income[i])
            for r in range(races):
                cross_factor_ref[pl.ds(bases[i] + r * sizes, sizes), :] = (
                    size_factor[i] * race_factor[i][r : r + 1]
                )
            cross_factor_ref[pl.ds(bases[i] + cross, cross_rows - cross), :] = jnp.zeros(
                (cross_rows - cross, LANES), F32
            )

    def pack(group):
        even = [sum_ref[t, pl.ds(0, pairs, stride=2)] for t in group]
        odd = [sum_ref[t, pl.ds(1, pairs, stride=2)] for t in group]
        even = [x + pltpu.roll(x, 96, 1) for x in even]
        odd = [x + pltpu.roll(x, 96, 1) for x in odd]
        packed = [
            jnp.where(
                lane < 32,
                x,
                jnp.where(
                    lane < 64,
                    pltpu.roll(x, 96, 1),
                    jnp.where(lane < 96, pltpu.roll(y, 64, 1), pltpu.roll(y, 32, 1)),
                ),
            )
            for x, y in zip(even, odd)
        ]
        for t, x in zip(group, packed):
            at = pl.ds(ids_ref[t], pairs, stride=pumas)
            rows_ref[at, :] = rows_ref[at, :] + x

    def work(group):
        margin = group_sums([sum_ref[t, 0:ages] for t in group], sex0)
        for t, x in zip(group, margin):
            age_factor_ref[t, 0:ages] = age_target_ref[t, 0:ages] / x
        each(group.start, group.stop, add_ages)
        small_steps(group)
        each(group.start, group.stop, add_scaled)
        pack(group)

    before = None
    for start in range(0, tracts, GROUP):
        if before is not None:
            work(before)
        before = range(start, min(start + GROUP, tracts))
        lax.fori_loop(before.start, before.stop, arrive, 0)
    work(before)
    put_halves(rows_ref, [keep_ref], [send_ref])


def race_half(cells_ref, factor_ref, cross_factor_ref, chunk_refs, cross_ref, rows_ref, scalar_ref, half, pumas, ages, cross):
    tracts = cells_ref.shape[0]
    cross_rows = round_up(cross + 1, 8)
    pairs = sum(ref.shape[0] for ref in chunk_refs) // pumas
    count = 2 * pairs
    stride = round_up(count, 8)
    rows_ref[...] = jnp.zeros(rows_ref.shape, F32)
    lane = lane_ids(1)

    def add_ages(t):
        factor = factor_ref[t, 0:ages]
        cells = cells_ref.at[t, pl.ds(half * count, count)]
        age_sums(cells, factor, cross_ref, t * stride, count)

    each(0, tracts, add_ages)
    every = range(tracts)
    halves = []
    for first in range(2):
        margin = [
            cross_ref[pl.ds(t * stride + first, pairs, stride=2), :]
            * cross_factor_ref[pl.ds(t * cross_rows + half * count + first, pairs, stride=2), :]
            for t in every
        ]
        halves.append([x + pltpu.roll(x, 64, 1) for x in margin])
    for t in every:
        at = pl.ds(scalar_ref[t], pairs, stride=pumas)
        rows_ref[at, :] = rows_ref[at, :] + jnp.where(lane < 64, halves[0][t], halves[1][t])
    start = 0
    for ref in chunk_refs:
        ref[...] = rows_ref[start : start + ref.shape[0], :]
        start += ref.shape[0]


def race_send_kernel(
    ids_ref, cells_ref, age_factor_ref, cross_factor_ref, target_ref,
    own_ref, other_ref, *refs, cross
):
    *chunk_refs, scaled_factor_ref, cross_ref, age_rows_ref, rows_ref, scalar_ref = refs
    ages = 2 * (target_ref.shape[1] // LANES) + target_ref.shape[1] % LANES // 64
    pairs = (ages + 1) // 2
    pumas = target_ref.shape[0]
    every = range(cells_ref.shape[0])
    load_puma_numbers(ids_ref, scalar_ref)
    factor_rows(target_ref, [own_ref], [other_ref], age_rows_ref)
    lane = lane_ids(1)
    packed = [age_rows_ref[pl.ds(scalar_ref[t], pairs, stride=pumas), :] for t in every]
    quarter = [pltpu.roll(x, 32, 1) for x in packed]
    half = [pltpu.roll(x, 64, 1) for x in packed]
    back = [pltpu.roll(x, 96, 1) for x in packed]
    for t in every:
        even = jnp.where(lane < 32, packed[t], jnp.where(lane < 96, quarter[t], half[t]))
        odd = jnp.where(lane < 32, half[t], jnp.where(lane < 96, back[t], packed[t]))
        for first, factor in enumerate((even, odd)):
            at = pl.ds(first, pairs, stride=2)
            scaled_factor_ref[t, at] = factor * age_factor_ref[t, at]
    race_half(
        cells_ref, scaled_factor_ref, cross_factor_ref, chunk_refs, cross_ref, rows_ref, scalar_ref,
        1 - half_of(lax.axis_index("tract")), pumas, ages, cross,
    )


def race_keep_kernel(ids_ref, cells_ref, factor_ref, cross_factor_ref, *refs, ages, pumas, cross):
    *chunk_refs, cross_ref, rows_ref, scalar_ref = refs
    load_puma_numbers(ids_ref, scalar_ref)
    race_half(
        cells_ref, factor_ref, cross_factor_ref, chunk_refs, cross_ref, rows_ref, scalar_ref,
        half_of(lax.axis_index("tract")), pumas, ages, cross,
    )


def final_kernel(
    ids_ref, cells_ref, scaled_factor_ref, cross_factor_ref, target_ref, *refs
):
    *chunk_refs, out_ref, result_ref, cross_ref, rows_ref, scalar_ref, sems = refs
    chunks = len(chunk_refs) // 2
    tracts, cross, ages, _ = out_ref.shape
    cross_rows = round_up(cross + 1, 8)
    cross_pairs = (cross + 1) // 2
    pumas = target_ref.shape[0]
    load_puma_numbers(ids_ref, scalar_ref)
    factor_rows(target_ref, chunk_refs[:chunks], chunk_refs[chunks:], rows_ref)
    lane = lane_ids(1)

    def unpack(t):
        base = t * cross_rows
        packed = rows_ref[pl.ds(scalar_ref[t], cross_pairs, stride=pumas), :]
        half = pltpu.roll(packed, 64, 1)
        for first, factor in enumerate(
            (jnp.where(lane < 64, packed, half), jnp.where(lane < 64, half, packed))
        ):
            at = pl.ds(base + first, cross_pairs, stride=2)
            cross_ref[at, :] = factor * cross_factor_ref[at, :]

    def scale(t):
        factor = scaled_factor_ref[t, 0:ages]
        base = t * cross_rows
        for rs in range(cross):
            result_ref[t, rs] = cells_ref[t, rs] * factor * cross_ref[pl.ds(base + rs, 1), :]

    def send(t, priority):
        pltpu.make_async_copy(result_ref.at[t], out_ref.at[t], sems.at[t]).start(priority=priority)

    def step(i, carry):
        for k in range(2):
            t = 2 * i + k
            scale(t)
            unpack(lax.min(t + 1, tracts - 1))
            send(t, k)
        return carry

    unpack(0)
    lax.fori_loop(0, tracts // 2, step, 0)
    if tracts % 2:
        scale(tracts - 1)
        send(tracts - 1, 0)
    for t in range(tracts):
        pltpu.make_async_copy(result_ref.at[t], out_ref.at[t], sems.at[t]).wait()


def call(kernel, out_shapes, in_spaces, out_spaces, scratch):
    def spec(space):
        return pl.BlockSpec(memory_space=space)

    run = pl.pallas_call(
        kernel,
        out_shape=[
            space(shape, F32) for shape, space in zip(out_shapes, out_spaces, strict=True)
        ],
        in_specs=[spec(space) for space in in_spaces],
        out_specs=[spec(space) for space in out_spaces],
        scratch_shapes=scratch,
        compiler_params=pltpu.CompilerParams(vmem_limit_bytes=40 << 20),
    )

    def placed(*args):
        return run(*map(pltpu.with_memory_space_constraint, args, in_spaces))

    return placed


def per_device(
    devices,
    table, age_sex, race_hisp, size_tenure, tenure_income, puma_age, puma_race, tract_puma,
):
    tracts, ages, races, sizes, inner = table.shape
    pumas = puma_age.shape[0]
    cross = races * sizes
    age_pairs, cross_pairs = (ages + 1) // 2, (cross + 1) // 2
    age_rows = 2 * round_up(age_pairs, 8)
    cross_rows = tracts * round_up(cross + 1, 8) + 2 * round_up(cross_pairs, 8)
    age_sum_rows, cross_sum_rows = (round_up(x, 8) * pumas for x in (age_pairs, cross_pairs))
    vmem, hbm = pltpu.VMEM, pltpu.HBM

    cells = table.transpose(0, 2, 3, 1, 4).reshape(tracts, cross, ages, inner)
    cells_scratch = pltpu.VMEM((tracts, cross, ages, inner), F32)
    cross_scratch = pltpu.VMEM((cross_rows, LANES), F32)
    copy_sems = pltpu.SemaphoreType.DMA((tracts,))
    numbers_scratch = pltpu.SMEM((tracts,), jnp.int32)

    bits = [1 << k for k in range(1, devices.bit_length() - 1)]
    orders = (bits, bits[1:] + bits[:1])

    def swap(x, partner):
        return lax.ppermute(x, "tract", [(i, partner(i)) for i in range(devices)])

    def totals(keep, send):
        keep = [x + swap(y, lambda i: i ^ 1) for x, y in zip(keep, send)]
        for step in range(len(bits)):
            keep = [x + swap(x, lambda i: i ^ orders[i.bit_count() % 2][step] ^ 1) for x in keep]
        return *keep, *[swap(x, lambda i: i ^ 1) for x in keep]

    age_half, cross_half = -(-age_pairs // 2), -(-cross_pairs // 2)
    cross_chunks = [cross_half - cross_half // 2, cross_half // 2]
    age_shape, cross_shape = (tracts, age_rows, LANES), (cross_rows, LANES)
    small = [age_sex, race_hisp, size_tenure, tenure_income]
    keep, send, age_factor, cross_factor, cells = call(
        functools.partial(rake_kernel, races=races, sizes=sizes, pumas=pumas),
        [(age_half * pumas, LANES)] * 2
        + [age_shape, cross_shape, (tracts, 4 * cross_half, ages, inner)],
        [hbm] * 6,
        [vmem] * 5,
        [
            pltpu.VMEM(age_shape, F32),
            cross_scratch,
            pltpu.VMEM((age_sum_rows, LANES), F32),
            pltpu.VMEM(age_shape, F32),
            pltpu.VMEM((tracts, round_up(races, 8), LANES), F32),
            pltpu.VMEM((tracts, round_up(sizes, 8), LANES), F32),
            numbers_scratch,
        ]
        + [pltpu.VMEM(x.shape, F32) for x in small]
        + [copy_sems, pltpu.SemaphoreType.DMA((1 + len(small),))],
    )(tract_puma, cells, *small)

    half_scratch = [
        pltpu.VMEM((tracts * round_up(2 * cross_half, 8) + 16, LANES), F32),
        pltpu.VMEM((round_up(cross_half, 8) * pumas, LANES), F32),
    ]
    chunk_shapes = [(rows * pumas, LANES) for rows in cross_chunks]
    *send, scaled_factor = call(
        functools.partial(race_send_kernel, cross=cross),
        chunk_shapes + [age_shape],
        [vmem] * 7,
        [vmem] * (len(cross_chunks) + 1),
        [half_scratch[0], pltpu.VMEM((age_sum_rows, LANES), F32), half_scratch[1], numbers_scratch],
    )(tract_puma, cells, age_factor, cross_factor, puma_age, *totals([keep], [send]))
    keep = call(
        functools.partial(race_keep_kernel, ages=ages, pumas=pumas, cross=cross),
        chunk_shapes,
        [vmem] * 4,
        [vmem] * len(cross_chunks),
        half_scratch + [numbers_scratch],
    )(tract_puma, cells, scaled_factor, cross_factor)

    out, = call(
        final_kernel,
        [(tracts, cross, ages, inner)],
        [vmem] * (5 + 2 * len(cross_chunks)),
        [hbm],
        [
            cells_scratch,
            cross_scratch,
            pltpu.VMEM((cross_sum_rows, LANES), F32),
            numbers_scratch,
            copy_sems,
        ],
    )(tract_puma, cells, scaled_factor, cross_factor, puma_race, *totals(keep, send))
    return out.reshape(tracts, races, sizes, ages, inner).transpose(0, 3, 1, 2, 4)


def solution(mesh):
    in_specs = (
        P(("grp", "tract"), None, None, None, None),
        P(("grp", "tract"), None),
        P(("grp", "tract"), None),
        P(("grp", "tract"), None),
        P(("grp", "tract"), None),
        P("grp", None),
        P("grp", None),
        P(("grp", "tract")),
    )
    out_specs = P(("grp", "tract"), None, None, None, None)
    return jax.shard_map(
        functools.partial(per_device, mesh.shape["tract"]),
        mesh=mesh, in_specs=in_specs, out_specs=out_specs, check_vma=False,
    )
```

```python
import functools

import jax
import jax.numpy as jnp
from jax import lax
from jax.experimental import pallas as pl
from jax.experimental.pallas import tpu as pltpu
from jax.sharding import PartitionSpec as P

LANES = 128
GROUP = 6
F32 = jnp.float32


def round_up(value, step):
    return -(-value // step) * step


def lane_ids(rows):
    return lax.broadcasted_iota(jnp.int32, (rows, LANES), 1)


def masked_lane_sum(value, mask):
    return jnp.sum(jnp.where(mask, value, 0.0), axis=-1, keepdims=True)


def column_of(row, rows, step, offset):
    width = row.shape[-1]
    lane = lax.broadcasted_iota(jnp.int32, (rows, width), 1)
    sub = lax.broadcasted_iota(jnp.int32, (rows, width), 0)
    return jnp.sum(jnp.where(lane == step * sub + offset, row, 0.0), axis=-1, keepdims=True)


def half_of(index):
    total = index
    for k in range(1, 16):
        total = total + lax.shift_right_logical(index, k)
    return lax.rem(total, 2)


def factor_rows(target_ref, own_refs, other_refs, rows_ref):
    pumas, columns = target_ref.shape
    half = half_of(lax.axis_index("tract"))
    half_rows = sum(ref.shape[0] for ref in own_refs)
    for refs, which in ((own_refs, half), (other_refs, 1 - half)):
        start = which * half_rows
        for ref in refs:
            rows_ref[pl.ds(pl.multiple_of(start, 8), ref.shape[0]), :] = ref[...]
            start = start + ref.shape[0]
    for first in range(0, columns, LANES):
        width = min(columns - first, LANES)
        at = slice(first // LANES * pumas, (first // LANES + 1) * pumas)
        rows_ref[at, 0:width] = target_ref[:, first : first + width] / rows_ref[at, 0:width]


def load_puma_numbers(ids_ref, scalar_ref):
    ids = ids_ref[...]
    for t in range(scalar_ref.shape[0]):
        scalar_ref[t] = ids[t]


def put_halves(rows_ref, keep_refs, send_refs):
    half = half_of(lax.axis_index("tract"))
    half_rows = sum(ref.shape[0] for ref in keep_refs)
    for refs, which in ((keep_refs, half), (send_refs, 1 - half)):
        start = which * half_rows
        for ref in refs:
            ref[...] = rows_ref[pl.ds(pl.multiple_of(start, 8), ref.shape[0]), :]
            start = start + ref.shape[0]


def merge(first, second, step):
    low = lax.rem(lax.broadcasted_iota(jnp.int32, (8, 1), 0) // step, 2) == 0
    if step == 4:
        return jnp.where(low, first, second) + pltpu.roll(jnp.where(low, second, first), 4, 0)
    return jnp.where(low, first + pltpu.roll(first, 8 - step, 0), second + pltpu.roll(second, step, 0))


def each(start, stop, body):
    def turn(i, carry):
        body(start + 2 * i)
        body(start + 2 * i + 1)
        return carry

    lax.fori_loop(0, (stop - start) // 2, turn, 0)
    if (stop - start) % 2:
        body(stop - 1)


def age_sums(cells_ref, factor, cross_ref, base, count):
    ages = factor.shape[0]

    def tile(k):
        total = None
        for at in range(0, ages, 8):
            stop = min(at + 8, ages)
            part = cells_ref[k, at:stop] * factor[at:stop]
            if stop < at + 8:
                part = jnp.concatenate([part, jnp.zeros((at + 8 - stop, LANES), F32)], axis=0)
            total = part if total is None else total + part
        return total

    for start in range(0, count, 8):
        tiles = [tile(k) for k in range(start, min(start + 8, count))]
        if len(tiles) < 8:
            for k, x in enumerate(tiles):
                cross_ref[pl.ds(base + start + k, 1), :] = jnp.sum(x, axis=0, keepdims=True)
            continue
        tiles = [merge(tiles[k], tiles[k + 4], 4) for k in range(4)]
        tiles = [merge(tiles[k], tiles[k + 2], 2) for k in range(2)]
        cross_ref[pl.ds(pl.multiple_of(base + start, 8), 8), :] = merge(tiles[0], tiles[1], 1)


def pair_sum(term, count):
    first, second = term(0), term(1)
    for k in range(2, count, 2):
        first = first + term(k)
        if k + 1 < count:
            second = second + term(k + 1)
    return first + second


def rake_kernel(
    ids_hbm, table_hbm, age_sex_hbm, race_hisp_hbm, size_tenure_hbm, tenure_income_hbm,
    keep_ref, send_ref, age_factor_ref, cross_factor_ref, cells_ref,
    sum_ref, cross_ref, rows_ref, age_target_ref, race_target_ref, size_target_ref,
    ids_ref, age_sex_ref, race_hisp_ref, size_tenure_ref, tenure_income_ref,
    sems, small_sems,
    *, races, sizes, pumas,
):
    tracts, cross, ages, _ = table_hbm.shape
    cross_rows = round_up(cross + 1, 8)
    pairs = (ages + 1) // 2
    small = [
        pltpu.make_async_copy(source, target, small_sems.at[i])
        for i, (source, target) in enumerate((
            (ids_hbm, ids_ref),
            (age_sex_hbm, age_sex_ref),
            (race_hisp_hbm, race_hisp_ref),
            (size_tenure_hbm, size_tenure_ref),
            (tenure_income_hbm, tenure_income_ref),
        ))
    ]

    def table_copy(t):
        return pltpu.make_async_copy(table_hbm.at[t], cells_ref.at[t, 0:cross], sems.at[t])

    for copy in small:
        copy.start()
    for t in range(tracts):
        table_copy(t).start(priority=0 if t < GROUP else 1)
    lane = lane_ids(1)
    sex0 = lane < 64
    hisp0 = (lane // 32) % 2 == 0
    ten0 = (lane // 16) % 2 == 0

    rows_ref[...] = jnp.zeros(rows_ref.shape, F32)
    for copy in small:
        copy.wait()
    for source_ref, target_ref, rows, mask in (
        (age_sex_ref, age_target_ref, ages, sex0),
        (race_hisp_ref, race_target_ref, races, hisp0),
        (size_tenure_ref, size_target_ref, sizes, ten0),
    ):
        for t in range(tracts):
            row = source_ref[t : t + 1, :]
            target_ref[t, 0:rows] = jnp.where(
                mask, column_of(row, rows, 2, 0), column_of(row, rows, 2, 1)
            )

    def group_sums(values, mask):
        first = [masked_lane_sum(x, mask) for x in values]
        second = [masked_lane_sum(x, ~mask) for x in values]
        return [jnp.where(mask, x, y) for x, y in zip(first, second)]

    def arrive(t, carry):
        table_copy(t).wait()
        sum_ref[t, 0:ages] = pair_sum(lambda rs: cells_ref[t, rs], cross)
        return carry

    def add_ages(t):
        age_sums(cells_ref.at[t], age_factor_ref[t, 0:ages], cross_ref, t * cross_rows, cross)

    def add_scaled(t):
        base = t * cross_rows
        total = pair_sum(
            lambda rs: cells_ref[t, rs] * cross_factor_ref[pl.ds(base + rs, 1), :], cross
        )
        sum_ref[t, 0:ages] = total * age_factor_ref[t, 0:ages]
        sum_ref[t, ages : 2 * pairs] = jnp.zeros((2 * pairs - ages, LANES), F32)

    def small_steps(group):
        bases = [t * cross_rows for t in group]
        by_race = [
            sum(cross_ref[pl.ds(base + s, races, stride=sizes), :] for s in range(sizes))
            for base in bases
        ]
        race_factor = [
            race_target_ref[t, 0:races] / margin for t, margin in zip(group, group_sums(by_race, hisp0))
        ]
        by_size = [
            sum(
                cross_ref[pl.ds(base + r * sizes, sizes), :] * factor[r : r + 1]
                for r in range(races)
            )
            for base, factor in zip(bases, race_factor)
        ]
        size_factor = [
            size_target_ref[t, 0:sizes] / margin for t, margin in zip(group, group_sums(by_size, ten0))
        ]
        by_income = [jnp.sum(x * y, axis=0, keepdims=True) for x, y in zip(by_size, size_factor)]
        by_income = [x + pltpu.roll(x, 64, 1) for x in by_income]
        by_income = [x + pltpu.roll(x, 32, 1) for x in by_income]
        for i, t in enumerate(group):
            target = jnp.concatenate([tenure_income_ref[t : t + 1, :]] * 4, axis=1)
            age_factor_ref[t, 0:ages] = age_factor_ref[t, 0:ages] * (target / by_income[i])
            for r in range(races):
                cross_factor_ref[pl.ds(bases[i] + r * sizes, sizes), :] = (
                    size_factor[i] * race_factor[i][r : r + 1]
                )
            cross_factor_ref[pl.ds(bases[i] + cross, cross_rows - cross), :] = jnp.zeros(
                (cross_rows - cross, LANES), F32
            )

    def pack(group):
        even = [sum_ref[t, pl.ds(0, pairs, stride=2)] for t in group]
        odd = [sum_ref[t, pl.ds(1, pairs, stride=2)] for t in group]
        even = [x + pltpu.roll(x, 96, 1) for x in even]
        odd = [x + pltpu.roll(x, 96, 1) for x in odd]
        packed = [
            jnp.where(
                lane < 32,
                x,
                jnp.where(
                    lane < 64,
                    pltpu.roll(x, 96, 1),
                    jnp.where(lane < 96, pltpu.roll(y, 64, 1), pltpu.roll(y, 32, 1)),
                ),
            )
            for x, y in zip(even, odd)
        ]
        for t, x in zip(group, packed):
            at = pl.ds(ids_ref[t], pairs, stride=pumas)
            rows_ref[at, :] = rows_ref[at, :] + x

    def work(group):
        margin = group_sums([sum_ref[t, 0:ages] for t in group], sex0)
        for t, x in zip(group, margin):
            age_factor_ref[t, 0:ages] = age_target_ref[t, 0:ages] / x
        each(group.start, group.stop, add_ages)
        small_steps(group)
        each(group.start, group.stop, add_scaled)
        pack(group)

    before = None
    for start in range(0, tracts, GROUP):
        if before is not None:
            work(before)
        before = range(start, min(start + GROUP, tracts))
        lax.fori_loop(before.start, before.stop, arrive, 0)
    work(before)
    put_halves(rows_ref, [keep_ref], [send_ref])


def race_half(cells_ref, factor_ref, cross_factor_ref, chunk_refs, cross_ref, rows_ref, scalar_ref, half, pumas, ages, cross):
    tracts = cells_ref.shape[0]
    cross_rows = round_up(cross + 1, 8)
    pairs = sum(ref.shape[0] for ref in chunk_refs) // pumas
    count = 2 * pairs
    stride = round_up(count, 8)
    rows_ref[...] = jnp.zeros(rows_ref.shape, F32)
    lane = lane_ids(1)

    def add_ages(t):
        factor = factor_ref[t, 0:ages]
        cells = cells_ref.at[t, pl.ds(half * count, count)]
        age_sums(cells, factor, cross_ref, t * stride, count)

    each(0, tracts, add_ages)
    every = range(tracts)
    halves = []
    for first in range(2):
        margin = [
            cross_ref[pl.ds(t * stride + first, pairs, stride=2), :]
            * cross_factor_ref[pl.ds(t * cross_rows + half * count + first, pairs, stride=2), :]
            for t in every
        ]
        halves.append([x + pltpu.roll(x, 64, 1) for x in margin])
    for t in every:
        at = pl.ds(scalar_ref[t], pairs, stride=pumas)
        rows_ref[at, :] = rows_ref[at, :] + jnp.where(lane < 64, halves[0][t], halves[1][t])
    start = 0
    for ref in chunk_refs:
        ref[...] = rows_ref[start : start + ref.shape[0], :]
        start += ref.shape[0]


def race_send_kernel(
    ids_ref, cells_ref, age_factor_ref, cross_factor_ref, target_ref,
    own_ref, other_ref, *refs, cross
):
    *chunk_refs, scaled_factor_ref, cross_ref, age_rows_ref, rows_ref, scalar_ref = refs
    ages = 2 * (target_ref.shape[1] // LANES) + target_ref.shape[1] % LANES // 64
    pairs = (ages + 1) // 2
    pumas = target_ref.shape[0]
    every = range(cells_ref.shape[0])
    load_puma_numbers(ids_ref, scalar_ref)
    factor_rows(target_ref, [own_ref], [other_ref], age_rows_ref)
    lane = lane_ids(1)
    packed = [age_rows_ref[pl.ds(scalar_ref[t], pairs, stride=pumas), :] for t in every]
    quarter = [pltpu.roll(x, 32, 1) for x in packed]
    half = [pltpu.roll(x, 64, 1) for x in packed]
    back = [pltpu.roll(x, 96, 1) for x in packed]
    for t in every:
        even = jnp.where(lane < 32, packed[t], jnp.where(lane < 96, quarter[t], half[t]))
        odd = jnp.where(lane < 32, half[t], jnp.where(lane < 96, back[t], packed[t]))
        for first, factor in enumerate((even, odd)):
            at = pl.ds(first, pairs, stride=2)
            scaled_factor_ref[t, at] = factor * age_factor_ref[t, at]
    race_half(
        cells_ref, scaled_factor_ref, cross_factor_ref, chunk_refs, cross_ref, rows_ref, scalar_ref,
        1 - half_of(lax.axis_index("tract")), pumas, ages, cross,
    )


def race_keep_kernel(ids_ref, cells_ref, factor_ref, cross_factor_ref, *refs, ages, pumas, cross):
    *chunk_refs, cross_ref, rows_ref, scalar_ref = refs
    load_puma_numbers(ids_ref, scalar_ref)
    race_half(
        cells_ref, factor_ref, cross_factor_ref, chunk_refs, cross_ref, rows_ref, scalar_ref,
        half_of(lax.axis_index("tract")), pumas, ages, cross,
    )


def final_kernel(
    ids_ref, cells_ref, scaled_factor_ref, cross_factor_ref, target_ref, *refs
):
    *chunk_refs, out_ref, result_ref, cross_ref, rows_ref, scalar_ref, sems = refs
    chunks = len(chunk_refs) // 2
    tracts, cross, ages, _ = out_ref.shape
    cross_rows = round_up(cross + 1, 8)
    cross_pairs = (cross + 1) // 2
    pumas = target_ref.shape[0]
    load_puma_numbers(ids_ref, scalar_ref)
    factor_rows(target_ref, chunk_refs[:chunks], chunk_refs[chunks:], rows_ref)
    lane = lane_ids(1)

    def unpack(t):
        base = t * cross_rows
        packed = rows_ref[pl.ds(scalar_ref[t], cross_pairs, stride=pumas), :]
        half = pltpu.roll(packed, 64, 1)
        for first, factor in enumerate(
            (jnp.where(lane < 64, packed, half), jnp.where(lane < 64, half, packed))
        ):
            at = pl.ds(base + first, cross_pairs, stride=2)
            cross_ref[at, :] = factor * cross_factor_ref[at, :]

    def scale(t):
        factor = scaled_factor_ref[t, 0:ages]
        base = t * cross_rows
        for rs in range(cross):
            result_ref[t, rs] = cells_ref[t, rs] * factor * cross_ref[pl.ds(base + rs, 1), :]

    def send(t):
        pltpu.make_async_copy(result_ref.at[t], out_ref.at[t], sems.at[t]).start()

    def step(t, carry):
        scale(t)
        unpack(t + 1)
        send(t)
        return carry

    unpack(0)
    lax.fori_loop(0, tracts - 1, step, 0)
    scale(tracts - 1)
    send(tracts - 1)
    for t in range(tracts):
        pltpu.make_async_copy(result_ref.at[t], out_ref.at[t], sems.at[t]).wait()


def call(kernel, out_shapes, in_spaces, out_spaces, scratch):
    def spec(space):
        return pl.BlockSpec(memory_space=space)

    run = pl.pallas_call(
        kernel,
        out_shape=[
            space(shape, F32) for shape, space in zip(out_shapes, out_spaces, strict=True)
        ],
        in_specs=[spec(space) for space in in_spaces],
        out_specs=[spec(space) for space in out_spaces],
        scratch_shapes=scratch,
        compiler_params=pltpu.CompilerParams(vmem_limit_bytes=40 << 20),
    )

    def placed(*args):
        return run(*map(pltpu.with_memory_space_constraint, args, in_spaces))

    return placed


def per_device(
    devices,
    table, age_sex, race_hisp, size_tenure, tenure_income, puma_age, puma_race, tract_puma,
):
    tracts, ages, races, sizes, inner = table.shape
    pumas = puma_age.shape[0]
    cross = races * sizes
    age_pairs, cross_pairs = (ages + 1) // 2, (cross + 1) // 2
    age_rows = 2 * round_up(age_pairs, 8)
    cross_rows = tracts * round_up(cross + 1, 8) + 2 * round_up(cross_pairs, 8)
    age_sum_rows, cross_sum_rows = (round_up(x, 8) * pumas for x in (age_pairs, cross_pairs))
    vmem, hbm = pltpu.VMEM, pltpu.HBM

    cells = table.transpose(0, 2, 3, 1, 4).reshape(tracts, cross, ages, inner)
    cells_scratch = pltpu.VMEM((tracts, cross, ages, inner), F32)
    cross_scratch = pltpu.VMEM((cross_rows, LANES), F32)
    copy_sems = pltpu.SemaphoreType.DMA((tracts,))
    numbers_scratch = pltpu.SMEM((tracts,), jnp.int32)

    bits = [1 << k for k in range(1, devices.bit_length() - 1)]
    orders = (bits, bits[1:] + bits[:1])

    def swap(x, partner):
        return lax.ppermute(x, "tract", [(i, partner(i)) for i in range(devices)])

    def totals(keep, send):
        keep = [x + swap(y, lambda i: i ^ 1) for x, y in zip(keep, send)]
        for step in range(len(bits)):
            keep = [x + swap(x, lambda i: i ^ orders[i.bit_count() % 2][step] ^ 1) for x in keep]
        return *keep, *[swap(x, lambda i: i ^ 1) for x in keep]

    age_half, cross_half = -(-age_pairs // 2), -(-cross_pairs // 2)
    cross_chunks = [cross_half - cross_half // 2, cross_half // 2]
    age_shape, cross_shape = (tracts, age_rows, LANES), (cross_rows, LANES)
    small = [age_sex, race_hisp, size_tenure, tenure_income]
    keep, send, age_factor, cross_factor, cells = call(
        functools.partial(rake_kernel, races=races, sizes=sizes, pumas=pumas),
        [(age_half * pumas, LANES)] * 2
        + [age_shape, cross_shape, (tracts, 4 * cross_half, ages, inner)],
        [hbm] * 6,
        [vmem] * 5,
        [
            pltpu.VMEM(age_shape, F32),
            cross_scratch,
            pltpu.VMEM((age_sum_rows, LANES), F32),
            pltpu.VMEM(age_shape, F32),
            pltpu.VMEM((tracts, round_up(races, 8), LANES), F32),
            pltpu.VMEM((tracts, round_up(sizes, 8), LANES), F32),
            numbers_scratch,
        ]
        + [pltpu.VMEM(x.shape, F32) for x in small]
        + [copy_sems, pltpu.SemaphoreType.DMA((1 + len(small),))],
    )(tract_puma, cells, *small)

    half_scratch = [
        pltpu.VMEM((tracts * round_up(2 * cross_half, 8) + 16, LANES), F32),
        pltpu.VMEM((round_up(cross_half, 8) * pumas, LANES), F32),
    ]
    chunk_shapes = [(rows * pumas, LANES) for rows in cross_chunks]
    *send, scaled_factor = call(
        functools.partial(race_send_kernel, cross=cross),
        chunk_shapes + [age_shape],
        [vmem] * 7,
        [vmem] * (len(cross_chunks) + 1),
        [half_scratch[0], pltpu.VMEM((age_sum_rows, LANES), F32), half_scratch[1], numbers_scratch],
    )(tract_puma, cells, age_factor, cross_factor, puma_age, *totals([keep], [send]))
    keep = call(
        functools.partial(race_keep_kernel, ages=ages, pumas=pumas, cross=cross),
        chunk_shapes,
        [vmem] * 4,
        [vmem] * len(cross_chunks),
        half_scratch + [numbers_scratch],
    )(tract_puma, cells, scaled_factor, cross_factor)

    out, = call(
        final_kernel,
        [(tracts, cross, ages, inner)],
        [vmem] * (5 + 2 * len(cross_chunks)),
        [hbm],
        [
            cells_scratch,
            cross_scratch,
            pltpu.VMEM((cross_sum_rows, LANES), F32),
            numbers_scratch,
            copy_sems,
        ],
    )(tract_puma, cells, scaled_factor, cross_factor, puma_race, *totals(keep, send))
    return out.reshape(tracts, races, sizes, ages, inner).transpose(0, 3, 1, 2, 4)


def solution(mesh):
    in_specs = (
        P(("grp", "tract"), None, None, None, None),
        P(("grp", "tract"), None),
        P(("grp", "tract"), None),
        P(("grp", "tract"), None),
        P(("grp", "tract"), None),
        P("grp", None),
        P("grp", None),
        P(("grp", "tract")),
    )
    out_specs = P(("grp", "tract"), None, None, None, None)
    return jax.shard_map(
        functools.partial(per_device, mesh.shape["tract"]),
        mesh=mesh, in_specs=in_specs, out_specs=out_specs, check_vma=False,
    )
```

```python
import functools

import jax
import jax.numpy as jnp
from jax import lax
from jax.experimental import pallas as pl
from jax.experimental.pallas import tpu as pltpu
from jax.sharding import PartitionSpec as P

LANES = 128
GROUP = 6
FIRST = 6
F32 = jnp.float32


def round_up(value, step):
    return -(-value // step) * step


def lane_ids(rows):
    return lax.broadcasted_iota(jnp.int32, (rows, LANES), 1)


def masked_lane_sum(value, mask):
    return jnp.sum(jnp.where(mask, value, 0.0), axis=-1, keepdims=True)


def column_of(row, rows, step, offset):
    width = row.shape[-1]
    lane = lax.broadcasted_iota(jnp.int32, (rows, width), 1)
    sub = lax.broadcasted_iota(jnp.int32, (rows, width), 0)
    return jnp.sum(jnp.where(lane == step * sub + offset, row, 0.0), axis=-1, keepdims=True)


def half_of(index):
    total = index
    for k in range(1, 16):
        total = total + lax.shift_right_logical(index, k)
    return lax.rem(total, 2)


def factor_rows(target_ref, own_refs, other_refs, rows_ref):
    pumas, columns = target_ref.shape
    half = half_of(lax.axis_index("tract"))
    half_rows = sum(ref.shape[0] for ref in own_refs)
    for refs, which in ((own_refs, half), (other_refs, 1 - half)):
        start = which * half_rows
        for ref in refs:
            rows_ref[pl.ds(pl.multiple_of(start, 8), ref.shape[0]), :] = ref[...]
            start = start + ref.shape[0]
    for first in range(0, columns, LANES):
        width = min(columns - first, LANES)
        at = slice(first // LANES * pumas, (first // LANES + 1) * pumas)
        rows_ref[at, 0:width] = target_ref[:, first : first + width] / rows_ref[at, 0:width]


def load_puma_numbers(ids_ref, scalar_ref):
    ids = ids_ref[...]
    for t in range(scalar_ref.shape[0]):
        scalar_ref[t] = ids[t]


def put_halves(rows_ref, keep_refs, send_refs):
    half = half_of(lax.axis_index("tract"))
    half_rows = sum(ref.shape[0] for ref in keep_refs)
    for refs, which in ((keep_refs, half), (send_refs, 1 - half)):
        start = which * half_rows
        for ref in refs:
            ref[...] = rows_ref[pl.ds(pl.multiple_of(start, 8), ref.shape[0]), :]
            start = start + ref.shape[0]


def merge(first, second, step):
    low = lax.rem(lax.broadcasted_iota(jnp.int32, (8, 1), 0) // step, 2) == 0
    if step == 4:
        return jnp.where(low, first, second) + pltpu.roll(jnp.where(low, second, first), 4, 0)
    return jnp.where(low, first + pltpu.roll(first, 8 - step, 0), second + pltpu.roll(second, step, 0))


def each(start, stop, body):
    def turn(i, carry):
        body(start + 2 * i)
        body(start + 2 * i + 1)
        return carry

    lax.fori_loop(0, (stop - start) // 2, turn, 0)
    if (stop - start) % 2:
        body(stop - 1)


def age_sums(cells_ref, factor, cross_ref, base, count):
    ages = factor.shape[0]

    def tile(k):
        total = None
        for at in range(0, ages, 8):
            stop = min(at + 8, ages)
            part = cells_ref[k, at:stop] * factor[at:stop]
            if stop < at + 8:
                part = jnp.concatenate([part, jnp.zeros((at + 8 - stop, LANES), F32)], axis=0)
            total = part if total is None else total + part
        return total

    for start in range(0, count, 8):
        tiles = [tile(k) for k in range(start, min(start + 8, count))]
        if len(tiles) < 8:
            for k, x in enumerate(tiles):
                cross_ref[pl.ds(base + start + k, 1), :] = jnp.sum(x, axis=0, keepdims=True)
            continue
        tiles = [merge(tiles[k], tiles[k + 4], 4) for k in range(4)]
        tiles = [merge(tiles[k], tiles[k + 2], 2) for k in range(2)]
        cross_ref[pl.ds(pl.multiple_of(base + start, 8), 8), :] = merge(tiles[0], tiles[1], 1)


def pair_sum(term, count):
    first, second = term(0), term(1)
    for k in range(2, count, 2):
        first = first + term(k)
        if k + 1 < count:
            second = second + term(k + 1)
    return first + second


def rake_kernel(
    ids_hbm, table_hbm, age_sex_hbm, race_hisp_hbm, size_tenure_hbm, tenure_income_hbm,
    keep_ref, send_ref, age_factor_ref, cross_factor_ref, cells_ref,
    sum_ref, cross_ref, rows_ref, age_target_ref, race_target_ref, size_target_ref,
    ids_ref, age_sex_ref, race_hisp_ref, size_tenure_ref, tenure_income_ref,
    sems, small_sems,
    *, races, sizes, pumas,
):
    tracts, cross, ages, _ = table_hbm.shape
    cross_rows = round_up(cross + 1, 8)
    pairs = (ages + 1) // 2
    small = [
        pltpu.make_async_copy(source, target, small_sems.at[i])
        for i, (source, target) in enumerate((
            (ids_hbm, ids_ref),
            (age_sex_hbm, age_sex_ref),
            (race_hisp_hbm, race_hisp_ref),
            (size_tenure_hbm, size_tenure_ref),
            (tenure_income_hbm, tenure_income_ref),
        ))
    ]

    def table_copy(t):
        return pltpu.make_async_copy(table_hbm.at[t], cells_ref.at[t, 0:cross], sems.at[t])

    for copy in small:
        copy.start()
    for t in range(min(FIRST, tracts)):
        table_copy(t).start()
    lane = lane_ids(1)
    sex0 = lane < 64
    hisp0 = (lane // 32) % 2 == 0
    ten0 = (lane // 16) % 2 == 0

    rows_ref[...] = jnp.zeros(rows_ref.shape, F32)
    for copy in small:
        copy.wait()
    for source_ref, target_ref, rows, mask in (
        (age_sex_ref, age_target_ref, ages, sex0),
        (race_hisp_ref, race_target_ref, races, hisp0),
        (size_tenure_ref, size_target_ref, sizes, ten0),
    ):
        for t in range(tracts):
            row = source_ref[t : t + 1, :]
            target_ref[t, 0:rows] = jnp.where(
                mask, column_of(row, rows, 2, 0), column_of(row, rows, 2, 1)
            )

    for t in range(FIRST, tracts):
        table_copy(t).start()

    def group_sums(values, mask):
        first = [masked_lane_sum(x, mask) for x in values]
        second = [masked_lane_sum(x, ~mask) for x in values]
        return [jnp.where(mask, x, y) for x, y in zip(first, second)]

    def arrive(t, carry):
        table_copy(t).wait()
        sum_ref[t, 0:ages] = pair_sum(lambda rs: cells_ref[t, rs], cross)
        return carry

    def add_ages(t):
        age_sums(cells_ref.at[t], age_factor_ref[t, 0:ages], cross_ref, t * cross_rows, cross)

    def add_scaled(t):
        base = t * cross_rows
        total = pair_sum(
            lambda rs: cells_ref[t, rs] * cross_factor_ref[pl.ds(base + rs, 1), :], cross
        )
        sum_ref[t, 0:ages] = total * age_factor_ref[t, 0:ages]
        sum_ref[t, ages : 2 * pairs] = jnp.zeros((2 * pairs - ages, LANES), F32)

    def small_steps(group):
        bases = [t * cross_rows for t in group]
        by_race = [
            sum(cross_ref[pl.ds(base + s, races, stride=sizes), :] for s in range(sizes))
            for base in bases
        ]
        race_factor = [
            race_target_ref[t, 0:races] / margin for t, margin in zip(group, group_sums(by_race, hisp0))
        ]
        by_size = [
            sum(
                cross_ref[pl.ds(base + r * sizes, sizes), :] * factor[r : r + 1]
                for r in range(races)
            )
            for base, factor in zip(bases, race_factor)
        ]
        size_factor = [
            size_target_ref[t, 0:sizes] / margin for t, margin in zip(group, group_sums(by_size, ten0))
        ]
        by_income = [jnp.sum(x * y, axis=0, keepdims=True) for x, y in zip(by_size, size_factor)]
        by_income = [x + pltpu.roll(x, 64, 1) for x in by_income]
        by_income = [x + pltpu.roll(x, 32, 1) for x in by_income]
        for i, t in enumerate(group):
            target = jnp.concatenate([tenure_income_ref[t : t + 1, :]] * 4, axis=1)
            age_factor_ref[t, 0:ages] = age_factor_ref[t, 0:ages] * (target / by_income[i])
            for r in range(races):
                cross_factor_ref[pl.ds(bases[i] + r * sizes, sizes), :] = (
                    size_factor[i] * race_factor[i][r : r + 1]
                )
            cross_factor_ref[pl.ds(bases[i] + cross, cross_rows - cross), :] = jnp.zeros(
                (cross_rows - cross, LANES), F32
            )

    def pack(group):
        even = [sum_ref[t, pl.ds(0, pairs, stride=2)] for t in group]
        odd = [sum_ref[t, pl.ds(1, pairs, stride=2)] for t in group]
        even = [x + pltpu.roll(x, 96, 1) for x in even]
        odd = [x + pltpu.roll(x, 96, 1) for x in odd]
        packed = [
            jnp.where(
                lane < 32,
                x,
                jnp.where(
                    lane < 64,
                    pltpu.roll(x, 96, 1),
                    jnp.where(lane < 96, pltpu.roll(y, 64, 1), pltpu.roll(y, 32, 1)),
                ),
            )
            for x, y in zip(even, odd)
        ]
        for t, x in zip(group, packed):
            at = pl.ds(ids_ref[t], pairs, stride=pumas)
            rows_ref[at, :] = rows_ref[at, :] + x

    def work(group):
        margin = group_sums([sum_ref[t, 0:ages] for t in group], sex0)
        for t, x in zip(group, margin):
            age_factor_ref[t, 0:ages] = age_target_ref[t, 0:ages] / x
        each(group.start, group.stop, add_ages)
        small_steps(group)
        each(group.start, group.stop, add_scaled)
        pack(group)

    before = None
    for start in range(0, tracts, GROUP):
        if before is not None:
            work(before)
        before = range(start, min(start + GROUP, tracts))
        lax.fori_loop(before.start, before.stop, arrive, 0)
    work(before)
    put_halves(rows_ref, [keep_ref], [send_ref])


def race_half(cells_ref, factor_ref, cross_factor_ref, chunk_refs, cross_ref, rows_ref, scalar_ref, half, pumas, ages, cross):
    tracts = cells_ref.shape[0]
    cross_rows = round_up(cross + 1, 8)
    pairs = sum(ref.shape[0] for ref in chunk_refs) // pumas
    count = 2 * pairs
    stride = round_up(count, 8)
    rows_ref[...] = jnp.zeros(rows_ref.shape, F32)
    lane = lane_ids(1)

    def add_ages(t):
        factor = factor_ref[t, 0:ages]
        cells = cells_ref.at[t, pl.ds(half * count, count)]
        age_sums(cells, factor, cross_ref, t * stride, count)

    each(0, tracts, add_ages)
    every = range(tracts)
    halves = []
    for first in range(2):
        margin = [
            cross_ref[pl.ds(t * stride + first, pairs, stride=2), :]
            * cross_factor_ref[pl.ds(t * cross_rows + half * count + first, pairs, stride=2), :]
            for t in every
        ]
        halves.append([x + pltpu.roll(x, 64, 1) for x in margin])
    for t in every:
        at = pl.ds(scalar_ref[t], pairs, stride=pumas)
        rows_ref[at, :] = rows_ref[at, :] + jnp.where(lane < 64, halves[0][t], halves[1][t])
    start = 0
    for ref in chunk_refs:
        ref[...] = rows_ref[start : start + ref.shape[0], :]
        start += ref.shape[0]


def race_send_kernel(
    ids_ref, cells_ref, age_factor_ref, cross_factor_ref, target_ref,
    own_ref, other_ref, *refs, cross
):
    *chunk_refs, scaled_factor_ref, cross_ref, age_rows_ref, rows_ref, scalar_ref = refs
    ages = 2 * (target_ref.shape[1] // LANES) + target_ref.shape[1] % LANES // 64
    pairs = (ages + 1) // 2
    pumas = target_ref.shape[0]
    every = range(cells_ref.shape[0])
    load_puma_numbers(ids_ref, scalar_ref)
    factor_rows(target_ref, [own_ref], [other_ref], age_rows_ref)
    lane = lane_ids(1)
    packed = [age_rows_ref[pl.ds(scalar_ref[t], pairs, stride=pumas), :] for t in every]
    quarter = [pltpu.roll(x, 32, 1) for x in packed]
    half = [pltpu.roll(x, 64, 1) for x in packed]
    back = [pltpu.roll(x, 96, 1) for x in packed]
    for t in every:
        even = jnp.where(lane < 32, packed[t], jnp.where(lane < 96, quarter[t], half[t]))
        odd = jnp.where(lane < 32, half[t], jnp.where(lane < 96, back[t], packed[t]))
        for first, factor in enumerate((even, odd)):
            at = pl.ds(first, pairs, stride=2)
            scaled_factor_ref[t, at] = factor * age_factor_ref[t, at]
    race_half(
        cells_ref, scaled_factor_ref, cross_factor_ref, chunk_refs, cross_ref, rows_ref, scalar_ref,
        1 - half_of(lax.axis_index("tract")), pumas, ages, cross,
    )


def race_keep_kernel(ids_ref, cells_ref, factor_ref, cross_factor_ref, *refs, ages, pumas, cross):
    *chunk_refs, cross_ref, rows_ref, scalar_ref = refs
    load_puma_numbers(ids_ref, scalar_ref)
    race_half(
        cells_ref, factor_ref, cross_factor_ref, chunk_refs, cross_ref, rows_ref, scalar_ref,
        half_of(lax.axis_index("tract")), pumas, ages, cross,
    )


def final_kernel(
    ids_ref, cells_ref, scaled_factor_ref, cross_factor_ref, target_ref, *refs
):
    *chunk_refs, out_ref, result_ref, cross_ref, rows_ref, scalar_ref, sems = refs
    chunks = len(chunk_refs) // 2
    tracts, cross, ages, _ = out_ref.shape
    cross_rows = round_up(cross + 1, 8)
    cross_pairs = (cross + 1) // 2
    pumas = target_ref.shape[0]
    load_puma_numbers(ids_ref, scalar_ref)
    factor_rows(target_ref, chunk_refs[:chunks], chunk_refs[chunks:], rows_ref)
    lane = lane_ids(1)

    def unpack(t):
        base = t * cross_rows
        packed = rows_ref[pl.ds(scalar_ref[t], cross_pairs, stride=pumas), :]
        half = pltpu.roll(packed, 64, 1)
        for first, factor in enumerate(
            (jnp.where(lane < 64, packed, half), jnp.where(lane < 64, half, packed))
        ):
            at = pl.ds(base + first, cross_pairs, stride=2)
            cross_ref[at, :] = factor * cross_factor_ref[at, :]

    def scale(t):
        factor = scaled_factor_ref[t, 0:ages]
        base = t * cross_rows
        for rs in range(cross):
            result_ref[t, rs] = cells_ref[t, rs] * factor * cross_ref[pl.ds(base + rs, 1), :]

    def send(t):
        pltpu.make_async_copy(result_ref.at[t], out_ref.at[t], sems.at[t]).start()

    def step(t, carry):
        scale(t)
        unpack(t + 1)
        send(t)
        return carry

    unpack(0)
    lax.fori_loop(0, tracts - 1, step, 0)
    scale(tracts - 1)
    send(tracts - 1)
    for t in range(tracts):
        pltpu.make_async_copy(result_ref.at[t], out_ref.at[t], sems.at[t]).wait()


def call(kernel, out_shapes, in_spaces, out_spaces, scratch):
    def spec(space):
        return pl.BlockSpec(memory_space=space)

    run = pl.pallas_call(
        kernel,
        out_shape=[
            space(shape, F32) for shape, space in zip(out_shapes, out_spaces, strict=True)
        ],
        in_specs=[spec(space) for space in in_spaces],
        out_specs=[spec(space) for space in out_spaces],
        scratch_shapes=scratch,
        compiler_params=pltpu.CompilerParams(vmem_limit_bytes=40 << 20),
    )

    def placed(*args):
        return run(*map(pltpu.with_memory_space_constraint, args, in_spaces))

    return placed


def per_device(
    devices,
    table, age_sex, race_hisp, size_tenure, tenure_income, puma_age, puma_race, tract_puma,
):
    tracts, ages, races, sizes, inner = table.shape
    pumas = puma_age.shape[0]
    cross = races * sizes
    age_pairs, cross_pairs = (ages + 1) // 2, (cross + 1) // 2
    age_rows = 2 * round_up(age_pairs, 8)
    cross_rows = tracts * round_up(cross + 1, 8) + 2 * round_up(cross_pairs, 8)
    age_sum_rows, cross_sum_rows = (round_up(x, 8) * pumas for x in (age_pairs, cross_pairs))
    vmem, hbm = pltpu.VMEM, pltpu.HBM

    cells = table.transpose(0, 2, 3, 1, 4).reshape(tracts, cross, ages, inner)
    cells_scratch = pltpu.VMEM((tracts, cross, ages, inner), F32)
    cross_scratch = pltpu.VMEM((cross_rows, LANES), F32)
    copy_sems = pltpu.SemaphoreType.DMA((tracts,))
    numbers_scratch = pltpu.SMEM((tracts,), jnp.int32)

    bits = [1 << k for k in range(1, devices.bit_length() - 1)]
    orders = (bits, bits[1:] + bits[:1])

    def swap(x, partner):
        return lax.ppermute(x, "tract", [(i, partner(i)) for i in range(devices)])

    def totals(keep, send):
        keep = [x + swap(y, lambda i: i ^ 1) for x, y in zip(keep, send)]
        for step in range(len(bits)):
            keep = [x + swap(x, lambda i: i ^ orders[i.bit_count() % 2][step] ^ 1) for x in keep]
        return *keep, *[swap(x, lambda i: i ^ 1) for x in keep]

    age_half, cross_half = -(-age_pairs // 2), -(-cross_pairs // 2)
    cross_chunks = [cross_half - 2 * (cross_half // 3), cross_half // 3, cross_half // 3]
    age_shape, cross_shape = (tracts, age_rows, LANES), (cross_rows, LANES)
    small = [age_sex, race_hisp, size_tenure, tenure_income]
    keep, send, age_factor, cross_factor, cells = call(
        functools.partial(rake_kernel, races=races, sizes=sizes, pumas=pumas),
        [(age_half * pumas, LANES)] * 2
        + [age_shape, cross_shape, (tracts, 4 * cross_half, ages, inner)],
        [hbm] * 6,
        [vmem] * 5,
        [
            pltpu.VMEM(age_shape, F32),
            cross_scratch,
            pltpu.VMEM((age_sum_rows, LANES), F32),
            pltpu.VMEM(age_shape, F32),
            pltpu.VMEM((tracts, round_up(races, 8), LANES), F32),
            pltpu.VMEM((tracts, round_up(sizes, 8), LANES), F32),
            numbers_scratch,
        ]
        + [pltpu.VMEM(x.shape, F32) for x in small]
        + [copy_sems, pltpu.SemaphoreType.DMA((1 + len(small),))],
    )(tract_puma, cells, *small)

    half_scratch = [
        pltpu.VMEM((tracts * round_up(2 * cross_half, 8) + 16, LANES), F32),
        pltpu.VMEM((round_up(cross_half, 8) * pumas, LANES), F32),
    ]
    chunk_shapes = [(rows * pumas, LANES) for rows in cross_chunks]
    *send, scaled_factor = call(
        functools.partial(race_send_kernel, cross=cross),
        chunk_shapes + [age_shape],
        [vmem] * 7,
        [vmem] * (len(cross_chunks) + 1),
        [half_scratch[0], pltpu.VMEM((age_sum_rows, LANES), F32), half_scratch[1], numbers_scratch],
    )(tract_puma, cells, age_factor, cross_factor, puma_age, *totals([keep], [send]))
    keep = call(
        functools.partial(race_keep_kernel, ages=ages, pumas=pumas, cross=cross),
        chunk_shapes,
        [vmem] * 4,
        [vmem] * len(cross_chunks),
        half_scratch + [numbers_scratch],
    )(tract_puma, cells, scaled_factor, cross_factor)

    out, = call(
        final_kernel,
        [(tracts, cross, ages, inner)],
        [vmem] * (5 + 2 * len(cross_chunks)),
        [hbm],
        [
            cells_scratch,
            cross_scratch,
            pltpu.VMEM((cross_sum_rows, LANES), F32),
            numbers_scratch,
            copy_sems,
        ],
    )(tract_puma, cells, scaled_factor, cross_factor, puma_race, *totals(keep, send))
    return out.reshape(tracts, races, sizes, ages, inner).transpose(0, 3, 1, 2, 4)


def solution(mesh):
    in_specs = (
        P(("grp", "tract"), None, None, None, None),
        P(("grp", "tract"), None),
        P(("grp", "tract"), None),
        P(("grp", "tract"), None),
        P(("grp", "tract"), None),
        P("grp", None),
        P("grp", None),
        P(("grp", "tract")),
    )
    out_specs = P(("grp", "tract"), None, None, None, None)
    return jax.shard_map(
        functools.partial(per_device, mesh.shape["tract"]),
        mesh=mesh, in_specs=in_specs, out_specs=out_specs, check_vma=False,
    )
```

```python
import functools

import jax
import jax.numpy as jnp
from jax import lax
from jax.experimental import pallas as pl
from jax.experimental.pallas import tpu as pltpu
from jax.sharding import PartitionSpec as P

LANES = 128
GROUP = 6
FIRST = 6
F32 = jnp.float32


def round_up(value, step):
    return -(-value // step) * step


def lane_ids(rows):
    return lax.broadcasted_iota(jnp.int32, (rows, LANES), 1)


def masked_lane_sum(value, mask):
    return jnp.sum(jnp.where(mask, value, 0.0), axis=-1, keepdims=True)


def column_of(row, rows, step, offset):
    width = row.shape[-1]
    lane = lax.broadcasted_iota(jnp.int32, (rows, width), 1)
    sub = lax.broadcasted_iota(jnp.int32, (rows, width), 0)
    return jnp.sum(jnp.where(lane == step * sub + offset, row, 0.0), axis=-1, keepdims=True)


def half_of(index):
    total = index
    for k in range(1, 16):
        total = total + lax.shift_right_logical(index, k)
    return lax.rem(total, 2)


def factor_rows(target_ref, own_refs, other_refs, rows_ref):
    pumas, columns = target_ref.shape
    half = half_of(lax.axis_index("tract"))
    half_rows = sum(ref.shape[0] for ref in own_refs)
    for refs, which in ((own_refs, half), (other_refs, 1 - half)):
        start = which * half_rows
        for ref in refs:
            rows_ref[pl.ds(pl.multiple_of(start, 8), ref.shape[0]), :] = ref[...]
            start = start + ref.shape[0]
    for first in range(0, columns, LANES):
        width = min(columns - first, LANES)
        at = slice(first // LANES * pumas, (first // LANES + 1) * pumas)
        rows_ref[at, 0:width] = target_ref[:, first : first + width] / rows_ref[at, 0:width]


def load_puma_numbers(ids_ref, scalar_ref):
    ids = ids_ref[...]
    for t in range(scalar_ref.shape[0]):
        scalar_ref[t] = ids[t]


def put_halves(rows_ref, keep_refs, send_refs):
    half = half_of(lax.axis_index("tract"))
    half_rows = sum(ref.shape[0] for ref in keep_refs)
    for refs, which in ((keep_refs, half), (send_refs, 1 - half)):
        start = which * half_rows
        for ref in refs:
            ref[...] = rows_ref[pl.ds(pl.multiple_of(start, 8), ref.shape[0]), :]
            start = start + ref.shape[0]


def merge(first, second, step):
    low = lax.rem(lax.broadcasted_iota(jnp.int32, (8, 1), 0) // step, 2) == 0
    if step == 4:
        return jnp.where(low, first, second) + pltpu.roll(jnp.where(low, second, first), 4, 0)
    return jnp.where(low, first + pltpu.roll(first, 8 - step, 0), second + pltpu.roll(second, step, 0))


def each(start, stop, body, width=3):
    def turn(i, carry):
        for k in range(width):
            body(start + width * i + k)
        return carry

    turns = (stop - start) // width
    lax.fori_loop(0, turns, turn, 0)
    for t in range(start + width * turns, stop):
        body(t)


def age_sums(cells_ref, factor, cross_ref, base, count):
    ages = factor.shape[0]

    def tile(k):
        total = None
        for at in range(0, ages, 8):
            stop = min(at + 8, ages)
            part = cells_ref[k, at:stop] * factor[at:stop]
            if stop < at + 8:
                part = jnp.concatenate([part, jnp.zeros((at + 8 - stop, LANES), F32)], axis=0)
            total = part if total is None else total + part
        return total

    for start in range(0, count, 8):
        tiles = [tile(k) for k in range(start, min(start + 8, count))]
        if len(tiles) < 8:
            for k, x in enumerate(tiles):
                cross_ref[pl.ds(base + start + k, 1), :] = jnp.sum(x, axis=0, keepdims=True)
            continue
        tiles = [merge(tiles[k], tiles[k + 4], 4) for k in range(4)]
        tiles = [merge(tiles[k], tiles[k + 2], 2) for k in range(2)]
        cross_ref[pl.ds(pl.multiple_of(base + start, 8), 8), :] = merge(tiles[0], tiles[1], 1)


def pair_sum(term, count):
    first, second = term(0), term(1)
    for k in range(2, count, 2):
        first = first + term(k)
        if k + 1 < count:
            second = second + term(k + 1)
    return first + second


def rake_kernel(
    ids_hbm, table_hbm, age_sex_hbm, race_hisp_hbm, size_tenure_hbm, tenure_income_hbm,
    keep_ref, send_ref, age_factor_ref, cross_factor_ref, cells_ref,
    sum_ref, cross_ref, rows_ref, age_target_ref, race_target_ref, size_target_ref,
    ids_ref, age_sex_ref, race_hisp_ref, size_tenure_ref, tenure_income_ref,
    sems, small_sems,
    *, races, sizes, pumas,
):
    tracts, cross, ages, _ = table_hbm.shape
    cross_rows = round_up(cross + 1, 8)
    pairs = (ages + 1) // 2
    small = [
        pltpu.make_async_copy(source, target, small_sems.at[i])
        for i, (source, target) in enumerate((
            (ids_hbm, ids_ref),
            (age_sex_hbm, age_sex_ref),
            (race_hisp_hbm, race_hisp_ref),
            (size_tenure_hbm, size_tenure_ref),
            (tenure_income_hbm, tenure_income_ref),
        ))
    ]

    def table_copy(t):
        return pltpu.make_async_copy(table_hbm.at[t], cells_ref.at[t, 0:cross], sems.at[t])

    for copy in small:
        copy.start()
    for t in range(min(FIRST, tracts)):
        table_copy(t).start()
    lane = lane_ids(1)
    sex0 = lane < 64
    hisp0 = (lane // 32) % 2 == 0
    ten0 = (lane // 16) % 2 == 0

    rows_ref[...] = jnp.zeros(rows_ref.shape, F32)
    for copy in small:
        copy.wait()
    for source_ref, target_ref, rows, mask in (
        (age_sex_ref, age_target_ref, ages, sex0),
        (race_hisp_ref, race_target_ref, races, hisp0),
        (size_tenure_ref, size_target_ref, sizes, ten0),
    ):
        for t in range(tracts):
            row = source_ref[t : t + 1, :]
            target_ref[t, 0:rows] = jnp.where(
                mask, column_of(row, rows, 2, 0), column_of(row, rows, 2, 1)
            )

    for t in range(FIRST, tracts):
        table_copy(t).start()

    def group_sums(values, mask):
        first = [masked_lane_sum(x, mask) for x in values]
        second = [masked_lane_sum(x, ~mask) for x in values]
        return [jnp.where(mask, x, y) for x, y in zip(first, second)]

    def arrive(t):
        table_copy(t).wait()
        sum_ref[t, 0:ages] = pair_sum(lambda rs: cells_ref[t, rs], cross)

    def add_ages(t):
        age_sums(cells_ref.at[t], age_factor_ref[t, 0:ages], cross_ref, t * cross_rows, cross)

    def add_scaled(t):
        base = t * cross_rows
        total = pair_sum(
            lambda rs: cells_ref[t, rs] * cross_factor_ref[pl.ds(base + rs, 1), :], cross
        )
        sum_ref[t, 0:ages] = total * age_factor_ref[t, 0:ages]
        sum_ref[t, ages : 2 * pairs] = jnp.zeros((2 * pairs - ages, LANES), F32)

    def small_steps(group):
        bases = [t * cross_rows for t in group]
        by_race = [
            sum(cross_ref[pl.ds(base + s, races, stride=sizes), :] for s in range(sizes))
            for base in bases
        ]
        race_factor = [
            race_target_ref[t, 0:races] / margin for t, margin in zip(group, group_sums(by_race, hisp0))
        ]
        by_size = [
            sum(
                cross_ref[pl.ds(base + r * sizes, sizes), :] * factor[r : r + 1]
                for r in range(races)
            )
            for base, factor in zip(bases, race_factor)
        ]
        size_factor = [
            size_target_ref[t, 0:sizes] / margin for t, margin in zip(group, group_sums(by_size, ten0))
        ]
        by_income = [jnp.sum(x * y, axis=0, keepdims=True) for x, y in zip(by_size, size_factor)]
        by_income = [x + pltpu.roll(x, 64, 1) for x in by_income]
        by_income = [x + pltpu.roll(x, 32, 1) for x in by_income]
        for i, t in enumerate(group):
            target = jnp.concatenate([tenure_income_ref[t : t + 1, :]] * 4, axis=1)
            age_factor_ref[t, 0:ages] = age_factor_ref[t, 0:ages] * (target / by_income[i])
            for r in range(races):
                cross_factor_ref[pl.ds(bases[i] + r * sizes, sizes), :] = (
                    size_factor[i] * race_factor[i][r : r + 1]
                )
            cross_factor_ref[pl.ds(bases[i] + cross, cross_rows - cross), :] = jnp.zeros(
                (cross_rows - cross, LANES), F32
            )

    def pack(group):
        even = [sum_ref[t, pl.ds(0, pairs, stride=2)] for t in group]
        odd = [sum_ref[t, pl.ds(1, pairs, stride=2)] for t in group]
        even = [x + pltpu.roll(x, 96, 1) for x in even]
        odd = [x + pltpu.roll(x, 96, 1) for x in odd]
        packed = [
            jnp.where(
                lane < 32,
                x,
                jnp.where(
                    lane < 64,
                    pltpu.roll(x, 96, 1),
                    jnp.where(lane < 96, pltpu.roll(y, 64, 1), pltpu.roll(y, 32, 1)),
                ),
            )
            for x, y in zip(even, odd)
        ]
        for t, x in zip(group, packed):
            at = pl.ds(ids_ref[t], pairs, stride=pumas)
            rows_ref[at, :] = rows_ref[at, :] + x

    def work(group):
        margin = group_sums([sum_ref[t, 0:ages] for t in group], sex0)
        for t, x in zip(group, margin):
            age_factor_ref[t, 0:ages] = age_target_ref[t, 0:ages] / x
        each(group.start, group.stop, add_ages)
        small_steps(group)
        each(group.start, group.stop, add_scaled)
        pack(group)

    before = None
    for start in range(0, tracts, GROUP):
        if before is not None:
            work(before)
        before = range(start, min(start + GROUP, tracts))
        each(before.start, before.stop, arrive, 1)
    work(before)
    put_halves(rows_ref, [keep_ref], [send_ref])


def race_half(cells_ref, factor_ref, cross_factor_ref, chunk_refs, cross_ref, rows_ref, scalar_ref, half, pumas, ages, cross):
    tracts = cells_ref.shape[0]
    cross_rows = round_up(cross + 1, 8)
    pairs = sum(ref.shape[0] for ref in chunk_refs) // pumas
    count = 2 * pairs
    stride = round_up(count, 8)
    rows_ref[...] = jnp.zeros(rows_ref.shape, F32)
    lane = lane_ids(1)

    def add_ages(t):
        factor = factor_ref[t, 0:ages]
        cells = cells_ref.at[t, pl.ds(half * count, count)]
        age_sums(cells, factor, cross_ref, t * stride, count)

    each(0, tracts, add_ages)
    every = range(tracts)
    halves = []
    for first in range(2):
        margin = [
            cross_ref[pl.ds(t * stride + first, pairs, stride=2), :]
            * cross_factor_ref[pl.ds(t * cross_rows + half * count + first, pairs, stride=2), :]
            for t in every
        ]
        halves.append([x + pltpu.roll(x, 64, 1) for x in margin])
    for t in every:
        at = pl.ds(scalar_ref[t], pairs, stride=pumas)
        rows_ref[at, :] = rows_ref[at, :] + jnp.where(lane < 64, halves[0][t], halves[1][t])
    start = 0
    for ref in chunk_refs:
        ref[...] = rows_ref[start : start + ref.shape[0], :]
        start += ref.shape[0]


def race_send_kernel(
    ids_ref, cells_ref, age_factor_ref, cross_factor_ref, target_ref,
    own_ref, other_ref, *refs, cross
):
    *chunk_refs, scaled_factor_ref, cross_ref, age_rows_ref, rows_ref, scalar_ref = refs
    ages = 2 * (target_ref.shape[1] // LANES) + target_ref.shape[1] % LANES // 64
    pairs = (ages + 1) // 2
    pumas = target_ref.shape[0]
    every = range(cells_ref.shape[0])
    load_puma_numbers(ids_ref, scalar_ref)
    factor_rows(target_ref, [own_ref], [other_ref], age_rows_ref)
    lane = lane_ids(1)
    packed = [age_rows_ref[pl.ds(scalar_ref[t], pairs, stride=pumas), :] for t in every]
    quarter = [pltpu.roll(x, 32, 1) for x in packed]
    half = [pltpu.roll(x, 64, 1) for x in packed]
    back = [pltpu.roll(x, 96, 1) for x in packed]
    for t in every:
        even = jnp.where(lane < 32, packed[t], jnp.where(lane < 96, quarter[t], half[t]))
        odd = jnp.where(lane < 32, half[t], jnp.where(lane < 96, back[t], packed[t]))
        for first, factor in enumerate((even, odd)):
            at = pl.ds(first, pairs, stride=2)
            scaled_factor_ref[t, at] = factor * age_factor_ref[t, at]
    race_half(
        cells_ref, scaled_factor_ref, cross_factor_ref, chunk_refs, cross_ref, rows_ref, scalar_ref,
        1 - half_of(lax.axis_index("tract")), pumas, ages, cross,
    )


def race_keep_kernel(ids_ref, cells_ref, factor_ref, cross_factor_ref, *refs, ages, pumas, cross):
    *chunk_refs, cross_ref, rows_ref, scalar_ref = refs
    load_puma_numbers(ids_ref, scalar_ref)
    race_half(
        cells_ref, factor_ref, cross_factor_ref, chunk_refs, cross_ref, rows_ref, scalar_ref,
        half_of(lax.axis_index("tract")), pumas, ages, cross,
    )


def final_kernel(
    ids_ref, cells_ref, scaled_factor_ref, cross_factor_ref, target_ref, *refs
):
    *chunk_refs, out_ref, result_ref, cross_ref, rows_ref, scalar_ref, sems = refs
    chunks = len(chunk_refs) // 2
    tracts, cross, ages, _ = out_ref.shape
    cross_rows = round_up(cross + 1, 8)
    cross_pairs = (cross + 1) // 2
    pumas = target_ref.shape[0]
    load_puma_numbers(ids_ref, scalar_ref)
    factor_rows(target_ref, chunk_refs[:chunks], chunk_refs[chunks:], rows_ref)
    lane = lane_ids(1)

    def unpack(t):
        base = t * cross_rows
        packed = rows_ref[pl.ds(scalar_ref[t], cross_pairs, stride=pumas), :]
        half = pltpu.roll(packed, 64, 1)
        for first, factor in enumerate(
            (jnp.where(lane < 64, packed, half), jnp.where(lane < 64, half, packed))
        ):
            at = pl.ds(base + first, cross_pairs, stride=2)
            cross_ref[at, :] = factor * cross_factor_ref[at, :]

    def scale(t):
        factor = scaled_factor_ref[t, 0:ages]
        base = t * cross_rows
        for rs in range(cross):
            result_ref[t, rs] = cells_ref[t, rs] * factor * cross_ref[pl.ds(base + rs, 1), :]

    def send(t):
        pltpu.make_async_copy(result_ref.at[t], out_ref.at[t], sems.at[t]).start()

    def step(t, carry):
        scale(t)
        unpack(t + 1)
        send(t)
        return carry

    unpack(0)
    lax.fori_loop(0, tracts - 1, step, 0)
    scale(tracts - 1)
    send(tracts - 1)
    for t in range(tracts):
        pltpu.make_async_copy(result_ref.at[t], out_ref.at[t], sems.at[t]).wait()


def call(kernel, out_shapes, in_spaces, out_spaces, scratch):
    def spec(space):
        return pl.BlockSpec(memory_space=space)

    run = pl.pallas_call(
        kernel,
        out_shape=[
            space(shape, F32) for shape, space in zip(out_shapes, out_spaces, strict=True)
        ],
        in_specs=[spec(space) for space in in_spaces],
        out_specs=[spec(space) for space in out_spaces],
        scratch_shapes=scratch,
        compiler_params=pltpu.CompilerParams(vmem_limit_bytes=40 << 20),
    )

    def placed(*args):
        return run(*map(pltpu.with_memory_space_constraint, args, in_spaces))

    return placed


def per_device(
    devices,
    table, age_sex, race_hisp, size_tenure, tenure_income, puma_age, puma_race, tract_puma,
):
    tracts, ages, races, sizes, inner = table.shape
    pumas = puma_age.shape[0]
    cross = races * sizes
    age_pairs, cross_pairs = (ages + 1) // 2, (cross + 1) // 2
    age_rows = 2 * round_up(age_pairs, 8)
    cross_rows = tracts * round_up(cross + 1, 8) + 2 * round_up(cross_pairs, 8)
    age_sum_rows, cross_sum_rows = (round_up(x, 8) * pumas for x in (age_pairs, cross_pairs))
    vmem, hbm = pltpu.VMEM, pltpu.HBM

    cells = table.transpose(0, 2, 3, 1, 4).reshape(tracts, cross, ages, inner)
    cells_scratch = pltpu.VMEM((tracts, cross, ages, inner), F32)
    cross_scratch = pltpu.VMEM((cross_rows, LANES), F32)
    copy_sems = pltpu.SemaphoreType.DMA((tracts,))
    numbers_scratch = pltpu.SMEM((tracts,), jnp.int32)

    bits = [1 << k for k in range(1, devices.bit_length() - 1)]
    orders = (bits, bits[1:] + bits[:1])

    def swap(x, partner):
        return lax.ppermute(x, "tract", [(i, partner(i)) for i in range(devices)])

    def totals(keep, send):
        keep = [x + swap(y, lambda i: i ^ 1) for x, y in zip(keep, send)]
        for step in range(len(bits)):
            keep = [x + swap(x, lambda i: i ^ orders[i.bit_count() % 2][step] ^ 1) for x in keep]
        return *keep, *[swap(x, lambda i: i ^ 1) for x in keep]

    age_half, cross_half = -(-age_pairs // 2), -(-cross_pairs // 2)
    cross_chunks = [cross_half - cross_half // 2, cross_half // 2]
    age_shape, cross_shape = (tracts, age_rows, LANES), (cross_rows, LANES)
    small = [age_sex, race_hisp, size_tenure, tenure_income]
    keep, send, age_factor, cross_factor, cells = call(
        functools.partial(rake_kernel, races=races, sizes=sizes, pumas=pumas),
        [(age_half * pumas, LANES)] * 2
        + [age_shape, cross_shape, (tracts, 4 * cross_half, ages, inner)],
        [hbm] * 6,
        [vmem] * 5,
        [
            pltpu.VMEM(age_shape, F32),
            cross_scratch,
            pltpu.VMEM((age_sum_rows, LANES), F32),
            pltpu.VMEM(age_shape, F32),
            pltpu.VMEM((tracts, round_up(races, 8), LANES), F32),
            pltpu.VMEM((tracts, round_up(sizes, 8), LANES), F32),
            numbers_scratch,
        ]
        + [pltpu.VMEM(x.shape, F32) for x in small]
        + [copy_sems, pltpu.SemaphoreType.DMA((1 + len(small),))],
    )(tract_puma, cells, *small)

    half_scratch = [
        pltpu.VMEM((tracts * round_up(2 * cross_half, 8) + 16, LANES), F32),
        pltpu.VMEM((round_up(cross_half, 8) * pumas, LANES), F32),
    ]
    chunk_shapes = [(rows * pumas, LANES) for rows in cross_chunks]
    *send, scaled_factor = call(
        functools.partial(race_send_kernel, cross=cross),
        chunk_shapes + [age_shape],
        [vmem] * 7,
        [vmem] * (len(cross_chunks) + 1),
        [half_scratch[0], pltpu.VMEM((age_sum_rows, LANES), F32), half_scratch[1], numbers_scratch],
    )(tract_puma, cells, age_factor, cross_factor, puma_age, *totals([keep], [send]))
    keep = call(
        functools.partial(race_keep_kernel, ages=ages, pumas=pumas, cross=cross),
        chunk_shapes,
        [vmem] * 4,
        [vmem] * len(cross_chunks),
        half_scratch + [numbers_scratch],
    )(tract_puma, cells, scaled_factor, cross_factor)

    out, = call(
        final_kernel,
        [(tracts, cross, ages, inner)],
        [vmem] * (5 + 2 * len(cross_chunks)),
        [hbm],
        [
            cells_scratch,
            cross_scratch,
            pltpu.VMEM((cross_sum_rows, LANES), F32),
            numbers_scratch,
            copy_sems,
        ],
    )(tract_puma, cells, scaled_factor, cross_factor, puma_race, *totals(keep, send))
    return out.reshape(tracts, races, sizes, ages, inner).transpose(0, 3, 1, 2, 4)


def solution(mesh):
    in_specs = (
        P(("grp", "tract"), None, None, None, None),
        P(("grp", "tract"), None),
        P(("grp", "tract"), None),
        P(("grp", "tract"), None),
        P(("grp", "tract"), None),
        P("grp", None),
        P("grp", None),
        P(("grp", "tract")),
    )
    out_specs = P(("grp", "tract"), None, None, None, None)
    return jax.shard_map(
        functools.partial(per_device, mesh.shape["tract"]),
        mesh=mesh, in_specs=in_specs, out_specs=out_specs, check_vma=False,
    )
```

```python
import functools

import jax
import jax.numpy as jnp
from jax import lax
from jax.experimental import pallas as pl
from jax.experimental.pallas import tpu as pltpu
from jax.sharding import PartitionSpec as P

LANES = 128
GROUP = 6
FIRST = 6
F32 = jnp.float32


def round_up(value, step):
    return -(-value // step) * step


def lane_ids(rows):
    return lax.broadcasted_iota(jnp.int32, (rows, LANES), 1)


def masked_lane_sum(value, mask):
    return jnp.sum(jnp.where(mask, value, 0.0), axis=-1, keepdims=True)


def column_of(row, rows, step, offset):
    width = row.shape[-1]
    lane = lax.broadcasted_iota(jnp.int32, (rows, width), 1)
    sub = lax.broadcasted_iota(jnp.int32, (rows, width), 0)
    return jnp.sum(jnp.where(lane == step * sub + offset, row, 0.0), axis=-1, keepdims=True)


def half_of(index):
    total = index
    for k in range(1, 16):
        total = total + lax.shift_right_logical(index, k)
    return lax.rem(total, 2)


def factor_rows(target_ref, own_refs, other_refs, rows_ref):
    pumas, columns = target_ref.shape
    half = half_of(lax.axis_index("tract"))
    half_rows = sum(ref.shape[0] for ref in own_refs)
    for refs, which in ((own_refs, half), (other_refs, 1 - half)):
        start = which * half_rows
        for ref in refs:
            rows_ref[pl.ds(pl.multiple_of(start, 8), ref.shape[0]), :] = ref[...]
            start = start + ref.shape[0]
    for first in range(0, columns, LANES):
        width = min(columns - first, LANES)
        at = slice(first // LANES * pumas, (first // LANES + 1) * pumas)
        rows_ref[at, 0:width] = target_ref[:, first : first + width] / rows_ref[at, 0:width]


def load_puma_numbers(ids_ref, scalar_ref):
    ids = ids_ref[...]
    for t in range(scalar_ref.shape[0]):
        scalar_ref[t] = ids[t]


def put_halves(rows_ref, keep_refs, send_refs):
    half = half_of(lax.axis_index("tract"))
    half_rows = sum(ref.shape[0] for ref in keep_refs)
    for refs, which in ((keep_refs, half), (send_refs, 1 - half)):
        start = which * half_rows
        for ref in refs:
            ref[...] = rows_ref[pl.ds(pl.multiple_of(start, 8), ref.shape[0]), :]
            start = start + ref.shape[0]


def merge(first, second, step):
    low = lax.rem(lax.broadcasted_iota(jnp.int32, (8, 1), 0) // step, 2) == 0
    if step == 4:
        return jnp.where(low, first, second) + pltpu.roll(jnp.where(low, second, first), 4, 0)
    return jnp.where(low, first + pltpu.roll(first, 8 - step, 0), second + pltpu.roll(second, step, 0))


def each(start, stop, body, width=3):
    def turn(i, carry):
        for k in range(width):
            body(start + width * i + k)
        return carry

    turns = (stop - start) // width
    lax.fori_loop(0, turns, turn, 0)
    for t in range(start + width * turns, stop):
        body(t)


def age_sums(cells_ref, factor, cross_ref, base, count):
    ages = factor.shape[0]

    def tile(k):
        total = None
        for at in range(0, ages, 8):
            stop = min(at + 8, ages)
            part = cells_ref[k, at:stop] * factor[at:stop]
            if stop < at + 8:
                part = jnp.concatenate([part, jnp.zeros((at + 8 - stop, LANES), F32)], axis=0)
            total = part if total is None else total + part
        return total

    for start in range(0, count, 8):
        tiles = [tile(k) for k in range(start, min(start + 8, count))]
        if len(tiles) < 8:
            for k, x in enumerate(tiles):
                cross_ref[pl.ds(base + start + k, 1), :] = jnp.sum(x, axis=0, keepdims=True)
            continue
        tiles = [merge(tiles[k], tiles[k + 4], 4) for k in range(4)]
        tiles = [merge(tiles[k], tiles[k + 2], 2) for k in range(2)]
        cross_ref[pl.ds(pl.multiple_of(base + start, 8), 8), :] = merge(tiles[0], tiles[1], 1)


def pair_sum(term, count):
    first, second = term(0), term(1)
    for k in range(2, count, 2):
        first = first + term(k)
        if k + 1 < count:
            second = second + term(k + 1)
    return first + second


def rake_kernel(
    ids_hbm, table_hbm, age_sex_hbm, race_hisp_hbm, size_tenure_hbm, tenure_income_hbm,
    keep_ref, send_ref, age_factor_ref, cross_factor_ref, cells_ref,
    sum_ref, cross_ref, rows_ref, age_target_ref, race_target_ref, size_target_ref,
    ids_ref, age_sex_ref, race_hisp_ref, size_tenure_ref, tenure_income_ref,
    sems, small_sems,
    *, races, sizes, pumas,
):
    tracts, cross, ages, _ = table_hbm.shape
    cross_rows = round_up(cross + 1, 8)
    pairs = (ages + 1) // 2
    small = [
        pltpu.make_async_copy(source, target, small_sems.at[i])
        for i, (source, target) in enumerate((
            (ids_hbm, ids_ref),
            (age_sex_hbm, age_sex_ref),
            (race_hisp_hbm, race_hisp_ref),
            (size_tenure_hbm, size_tenure_ref),
            (tenure_income_hbm, tenure_income_ref),
        ))
    ]

    def table_copy(t):
        return pltpu.make_async_copy(table_hbm.at[t], cells_ref.at[t, 0:cross], sems.at[t])

    for copy in small:
        copy.start()
    for t in range(min(FIRST, tracts)):
        table_copy(t).start()
    lane = lane_ids(1)
    sex0 = lane < 64
    hisp0 = (lane // 32) % 2 == 0
    ten0 = (lane // 16) % 2 == 0

    rows_ref[...] = jnp.zeros(rows_ref.shape, F32)
    for copy in small:
        copy.wait()
    for source_ref, target_ref, rows, mask in (
        (age_sex_ref, age_target_ref, ages, sex0),
        (race_hisp_ref, race_target_ref, races, hisp0),
        (size_tenure_ref, size_target_ref, sizes, ten0),
    ):
        for t in range(tracts):
            row = source_ref[t : t + 1, :]
            target_ref[t, 0:rows] = jnp.where(
                mask, column_of(row, rows, 2, 0), column_of(row, rows, 2, 1)
            )

    for t in range(FIRST, tracts):
        table_copy(t).start()

    def group_sums(values, mask):
        first = [masked_lane_sum(x, mask) for x in values]
        second = [masked_lane_sum(x, ~mask) for x in values]
        return [jnp.where(mask, x, y) for x, y in zip(first, second)]

    def arrive(t):
        table_copy(t).wait()
        sum_ref[t, 0:ages] = pair_sum(lambda rs: cells_ref[t, rs], cross)

    def add_ages(t):
        age_sums(cells_ref.at[t], age_factor_ref[t, 0:ages], cross_ref, t * cross_rows, cross)

    def add_scaled(t):
        base = t * cross_rows
        total = pair_sum(
            lambda rs: cells_ref[t, rs] * cross_factor_ref[pl.ds(base + rs, 1), :], cross
        )
        sum_ref[t, 0:ages] = total * age_factor_ref[t, 0:ages]
        sum_ref[t, ages : 2 * pairs] = jnp.zeros((2 * pairs - ages, LANES), F32)

    def small_steps(group):
        bases = [t * cross_rows for t in group]
        by_race = [
            sum(cross_ref[pl.ds(base + s, races, stride=sizes), :] for s in range(sizes))
            for base in bases
        ]
        race_factor = [
            race_target_ref[t, 0:races] / margin for t, margin in zip(group, group_sums(by_race, hisp0))
        ]
        by_size = [
            sum(
                cross_ref[pl.ds(base + r * sizes, sizes), :] * factor[r : r + 1]
                for r in range(races)
            )
            for base, factor in zip(bases, race_factor)
        ]
        size_factor = [
            size_target_ref[t, 0:sizes] / margin for t, margin in zip(group, group_sums(by_size, ten0))
        ]
        by_income = [jnp.sum(x * y, axis=0, keepdims=True) for x, y in zip(by_size, size_factor)]
        by_income = [x + pltpu.roll(x, 64, 1) for x in by_income]
        by_income = [x + pltpu.roll(x, 32, 1) for x in by_income]
        for i, t in enumerate(group):
            target = jnp.concatenate([tenure_income_ref[t : t + 1, :]] * 4, axis=1)
            age_factor_ref[t, 0:ages] = age_factor_ref[t, 0:ages] * (target / by_income[i])
            for r in range(races):
                cross_factor_ref[pl.ds(bases[i] + r * sizes, sizes), :] = (
                    size_factor[i] * race_factor[i][r : r + 1]
                )
            cross_factor_ref[pl.ds(bases[i] + cross, cross_rows - cross), :] = jnp.zeros(
                (cross_rows - cross, LANES), F32
            )

    def pack(group):
        even = [sum_ref[t, pl.ds(0, pairs, stride=2)] for t in group]
        odd = [sum_ref[t, pl.ds(1, pairs, stride=2)] for t in group]
        even = [x + pltpu.roll(x, 96, 1) for x in even]
        odd = [x + pltpu.roll(x, 96, 1) for x in odd]
        packed = [
            jnp.where(
                lane < 32,
                x,
                jnp.where(
                    lane < 64,
                    pltpu.roll(x, 96, 1),
                    jnp.where(lane < 96, pltpu.roll(y, 64, 1), pltpu.roll(y, 32, 1)),
                ),
            )
            for x, y in zip(even, odd)
        ]
        for t, x in zip(group, packed):
            at = pl.ds(ids_ref[t], pairs, stride=pumas)
            rows_ref[at, :] = rows_ref[at, :] + x

    def work(group):
        margin = group_sums([sum_ref[t, 0:ages] for t in group], sex0)
        for t, x in zip(group, margin):
            age_factor_ref[t, 0:ages] = age_target_ref[t, 0:ages] / x
        each(group.start, group.stop, add_ages)
        small_steps(group)
        each(group.start, group.stop, add_scaled)
        pack(group)

    before = None
    for start in range(0, tracts, GROUP):
        if before is not None:
            work(before)
        before = range(start, min(start + GROUP, tracts))
        each(before.start, before.stop, arrive, 1)
    work(before)
    put_halves(rows_ref, [keep_ref], [send_ref])


def race_half(cells_ref, factor_ref, cross_factor_ref, chunk_refs, cross_ref, rows_ref, scalar_ref, half, pumas, ages, cross):
    tracts = cells_ref.shape[0]
    cross_rows = round_up(cross + 1, 8)
    pairs = sum(ref.shape[0] for ref in chunk_refs) // pumas
    count = 2 * pairs
    stride = round_up(count, 8)
    rows_ref[...] = jnp.zeros(rows_ref.shape, F32)
    lane = lane_ids(1)

    def add_ages(t):
        factor = factor_ref[t, 0:ages]
        cells = cells_ref.at[t, pl.ds(half * count, count)]
        age_sums(cells, factor, cross_ref, t * stride, count)

    each(0, tracts, add_ages)
    every = range(tracts)
    halves = []
    for first in range(2):
        margin = [
            cross_ref[pl.ds(t * stride + first, pairs, stride=2), :]
            * cross_factor_ref[pl.ds(t * cross_rows + half * count + first, pairs, stride=2), :]
            for t in every
        ]
        halves.append([x + pltpu.roll(x, 64, 1) for x in margin])
    for t in every:
        at = pl.ds(scalar_ref[t], pairs, stride=pumas)
        rows_ref[at, :] = rows_ref[at, :] + jnp.where(lane < 64, halves[0][t], halves[1][t])
    start = 0
    for ref in chunk_refs:
        ref[...] = rows_ref[start : start + ref.shape[0], :]
        start += ref.shape[0]


def race_send_kernel(
    ids_ref, cells_ref, age_factor_ref, cross_factor_ref, target_ref,
    own_ref, other_ref, *refs, cross
):
    *chunk_refs, scaled_factor_ref, cross_ref, age_rows_ref, rows_ref, scalar_ref = refs
    ages = 2 * (target_ref.shape[1] // LANES) + target_ref.shape[1] % LANES // 64
    pairs = (ages + 1) // 2
    pumas = target_ref.shape[0]
    every = range(cells_ref.shape[0])
    load_puma_numbers(ids_ref, scalar_ref)
    factor_rows(target_ref, [own_ref], [other_ref], age_rows_ref)
    lane = lane_ids(1)
    packed = [age_rows_ref[pl.ds(scalar_ref[t], pairs, stride=pumas), :] for t in every]
    quarter = [pltpu.roll(x, 32, 1) for x in packed]
    half = [pltpu.roll(x, 64, 1) for x in packed]
    back = [pltpu.roll(x, 96, 1) for x in packed]
    for t in every:
        even = jnp.where(lane < 32, packed[t], jnp.where(lane < 96, quarter[t], half[t]))
        odd = jnp.where(lane < 32, half[t], jnp.where(lane < 96, back[t], packed[t]))
        for first, factor in enumerate((even, odd)):
            at = pl.ds(first, pairs, stride=2)
            scaled_factor_ref[t, at] = factor * age_factor_ref[t, at]
    race_half(
        cells_ref, scaled_factor_ref, cross_factor_ref, chunk_refs, cross_ref, rows_ref, scalar_ref,
        1 - half_of(lax.axis_index("tract")), pumas, ages, cross,
    )


def race_keep_kernel(ids_ref, cells_ref, factor_ref, cross_factor_ref, *refs, ages, pumas, cross):
    *chunk_refs, cross_ref, rows_ref, scalar_ref = refs
    load_puma_numbers(ids_ref, scalar_ref)
    race_half(
        cells_ref, factor_ref, cross_factor_ref, chunk_refs, cross_ref, rows_ref, scalar_ref,
        half_of(lax.axis_index("tract")), pumas, ages, cross,
    )


def final_kernel(
    ids_ref, cells_ref, scaled_factor_ref, cross_factor_ref, target_ref, *refs
):
    *chunk_refs, out_ref, result_ref, cross_ref, rows_ref, scalar_ref, sems = refs
    chunks = len(chunk_refs) // 2
    tracts, cross, ages, _ = out_ref.shape
    cross_rows = round_up(cross + 1, 8)
    cross_pairs = (cross + 1) // 2
    pumas = target_ref.shape[0]
    load_puma_numbers(ids_ref, scalar_ref)
    factor_rows(target_ref, chunk_refs[:chunks], chunk_refs[chunks:], rows_ref)
    lane = lane_ids(1)

    def unpack(t):
        base = t * cross_rows
        packed = rows_ref[pl.ds(scalar_ref[t], cross_pairs, stride=pumas), :]
        half = pltpu.roll(packed, 64, 1)
        for first, factor in enumerate(
            (jnp.where(lane < 64, packed, half), jnp.where(lane < 64, half, packed))
        ):
            at = pl.ds(base + first, cross_pairs, stride=2)
            cross_ref[at, :] = factor * cross_factor_ref[at, :]

    def scale(t):
        factor = scaled_factor_ref[t, 0:ages]
        base = t * cross_rows
        for rs in range(cross):
            result_ref[t, rs] = cells_ref[t, rs] * factor * cross_ref[pl.ds(base + rs, 1), :]

    def send(t):
        pltpu.make_async_copy(result_ref.at[t], out_ref.at[t], sems.at[t]).start()

    def step(t, carry):
        scale(t)
        unpack(t + 1)
        send(t)
        return carry

    unpack(0)
    lax.fori_loop(0, tracts - 1, step, 0)
    scale(tracts - 1)
    send(tracts - 1)
    for t in range(tracts):
        pltpu.make_async_copy(result_ref.at[t], out_ref.at[t], sems.at[t]).wait()


def call(kernel, out_shapes, in_spaces, out_spaces, scratch):
    def spec(space):
        return pl.BlockSpec(memory_space=space)

    run = pl.pallas_call(
        kernel,
        out_shape=[
            space(shape, F32) for shape, space in zip(out_shapes, out_spaces, strict=True)
        ],
        in_specs=[spec(space) for space in in_spaces],
        out_specs=[spec(space) for space in out_spaces],
        scratch_shapes=scratch,
        compiler_params=pltpu.CompilerParams(vmem_limit_bytes=40 << 20),
    )

    def placed(*args):
        return run(*map(pltpu.with_memory_space_constraint, args, in_spaces))

    return placed


def per_device(
    devices,
    table, age_sex, race_hisp, size_tenure, tenure_income, puma_age, puma_race, tract_puma,
):
    tracts, ages, races, sizes, inner = table.shape
    pumas = puma_age.shape[0]
    cross = races * sizes
    age_pairs, cross_pairs = (ages + 1) // 2, (cross + 1) // 2
    age_rows = 2 * round_up(age_pairs, 8)
    cross_rows = tracts * round_up(cross + 1, 8) + 2 * round_up(cross_pairs, 8)
    age_sum_rows, cross_sum_rows = (round_up(x, 8) * pumas for x in (age_pairs, cross_pairs))
    vmem, hbm = pltpu.VMEM, pltpu.HBM

    cells = table.transpose(0, 2, 3, 1, 4).reshape(tracts, cross, ages, inner)
    cells_scratch = pltpu.VMEM((tracts, cross, ages, inner), F32)
    cross_scratch = pltpu.VMEM((cross_rows, LANES), F32)
    copy_sems = pltpu.SemaphoreType.DMA((tracts,))
    numbers_scratch = pltpu.SMEM((tracts,), jnp.int32)

    bits = [1 << k for k in range(1, devices.bit_length() - 1)]
    orders = (bits, bits[1:] + bits[:1])

    def swap(x, partner):
        return lax.ppermute(x, "tract", [(i, partner(i)) for i in range(devices)])

    def totals(keep, send):
        keep = [x + swap(y, lambda i: i ^ 1) for x, y in zip(keep, send)]
        for step in range(len(bits)):
            keep = [x + swap(x, lambda i: i ^ orders[i.bit_count() % 2][step] ^ 1) for x in keep]
        return *keep, *[swap(x, lambda i: i ^ 1) for x in keep]

    age_half, cross_half = -(-age_pairs // 2), -(-cross_pairs // 2)
    cross_chunks = [cross_half - cross_half * 2 // 5, cross_half * 2 // 5]
    age_shape, cross_shape = (tracts, age_rows, LANES), (cross_rows, LANES)
    small = [age_sex, race_hisp, size_tenure, tenure_income]
    keep, send, age_factor, cross_factor, cells = call(
        functools.partial(rake_kernel, races=races, sizes=sizes, pumas=pumas),
        [(age_half * pumas, LANES)] * 2
        + [age_shape, cross_shape, (tracts, 4 * cross_half, ages, inner)],
        [hbm] * 6,
        [vmem] * 5,
        [
            pltpu.VMEM(age_shape, F32),
            cross_scratch,
            pltpu.VMEM((age_sum_rows, LANES), F32),
            pltpu.VMEM(age_shape, F32),
            pltpu.VMEM((tracts, round_up(races, 8), LANES), F32),
            pltpu.VMEM((tracts, round_up(sizes, 8), LANES), F32),
            numbers_scratch,
        ]
        + [pltpu.VMEM(x.shape, F32) for x in small]
        + [copy_sems, pltpu.SemaphoreType.DMA((1 + len(small),))],
    )(tract_puma, cells, *small)

    half_scratch = [
        pltpu.VMEM((tracts * round_up(2 * cross_half, 8) + 16, LANES), F32),
        pltpu.VMEM((round_up(cross_half, 8) * pumas, LANES), F32),
    ]
    chunk_shapes = [(rows * pumas, LANES) for rows in cross_chunks]
    *send, scaled_factor = call(
        functools.partial(race_send_kernel, cross=cross),
        chunk_shapes + [age_shape],
        [vmem] * 7,
        [vmem] * (len(cross_chunks) + 1),
        [half_scratch[0], pltpu.VMEM((age_sum_rows, LANES), F32), half_scratch[1], numbers_scratch],
    )(tract_puma, cells, age_factor, cross_factor, puma_age, *totals([keep], [send]))
    keep = call(
        functools.partial(race_keep_kernel, ages=ages, pumas=pumas, cross=cross),
        chunk_shapes,
        [vmem] * 4,
        [vmem] * len(cross_chunks),
        half_scratch + [numbers_scratch],
    )(tract_puma, cells, scaled_factor, cross_factor)

    out, = call(
        final_kernel,
        [(tracts, cross, ages, inner)],
        [vmem] * (5 + 2 * len(cross_chunks)),
        [hbm],
        [
            cells_scratch,
            cross_scratch,
            pltpu.VMEM((cross_sum_rows, LANES), F32),
            numbers_scratch,
            copy_sems,
        ],
    )(tract_puma, cells, scaled_factor, cross_factor, puma_race, *totals(keep, send))
    return out.reshape(tracts, races, sizes, ages, inner).transpose(0, 3, 1, 2, 4)


def solution(mesh):
    in_specs = (
        P(("grp", "tract"), None, None, None, None),
        P(("grp", "tract"), None),
        P(("grp", "tract"), None),
        P(("grp", "tract"), None),
        P(("grp", "tract"), None),
        P("grp", None),
        P("grp", None),
        P(("grp", "tract")),
    )
    out_specs = P(("grp", "tract"), None, None, None, None)
    return jax.shard_map(
        functools.partial(per_device, mesh.shape["tract"]),
        mesh=mesh, in_specs=in_specs, out_specs=out_specs, check_vma=False,
    )
```

```python
import functools

import jax
import jax.numpy as jnp
from jax import lax
from jax.experimental import pallas as pl
from jax.experimental.pallas import tpu as pltpu
from jax.sharding import PartitionSpec as P

LANES = 128
GROUP = 6
FIRST = 6
F32 = jnp.float32


def round_up(value, step):
    return -(-value // step) * step


def lane_ids(rows):
    return lax.broadcasted_iota(jnp.int32, (rows, LANES), 1)


def masked_lane_sum(value, mask):
    return jnp.sum(jnp.where(mask, value, 0.0), axis=-1, keepdims=True)


def column_of(row, rows, step, offset):
    width = row.shape[-1]
    lane = lax.broadcasted_iota(jnp.int32, (rows, width), 1)
    sub = lax.broadcasted_iota(jnp.int32, (rows, width), 0)
    return jnp.sum(jnp.where(lane == step * sub + offset, row, 0.0), axis=-1, keepdims=True)


def half_of(index):
    total = index
    for k in range(1, 16):
        total = total + lax.shift_right_logical(index, k)
    return lax.rem(total, 2)


def factor_rows(target_ref, own_refs, other_refs, rows_ref):
    pumas, columns = target_ref.shape
    half = half_of(lax.axis_index("tract"))
    half_rows = sum(ref.shape[0] for ref in own_refs)
    for refs, which in ((own_refs, half), (other_refs, 1 - half)):
        start = which * half_rows
        for ref in refs:
            rows_ref[pl.ds(pl.multiple_of(start, 8), ref.shape[0]), :] = ref[...]
            start = start + ref.shape[0]
    for first in range(0, columns, LANES):
        width = min(columns - first, LANES)
        at = slice(first // LANES * pumas, (first // LANES + 1) * pumas)
        rows_ref[at, 0:width] = target_ref[:, first : first + width] / rows_ref[at, 0:width]


def load_puma_numbers(ids_ref, scalar_ref):
    ids = ids_ref[...]
    for t in range(scalar_ref.shape[0]):
        scalar_ref[t] = ids[t]


def put_halves(rows_ref, keep_refs, send_refs):
    half = half_of(lax.axis_index("tract"))
    half_rows = sum(ref.shape[0] for ref in keep_refs)
    for refs, which in ((keep_refs, half), (send_refs, 1 - half)):
        start = which * half_rows
        for ref in refs:
            ref[...] = rows_ref[pl.ds(pl.multiple_of(start, 8), ref.shape[0]), :]
            start = start + ref.shape[0]


def merge(first, second, step):
    low = lax.rem(lax.broadcasted_iota(jnp.int32, (8, 1), 0) // step, 2) == 0
    if step == 4:
        return jnp.where(low, first, second) + pltpu.roll(jnp.where(low, second, first), 4, 0)
    return jnp.where(low, first + pltpu.roll(first, 8 - step, 0), second + pltpu.roll(second, step, 0))


def each(start, stop, body, width=3):
    def turn(i, carry):
        for k in range(width):
            body(start + width * i + k)
        return carry

    turns = (stop - start) // width
    lax.fori_loop(0, turns, turn, 0)
    for t in range(start + width * turns, stop):
        body(t)


def age_sums(cells_ref, factor, cross_ref, base, count):
    ages = factor.shape[0]

    def tile(k):
        total = None
        for at in range(0, ages, 8):
            stop = min(at + 8, ages)
            part = cells_ref[k, at:stop] * factor[at:stop]
            if stop < at + 8:
                part = jnp.concatenate([part, jnp.zeros((at + 8 - stop, LANES), F32)], axis=0)
            total = part if total is None else total + part
        return total

    for start in range(0, count, 8):
        tiles = [tile(k) for k in range(start, min(start + 8, count))]
        if len(tiles) < 8:
            for k, x in enumerate(tiles):
                cross_ref[pl.ds(base + start + k, 1), :] = jnp.sum(x, axis=0, keepdims=True)
            continue
        tiles = [merge(tiles[k], tiles[k + 4], 4) for k in range(4)]
        tiles = [merge(tiles[k], tiles[k + 2], 2) for k in range(2)]
        cross_ref[pl.ds(pl.multiple_of(base + start, 8), 8), :] = merge(tiles[0], tiles[1], 1)


def pair_sum(term, count):
    first, second = term(0), term(1)
    for k in range(2, count, 2):
        first = first + term(k)
        if k + 1 < count:
            second = second + term(k + 1)
    return first + second


def rake_kernel(
    ids_hbm, table_hbm, age_sex_hbm, race_hisp_hbm, size_tenure_hbm, tenure_income_hbm,
    keep_ref, send_ref, age_factor_ref, cross_factor_ref, cells_ref,
    sum_ref, cross_ref, rows_ref, age_target_ref, race_target_ref, size_target_ref,
    ids_ref, age_sex_ref, race_hisp_ref, size_tenure_ref, tenure_income_ref,
    sems, small_sems,
    *, races, sizes, pumas,
):
    tracts, cross, ages, _ = table_hbm.shape
    cross_rows = round_up(cross + 1, 8)
    pairs = (ages + 1) // 2
    small = [
        pltpu.make_async_copy(source, target, small_sems.at[i])
        for i, (source, target) in enumerate((
            (ids_hbm, ids_ref),
            (age_sex_hbm, age_sex_ref),
            (race_hisp_hbm, race_hisp_ref),
            (size_tenure_hbm, size_tenure_ref),
            (tenure_income_hbm, tenure_income_ref),
        ))
    ]

    def table_copy(t):
        return pltpu.make_async_copy(table_hbm.at[t], cells_ref.at[t, 0:cross], sems.at[t])

    for copy in small:
        copy.start()
    for t in range(min(FIRST, tracts)):
        table_copy(t).start()
    lane = lane_ids(1)
    sex0 = lane < 64
    hisp0 = (lane // 32) % 2 == 0
    ten0 = (lane // 16) % 2 == 0

    rows_ref[...] = jnp.zeros(rows_ref.shape, F32)
    for copy in small:
        copy.wait()
    for t in range(FIRST, tracts):
        table_copy(t).start()
    for source_ref, target_ref, rows, mask in (
        (age_sex_ref, age_target_ref, ages, sex0),
        (race_hisp_ref, race_target_ref, races, hisp0),
        (size_tenure_ref, size_target_ref, sizes, ten0),
    ):
        for t in range(tracts):
            row = source_ref[t : t + 1, :]
            target_ref[t, 0:rows] = jnp.where(
                mask, column_of(row, rows, 2, 0), column_of(row, rows, 2, 1)
            )

    def group_sums(values, mask):
        first = [masked_lane_sum(x, mask) for x in values]
        second = [masked_lane_sum(x, ~mask) for x in values]
        return [jnp.where(mask, x, y) for x, y in zip(first, second)]

    def arrive(t):
        table_copy(t).wait()
        sum_ref[t, 0:ages] = pair_sum(lambda rs: cells_ref[t, rs], cross)

    def add_ages(t):
        age_sums(cells_ref.at[t], age_factor_ref[t, 0:ages], cross_ref, t * cross_rows, cross)

    def add_scaled(t):
        base = t * cross_rows
        total = pair_sum(
            lambda rs: cells_ref[t, rs] * cross_factor_ref[pl.ds(base + rs, 1), :], cross
        )
        sum_ref[t, 0:ages] = total * age_factor_ref[t, 0:ages]
        sum_ref[t, ages : 2 * pairs] = jnp.zeros((2 * pairs - ages, LANES), F32)

    def small_steps(group):
        bases = [t * cross_rows for t in group]
        by_race = [
            sum(cross_ref[pl.ds(base + s, races, stride=sizes), :] for s in range(sizes))
            for base in bases
        ]
        race_factor = [
            race_target_ref[t, 0:races] / margin for t, margin in zip(group, group_sums(by_race, hisp0))
        ]
        by_size = [
            sum(
                cross_ref[pl.ds(base + r * sizes, sizes), :] * factor[r : r + 1]
                for r in range(races)
            )
            for base, factor in zip(bases, race_factor)
        ]
        size_factor = [
            size_target_ref[t, 0:sizes] / margin for t, margin in zip(group, group_sums(by_size, ten0))
        ]
        by_income = [jnp.sum(x * y, axis=0, keepdims=True) for x, y in zip(by_size, size_factor)]
        by_income = [x + pltpu.roll(x, 64, 1) for x in by_income]
        by_income = [x + pltpu.roll(x, 32, 1) for x in by_income]
        for i, t in enumerate(group):
            target = jnp.concatenate([tenure_income_ref[t : t + 1, :]] * 4, axis=1)
            age_factor_ref[t, 0:ages] = age_factor_ref[t, 0:ages] * (target / by_income[i])
            for r in range(races):
                cross_factor_ref[pl.ds(bases[i] + r * sizes, sizes), :] = (
                    size_factor[i] * race_factor[i][r : r + 1]
                )
            cross_factor_ref[pl.ds(bases[i] + cross, cross_rows - cross), :] = jnp.zeros(
                (cross_rows - cross, LANES), F32
            )

    def pack(group):
        even = [sum_ref[t, pl.ds(0, pairs, stride=2)] for t in group]
        odd = [sum_ref[t, pl.ds(1, pairs, stride=2)] for t in group]
        even = [x + pltpu.roll(x, 96, 1) for x in even]
        odd = [x + pltpu.roll(x, 96, 1) for x in odd]
        packed = [
            jnp.where(
                lane < 32,
                x,
                jnp.where(
                    lane < 64,
                    pltpu.roll(x, 96, 1),
                    jnp.where(lane < 96, pltpu.roll(y, 64, 1), pltpu.roll(y, 32, 1)),
                ),
            )
            for x, y in zip(even, odd)
        ]
        for t, x in zip(group, packed):
            at = pl.ds(ids_ref[t], pairs, stride=pumas)
            rows_ref[at, :] = rows_ref[at, :] + x

    def work(group):
        margin = group_sums([sum_ref[t, 0:ages] for t in group], sex0)
        for t, x in zip(group, margin):
            age_factor_ref[t, 0:ages] = age_target_ref[t, 0:ages] / x
        each(group.start, group.stop, add_ages)
        small_steps(group)
        each(group.start, group.stop, add_scaled)
        pack(group)

    before = None
    for start in range(0, tracts, GROUP):
        if before is not None:
            work(before)
        before = range(start, min(start + GROUP, tracts))
        each(before.start, before.stop, arrive, 1)
    work(before)
    put_halves(rows_ref, [keep_ref], [send_ref])


def race_half(cells_ref, factor_ref, cross_factor_ref, chunk_refs, cross_ref, rows_ref, scalar_ref, half, pumas, ages, cross):
    tracts = cells_ref.shape[0]
    cross_rows = round_up(cross + 1, 8)
    pairs = sum(ref.shape[0] for ref in chunk_refs) // pumas
    count = 2 * pairs
    stride = round_up(count, 8)
    rows_ref[...] = jnp.zeros(rows_ref.shape, F32)
    lane = lane_ids(1)

    def add_ages(t):
        factor = factor_ref[t, 0:ages]
        cells = cells_ref.at[t, pl.ds(half * count, count)]
        age_sums(cells, factor, cross_ref, t * stride, count)

    each(0, tracts, add_ages)
    every = range(tracts)
    halves = []
    for first in range(2):
        margin = [
            cross_ref[pl.ds(t * stride + first, pairs, stride=2), :]
            * cross_factor_ref[pl.ds(t * cross_rows + half * count + first, pairs, stride=2), :]
            for t in every
        ]
        halves.append([x + pltpu.roll(x, 64, 1) for x in margin])
    for t in every:
        at = pl.ds(scalar_ref[t], pairs, stride=pumas)
        rows_ref[at, :] = rows_ref[at, :] + jnp.where(lane < 64, halves[0][t], halves[1][t])
    start = 0
    for ref in chunk_refs:
        ref[...] = rows_ref[start : start + ref.shape[0], :]
        start += ref.shape[0]


def race_send_kernel(
    ids_ref, cells_ref, age_factor_ref, cross_factor_ref, target_ref,
    own_ref, other_ref, *refs, cross
):
    *chunk_refs, scaled_factor_ref, cross_ref, age_rows_ref, rows_ref, scalar_ref = refs
    ages = 2 * (target_ref.shape[1] // LANES) + target_ref.shape[1] % LANES // 64
    pairs = (ages + 1) // 2
    pumas = target_ref.shape[0]
    every = range(cells_ref.shape[0])
    load_puma_numbers(ids_ref, scalar_ref)
    factor_rows(target_ref, [own_ref], [other_ref], age_rows_ref)
    lane = lane_ids(1)
    packed = [age_rows_ref[pl.ds(scalar_ref[t], pairs, stride=pumas), :] for t in every]
    quarter = [pltpu.roll(x, 32, 1) for x in packed]
    half = [pltpu.roll(x, 64, 1) for x in packed]
    back = [pltpu.roll(x, 96, 1) for x in packed]
    for t in every:
        even = jnp.where(lane < 32, packed[t], jnp.where(lane < 96, quarter[t], half[t]))
        odd = jnp.where(lane < 32, half[t], jnp.where(lane < 96, back[t], packed[t]))
        for first, factor in enumerate((even, odd)):
            at = pl.ds(first, pairs, stride=2)
            scaled_factor_ref[t, at] = factor * age_factor_ref[t, at]
    race_half(
        cells_ref, scaled_factor_ref, cross_factor_ref, chunk_refs, cross_ref, rows_ref, scalar_ref,
        1 - half_of(lax.axis_index("tract")), pumas, ages, cross,
    )


def race_keep_kernel(ids_ref, cells_ref, factor_ref, cross_factor_ref, *refs, ages, pumas, cross):
    *chunk_refs, cross_ref, rows_ref, scalar_ref = refs
    load_puma_numbers(ids_ref, scalar_ref)
    race_half(
        cells_ref, factor_ref, cross_factor_ref, chunk_refs, cross_ref, rows_ref, scalar_ref,
        half_of(lax.axis_index("tract")), pumas, ages, cross,
    )


def final_kernel(
    ids_ref, cells_ref, scaled_factor_ref, cross_factor_ref, target_ref, *refs
):
    *chunk_refs, out_ref, result_ref, cross_ref, rows_ref, scalar_ref, sems = refs
    chunks = len(chunk_refs) // 2
    tracts, cross, ages, _ = out_ref.shape
    cross_rows = round_up(cross + 1, 8)
    cross_pairs = (cross + 1) // 2
    pumas = target_ref.shape[0]
    load_puma_numbers(ids_ref, scalar_ref)
    factor_rows(target_ref, chunk_refs[:chunks], chunk_refs[chunks:], rows_ref)
    lane = lane_ids(1)

    def unpack(t):
        base = t * cross_rows
        packed = rows_ref[pl.ds(scalar_ref[t], cross_pairs, stride=pumas), :]
        half = pltpu.roll(packed, 64, 1)
        for first, factor in enumerate(
            (jnp.where(lane < 64, packed, half), jnp.where(lane < 64, half, packed))
        ):
            at = pl.ds(base + first, cross_pairs, stride=2)
            cross_ref[at, :] = factor * cross_factor_ref[at, :]

    def scale(t):
        factor = scaled_factor_ref[t, 0:ages]
        base = t * cross_rows
        for rs in range(cross):
            result_ref[t, rs] = cells_ref[t, rs] * factor * cross_ref[pl.ds(base + rs, 1), :]

    def send(t):
        pltpu.make_async_copy(result_ref.at[t], out_ref.at[t], sems.at[t]).start()

    def step(t, carry):
        scale(t)
        unpack(t + 1)
        send(t)
        return carry

    unpack(0)
    lax.fori_loop(0, tracts - 1, step, 0)
    scale(tracts - 1)
    send(tracts - 1)
    for t in range(tracts):
        pltpu.make_async_copy(result_ref.at[t], out_ref.at[t], sems.at[t]).wait()


def call(kernel, out_shapes, in_spaces, out_spaces, scratch):
    def spec(space):
        return pl.BlockSpec(memory_space=space)

    run = pl.pallas_call(
        kernel,
        out_shape=[
            space(shape, F32) for shape, space in zip(out_shapes, out_spaces, strict=True)
        ],
        in_specs=[spec(space) for space in in_spaces],
        out_specs=[spec(space) for space in out_spaces],
        scratch_shapes=scratch,
        compiler_params=pltpu.CompilerParams(vmem_limit_bytes=40 << 20),
    )

    def placed(*args):
        return run(*map(pltpu.with_memory_space_constraint, args, in_spaces))

    return placed


def per_device(
    devices,
    table, age_sex, race_hisp, size_tenure, tenure_income, puma_age, puma_race, tract_puma,
):
    tracts, ages, races, sizes, inner = table.shape
    pumas = puma_age.shape[0]
    cross = races * sizes
    age_pairs, cross_pairs = (ages + 1) // 2, (cross + 1) // 2
    age_rows = 2 * round_up(age_pairs, 8)
    cross_rows = tracts * round_up(cross + 1, 8) + 2 * round_up(cross_pairs, 8)
    age_sum_rows, cross_sum_rows = (round_up(x, 8) * pumas for x in (age_pairs, cross_pairs))
    vmem, hbm = pltpu.VMEM, pltpu.HBM

    cells = table.transpose(0, 2, 3, 1, 4).reshape(tracts, cross, ages, inner)
    cells_scratch = pltpu.VMEM((tracts, cross, ages, inner), F32)
    cross_scratch = pltpu.VMEM((cross_rows, LANES), F32)
    copy_sems = pltpu.SemaphoreType.DMA((tracts,))
    numbers_scratch = pltpu.SMEM((tracts,), jnp.int32)

    bits = [1 << k for k in range(1, devices.bit_length() - 1)]
    orders = (bits, bits[1:] + bits[:1])

    def swap(x, partner):
        return lax.ppermute(x, "tract", [(i, partner(i)) for i in range(devices)])

    def totals(keep, send):
        keep = [x + swap(y, lambda i: i ^ 1) for x, y in zip(keep, send)]
        for step in range(len(bits)):
            keep = [x + swap(x, lambda i: i ^ orders[i.bit_count() % 2][step] ^ 1) for x in keep]
        return *keep, *[swap(x, lambda i: i ^ 1) for x in keep]

    age_half, cross_half = -(-age_pairs // 2), -(-cross_pairs // 2)
    cross_chunks = [cross_half - cross_half // 2, cross_half // 2]
    age_shape, cross_shape = (tracts, age_rows, LANES), (cross_rows, LANES)
    small = [age_sex, race_hisp, size_tenure, tenure_income]
    keep, send, age_factor, cross_factor, cells = call(
        functools.partial(rake_kernel, races=races, sizes=sizes, pumas=pumas),
        [(age_half * pumas, LANES)] * 2
        + [age_shape, cross_shape, (tracts, 4 * cross_half, ages, inner)],
        [hbm] * 6,
        [vmem] * 5,
        [
            pltpu.VMEM(age_shape, F32),
            cross_scratch,
            pltpu.VMEM((age_sum_rows, LANES), F32),
            pltpu.VMEM(age_shape, F32),
            pltpu.VMEM((tracts, round_up(races, 8), LANES), F32),
            pltpu.VMEM((tracts, round_up(sizes, 8), LANES), F32),
            numbers_scratch,
        ]
        + [pltpu.VMEM(x.shape, F32) for x in small]
        + [copy_sems, pltpu.SemaphoreType.DMA((1 + len(small),))],
    )(tract_puma, cells, *small)

    half_scratch = [
        pltpu.VMEM((tracts * round_up(2 * cross_half, 8) + 16, LANES), F32),
        pltpu.VMEM((round_up(cross_half, 8) * pumas, LANES), F32),
    ]
    chunk_shapes = [(rows * pumas, LANES) for rows in cross_chunks]
    *send, scaled_factor = call(
        functools.partial(race_send_kernel, cross=cross),
        chunk_shapes + [age_shape],
        [vmem] * 7,
        [vmem] * (len(cross_chunks) + 1),
        [half_scratch[0], pltpu.VMEM((age_sum_rows, LANES), F32), half_scratch[1], numbers_scratch],
    )(tract_puma, cells, age_factor, cross_factor, puma_age, *totals([keep], [send]))
    keep = call(
        functools.partial(race_keep_kernel, ages=ages, pumas=pumas, cross=cross),
        chunk_shapes,
        [vmem] * 4,
        [vmem] * len(cross_chunks),
        half_scratch + [numbers_scratch],
    )(tract_puma, cells, scaled_factor, cross_factor)

    out, = call(
        final_kernel,
        [(tracts, cross, ages, inner)],
        [vmem] * (5 + 2 * len(cross_chunks)),
        [hbm],
        [
            cells_scratch,
            cross_scratch,
            pltpu.VMEM((cross_sum_rows, LANES), F32),
            numbers_scratch,
            copy_sems,
        ],
    )(tract_puma, cells, scaled_factor, cross_factor, puma_race, *totals(keep, send))
    return out.reshape(tracts, races, sizes, ages, inner).transpose(0, 3, 1, 2, 4)


def solution(mesh):
    in_specs = (
        P(("grp", "tract"), None, None, None, None),
        P(("grp", "tract"), None),
        P(("grp", "tract"), None),
        P(("grp", "tract"), None),
        P(("grp", "tract"), None),
        P("grp", None),
        P("grp", None),
        P(("grp", "tract")),
    )
    out_specs = P(("grp", "tract"), None, None, None, None)
    return jax.shard_map(
        functools.partial(per_device, mesh.shape["tract"]),
        mesh=mesh, in_specs=in_specs, out_specs=out_specs, check_vma=False,
    )
```

```python
import functools

import jax
import jax.numpy as jnp
from jax import lax
from jax.experimental import pallas as pl
from jax.experimental.pallas import tpu as pltpu
from jax.sharding import PartitionSpec as P

LANES = 128
GROUP = 6
FIRST = 6
F32 = jnp.float32


def round_up(value, step):
    return -(-value // step) * step


def lane_ids(rows):
    return lax.broadcasted_iota(jnp.int32, (rows, LANES), 1)


def masked_lane_sum(value, mask):
    return jnp.sum(jnp.where(mask, value, 0.0), axis=-1, keepdims=True)


def column_of(row, rows, step, offset):
    width = row.shape[-1]
    lane = lax.broadcasted_iota(jnp.int32, (rows, width), 1)
    sub = lax.broadcasted_iota(jnp.int32, (rows, width), 0)
    return jnp.sum(jnp.where(lane == step * sub + offset, row, 0.0), axis=-1, keepdims=True)


def half_of(index):
    total = index
    for k in range(1, 16):
        total = total + lax.shift_right_logical(index, k)
    return lax.rem(total, 2)


def factor_rows(target_ref, own_refs, other_refs, rows_ref):
    pumas, columns = target_ref.shape
    half = half_of(lax.axis_index("tract"))
    half_rows = sum(ref.shape[0] for ref in own_refs)
    for refs, which in ((own_refs, half), (other_refs, 1 - half)):
        start = which * half_rows
        for ref in refs:
            rows_ref[pl.ds(pl.multiple_of(start, 8), ref.shape[0]), :] = ref[...]
            start = start + ref.shape[0]
    for first in range(0, columns, LANES):
        width = min(columns - first, LANES)
        at = slice(first // LANES * pumas, (first // LANES + 1) * pumas)
        rows_ref[at, 0:width] = target_ref[:, first : first + width] / rows_ref[at, 0:width]


def load_puma_numbers(ids_ref, scalar_ref):
    ids = ids_ref[...]
    for t in range(scalar_ref.shape[0]):
        scalar_ref[t] = ids[t]


def put_halves(rows_ref, keep_refs, send_refs):
    half = half_of(lax.axis_index("tract"))
    half_rows = sum(ref.shape[0] for ref in keep_refs)
    for refs, which in ((keep_refs, half), (send_refs, 1 - half)):
        start = which * half_rows
        for ref in refs:
            ref[...] = rows_ref[pl.ds(pl.multiple_of(start, 8), ref.shape[0]), :]
            start = start + ref.shape[0]


def merge(first, second, step):
    low = lax.rem(lax.broadcasted_iota(jnp.int32, (8, 1), 0) // step, 2) == 0
    if step == 4:
        return jnp.where(low, first, second) + pltpu.roll(jnp.where(low, second, first), 4, 0)
    return jnp.where(low, first + pltpu.roll(first, 8 - step, 0), second + pltpu.roll(second, step, 0))


def each(start, stop, body, width=3):
    def turn(i, carry):
        for k in range(width):
            body(start + width * i + k)
        return carry

    turns = (stop - start) // width
    lax.fori_loop(0, turns, turn, 0)
    for t in range(start + width * turns, stop):
        body(t)


def age_sums(cells_ref, factor, cross_ref, base, count):
    ages = factor.shape[0]

    def tile(k):
        total = None
        for at in range(0, ages, 8):
            stop = min(at + 8, ages)
            part = cells_ref[k, at:stop] * factor[at:stop]
            if stop < at + 8:
                part = jnp.concatenate([part, jnp.zeros((at + 8 - stop, LANES), F32)], axis=0)
            total = part if total is None else total + part
        return total

    for start in range(0, count, 8):
        tiles = [tile(k) for k in range(start, min(start + 8, count))]
        if len(tiles) < 8:
            for k, x in enumerate(tiles):
                cross_ref[pl.ds(base + start + k, 1), :] = jnp.sum(x, axis=0, keepdims=True)
            continue
        tiles = [merge(tiles[k], tiles[k + 4], 4) for k in range(4)]
        tiles = [merge(tiles[k], tiles[k + 2], 2) for k in range(2)]
        cross_ref[pl.ds(pl.multiple_of(base + start, 8), 8), :] = merge(tiles[0], tiles[1], 1)


def pair_sum(term, count):
    first, second = term(0), term(1)
    for k in range(2, count, 2):
        first = first + term(k)
        if k + 1 < count:
            second = second + term(k + 1)
    return first + second


def rake_kernel(
    ids_hbm, table_hbm, age_sex_hbm, race_hisp_hbm, size_tenure_hbm, tenure_income_hbm,
    keep_ref, send_ref, age_factor_ref, cross_factor_ref, cells_ref,
    sum_ref, cross_ref, rows_ref, age_target_ref, race_target_ref, size_target_ref,
    ids_ref, age_sex_ref, race_hisp_ref, size_tenure_ref, tenure_income_ref,
    sems, small_sems,
    *, races, sizes, pumas,
):
    tracts, cross, ages, _ = table_hbm.shape
    cross_rows = round_up(cross + 1, 8)
    pairs = (ages + 1) // 2
    small = [
        pltpu.make_async_copy(source, target, small_sems.at[i])
        for i, (source, target) in enumerate((
            (ids_hbm, ids_ref),
            (age_sex_hbm, age_sex_ref),
            (race_hisp_hbm, race_hisp_ref),
            (size_tenure_hbm, size_tenure_ref),
            (tenure_income_hbm, tenure_income_ref),
        ))
    ]

    def table_copy(t):
        return pltpu.make_async_copy(table_hbm.at[t], cells_ref.at[t, 0:cross], sems.at[t])

    for copy in small:
        copy.start()
    for t in range(min(FIRST, tracts)):
        table_copy(t).start()
    lane = lane_ids(1)
    sex0 = lane < 64
    hisp0 = (lane // 32) % 2 == 0
    ten0 = (lane // 16) % 2 == 0

    rows_ref[...] = jnp.zeros(rows_ref.shape, F32)
    for copy in small:
        copy.wait()
    for t in range(FIRST, tracts):
        table_copy(t).start()
    for source_ref, target_ref, rows, mask in (
        (age_sex_ref, age_target_ref, ages, sex0),
        (race_hisp_ref, race_target_ref, races, hisp0),
        (size_tenure_ref, size_target_ref, sizes, ten0),
    ):
        for t in range(tracts):
            row = source_ref[t : t + 1, :]
            target_ref[t, 0:rows] = jnp.where(
                mask, column_of(row, rows, 2, 0), column_of(row, rows, 2, 1)
            )

    def group_sums(values, mask):
        first = [masked_lane_sum(x, mask) for x in values]
        second = [masked_lane_sum(x, ~mask) for x in values]
        return [jnp.where(mask, x, y) for x, y in zip(first, second)]

    def arrive(t):
        table_copy(t).wait()
        sum_ref[t, 0:ages] = pair_sum(lambda rs: cells_ref[t, rs], cross)

    def add_ages(t):
        age_sums(cells_ref.at[t], age_factor_ref[t, 0:ages], cross_ref, t * cross_rows, cross)

    def add_scaled(t):
        base = t * cross_rows
        total = pair_sum(
            lambda rs: cells_ref[t, rs] * cross_factor_ref[pl.ds(base + rs, 1), :], cross
        )
        sum_ref[t, 0:ages] = total * age_factor_ref[t, 0:ages]
        sum_ref[t, ages : 2 * pairs] = jnp.zeros((2 * pairs - ages, LANES), F32)

    def small_steps(group):
        bases = [t * cross_rows for t in group]
        by_race = [
            sum(cross_ref[pl.ds(base + s, races, stride=sizes), :] for s in range(sizes))
            for base in bases
        ]
        race_factor = [
            race_target_ref[t, 0:races] / margin for t, margin in zip(group, group_sums(by_race, hisp0))
        ]
        by_size = [
            sum(
                cross_ref[pl.ds(base + r * sizes, sizes), :] * factor[r : r + 1]
                for r in range(races)
            )
            for base, factor in zip(bases, race_factor)
        ]
        size_factor = [
            size_target_ref[t, 0:sizes] / margin for t, margin in zip(group, group_sums(by_size, ten0))
        ]
        by_income = [jnp.sum(x * y, axis=0, keepdims=True) for x, y in zip(by_size, size_factor)]
        by_income = [x + pltpu.roll(x, 64, 1) for x in by_income]
        by_income = [x + pltpu.roll(x, 32, 1) for x in by_income]
        for i, t in enumerate(group):
            target = jnp.concatenate([tenure_income_ref[t : t + 1, :]] * 4, axis=1)
            age_factor_ref[t, 0:ages] = age_factor_ref[t, 0:ages] * (target / by_income[i])
            for r in range(races):
                cross_factor_ref[pl.ds(bases[i] + r * sizes, sizes), :] = (
                    size_factor[i] * race_factor[i][r : r + 1]
                )
            cross_factor_ref[pl.ds(bases[i] + cross, cross_rows - cross), :] = jnp.zeros(
                (cross_rows - cross, LANES), F32
            )

    def pack(group):
        even = [sum_ref[t, pl.ds(0, pairs, stride=2)] for t in group]
        odd = [sum_ref[t, pl.ds(1, pairs, stride=2)] for t in group]
        even = [x + pltpu.roll(x, 96, 1) for x in even]
        odd = [x + pltpu.roll(x, 96, 1) for x in odd]
        packed = [
            jnp.where(
                lane < 32,
                x,
                jnp.where(
                    lane < 64,
                    pltpu.roll(x, 96, 1),
                    jnp.where(lane < 96, pltpu.roll(y, 64, 1), pltpu.roll(y, 32, 1)),
                ),
            )
            for x, y in zip(even, odd)
        ]
        for t, x in zip(group, packed):
            at = pl.ds(ids_ref[t], pairs, stride=pumas)
            rows_ref[at, :] = rows_ref[at, :] + x

    def work(group):
        margin = group_sums([sum_ref[t, 0:ages] for t in group], sex0)
        for t, x in zip(group, margin):
            age_factor_ref[t, 0:ages] = age_target_ref[t, 0:ages] / x
        each(group.start, group.stop, add_ages)
        small_steps(group)
        each(group.start, group.stop, add_scaled)

    before = None
    for start in range(0, tracts, GROUP):
        if before is not None:
            work(before)
        before = range(start, min(start + GROUP, tracts))
        each(before.start, before.stop, arrive, 1)
    work(before)
    pack(range(tracts))
    put_halves(rows_ref, [keep_ref], [send_ref])


def race_half(cells_ref, factor_ref, cross_factor_ref, chunk_refs, cross_ref, rows_ref, scalar_ref, half, pumas, ages, cross):
    tracts = cells_ref.shape[0]
    cross_rows = round_up(cross + 1, 8)
    pairs = sum(ref.shape[0] for ref in chunk_refs) // pumas
    count = 2 * pairs
    stride = round_up(count, 8)
    rows_ref[...] = jnp.zeros(rows_ref.shape, F32)
    lane = lane_ids(1)

    def add_ages(t):
        factor = factor_ref[t, 0:ages]
        cells = cells_ref.at[t, pl.ds(half * count, count)]
        age_sums(cells, factor, cross_ref, t * stride, count)

    each(0, tracts, add_ages)
    every = range(tracts)
    halves = []
    for first in range(2):
        margin = [
            cross_ref[pl.ds(t * stride + first, pairs, stride=2), :]
            * cross_factor_ref[pl.ds(t * cross_rows + half * count + first, pairs, stride=2), :]
            for t in every
        ]
        halves.append([x + pltpu.roll(x, 64, 1) for x in margin])
    for t in every:
        at = pl.ds(scalar_ref[t], pairs, stride=pumas)
        rows_ref[at, :] = rows_ref[at, :] + jnp.where(lane < 64, halves[0][t], halves[1][t])
    start = 0
    for ref in chunk_refs:
        ref[...] = rows_ref[start : start + ref.shape[0], :]
        start += ref.shape[0]


def race_send_kernel(
    ids_ref, cells_ref, age_factor_ref, cross_factor_ref, target_ref,
    own_ref, other_ref, *refs, cross
):
    *chunk_refs, scaled_factor_ref, cross_ref, age_rows_ref, rows_ref, scalar_ref = refs
    ages = 2 * (target_ref.shape[1] // LANES) + target_ref.shape[1] % LANES // 64
    pairs = (ages + 1) // 2
    pumas = target_ref.shape[0]
    every = range(cells_ref.shape[0])
    load_puma_numbers(ids_ref, scalar_ref)
    factor_rows(target_ref, [own_ref], [other_ref], age_rows_ref)
    lane = lane_ids(1)
    packed = [age_rows_ref[pl.ds(scalar_ref[t], pairs, stride=pumas), :] for t in every]
    quarter = [pltpu.roll(x, 32, 1) for x in packed]
    half = [pltpu.roll(x, 64, 1) for x in packed]
    back = [pltpu.roll(x, 96, 1) for x in packed]
    for t in every:
        even = jnp.where(lane < 32, packed[t], jnp.where(lane < 96, quarter[t], half[t]))
        odd = jnp.where(lane < 32, half[t], jnp.where(lane < 96, back[t], packed[t]))
        for first, factor in enumerate((even, odd)):
            at = pl.ds(first, pairs, stride=2)
            scaled_factor_ref[t, at] = factor * age_factor_ref[t, at]
    race_half(
        cells_ref, scaled_factor_ref, cross_factor_ref, chunk_refs, cross_ref, rows_ref, scalar_ref,
        1 - half_of(lax.axis_index("tract")), pumas, ages, cross,
    )


def race_keep_kernel(ids_ref, cells_ref, factor_ref, cross_factor_ref, *refs, ages, pumas, cross):
    *chunk_refs, cross_ref, rows_ref, scalar_ref = refs
    load_puma_numbers(ids_ref, scalar_ref)
    race_half(
        cells_ref, factor_ref, cross_factor_ref, chunk_refs, cross_ref, rows_ref, scalar_ref,
        half_of(lax.axis_index("tract")), pumas, ages, cross,
    )


def final_kernel(
    ids_ref, cells_ref, scaled_factor_ref, cross_factor_ref, target_ref, *refs
):
    *chunk_refs, out_ref, result_ref, cross_ref, rows_ref, scalar_ref, sems = refs
    chunks = len(chunk_refs) // 2
    tracts, cross, ages, _ = out_ref.shape
    cross_rows = round_up(cross + 1, 8)
    cross_pairs = (cross + 1) // 2
    pumas = target_ref.shape[0]
    load_puma_numbers(ids_ref, scalar_ref)
    factor_rows(target_ref, chunk_refs[:chunks], chunk_refs[chunks:], rows_ref)
    lane = lane_ids(1)

    def unpack(t):
        base = t * cross_rows
        packed = rows_ref[pl.ds(scalar_ref[t], cross_pairs, stride=pumas), :]
        half = pltpu.roll(packed, 64, 1)
        for first, factor in enumerate(
            (jnp.where(lane < 64, packed, half), jnp.where(lane < 64, half, packed))
        ):
            at = pl.ds(base + first, cross_pairs, stride=2)
            cross_ref[at, :] = factor * cross_factor_ref[at, :]

    def scale(t):
        factor = scaled_factor_ref[t, 0:ages]
        base = t * cross_rows
        for rs in range(cross):
            result_ref[t, rs] = cells_ref[t, rs] * factor * cross_ref[pl.ds(base + rs, 1), :]

    def send(t):
        pltpu.make_async_copy(result_ref.at[t], out_ref.at[t], sems.at[t]).start()

    def step(t, carry):
        scale(t)
        unpack(t + 1)
        send(t)
        return carry

    unpack(0)
    lax.fori_loop(0, tracts - 1, step, 0)
    scale(tracts - 1)
    send(tracts - 1)
    for t in range(tracts):
        pltpu.make_async_copy(result_ref.at[t], out_ref.at[t], sems.at[t]).wait()


def call(kernel, out_shapes, in_spaces, out_spaces, scratch):
    def spec(space):
        return pl.BlockSpec(memory_space=space)

    run = pl.pallas_call(
        kernel,
        out_shape=[
            space(shape, F32) for shape, space in zip(out_shapes, out_spaces, strict=True)
        ],
        in_specs=[spec(space) for space in in_spaces],
        out_specs=[spec(space) for space in out_spaces],
        scratch_shapes=scratch,
        compiler_params=pltpu.CompilerParams(vmem_limit_bytes=40 << 20),
    )

    def placed(*args):
        return run(*map(pltpu.with_memory_space_constraint, args, in_spaces))

    return placed


def per_device(
    devices,
    table, age_sex, race_hisp, size_tenure, tenure_income, puma_age, puma_race, tract_puma,
):
    tracts, ages, races, sizes, inner = table.shape
    pumas = puma_age.shape[0]
    cross = races * sizes
    age_pairs, cross_pairs = (ages + 1) // 2, (cross + 1) // 2
    age_rows = 2 * round_up(age_pairs, 8)
    cross_rows = tracts * round_up(cross + 1, 8) + 2 * round_up(cross_pairs, 8)
    age_sum_rows, cross_sum_rows = (round_up(x, 8) * pumas for x in (age_pairs, cross_pairs))
    vmem, hbm = pltpu.VMEM, pltpu.HBM

    cells = table.transpose(0, 2, 3, 1, 4).reshape(tracts, cross, ages, inner)
    cells_scratch = pltpu.VMEM((tracts, cross, ages, inner), F32)
    cross_scratch = pltpu.VMEM((cross_rows, LANES), F32)
    copy_sems = pltpu.SemaphoreType.DMA((tracts,))
    numbers_scratch = pltpu.SMEM((tracts,), jnp.int32)

    bits = [1 << k for k in range(1, devices.bit_length() - 1)]
    orders = (bits, bits[1:] + bits[:1])

    def swap(x, partner):
        return lax.ppermute(x, "tract", [(i, partner(i)) for i in range(devices)])

    def totals(keep, send):
        keep = [x + swap(y, lambda i: i ^ 1) for x, y in zip(keep, send)]
        for step in range(len(bits)):
            keep = [x + swap(x, lambda i: i ^ orders[i.bit_count() % 2][step] ^ 1) for x in keep]
        return *keep, *[swap(x, lambda i: i ^ 1) for x in keep]

    age_half, cross_half = -(-age_pairs // 2), -(-cross_pairs // 2)
    cross_chunks = [cross_half - cross_half // 2, cross_half // 2]
    age_shape, cross_shape = (tracts, age_rows, LANES), (cross_rows, LANES)
    small = [age_sex, race_hisp, size_tenure, tenure_income]
    keep, send, age_factor, cross_factor, cells = call(
        functools.partial(rake_kernel, races=races, sizes=sizes, pumas=pumas),
        [(age_half * pumas, LANES)] * 2
        + [age_shape, cross_shape, (tracts, 4 * cross_half, ages, inner)],
        [hbm] * 6,
        [vmem] * 5,
        [
            pltpu.VMEM(age_shape, F32),
            cross_scratch,
            pltpu.VMEM((age_sum_rows, LANES), F32),
            pltpu.VMEM(age_shape, F32),
            pltpu.VMEM((tracts, round_up(races, 8), LANES), F32),
            pltpu.VMEM((tracts, round_up(sizes, 8), LANES), F32),
            numbers_scratch,
        ]
        + [pltpu.VMEM(x.shape, F32) for x in small]
        + [copy_sems, pltpu.SemaphoreType.DMA((1 + len(small),))],
    )(tract_puma, cells, *small)

    half_scratch = [
        pltpu.VMEM((tracts * round_up(2 * cross_half, 8) + 16, LANES), F32),
        pltpu.VMEM((round_up(cross_half, 8) * pumas, LANES), F32),
    ]
    chunk_shapes = [(rows * pumas, LANES) for rows in cross_chunks]
    *send, scaled_factor = call(
        functools.partial(race_send_kernel, cross=cross),
        chunk_shapes + [age_shape],
        [vmem] * 7,
        [vmem] * (len(cross_chunks) + 1),
        [half_scratch[0], pltpu.VMEM((age_sum_rows, LANES), F32), half_scratch[1], numbers_scratch],
    )(tract_puma, cells, age_factor, cross_factor, puma_age, *totals([keep], [send]))
    keep = call(
        functools.partial(race_keep_kernel, ages=ages, pumas=pumas, cross=cross),
        chunk_shapes,
        [vmem] * 4,
        [vmem] * len(cross_chunks),
        half_scratch + [numbers_scratch],
    )(tract_puma, cells, scaled_factor, cross_factor)

    out, = call(
        final_kernel,
        [(tracts, cross, ages, inner)],
        [vmem] * (5 + 2 * len(cross_chunks)),
        [hbm],
        [
            cells_scratch,
            cross_scratch,
            pltpu.VMEM((cross_sum_rows, LANES), F32),
            numbers_scratch,
            copy_sems,
        ],
    )(tract_puma, cells, scaled_factor, cross_factor, puma_race, *totals(keep, send))
    return out.reshape(tracts, races, sizes, ages, inner).transpose(0, 3, 1, 2, 4)


def solution(mesh):
    in_specs = (
        P(("grp", "tract"), None, None, None, None),
        P(("grp", "tract"), None),
        P(("grp", "tract"), None),
        P(("grp", "tract"), None),
        P(("grp", "tract"), None),
        P("grp", None),
        P("grp", None),
        P(("grp", "tract")),
    )
    out_specs = P(("grp", "tract"), None, None, None, None)
    return jax.shard_map(
        functools.partial(per_device, mesh.shape["tract"]),
        mesh=mesh, in_specs=in_specs, out_specs=out_specs, check_vma=False,
    )
```
